32 devices in a mesh: stream: 2 (over y), img: 16 (over z, x, core).
Axes of the slice: x: 2, y: 2, z: 4, core: 2. Of those that a mesh axis runs over, the one named last changes fastest.
Arguments:
- block_in: bfloat16 [2, 25088, 2016], P('stream', 'img'), may hold values from -6 to 6
- out_cotangent: bfloat16 [2, 25088, 2016], P('stream', 'img'), may hold values from -6 to 6
- pair_target: int32 [64, 3], P('img'), may hold values from 0 to 1
- entry_weight: bfloat16 [4064256], P('img'), may hold values from -0.125 to 0.125
- entry_gain: float32 [2016], replicated, may hold values from 0.1 to 1.9
- entry_shift: float32 [2016], replicated, may hold values from -3 to 3
- group_weight: bfloat16 [1016064], P('img'), may hold values from -0.25 to 0.25
- group_gain: float32 [2016], replicated, may hold values from 0.1 to 1.9
- group_shift: float32 [2016], replicated, may hold values from -3 to 3
- squeeze_weight: bfloat16 [1016064], P('img'), may hold values from -0.25 to 0.25
- squeeze_bias: float32 [504], replicated, may hold values from -3 to 3
- excite_weight: bfloat16 [1016064], P('img'), may hold values from -0.25 to 0.25
- excite_bias: float32 [2016], replicated, may hold values from -4 to 4
- exit_weight: bfloat16 [4064256], P('img'), may hold values from -0.125 to 0.125
- exit_gain: float32 [2016], replicated, may hold values from 0.1 to 1.9
- exit_shift: float32 [2016], replicated, may hold values from -3 to 3
Outputs:
- block_out: bfloat16 [2, 25088, 2016], P('stream', 'img')
- input_grad: bfloat16 [2, 25088, 2016], P('stream', 'img')
- entry_weight_gradient: float32 [4064256], P('img')
- entry_gain_gradient: float32 [2016], replicated
- entry_shift_gradient: float32 [2016], replicated
- group_weight_gradient: float32 [1016064], P('img')
- group_gain_gradient: float32 [2016], replicated
- group_shift_gradient: float32 [2016], replicated
- squeeze_weight_gradient: float32 [1016064], P('img')
- squeeze_bias_gradient: float32 [504], replicated
- excite_weight_gradient: float32 [1016064], P('img')
- excite_bias_gradient: float32 [2016], replicated
- exit_weight_gradient: float32 [4064256], P('img')
- exit_gain_gradient: float32 [2016], replicated
- exit_shift_gradient: float32 [2016], replicated
The draws below stay inside these ranges and needn't reach their ends.
Inputs may be any that keep to these rules, and one draw needn't show every extreme that they name: `pair_target`: each small crop is paired with one global crop of the same image.
All inputs are finite; a program needn't handle non-finite values.
Results may differ from the reference program's by a relative error of at most 0.011.
Values may be sent and summed in bfloat16 or wider, within the bound.
A program may use at most 576 MiB of HBM per device.

```python
import jax
import jax.numpy as jnp
from jax import lax

CHANNELS = 2016
GROUPS = 36
SQUEEZE = 504
GROUP_WIDTH = 56
GLOBAL_SIDE = 14
SMALL_SIDE = 7
GLOBAL_CROPS = 2
SMALL_CROPS = 3
IMAGE_DEV = 4
MICRO_BATCHES = 2
IMAGES = 64
IMAGE_ROWS = 392
SMALL_ROWS = 147
N_IMG = 16


def place_ends(drawn, rng, low, top_value):
    index_at = [jax.random.randint(jax.random.fold_in(rng, axis), (), 0, length) for axis, length in enumerate(drawn.shape)]
    widest = drawn.shape.index(max(drawn.shape))
    beside = index_at[:widest] + [(index_at[widest] + 1) % drawn.shape[widest]] + index_at[widest + 1:]
    return drawn.at[tuple(index_at)].set(low).at[tuple(beside)].set(top_value)


def levels(own_key, dims, shards, smallest, top_value):
    def one(axis_at, shards_of):
        heights = jax.random.uniform(jax.random.fold_in(jax.random.fold_in(own_key, 6), axis_at), (shards_of,), jnp.float32, smallest / len(shards), top_value / len(shards))
        return jnp.repeat(jnp.exp(heights), dims[axis_at] // shards_of).reshape((-1,) + (1,) * (len(dims) - axis_at - 1))

    loudness = one(*shards[0])
    for cut in shards[1:]:
        loudness = loudness * one(*cut)
    return loudness


def noise(key, shape, scale, reach, split=(), kind=jnp.bfloat16):
    level = levels(key, shape, split, -0.22, 0.18) if split else 1.0
    values = jax.random.normal(key, shape, jnp.float32) * scale * level
    return jnp.minimum(jnp.maximum(values, -reach), reach).astype(kind)


def setup_inputs(seed: int = 0) -> dict:
    key_of = jax.random.split(jax.random.key(seed), 17)
    block_in = noise(key_of[0], (2, IMAGES * IMAGE_ROWS, CHANNELS), 1.0, 6.0, ((0, 2), (1, 16)))
    out_cotangent = noise(key_of[1], (2, IMAGES * IMAGE_ROWS, CHANNELS), 1.0, 6.0, ((0, 2), (1, 16)))
    pair_target = place_ends(jax.random.randint(key_of[2], (IMAGES, SMALL_CROPS), 0, GLOBAL_CROPS), jax.random.fold_in(key_of[2], 1), 0, GLOBAL_CROPS - 1).astype(jnp.int32)
    entry_weight = noise(key_of[3], (CHANNELS * CHANNELS,), CHANNELS ** -0.5, 0.125, ((0, 16),))
    entry_gain = jnp.clip(1.0 + 0.18 * jax.random.normal(key_of[4], (CHANNELS,), jnp.float32), 0.1, 1.9)
    entry_shift = noise(key_of[5], (CHANNELS,), 0.5, 3.0, (), jnp.float32)
    group_weight = noise(key_of[6], (9 * GROUPS * GROUP_WIDTH * GROUP_WIDTH,), (9 * GROUP_WIDTH) ** -0.5, 0.25, ((0, 16),))
    group_gain = jnp.clip(1.0 + 0.18 * jax.random.normal(key_of[7], (CHANNELS,), jnp.float32), 0.1, 1.9)
    group_shift = noise(key_of[8], (CHANNELS,), 0.5, 3.0, (), jnp.float32)
    squeeze_weight = noise(key_of[9], (CHANNELS * SQUEEZE,), (CHANNELS // 4) ** -0.5, 0.25, ((0, 16),))
    squeeze_bias = noise(key_of[10], (SQUEEZE,), 0.5, 3.0, (), jnp.float32)
    excite_weight = noise(key_of[11], (SQUEEZE * CHANNELS,), SQUEEZE ** -0.5, 0.25, ((0, 16),))
    excite_bias = noise(key_of[12], (CHANNELS,), 1.0, 4.0, (), jnp.float32)
    exit_weight = noise(key_of[13], (CHANNELS * CHANNELS,), CHANNELS ** -0.5, 0.125, ((0, 16),))
    exit_gain = jnp.clip(1.0 + 0.18 * jax.random.normal(key_of[14], (CHANNELS,), jnp.float32), 0.1, 1.9)
    exit_shift = noise(key_of[15], (CHANNELS,), 0.5, 3.0, (), jnp.float32)
    return {"block_in": block_in, "out_cotangent": out_cotangent, "pair_target": pair_target, "entry_weight": entry_weight, "entry_gain": entry_gain, "entry_shift": entry_shift, "group_weight": group_weight, "group_gain": group_gain, "group_shift": group_shift, "squeeze_weight": squeeze_weight, "squeeze_bias": squeeze_bias, "excite_weight": excite_weight, "excite_bias": excite_bias, "exit_weight": exit_weight, "exit_gain": exit_gain, "exit_shift": exit_shift}


epsilon = 1e-05
pair_scale = 4.0
highest = lax.Precision.HIGHEST

@jax.custom_vjp
def low(v):
    return lax.optimization_barrier(v.astype(jnp.bfloat16)).astype(jnp.float32)

@jax.custom_vjp
def low_back(v):
    return v

def low_keep(v):
    return (low(v), None)

def low_pass(kept, grad):
    return (grad,)

def back_keep(v):
    return (v, None)

def back_low(kept, grad):
    return (low(grad),)
low.defvjp(low_keep, low_pass)
low_back.defvjp(back_keep, back_low)

def normalize(values, norm_gain, norm_shift):
    average = lax.optimization_barrier(jnp.mean(values, axis=(0, 2, 3), keepdims=True))
    squares = lax.optimization_barrier(jnp.mean(values * values, axis=(0, 2, 3), keepdims=True))
    inverse = lax.rsqrt(squares - average * average + epsilon)
    return (values - average) * inverse * norm_gain + norm_shift

def half_block(inputs, crop_side, crop_count, params):
    entry_mat, entry_gain, entry_shift, group_mat, group_gain, group_shift, squeeze_mat, squeeze_bias, excite_mat, excite_bias, exit_mat, exit_gain, exit_shift = params
    images = inputs.shape[0]
    crop_rows = crop_count * crop_side * crop_side
    grouped_shape = (N_IMG, MICRO_BATCHES, IMAGE_DEV // MICRO_BATCHES, crop_rows, CHANNELS)
    entry_act = low_back(jnp.dot(inputs.reshape(-1, CHANNELS), entry_mat, precision=highest))
    hidden = low(jax.nn.silu(normalize(entry_act.reshape(grouped_shape), entry_gain, entry_shift)))
    spatial = hidden.reshape(images * crop_count, crop_side, crop_side, GROUPS, GROUP_WIDTH)
    padded = jnp.pad(spatial, ((0, 0), (1, 1), (1, 1), (0, 0), (0, 0)))
    group_act = jnp.zeros(spatial.shape, spatial.dtype)
    for offset in range(9):
        step_down = offset // 3
        step_across = offset % 3
        window = padded[:, step_down:step_down + crop_side, step_across:step_across + crop_side]
        group_act = group_act + jnp.einsum('nyxgi,gio->nyxgo', window, group_mat[offset], precision=highest)
    group_act = low_back(group_act)
    mixed_act = jax.nn.silu(normalize(group_act.reshape(grouped_shape), group_gain, group_shift))
    crop_view = mixed_act.reshape(images, crop_count, crop_side * crop_side, CHANNELS)
    pooled = lax.optimization_barrier(jnp.mean(crop_view, axis=2))
    squeeze_in = jnp.einsum('ncd,ds->ncs', pooled, squeeze_mat, precision=highest) + squeeze_bias
    excite_in = jnp.einsum('ncs,sd->ncd', jax.nn.silu(squeeze_in), excite_mat, precision=highest) + excite_bias
    gate_vals = jax.nn.sigmoid(excite_in)[:, :, None, :]
    scaled = low(crop_view * gate_vals).reshape(-1, CHANNELS)
    exit_act = low_back(jnp.dot(scaled, exit_mat, precision=highest))
    residual = inputs.reshape(grouped_shape) + normalize(exit_act.reshape(grouped_shape), exit_gain, exit_shift)
    result = jax.nn.silu(residual).reshape(images, crop_count, crop_side * crop_side, CHANNELS)
    return (result.reshape(images, crop_rows, CHANNELS), lax.optimization_barrier(jnp.mean(result, axis=2)))

def reference(block_in, out_cotangent, pair_target, entry_weight, entry_gain, entry_shift, group_weight, group_gain, group_shift, squeeze_weight, squeeze_bias, excite_weight, excite_bias, exit_weight, exit_gain, exit_shift):
    whole = block_in.astype(jnp.float32).reshape(2, IMAGES, IMAGE_ROWS, CHANNELS)
    cotangent = out_cotangent.astype(jnp.float32).reshape(2, IMAGES, IMAGE_ROWS, CHANNELS)
    params = (entry_weight.astype(jnp.float32).reshape(CHANNELS, CHANNELS), entry_gain.astype(jnp.float32), entry_shift.astype(jnp.float32), group_weight.astype(jnp.float32).reshape(9, GROUPS, GROUP_WIDTH, GROUP_WIDTH), group_gain.astype(jnp.float32), group_shift.astype(jnp.float32), squeeze_weight.astype(jnp.float32).reshape(CHANNELS, SQUEEZE), squeeze_bias.astype(jnp.float32), excite_weight.astype(jnp.float32).reshape(SQUEEZE, CHANNELS), excite_bias.astype(jnp.float32), exit_weight.astype(jnp.float32).reshape(CHANNELS, CHANNELS), exit_gain.astype(jnp.float32), exit_shift.astype(jnp.float32))

    def joined(global_in, small_in, *weights):
        out_global, embed_global = half_block(global_in, GLOBAL_SIDE, GLOBAL_CROPS, weights)
        out_small, embed_small = half_block(small_in, SMALL_SIDE, SMALL_CROPS, weights)
        choose = (pair_target[:, :, None] == jnp.arange(GLOBAL_CROPS, dtype=jnp.int32)[None, None, :]).astype(embed_small.dtype)
        summed = jnp.einsum('njk,njd->nkd', choose, embed_small, precision=highest)
        return (out_global, out_small, pair_scale * jnp.sum(low(summed) * low(embed_global)))
    outputs, pullback = jax.vjp(joined, whole[0], whole[1][:, :SMALL_ROWS], *params)
    grads = pullback((cotangent[0], cotangent[1][:, :SMALL_ROWS], jnp.ones_like(outputs[2])))
    spacing = ((0, 0), (0, IMAGE_ROWS - SMALL_ROWS), (0, 0))
    block_out = jnp.stack([outputs[0], jnp.pad(outputs[1], spacing)]).reshape(2, IMAGES * IMAGE_ROWS, CHANNELS).astype(jnp.bfloat16)
    input_grad = jnp.stack([grads[0], jnp.pad(grads[1], spacing)]).reshape(2, IMAGES * IMAGE_ROWS, CHANNELS).astype(jnp.bfloat16)
    flats = [piece.reshape(-1).astype(jnp.float32) for piece in grads[2:]]
    return (block_out, input_grad, flats[0], flats[1], flats[2], flats[3], flats[4], flats[5], flats[6], flats[7], flats[8], flats[9], flats[10], flats[11], flats[12])
```

```python
import functools

import jax
import jax.numpy as jnp
import numpy as np
from jax import lax
from jax.experimental import pallas as pl
from jax.experimental.pallas import tpu as pltpu
from jax.sharding import PartitionSpec as P

CHANNELS = 2016
GROUPS = 36
SQUEEZE = 504
GROUP_WIDTH = 56
GLOBAL_SIDE = 14
SMALL_SIDE = 7
GLOBAL_CROPS = 2
SMALL_CROPS = 3
IMAGE_DEV = 4
MICRO_BATCHES = 2
IMAGE_ROWS = 392
SMALL_ROWS = 147
ROWS = IMAGE_DEV * IMAGE_ROWS
HALF = ROWS // MICRO_BATCHES

BLOCK = 224
LANES = 256
BLOCKS = CHANNELS // BLOCK
WIDE = BLOCKS * LANES
PADDED = 2048
OUT_BLOCKS = PADDED // LANES

IMAGE_PAD = 424
TOP = 16
CONV_ROWS = IMAGE_DEV * IMAGE_PAD
DEEP_ROWS = 1792
PAD_ROWS = TOP + DEEP_ROWS + 16
CROPS = 16
CHUNK = 126
CHUNK_PAD = 128
SHARDS = CHANNELS // CHUNK
PAIR = 2 * CHUNK

EPSILON = 1e-05
PAIR_SCALE = 4.0
MESH = pl.DeviceIdType.MESH
HBM = pl.ANY
VMEM_LIMIT = 62 * 2**20

f32 = jnp.float32
bf16 = jnp.bfloat16


def dot(a, b, dims=((1,), (0,))):
    return lax.dot_general(a, b, (dims, ((), ())), preferred_element_type=f32)


def img_barrier(size):
    stream = lax.axis_index("stream")
    me = lax.axis_index("img")
    barrier = pltpu.get_barrier_semaphore()

    def greet(step, carry):
        pl.semaphore_signal(
            barrier, inc=1, device_id=(stream, lax.rem(me + step, size)), device_id_type=MESH
        )
        return carry

    lax.fori_loop(1, size, greet, 0)
    return barrier


def send_sums(size, slot, packed, sent, got, send_sem, recv_sem):
    stream = lax.axis_index("stream")
    me = lax.axis_index("img")
    sent[slot] = packed
    got[slot, me] = packed

    def send(step, carry):
        pltpu.make_async_remote_copy(
            src_ref=sent.at[slot],
            dst_ref=got.at[slot, me],
            send_sem=send_sem.at[slot],
            recv_sem=recv_sem.at[slot],
            device_id=(stream, lax.rem(me + step, size)),
            device_id_type=MESH,
        ).start()
        return carry

    lax.fori_loop(1, size, send, 0)


def take_sums(size, slot, got, send_sem, recv_sem):
    others = got.at[slot, pl.ds(0, size - 1)]
    pltpu.make_async_copy(others, others, recv_sem.at[slot]).wait()
    pltpu.make_async_copy(others, others, send_sem.at[slot]).wait()
    total = got[slot, 0]
    for peer in range(1, size):
        total = total + got[slot, peer]
    return total


def row_count(size):
    live = jnp.where(lax.axis_index("stream") == 0, IMAGE_ROWS, SMALL_ROWS)
    return (live * (size * (IMAGE_DEV // MICRO_BATCHES))).astype(f32)


def column_sum(values):
    return jnp.sum(values, axis=0, keepdims=True)


def moments(total, micro, tile, count):
    mean = total[4 * micro + tile : 4 * micro + tile + 1] / count
    square = total[4 * micro + 2 + tile : 4 * micro + 3 + tile] / count
    return mean, lax.rsqrt(square - mean * mean + EPSILON)


def edge_masks():
    place = np.arange(PAD_ROWS) - TOP
    column = (place % 212) % 14
    left = (column != 13).astype(np.float32)
    right = (column != 0).astype(np.float32)
    both = np.stack([left, right])
    return jnp.broadcast_to(jnp.asarray(both)[:, :, None], (2, PAD_ROWS, 128)).astype(bf16)


def scatter_rows(rows_ref, pads, edges):
    on_global = lax.axis_index("stream") == 0
    inside = lax.broadcasted_iota(jnp.int32, (200, 128), 0)

    @pl.when(on_global)
    def _():
        for image in range(IMAGE_DEV):
            for tile in range(2):
                start = IMAGE_ROWS * image
                base = TOP + IMAGE_PAD * image
                first = jnp.where(inside < 196, rows_ref[tile, start : start + 200], 0.0)
                second = jnp.where(
                    inside >= 4, rows_ref[tile, start + 192 : start + 392], 0.0
                )
                for place, piece in ((base, first), (base + 208, second)):
                    here = slice(place, place + 200)
                    pads[0, tile, here] = piece
                    pads[1, tile, here] = piece * edges[0, here].astype(f32)
                    pads[2, tile, here] = piece * edges[1, here].astype(f32)

    @pl.when(jnp.logical_not(on_global))
    def _():
        for image in range(IMAGE_DEV):
            for crop in range(SMALL_CROPS):
                for line in range(SMALL_SIDE):
                    start = IMAGE_ROWS * image + 49 * crop + 7 * line
                    base = TOP + IMAGE_PAD * image + 114 * crop + 14 * line
                    for tile in range(2):
                        piece = rows_ref[tile, start : start + 7]
                        for kind in range(3):
                            pads[kind, tile, base : base + 7] = piece


def compact_rows(wide, image, rows_ref, slot):
    start = IMAGE_ROWS * image
    inside = lax.broadcasted_iota(jnp.int32, (8, 128), 0)
    for tile in range(2):
        lanes = slice(128 * tile, 128 * tile + 128)
        rows_ref[slot, tile, start : start + 192] = wide[0:192, lanes]
        rows_ref[slot, tile, start + 192 : start + 200] = jnp.where(
            inside < 4, wide[192:200, lanes], wide[208:216, lanes]
        )
        rows_ref[slot, tile, start + 200 : start + 392] = wide[216:408, lanes]


def compact_small(wide_ref, image, rows_ref, slot):
    for crop in range(SMALL_CROPS):
        for line in range(SMALL_SIDE):
            start = IMAGE_ROWS * image + 49 * crop + 7 * line
            base = 114 * crop + 14 * line
            for tile in range(2):
                rows_ref[slot, tile, start : start + 7] = wide_ref[tile, base : base + 7]


def take_result(wide, image, rows_ref, slot, wide_ref):
    on_global = lax.axis_index("stream") == 0

    @pl.when(on_global)
    def _():
        compact_rows(wide, image, rows_ref, slot)

    @pl.when(jnp.logical_not(on_global))
    def _():
        wide_ref[0] = wide[:, 0:128]
        wide_ref[1] = wide[:, 128:256]
        compact_small(wide_ref, image, rows_ref, slot)


def stack_windows(pads, windows, image, sign):
    for offset in range(9):
        down, across = offset // 3 - 1, offset % 3 - 1
        shift = sign * (14 * down + across)
        kind = (0, 2, 1)[sign * across]
        start = TOP + IMAGE_PAD * image + shift
        for tile in range(2):
            at = LANES * offset + 128 * tile
            windows[IMAGE_PAD * image : IMAGE_PAD * (image + 1), at : at + 128] = pads[
                kind, tile, start : start + IMAGE_PAD
            ].astype(bf16)


def same_group(rows, lanes):
    row_group = lax.broadcasted_iota(jnp.int32, (rows, lanes), 0) // GROUP_WIDTH
    lane_group = lax.broadcasted_iota(jnp.int32, (rows, lanes), 1) // GROUP_WIDTH
    return row_group == lane_group


def entry_kernel(
    size,
    x_ref,
    weight_ref,
    conv_ref,
    param_ref,
    pool_ref,
    edges,
    fold_ref,
    act_out,
    turned_out,
    group_out,
    mixed_out,
    pooled_out,
    total_out,
    first_rows,
    second_rows,
    rows_ref,
    pads,
    windows,
    wide_ref,
    full_ref,
    sent,
    got,
    send_sem,
    recv_sem,
):
    step = pl.program_id(0)
    count = row_count(size)

    @pl.when(step == 0)
    def _():
        barrier = img_barrier(size)
        pads[...] = jnp.zeros_like(pads)
        full_ref[...] = jnp.zeros_like(full_ref)
        second_rows[...] = jnp.zeros_like(second_rows)
        pl.semaphore_wait(barrier, size - 1)

    @pl.when(step < BLOCKS)
    def _():
        slot = lax.rem(step, 2)
        parts = []
        for micro in range(MICRO_BATCHES):
            here = slice(HALF * micro, HALF * (micro + 1))
            act = dot(x_ref[here], weight_ref[...])
            act_out[here] = act
            for tile in range(2):
                first_rows[slot, tile, here] = act[:, 128 * tile : 128 * tile + 128]
            plain = column_sum(act)
            square = column_sum(act * act)
            parts += [plain[:, :128], plain[:, 128:], square[:, :128], square[:, 128:]]
        send_sums(size, step, jnp.concatenate(parts), sent, got, send_sem, recv_sem)

    @pl.when((step >= 1) & (step < BLOCKS + 1))
    def _():
        block = step - 1
        slot = lax.rem(block, 2)
        total = take_sums(size, block, got, send_sem, recv_sem)
        total_out[block, 0] = total
        param = param_ref[block]
        for micro in range(MICRO_BATCHES):
            here = slice(HALF * micro, HALF * (micro + 1))
            for tile in range(2):
                mean, inverse = moments(total, micro, tile, count)
                scale = 0.5 * inverse * param[tile : tile + 1]
                shift = 0.5 * param[2 + tile : 3 + tile] - mean * scale
                half = first_rows[slot, tile, here] * scale + shift
                rows_ref[tile, here] = half + half * jnp.tanh(half)
        scatter_rows(rows_ref, pads, edges)
        for tile in range(2):
            turned_out[0, 128 * tile : 128 * tile + 128] = pads[
                0, tile, TOP : TOP + DEEP_ROWS
            ].T.astype(bf16)
        same = same_group(BLOCK, LANES)
        for offset in range(9):
            full = dot(conv_ref[offset], fold_ref[...])
            full_ref[LANES * offset : LANES * offset + BLOCK] = jnp.where(
                same, full, 0.0
            ).astype(bf16)
        for image in range(IMAGE_DEV):
            stack_windows(pads, windows, image, 1)
            here = slice(IMAGE_PAD * image, IMAGE_PAD * (image + 1))
            wide = dot(windows[here], full_ref[...])
            take_result(wide, image, second_rows, slot, wide_ref)
        parts = []
        for micro in range(MICRO_BATCHES):
            here = slice(HALF * micro, HALF * (micro + 1))
            acts = [second_rows[slot, tile, here] for tile in range(2)]
            parts += [column_sum(act) for act in acts]
            parts += [column_sum(act * act) for act in acts]
        send_sums(
            size, BLOCKS + block, jnp.concatenate(parts), sent, got, send_sem, recv_sem
        )

    @pl.when(step >= 2)
    def _():
        block = step - 2
        slot = lax.rem(block, 2)
        total = take_sums(size, BLOCKS + block, got, send_sem, recv_sem)
        total_out[block, 1] = total
        param = param_ref[block]
        for micro in range(MICRO_BATCHES):
            here = slice(HALF * micro, HALF * (micro + 1))
            for tile in range(2):
                lanes = slice(128 * tile, 128 * tile + 128)
                mean, inverse = moments(total, micro, tile, count)
                scale = 0.5 * inverse * param[4 + tile : 5 + tile]
                shift = 0.5 * param[6 + tile : 7 + tile] - mean * scale
                act = second_rows[slot, tile, here]
                group_out[here, lanes] = act
                half = act * scale + shift
                mixed_out[here, lanes] = (half + half * jnp.tanh(half)).astype(bf16)
        pooled_out[...] = dot(pool_ref[...], mixed_out[...])


def run_entry(size, x, weight, conv, params, pool, edges, fold):
    def whole(shape):
        return pl.BlockSpec(shape, lambda i: (0,) * len(shape), pipeline_mode=pl.Buffered(1))

    def at(lag):
        return lambda i: jnp.clip(i - lag, 0, BLOCKS - 1)

    return pl.pallas_call(
        functools.partial(entry_kernel, size),
        grid=(BLOCKS + 2,),
        out_shape=(
            jax.ShapeDtypeStruct((ROWS, WIDE), f32),
            jax.ShapeDtypeStruct((BLOCKS, LANES, DEEP_ROWS), bf16),
            jax.ShapeDtypeStruct((ROWS, WIDE), f32),
            jax.ShapeDtypeStruct((ROWS, WIDE), bf16),
            jax.ShapeDtypeStruct((CROPS, WIDE), f32),
            jax.ShapeDtypeStruct((BLOCKS, 2, 8, 128), f32),
        ),
        in_specs=[
            whole((ROWS, PADDED)),
            pl.BlockSpec((PADDED, LANES), lambda i: (0, at(0)(i))),
            pl.BlockSpec((9, BLOCK, GROUP_WIDTH), lambda i: (0, at(1)(i), 0)),
            whole((BLOCKS, 8, 128)),
            whole((CROPS, ROWS)),
            whole((2, PAD_ROWS, 128)),
            whole((GROUP_WIDTH, LANES)),
        ],
        out_specs=(
            pl.BlockSpec((ROWS, LANES), lambda i: (0, at(0)(i))),
            pl.BlockSpec((1, LANES, DEEP_ROWS), lambda i: (at(1)(i), 0, 0)),
            pl.BlockSpec((ROWS, LANES), lambda i: (0, at(2)(i))),
            pl.BlockSpec((ROWS, LANES), lambda i: (0, at(2)(i))),
            pl.BlockSpec((CROPS, LANES), lambda i: (0, at(2)(i))),
            pl.BlockSpec((BLOCKS, 2, 8, 128), lambda i: (0, 0, 0, 0)),
        ),
        scratch_shapes=[
            pltpu.VMEM((2, 2, ROWS, 128), f32),
            pltpu.VMEM((2, 2, ROWS, 128), f32),
            pltpu.VMEM((2, ROWS, 128), f32),
            pltpu.VMEM((3, 2, PAD_ROWS, 128), f32),
            pltpu.VMEM((CONV_ROWS, 9 * LANES), bf16),
            pltpu.VMEM((2, IMAGE_PAD, 128), f32),
            pltpu.VMEM((9 * LANES, LANES), bf16),
            pltpu.VMEM((2 * BLOCKS, 8, 128), f32),
            pltpu.VMEM((2 * BLOCKS, size, 8, 128), f32),
            pltpu.SemaphoreType.DMA((2 * BLOCKS,)),
            pltpu.SemaphoreType.DMA((2 * BLOCKS,)),
        ],
        name="entry",
        compiler_params=pltpu.CompilerParams(
            collective_id=1, has_side_effects=True, vmem_limit_bytes=VMEM_LIMIT
        ),
        cost_estimate=pl.CostEstimate(
            flops=2 * ROWS * WIDE * (PADDED + 9 * LANES),
            bytes_accessed=70 * 2**20,
            transcendentals=2 * ROWS * WIDE,
        ),
    )(x, weight, conv, params, pool, edges, fold)


def whole(shape):
    return pl.BlockSpec(shape, lambda i: (0,) * len(shape), pipeline_mode=pl.Buffered(1))


def columns(rows, lag, blocks):
    return pl.BlockSpec((rows, LANES), lambda i: (0, jnp.clip(i - lag, 0, blocks - 1)))


def lane_halves(values):
    return [values[:, :128], values[:, 128:]]


def exit_kernel(
    size,
    scaled_ref,
    turned_ref,
    weight_ref,
    x_ref,
    cot_ref,
    param_ref,
    pair_ref,
    spread_ref,
    live_ref,
    out_out,
    delta_out,
    residual_out,
    weight_out,
    total_out,
    normed_ref,
    slope_ref,
    pair_sent,
    pair_got,
    sent,
    got,
    send_sem,
    recv_sem,
    pair_send,
    pair_recv,
):
    step = pl.program_id(0)
    count = row_count(size)
    stream = lax.axis_index("stream")
    me = lax.axis_index("img")
    area = jnp.where(stream == 0, GLOBAL_SIDE**2, SMALL_SIDE**2).astype(f32)
    blocks = OUT_BLOCKS

    def pair_copy(block):
        return pltpu.make_async_remote_copy(
            src_ref=pair_sent.at[block],
            dst_ref=pair_got.at[block],
            send_sem=pair_send.at[block],
            recv_sem=pair_recv.at[block],
            device_id=(1 - stream, me),
            device_id_type=MESH,
        )

    @pl.when(step == 0)
    def _():
        barrier = img_barrier(size)
        pl.semaphore_signal(
            barrier, inc=1, device_id=(1 - stream, me), device_id_type=MESH
        )
        pl.semaphore_wait(barrier, size)

    @pl.when(step < blocks)
    def _():
        slot = lax.rem(step, 4)
        parts = []
        for micro in range(MICRO_BATCHES):
            here = slice(HALF * micro, HALF * (micro + 1))
            act = dot(scaled_ref[here], weight_ref[...])
            normed_ref[slot, here] = act
            parts += lane_halves(column_sum(act)) + lane_halves(column_sum(act * act))
        send_sums(size, step, jnp.concatenate(parts), sent, got, send_sem, recv_sem)

    @pl.when((step >= 1) & (step < blocks + 1))
    def _():
        block = step - 1
        slot = lax.rem(block, 4)
        total = take_sums(size, block, got, send_sem, recv_sem)
        total_out[block, 0] = total
        param = param_ref[block]
        for micro in range(MICRO_BATCHES):
            here = slice(HALF * micro, HALF * (micro + 1))
            for tile in range(2):
                lanes = slice(128 * tile, 128 * tile + 128)
                mean, inverse = moments(total, micro, tile, count)
                normed = normed_ref[slot, here, lanes] * inverse - mean * inverse
                normed_ref[slot, here, lanes] = normed
                gain = 0.5 * param[tile : tile + 1]
                shift = 0.5 * param[2 + tile : 3 + tile]
                half = 0.5 * x_ref[here, lanes].astype(f32) + (normed * gain + shift)
                bent = jnp.tanh(half)
                out_out[here, lanes] = (
                    (half + half * bent) * live_ref[here].astype(f32)
                ).astype(bf16)
                slope_ref[lax.rem(block, 3), here, lanes] = (0.5 + 0.5 * bent) * (
                    1.0 + half * (1.0 - bent)
                )
        embed = dot(pair_ref[...], out_out[...]) / area
        pair_sent[block] = embed[:8].astype(bf16).astype(f32)
        pair_copy(block).start()

    @pl.when((step >= 2) & (step < blocks + 2))
    def _():
        block = step - 2
        slot = lax.rem(block, 4)
        pair_copy(block).wait()
        partner = pair_got[block]
        partner = jnp.concatenate([partner, jnp.zeros_like(partner)]).astype(bf16)
        parts = []
        for micro in range(MICRO_BATCHES):
            here = slice(HALF * micro, HALF * (micro + 1))
            pull = dot(spread_ref[here], partner) * (PAIR_SCALE / area)
            upstream = cot_ref[here].astype(f32) + pull
            delta = upstream * slope_ref[lax.rem(block, 3), here]
            slope_ref[lax.rem(block, 3), here] = delta
            residual_out[here] = delta.astype(bf16)
            parts += lane_halves(column_sum(delta))
            parts += lane_halves(column_sum(delta * normed_ref[slot, here]))
        send_sums(
            size, blocks + block, jnp.concatenate(parts), sent, got, send_sem, recv_sem
        )

    @pl.when(step >= 3)
    def _():
        block = step - 3
        slot = lax.rem(block, 4)
        moment = total_out[block, 0]
        total = take_sums(size, blocks + block, got, send_sem, recv_sem)
        total_out[block, 1] = total
        param = param_ref[block]
        for micro in range(MICRO_BATCHES):
            here = slice(HALF * micro, HALF * (micro + 1))
            for tile in range(2):
                lanes = slice(128 * tile, 128 * tile + 128)
                delta_out[here, lanes] = norm_back(
                    slope_ref[lax.rem(block, 3), here, lanes],
                    normed_ref[slot, here, lanes],
                    moment,
                    total,
                    micro,
                    tile,
                    param[tile : tile + 1],
                    count,
                ).astype(bf16)
        weight_out[...] = dot(turned_ref[...], delta_out[...]).astype(bf16)


def norm_back(upstream, normed, moment, total, micro, tile, gain, count):
    _, inverse = moments(moment, micro, tile, count)
    scale = gain * inverse
    plain = total[4 * micro + tile : 4 * micro + tile + 1] / count
    along = total[4 * micro + 2 + tile : 4 * micro + 3 + tile] / count
    return scale * upstream - (scale * plain + normed * (scale * along))


def run_exit(size, scaled, turned, weight, x, cot, params, pair, spread, live):
    blocks = OUT_BLOCKS
    return pl.pallas_call(
        functools.partial(exit_kernel, size),
        grid=(blocks + 3,),
        out_shape=(
            jax.ShapeDtypeStruct((ROWS, CHANNELS), bf16),
            jax.ShapeDtypeStruct((ROWS, PADDED), bf16),
            jax.ShapeDtypeStruct((ROWS, PADDED), bf16),
            jax.ShapeDtypeStruct((PADDED, PADDED), bf16),
            jax.ShapeDtypeStruct((blocks, 2, 8, 128), f32),
        ),
        in_specs=[
            whole((ROWS, PADDED)),
            whole((PADDED, ROWS)),
            columns(PADDED, 0, blocks),
            columns(ROWS, 1, blocks),
            columns(ROWS, 2, blocks),
            whole((blocks, 8, 128)),
            whole((CROPS, ROWS)),
            whole((ROWS, CROPS)),
            whole((ROWS, 128)),
        ],
        out_specs=(
            columns(ROWS, 1, blocks),
            columns(ROWS, 3, blocks),
            columns(ROWS, 2, blocks),
            columns(PADDED, 3, blocks),
            pl.BlockSpec((blocks, 2, 8, 128), lambda i: (0, 0, 0, 0)),
        ),
        scratch_shapes=[
            pltpu.VMEM((4, ROWS, LANES), f32),
            pltpu.VMEM((3, ROWS, LANES), f32),
            pltpu.VMEM((blocks, 8, LANES), f32),
            pltpu.VMEM((blocks, 8, LANES), f32),
            pltpu.VMEM((2 * blocks, 8, 128), f32),
            pltpu.VMEM((2 * blocks, size, 8, 128), f32),
            pltpu.SemaphoreType.DMA((2 * blocks,)),
            pltpu.SemaphoreType.DMA((2 * blocks,)),
            pltpu.SemaphoreType.DMA((blocks,)),
            pltpu.SemaphoreType.DMA((blocks,)),
        ],
        name="exit",
        compiler_params=pltpu.CompilerParams(
            collective_id=2, has_side_effects=True, vmem_limit_bytes=VMEM_LIMIT
        ),
        cost_estimate=pl.CostEstimate(
            flops=4 * ROWS * PADDED * PADDED,
            bytes_accessed=70 * 2**20,
            transcendentals=ROWS * PADDED,
        ),
    )(scaled, turned, weight, x, cot, params, pair, spread, live)


def gate_kernel(delta_ref, weight_ref, mixed_ref, pool_ref, scaled_out, gate_out):
    block = pl.program_id(0)
    first = jnp.minimum((BLOCK * block) // CHUNK, SHARDS - 3)
    row = lax.broadcasted_iota(jnp.int32, (LANES, 3 * CHUNK_PAD), 0)
    lane = lax.broadcasted_iota(jnp.int32, (LANES, 3 * CHUNK_PAD), 1)
    channel = CHUNK * (first + lane // CHUNK_PAD) + lane % CHUNK_PAD
    pick = (channel == BLOCK * block + row) & (row < BLOCK) & (lane % CHUNK_PAD < CHUNK)
    rows = pl.ds(pl.multiple_of(CHUNK_PAD * first, CHUNK_PAD), 3 * CHUNK_PAD)
    weight = dot(jnp.where(pick, 1.0, 0.0).astype(bf16), weight_ref[rows]).astype(bf16)
    grad = dot(delta_ref[...], weight, ((1,), (1,)))
    scaled_out[...] = grad
    gate_out[...] = dot(pool_ref[...], (grad * mixed_ref[...].astype(f32)).astype(bf16))


def run_gate(delta, weight, mixed, pool):
    return pl.pallas_call(
        gate_kernel,
        grid=(BLOCKS,),
        out_shape=(
            jax.ShapeDtypeStruct((ROWS, WIDE), f32),
            jax.ShapeDtypeStruct((CROPS, WIDE), f32),
        ),
        in_specs=[
            whole((ROWS, PADDED)),
            whole((PADDED, PADDED)),
            columns(ROWS, 0, BLOCKS),
            whole((CROPS, ROWS)),
        ],
        out_specs=(columns(ROWS, 0, BLOCKS), columns(CROPS, 0, BLOCKS)),
        name="gate",
        compiler_params=pltpu.CompilerParams(vmem_limit_bytes=VMEM_LIMIT),
        cost_estimate=pl.CostEstimate(
            flops=2 * ROWS * WIDE * PADDED, bytes_accessed=40 * 2**20, transcendentals=0
        ),
    )(delta, weight, mixed, pool)


def pair_lane(shape, dim):
    lane = lax.broadcasted_iota(jnp.int32, shape, dim)
    inside = lane % CHUNK_PAD
    return jnp.where(inside < CHUNK, CHUNK * (lane // CHUNK_PAD) + inside, -1)


def one_hot(match):
    return jnp.where(match, 1.0, 0.0).astype(bf16)


def prepare_kernel(x_ref, chunk_out, turned_out):
    pair = pl.program_id(0)
    depth = 384
    first = (PAIR * pair) // 128
    lanes = pl.ds(pl.multiple_of(128 * first, 128), depth)
    source = 128 * first - PAIR * pair
    there = lax.broadcasted_iota(jnp.int32, (depth, LANES), 0) + source
    pick = one_hot(there == pair_lane((depth, LANES), 1))
    chunk_out[...] = dot(x_ref[:, lanes], pick).astype(bf16)
    there = lax.broadcasted_iota(jnp.int32, (LANES, depth), 1) + source
    pick = one_hot(there == pair_lane((LANES, depth), 0))
    turned_out[...] = dot(pick, x_ref[:, lanes], ((1,), (1,))).astype(bf16)


def run_prepare(x):
    return pl.pallas_call(
        prepare_kernel,
        grid=(OUT_BLOCKS,),
        out_shape=(
            jax.ShapeDtypeStruct((ROWS, PADDED), bf16),
            jax.ShapeDtypeStruct((PADDED, ROWS), bf16),
        ),
        in_specs=[whole((ROWS, PADDED))],
        out_specs=(columns(ROWS, 0, OUT_BLOCKS), pl.BlockSpec((LANES, ROWS), lambda i: (i, 0))),
        name="prepare",
        compiler_params=pltpu.CompilerParams(vmem_limit_bytes=VMEM_LIMIT),
        cost_estimate=pl.CostEstimate(
            flops=4 * ROWS * 384 * PADDED, bytes_accessed=20 * 2**20, transcendentals=0
        ),
    )(x)


def scale_kernel(mixed_ref, gates_ref, spread_ref, scaled_out, turned_out, scaled):
    step = pl.program_id(0)

    @pl.when(step < BLOCKS)
    def _():
        gate = dot(spread_ref[...], gates_ref[...])
        lanes = pl.ds(pl.multiple_of(LANES * step, LANES), LANES)
        scaled[:, lanes] = (mixed_ref[...].astype(f32) * gate).astype(bf16)

    @pl.when(step >= BLOCKS)
    def _():
        pair = step - BLOCKS
        depth = 512
        start = PAIR * pair
        first = jnp.minimum((start + (LANES - BLOCK) * (start // BLOCK)) // 128, WIDE // 128 - 4)
        lanes = pl.ds(pl.multiple_of(128 * first, 128), depth)

        def pick(shape, dim):
            inside = pair_lane(shape, dim)
            channel = start + inside
            place = channel + (LANES - BLOCK) * (channel // BLOCK) - 128 * first
            there = lax.broadcasted_iota(jnp.int32, shape, 1 - dim)
            return one_hot((there == place) & (inside >= 0))

        scaled_out[...] = dot(scaled[:, lanes], pick((depth, LANES), 1)).astype(bf16)
        turned_out[...] = dot(pick((LANES, depth), 0), scaled[:, lanes], ((1,), (1,))).astype(
            bf16
        )


def run_scale(mixed, gates, spread):
    def pair(i):
        return jnp.maximum(i - BLOCKS, 0)

    return pl.pallas_call(
        scale_kernel,
        grid=(BLOCKS + OUT_BLOCKS,),
        out_shape=(
            jax.ShapeDtypeStruct((ROWS, PADDED), bf16),
            jax.ShapeDtypeStruct((PADDED, ROWS), bf16),
        ),
        in_specs=[
            columns(ROWS, 0, BLOCKS),
            columns(2 * CROPS, 0, BLOCKS),
            whole((ROWS, 2 * CROPS)),
        ],
        out_specs=(
            pl.BlockSpec((ROWS, LANES), lambda i: (0, pair(i))),
            pl.BlockSpec((LANES, ROWS), lambda i: (pair(i), 0)),
        ),
        scratch_shapes=[pltpu.VMEM((ROWS, WIDE), bf16)],
        name="scale",
        compiler_params=pltpu.CompilerParams(vmem_limit_bytes=VMEM_LIMIT),
        cost_estimate=pl.CostEstimate(
            flops=4 * ROWS * 512 * PADDED, bytes_accessed=30 * 2**20, transcendentals=0
        ),
    )(mixed, gates, spread)


def back_kernel(
    size,
    grad_ref,
    group_ref,
    gates_ref,
    spread_ref,
    act_ref,
    turned_ref,
    conv_ref,
    x_turned_ref,
    param_ref,
    moment_ref,
    edges,
    fold_ref,
    delta_out,
    weight_out,
    conv_out,
    total_out,
    normed_two,
    delta_two,
    normed_one,
    delta_one,
    rows_ref,
    pads,
    windows,
    wide_ref,
    full_ref,
    sent,
    got,
    send_sem,
    recv_sem,
):
    step = pl.program_id(0)
    count = row_count(size)

    @pl.when(step == 0)
    def _():
        barrier = img_barrier(size)
        pads[...] = jnp.zeros_like(pads)
        full_ref[...] = jnp.zeros_like(full_ref)
        delta_one[...] = jnp.zeros_like(delta_one)
        windows[CONV_ROWS:] = jnp.zeros_like(windows[CONV_ROWS:])
        pl.semaphore_wait(barrier, size - 1)

    @pl.when(step < BLOCKS)
    def _():
        slot = lax.rem(step, 2)
        moment = moment_ref[step, 1]
        param = param_ref[step]
        parts = []
        for micro in range(MICRO_BATCHES):
            here = slice(HALF * micro, HALF * (micro + 1))
            sums = []
            products = []
            for tile in range(2):
                lanes = slice(128 * tile, 128 * tile + 128)
                mean, inverse = moments(moment, micro, tile, count)
                normed = group_ref[here, lanes] * inverse - mean * inverse
                gain = 0.5 * param[4 + tile : 5 + tile]
                half = normed * gain + 0.5 * param[6 + tile : 7 + tile]
                bent = jnp.tanh(half)
                slope = (0.5 + 0.5 * bent) * (1.0 + half * (1.0 - bent))
                gate = dot(spread_ref[here], gates_ref[0, :, lanes])
                pooled = dot(spread_ref[here], gates_ref[1, :, lanes])
                delta = (grad_ref[here, lanes] * gate + pooled) * slope
                normed_two[slot, tile, here] = normed
                delta_two[slot, tile, here] = delta
                sums.append(column_sum(delta))
                products.append(column_sum(delta * normed))
            parts += sums + products
        send_sums(size, step, jnp.concatenate(parts), sent, got, send_sem, recv_sem)

    @pl.when((step >= 1) & (step < BLOCKS + 1))
    def _():
        block = step - 1
        slot = lax.rem(block, 2)
        total = take_sums(size, block, got, send_sem, recv_sem)
        total_out[block, 0] = total
        param = param_ref[block]
        moment = moment_ref[block, 1]
        for micro in range(MICRO_BATCHES):
            here = slice(HALF * micro, HALF * (micro + 1))
            for tile in range(2):
                rows_ref[tile, here] = norm_back(
                    delta_two[slot, tile, here],
                    normed_two[slot, tile, here],
                    moment,
                    total,
                    micro,
                    tile,
                    param[4 + tile : 5 + tile],
                    count,
                )
        scatter_rows(rows_ref, pads, edges)
        same = same_group(LANES, BLOCK)
        for offset in range(9):
            full = dot(fold_ref[...], conv_ref[offset], ((1,), (1,)))
            full_ref[LANES * offset : LANES * (offset + 1), :BLOCK] = jnp.where(
                same, full, 0.0
            ).astype(bf16)
        for image in range(IMAGE_DEV):
            stack_windows(pads, windows, image, -1)
            here = slice(IMAGE_PAD * image, IMAGE_PAD * (image + 1))
            wide = dot(windows[here], full_ref[...])
            take_result(wide, image, delta_one, slot, wide_ref)
        same = same_group(LANES, LANES)
        for offset in range(9):
            lanes = slice(LANES * offset, LANES * (offset + 1))
            grad = dot(turned_ref[0], windows[:, lanes])
            grad = jnp.where(same, grad, 0.0).astype(bf16)
            conv_out[offset] = dot(grad, fold_ref[...])[:BLOCK].astype(bf16)
        moment = moment_ref[block, 0]
        parts = []
        for micro in range(MICRO_BATCHES):
            here = slice(HALF * micro, HALF * (micro + 1))
            sums = []
            products = []
            for tile in range(2):
                lanes = slice(128 * tile, 128 * tile + 128)
                mean, inverse = moments(moment, micro, tile, count)
                normed = act_ref[here, lanes] * inverse - mean * inverse
                gain = 0.5 * param[tile : tile + 1]
                half = normed * gain + 0.5 * param[2 + tile : 3 + tile]
                bent = jnp.tanh(half)
                slope = (0.5 + 0.5 * bent) * (1.0 + half * (1.0 - bent))
                delta = delta_one[slot, tile, here] * slope
                normed_one[slot, tile, here] = normed
                delta_one[slot, tile, here] = delta
                sums.append(column_sum(delta))
                products.append(column_sum(delta * normed))
            parts += sums + products
        send_sums(
            size, BLOCKS + block, jnp.concatenate(parts), sent, got, send_sem, recv_sem
        )

    @pl.when(step >= 2)
    def _():
        block = step - 2
        slot = lax.rem(block, 2)
        total = take_sums(size, BLOCKS + block, got, send_sem, recv_sem)
        total_out[block, 1] = total
        param = param_ref[block]
        moment = moment_ref[block, 0]
        for micro in range(MICRO_BATCHES):
            here = slice(HALF * micro, HALF * (micro + 1))
            for tile in range(2):
                delta_out[here, 128 * tile : 128 * tile + 128] = norm_back(
                    delta_one[slot, tile, here],
                    normed_one[slot, tile, here],
                    moment,
                    total,
                    micro,
                    tile,
                    param[tile : tile + 1],
                    count,
                ).astype(bf16)
        weight_out[...] = dot(x_turned_ref[...], delta_out[...]).astype(bf16)


def run_back(
    size, grad, group, gates, spread, act, turned, conv, x_turned, params, moment, edges, fold
):
    return pl.pallas_call(
        functools.partial(back_kernel, size),
        grid=(BLOCKS + 2,),
        out_shape=(
            jax.ShapeDtypeStruct((ROWS, WIDE), bf16),
            jax.ShapeDtypeStruct((PADDED, WIDE), bf16),
            jax.ShapeDtypeStruct((9, CHANNELS, GROUP_WIDTH), bf16),
            jax.ShapeDtypeStruct((BLOCKS, 2, 8, 128), f32),
        ),
        in_specs=[
            columns(ROWS, 0, BLOCKS),
            columns(ROWS, 0, BLOCKS),
            pl.BlockSpec((2, 2 * CROPS, LANES), lambda i: (0, 0, jnp.clip(i, 0, BLOCKS - 1))),
            whole((ROWS, 2 * CROPS)),
            columns(ROWS, 1, BLOCKS),
            pl.BlockSpec((1, LANES, DEEP_ROWS), lambda i: (jnp.clip(i - 1, 0, BLOCKS - 1), 0, 0)),
            pl.BlockSpec((9, BLOCK, GROUP_WIDTH), lambda i: (0, jnp.clip(i - 1, 0, BLOCKS - 1), 0)),
            whole((PADDED, ROWS)),
            whole((BLOCKS, 8, 128)),
            whole((BLOCKS, 2, 8, 128)),
            whole((2, PAD_ROWS, 128)),
            whole((LANES, GROUP_WIDTH)),
        ],
        out_specs=(
            columns(ROWS, 2, BLOCKS),
            columns(PADDED, 2, BLOCKS),
            pl.BlockSpec((9, BLOCK, GROUP_WIDTH), lambda i: (0, jnp.clip(i - 1, 0, BLOCKS - 1), 0)),
            pl.BlockSpec((BLOCKS, 2, 8, 128), lambda i: (0, 0, 0, 0)),
        ),
        scratch_shapes=[
            pltpu.VMEM((2, 2, ROWS, 128), f32),
            pltpu.VMEM((2, 2, ROWS, 128), f32),
            pltpu.VMEM((2, 2, ROWS, 128), f32),
            pltpu.VMEM((2, 2, ROWS, 128), f32),
            pltpu.VMEM((2, ROWS, 128), f32),
            pltpu.VMEM((3, 2, PAD_ROWS, 128), f32),
            pltpu.VMEM((DEEP_ROWS, 9 * LANES), bf16),
            pltpu.VMEM((2, IMAGE_PAD, 128), f32),
            pltpu.VMEM((9 * LANES, LANES), bf16),
            pltpu.VMEM((2 * BLOCKS, 8, 128), f32),
            pltpu.VMEM((2 * BLOCKS, size, 8, 128), f32),
            pltpu.SemaphoreType.DMA((2 * BLOCKS,)),
            pltpu.SemaphoreType.DMA((2 * BLOCKS,)),
        ],
        name="back",
        compiler_params=pltpu.CompilerParams(
            collective_id=3, has_side_effects=True, vmem_limit_bytes=VMEM_LIMIT
        ),
        cost_estimate=pl.CostEstimate(
            flops=2 * ROWS * WIDE * (PADDED + 18 * LANES),
            bytes_accessed=90 * 2**20,
            transcendentals=2 * ROWS * WIDE,
        ),
    )(grad, group, gates, spread, act, turned, conv, x_turned, params, moment, edges, fold)


def split(values):
    high = values.astype(bf16)
    low = (values - high.astype(f32)).astype(bf16)
    return jnp.concatenate([high, low], axis=-2)


def silu_slope(values):
    sig_vals = jax.nn.sigmoid(values)
    return sig_vals * (1.0 + values * (1.0 - sig_vals))


def wide_lanes(values):
    lead = values.shape[:-1]
    blocks = values.reshape(lead + (BLOCKS, BLOCK))
    padded = jnp.pad(blocks, ((0, 0),) * len(lead) + ((0, 0), (0, LANES - BLOCK)))
    return padded.reshape(lead + (WIDE,))


def narrow_lanes(values):
    lead = values.shape[:-1]
    return values.reshape(lead + (BLOCKS, LANES))[..., :BLOCK].reshape(lead + (CHANNELS,))


def gather(piece, width, size):
    across = -(-width // 128) * 128
    pads = ((0, CHUNK_PAD - CHUNK), (0, across - width))
    if size == SHARDS:
        piece = jnp.pad(piece.reshape(CHUNK, width), pads)
        return lax.all_gather(piece, "img", axis=0, tiled=True)
    pieces = lax.all_gather(piece, "img", axis=0, tiled=True).reshape(SHARDS, CHUNK, width)
    return jnp.pad(pieces, ((0, 0),) + pads).reshape(PADDED, across)


def scatter(grads, width, size):
    if size == SHARDS:
        part = lax.psum_scatter(grads, "img", scatter_dimension=0, tiled=True)
        part = swap_sum(part)
        return part[:CHUNK, :width].reshape(-1)
    grads = grads.reshape(SHARDS, CHUNK_PAD, -1)[:, :CHUNK, :width].reshape(-1)
    return swap_sum(lax.psum_scatter(grads, "img", scatter_dimension=0, tiled=True))


def swap_sum(part):
    other = lax.ppermute(part, "stream", [(0, 1), (1, 0)])
    return part.astype(f32) + other.astype(f32)


def chunked(values):
    lead = values.shape[:-1]
    values = values.reshape(lead + (SHARDS, CHUNK))
    values = jnp.pad(values, ((0, 0),) * len(lead) + ((0, 0), (0, CHUNK_PAD - CHUNK)))
    return values.reshape(lead + (PADDED,))


def unchunked(values):
    lead = values.shape[:-1]
    values = values.reshape(lead + (SHARDS, CHUNK_PAD))[..., :CHUNK]
    return values.reshape(lead + (CHANNELS,))


def local(
    block_in,
    out_cotangent,
    pair_target,
    entry_weight,
    entry_gain,
    entry_shift,
    group_weight,
    group_gain,
    group_shift,
    squeeze_weight,
    squeeze_bias,
    excite_weight,
    excite_bias,
    exit_weight,
    exit_gain,
    exit_shift,
):
    size = lax.axis_size("img")
    stream = lax.axis_index("stream")
    on_global = stream == 0
    positions = jnp.arange(ROWS, dtype=jnp.int32)
    image_of = positions // IMAGE_ROWS
    within = positions % IMAGE_ROWS
    live = within < jnp.where(on_global, IMAGE_ROWS, SMALL_ROWS)
    area = jnp.where(on_global, GLOBAL_SIDE**2, SMALL_SIDE**2)
    crop_of = within // area
    crop_ids = jnp.arange(CROPS, dtype=jnp.int32)
    per_image = jnp.where(on_global, GLOBAL_CROPS, SMALL_CROPS)
    pool_full = live[None] & ((image_of * per_image + crop_of)[None] == crop_ids[:, None])
    pool = pool_full.astype(bf16)
    target_rows = jnp.zeros((ROWS,), jnp.int32)
    for slot in range(SMALL_CROPS):
        target_rows = jnp.where(
            crop_of == slot, jnp.repeat(pair_target[:, slot], IMAGE_ROWS), target_rows
        )
    pair_of = image_of * GLOBAL_CROPS + jnp.where(on_global, crop_of, target_rows)
    pair = (live[None] & (pair_of[None] == crop_ids[:, None])).astype(bf16)
    live_lanes = jnp.broadcast_to(live[:, None], (ROWS, 128)).astype(bf16)
    edges = edge_masks()

    pad_out = ((0, 0), (0, PADDED - CHANNELS))
    x = jnp.pad(jnp.where(live[:, None], block_in[0], 0), pad_out)
    cot = jnp.pad(jnp.where(live[:, None], out_cotangent[0], 0), pad_out)

    if size == SHARDS:
        entry_piece = wide_lanes(entry_weight.reshape(CHUNK, CHANNELS)).reshape(-1)
        entry_mat = gather(entry_piece, WIDE, size)
    else:
        entry_mat = wide_lanes(gather(entry_weight, CHANNELS, size)[:, :CHANNELS])
    lines = group_weight.shape[0] // GROUP_WIDTH if size == SHARDS else 0
    if lines:
        lines_pad = -(-lines // 16) * 16
        piece = group_weight.reshape(lines, GROUP_WIDTH)
        piece = jnp.pad(piece, ((0, lines_pad - lines), (0, 128 - GROUP_WIDTH)))
        conv = lax.all_gather(piece, "img", axis=0, tiled=False)[:, :lines, :GROUP_WIDTH]
    else:
        conv = lax.all_gather(group_weight, "img", axis=0, tiled=True)
    conv = conv.reshape(9, CHANNELS, GROUP_WIDTH)
    squeeze_mat = gather(squeeze_weight, SQUEEZE, size)[:, :SQUEEZE]
    excite_mat = gather(excite_weight, SQUEEZE, size)[:, :SQUEEZE]
    exit_mat = gather(exit_weight, CHANNELS, size)

    def rows_of(*vectors):
        kept = [wide_lanes(vector).reshape(BLOCKS, 2, 128) for vector in vectors]
        return jnp.concatenate(kept, axis=1)

    params = rows_of(entry_gain, entry_shift, group_gain, group_shift)
    exit_params = [
        jnp.pad(vector, (0, PADDED - CHANNELS)).reshape(OUT_BLOCKS, 2, 128)
        for vector in (exit_gain, exit_shift)
    ]
    exit_params = jnp.concatenate(exit_params * 2, axis=1)

    fold = np.zeros((LANES, GROUP_WIDTH), np.float32)
    fold[np.arange(BLOCK), np.arange(BLOCK) % GROUP_WIDTH] = 1
    fold = jnp.asarray(fold, bf16)
    x_chunked, x_turned = run_prepare(x)
    act, turned, group, mixed, pooled, moment = run_entry(
        size, x_chunked, entry_mat, conv, params, pool, edges, fold.T
    )

    def small_dot(a, b, dims=((1,), (0,))):
        return lax.dot_general(
            a, b.astype(f32), (dims, ((), ())), precision=lax.Precision.HIGHEST
        )

    quarters = CHANNELS // SQUEEZE
    quarter = jnp.eye(quarters, dtype=f32)

    def to_rows(values):
        spread_out = values[None, :, :, None] * quarter[:, None, None, :]
        return chunked(spread_out.reshape(quarters * CROPS, CHANNELS))

    def to_quarters(values):
        return values.reshape(CROPS, quarters, SQUEEZE).transpose(1, 0, 2).reshape(-1, SQUEEZE)

    pooled = chunked(narrow_lanes(pooled) / area.astype(f32))
    squeeze_in = small_dot(pooled, squeeze_mat) + squeeze_bias
    squeezed = jax.nn.silu(squeeze_in)
    squeezed_rows = to_rows(squeezed)
    excite_in = small_dot(squeezed_rows, excite_mat).reshape(quarters, CROPS, SQUEEZE)
    excite_in = excite_in.transpose(1, 0, 2).reshape(CROPS, CHANNELS)
    gate = jax.nn.sigmoid(excite_in + excite_bias)
    spread = jnp.concatenate([pool.T, pool.T], axis=1)
    gate_terms = split(wide_lanes(gate))
    scaled, scaled_turned = run_scale(mixed, gate_terms, spread)

    block_out, exit_delta, residual, exit_grad, exit_total = run_exit(
        size, scaled, scaled_turned, exit_mat, x, cot, exit_params, pair, pair.T, live_lanes
    )
    exit_shard = scatter(exit_grad, CHANNELS, size)
    scaled_grad, gate_grad = run_gate(exit_delta, exit_mat, mixed, pool)

    used = crop_ids < IMAGE_DEV * per_image
    gate_grad = jnp.where(used[:, None], narrow_lanes(gate_grad), 0.0)
    excite_delta = gate_grad * gate * (1.0 - gate)
    excite_quarters = to_quarters(excite_delta)
    back_rows = unchunked(small_dot(excite_quarters, excite_mat, ((1,), (1,))))
    back_rows = back_rows.reshape(quarters, CROPS, SQUEEZE, quarters)
    squeeze_delta = jnp.sum(back_rows * quarter[:, None, None, :], axis=(0, 3))
    squeeze_delta = squeeze_delta * silu_slope(squeeze_in)
    pooled_grad = unchunked(small_dot(squeeze_delta, squeeze_mat, ((1,), (1,))))
    pooled_grad = pooled_grad / area.astype(f32)
    beside = ((0, 0), (0, 512 - SQUEEZE))
    excite_grad = small_dot(squeezed_rows, jnp.pad(excite_quarters, beside), ((0,), (0,)))
    squeeze_grad = small_dot(pooled, jnp.pad(squeeze_delta, beside), ((0,), (0,)))
    excite_shard = scatter(excite_grad.astype(bf16), SQUEEZE, size)
    squeeze_shard = scatter(squeeze_grad.astype(bf16), SQUEEZE, size)
    gates = jnp.stack([gate_terms, split(wide_lanes(pooled_grad))])
    entry_delta, entry_grad, conv_grad, totals = run_back(
        size, scaled_grad, group, gates, spread, act, turned, conv, x_turned, params,
        moment, edges, fold,
    )
    input_grad = unchunked(dot(entry_delta, entry_mat, ((1,), (1,))))
    input_grad = input_grad + residual[:, :CHANNELS].astype(f32)
    input_grad = jnp.where(live[:, None], input_grad, 0.0).astype(bf16)

    if size == SHARDS:
        part = lax.psum_scatter(entry_grad, "img", scatter_dimension=0, tiled=True)
        part = swap_sum(part)
        entry_shard = narrow_lanes(part[:CHUNK]).reshape(-1)
    else:
        entry_shard = scatter(narrow_lanes(entry_grad), CHANNELS, size)
    if lines:
        conv_grad = conv_grad.reshape(SHARDS, lines, GROUP_WIDTH)
        conv_grad = jnp.pad(
            conv_grad, ((0, 0), (0, lines_pad - lines), (0, 128 - GROUP_WIDTH))
        ).reshape(-1, 128)
        conv_part = lax.psum_scatter(conv_grad, "img", scatter_dimension=0, tiled=True)
        conv_shard = swap_sum(conv_part)[:lines, :GROUP_WIDTH].reshape(-1)
    else:
        conv_part = lax.psum_scatter(
            conv_grad.reshape(-1), "img", scatter_dimension=0, tiled=True
        )
        conv_shard = swap_sum(conv_part)
    shards = (entry_shard, conv_shard, squeeze_shard, excite_shard, exit_shard)

    def folded(kept):
        kept = kept.reshape(-1, MICRO_BATCHES, 2, LANES).sum(axis=1)
        return kept[:, 1].reshape(-1), kept[:, 0].reshape(-1)

    group_gain_grad, group_shift_grad = [narrow_lanes(v) for v in folded(totals[:, 0])]
    entry_gain_grad, entry_shift_grad = [narrow_lanes(v) for v in folded(totals[:, 1])]
    exit_gain_grad, exit_shift_grad = [v[:CHANNELS] for v in folded(exit_total[:, 1])]
    bias_sums = lax.psum(
        (jnp.sum(squeeze_delta, axis=0), jnp.sum(excite_delta, axis=0)), ("stream", "img")
    )
    smalls = lax.psum(
        (
            entry_gain_grad,
            entry_shift_grad,
            group_gain_grad,
            group_shift_grad,
            exit_gain_grad,
            exit_shift_grad,
        ),
        "stream",
    )
    return (
        block_out[None],
        input_grad[None],
        shards[0],
        smalls[0],
        smalls[1],
        shards[1],
        smalls[2],
        smalls[3],
        shards[2],
        bias_sums[0],
        shards[3],
        bias_sums[1],
        shards[4],
        smalls[4],
        smalls[5],
    )


def solution(mesh):
    return jax.shard_map(
        local,
        mesh=mesh,
        in_specs=(
            P("stream", "img", None),
            P("stream", "img", None),
            P("img", None),
            P("img"),
            P(),
            P(),
            P("img"),
            P(),
            P(),
            P("img"),
            P(),
            P("img"),
            P(),
            P("img"),
            P(),
            P(),
        ),
        out_specs=(
            P("stream", "img", None),
            P("stream", "img", None),
            P("img"),
            P(),
            P(),
            P("img"),
            P(),
            P(),
            P("img"),
            P(),
            P("img"),
            P(),
            P("img"),
            P(),
            P(),
        ),
        check_vma=False,
    )
```

```python
import functools

import jax
import jax.numpy as jnp
import numpy as np
from jax import lax
from jax.experimental import pallas as pl
from jax.experimental.pallas import tpu as pltpu
from jax.sharding import PartitionSpec as P

CHANNELS = 2016
GROUPS = 36
SQUEEZE = 504
GROUP_WIDTH = 56
GLOBAL_SIDE = 14
SMALL_SIDE = 7
GLOBAL_CROPS = 2
SMALL_CROPS = 3
IMAGE_DEV = 4
MICRO_BATCHES = 2
IMAGE_ROWS = 392
SMALL_ROWS = 147
ROWS = IMAGE_DEV * IMAGE_ROWS
HALF = ROWS // MICRO_BATCHES

BLOCK = 224
LANES = 256
BLOCKS = CHANNELS // BLOCK
WIDE = BLOCKS * LANES
PADDED = 2048
OUT_BLOCKS = PADDED // LANES

IMAGE_PAD = 424
TOP = 16
CONV_ROWS = IMAGE_DEV * IMAGE_PAD
DEEP_ROWS = 1792
PAD_ROWS = TOP + DEEP_ROWS + 16
CROPS = 16
STEP = 112
STEPS = ROWS // STEP
HALF_STEPS = HALF // STEP
CHUNK = 126
CHUNK_PAD = 128
SHARDS = CHANNELS // CHUNK
PAIR = 2 * CHUNK

EPSILON = 1e-05
PAIR_SCALE = 4.0
MESH = pl.DeviceIdType.MESH
HBM = pl.ANY
VMEM_LIMIT = 62 * 2**20

f32 = jnp.float32
bf16 = jnp.bfloat16


def dot(a, b, dims=((1,), (0,))):
    return lax.dot_general(a, b, (dims, ((), ())), preferred_element_type=f32)


def img_barrier(size):
    stream = lax.axis_index("stream")
    me = lax.axis_index("img")
    barrier = pltpu.get_barrier_semaphore()

    def greet(step, carry):
        pl.semaphore_signal(
            barrier, inc=1, device_id=(stream, lax.rem(me + step, size)), device_id_type=MESH
        )
        return carry

    lax.fori_loop(1, size, greet, 0)
    return barrier


def send_sums(size, slot, packed, sent, got, send_sem, recv_sem):
    stream = lax.axis_index("stream")
    me = lax.axis_index("img")
    sent[slot] = packed
    got[slot, me] = packed

    def send(step, carry):
        pltpu.make_async_remote_copy(
            src_ref=sent.at[slot],
            dst_ref=got.at[slot, me],
            send_sem=send_sem.at[slot],
            recv_sem=recv_sem.at[slot],
            device_id=(stream, lax.rem(me + step, size)),
            device_id_type=MESH,
        ).start()
        return carry

    lax.fori_loop(1, size, send, 0)


def take_sums(size, slot, got, send_sem, recv_sem):
    others = got.at[slot, pl.ds(0, size - 1)]
    pltpu.make_async_copy(others, others, recv_sem.at[slot]).wait()
    pltpu.make_async_copy(others, others, send_sem.at[slot]).wait()
    total = got[slot, 0]
    for peer in range(1, size):
        total = total + got[slot, peer]
    return total


def row_count(size):
    live = jnp.where(lax.axis_index("stream") == 0, IMAGE_ROWS, SMALL_ROWS)
    return (live * (size * (IMAGE_DEV // MICRO_BATCHES))).astype(f32)


def column_sum(values):
    return jnp.sum(values, axis=0, keepdims=True)


def moments(total, micro, tile, count):
    mean = total[4 * micro + tile : 4 * micro + tile + 1] / count
    square = total[4 * micro + 2 + tile : 4 * micro + 3 + tile] / count
    return mean, lax.rsqrt(square - mean * mean + EPSILON)


def edge_masks():
    column = np.arange(IMAGE_PAD) % 212 % 14
    both = np.stack([column != 13, column != 0]).astype(np.float32)
    return jnp.broadcast_to(jnp.asarray(both)[:, :, None], (2, IMAGE_PAD, 128))


def chunk_rows(chunk):
    return slice(STEP * chunk, STEP * (chunk + 1))


def add_up(pieces):
    pieces = list(pieces)
    while len(pieces) > 1:
        odd = [pieces.pop()] if len(pieces) % 2 else []
        pieces = [pieces[i] + pieces[i + 1] for i in range(0, len(pieces), 2)] + odd
    return pieces[0]


def fold_rows(values):
    return add_up(values[8 * i : 8 * i + 8] for i in range(values.shape[0] // 8))


class Sums:
    def __init__(self):
        self.parts = {}

    def add(self, micro, tile, plain, product):
        for kind, values in ((0, plain), (1, product)):
            key = (micro, kind, tile)
            self.parts.setdefault(key, []).append(fold_rows(values))

    def packed(self):
        return jnp.concatenate([column_sum(add_up(self.parts[key])) for key in sorted(self.parts)])


def put_pads(piece, place, tile, pads, edges):
    here = slice(place, place + piece.shape[0])
    inner = (place - TOP) % IMAGE_PAD
    inner = slice(inner, inner + piece.shape[0])
    pads[0, tile, here] = piece
    pads[1, tile, here] = piece * edges[0, inner]
    pads[2, tile, here] = piece * edges[1, inner]


def pad_global(load, pads, edges):
    inside = lax.broadcasted_iota(jnp.int32, (8, 128), 0)
    for image in range(IMAGE_DEV):
        base = TOP + IMAGE_PAD * image
        start = IMAGE_ROWS * image
        for tile in range(2):
            middle = load(tile, start + 192, 8)
            first = load(tile, start, 192)
            put_pads(first, base, tile, pads, edges)
            put_pads(jnp.where(inside < 4, middle, 0.0), base + 192, tile, pads, edges)
            put_pads(jnp.where(inside >= 4, middle, 0.0), base + 208, tile, pads, edges)
            second = load(tile, start + 200, 192)
            put_pads(second, base + 216, tile, pads, edges)


def small_strips():
    for image in range(IMAGE_DEV):
        for crop in range(SMALL_CROPS):
            for line in range(SMALL_SIDE):
                start = IMAGE_ROWS * image + 49 * crop + 7 * line
                yield start, IMAGE_PAD * image + 114 * crop + 14 * line


def pad_small(rows_ref, pads):
    for start, base in small_strips():
        for tile in range(2):
            piece = rows_ref[tile, start : start + 7]
            for kind in range(3):
                pads[kind, tile, TOP + base : TOP + base + 7] = piece


def unpad_small(wide_ref, rows_ref):
    for start, base in small_strips():
        for tile in range(2):
            rows_ref[tile, start : start + 7] = wide_ref[tile, base : base + 7]


def unpadded(wide_ref, tile, first, count):
    pieces = []
    at = first
    while at < first + count:
        image, inner = divmod(at, 49)
        base = IMAGE_PAD * image
        stop = 49 * image + (24 if inner < 24 else 25 if inner == 24 else 49)
        stop = min(stop, first + count)
        length = 8 * (stop - at)
        if inner == 24:
            inside = lax.broadcasted_iota(jnp.int32, (8, 128), 0)
            pieces.append(
                jnp.where(
                    inside < 4,
                    wide_ref[tile, base + 192 : base + 200],
                    wide_ref[tile, base + 208 : base + 216],
                )
            )
        else:
            start = base + 8 * inner + (0 if inner < 24 else 16)
            pieces.append(wide_ref[tile, start : start + length])
        at = stop
    return pieces[0] if len(pieces) == 1 else jnp.concatenate(pieces)


def stack_windows(pads, windows, image, sign):
    for offset in range(9):
        down, across = offset // 3 - 1, offset % 3 - 1
        shift = sign * (14 * down + across)
        kind = (0, 2, 1)[sign * across]
        start = TOP + IMAGE_PAD * image + shift
        for tile in range(2):
            at = LANES * offset + 128 * tile
            windows[IMAGE_PAD * image : IMAGE_PAD * (image + 1), at : at + 128] = pads[
                kind, tile, start : start + IMAGE_PAD
            ].astype(bf16)


def same_group(rows, lanes):
    row_group = lax.broadcasted_iota(jnp.int32, (rows, lanes), 0) // GROUP_WIDTH
    lane_group = lax.broadcasted_iota(jnp.int32, (rows, lanes), 1) // GROUP_WIDTH
    return row_group == lane_group


def entry_kernel(
    size,
    x_ref,
    weight_ref,
    conv_ref,
    param_ref,
    pool_ref,
    edges,
    fold_ref,
    act_out,
    turned_out,
    group_out,
    mixed_out,
    pooled_out,
    total_out,
    first_rows,
    second_rows,
    rows_ref,
    pads,
    windows,
    wide_ref,
    full_ref,
    sent,
    got,
    send_sem,
    recv_sem,
):
    step = pl.program_id(0)
    count = row_count(size)
    on_global = lax.axis_index("stream") == 0

    @pl.when(step == 0)
    def _():
        barrier = img_barrier(size)
        pads[...] = jnp.zeros_like(pads)
        full_ref[...] = jnp.zeros_like(full_ref)
        second_rows[...] = jnp.zeros_like(second_rows)
        pl.semaphore_wait(barrier, size - 1)

    @pl.when(step < BLOCKS)
    def _():
        slot = lax.rem(step, 2)
        for micro in range(MICRO_BATCHES):
            here = slice(HALF * micro, HALF * (micro + 1))
            act = dot(x_ref[here], weight_ref[...])
            first_rows[slot, 0, here] = act[:, :128]
            first_rows[slot, 1, here] = act[:, 128:]
        sums = Sums()
        for chunk in range(STEPS):
            here = chunk_rows(chunk)
            for tile in range(2):
                act = first_rows[slot, tile, here]
                act_out[here, 128 * tile : 128 * tile + 128] = act
                sums.add(chunk // HALF_STEPS, tile, act, act * act)
        send_sums(size, step, sums.packed(), sent, got, send_sem, recv_sem)

    @pl.when((step >= 1) & (step < BLOCKS + 1))
    def _():
        block = step - 1
        slot = lax.rem(block, 2)
        total = take_sums(size, block, got, send_sem, recv_sem)
        total_out[block, 0] = total
        param = param_ref[block]
        scales = {}
        for micro in range(MICRO_BATCHES):
            for tile in range(2):
                mean, inverse = moments(total, micro, tile, count)
                scale = 0.5 * inverse * param[tile : tile + 1]
                scales[micro, tile] = scale, 0.5 * param[2 + tile : 3 + tile] - mean * scale

        def hidden(tile, start, length):
            scale, shift = scales[start // HALF, tile]
            half = first_rows[slot, tile, start : start + length] * scale + shift
            return half + half * jnp.tanh(half)

        same = same_group(BLOCK, LANES)
        for offset in range(9):
            full = dot(conv_ref[offset], fold_ref[...])
            full_ref[LANES * offset : LANES * offset + BLOCK] = jnp.where(
                same, full, 0.0
            ).astype(bf16)

        def convolve(image, target):
            stack_windows(pads, windows, image, 1)
            here = slice(IMAGE_PAD * image, IMAGE_PAD * (image + 1))
            wide = dot(windows[here], full_ref[...])
            target[0, here] = wide[:, :128]
            target[1, here] = wide[:, 128:]

        def turn():
            for tile in range(2):
                turned_out[0, 128 * tile : 128 * tile + 128] = pads[
                    0, tile, TOP : TOP + DEEP_ROWS
                ].T.astype(bf16)

        def send(sums):
            send_sums(size, BLOCKS + block, sums.packed(), sent, got, send_sem, recv_sem)

        @pl.when(on_global)
        def _():
            pad_global(hidden, pads, edges)
            turn()
            second = second_rows.at[slot]
            for image in range(IMAGE_DEV):
                convolve(image, second)
            sums = Sums()
            for chunk in range(STEPS):
                for tile in range(2):
                    act = unpadded(second, tile, STEP // 8 * chunk, STEP // 8)
                    sums.add(chunk // HALF_STEPS, tile, act, act * act)
            send(sums)

        @pl.when(jnp.logical_not(on_global))
        def _():
            for chunk in range(STEPS):
                for tile in range(2):
                    rows_ref[tile, chunk_rows(chunk)] = hidden(tile, STEP * chunk, STEP)
            pad_small(rows_ref, pads)
            turn()
            for image in range(IMAGE_DEV):
                convolve(image, wide_ref)
            second = second_rows.at[slot]
            unpad_small(wide_ref, second)
            sums = Sums()
            for chunk in range(STEPS):
                for tile in range(2):
                    act = second[tile, chunk_rows(chunk)]
                    sums.add(chunk // HALF_STEPS, tile, act, act * act)
            send(sums)

    @pl.when(step >= 2)
    def _():
        block = step - 2
        slot = lax.rem(block, 2)
        total = take_sums(size, BLOCKS + block, got, send_sem, recv_sem)
        total_out[block, 1] = total
        param = param_ref[block]
        second = second_rows.at[slot]

        def finish(load):
            for micro in range(MICRO_BATCHES):
                for tile in range(2):
                    lanes = slice(128 * tile, 128 * tile + 128)
                    mean, inverse = moments(total, micro, tile, count)
                    scale = 0.5 * inverse * param[4 + tile : 5 + tile]
                    shift = 0.5 * param[6 + tile : 7 + tile] - mean * scale
                    for chunk in range(HALF_STEPS * micro, HALF_STEPS * (micro + 1)):
                        here = chunk_rows(chunk)
                        act = load(tile, chunk)
                        group_out[here, lanes] = act
                        half = act * scale + shift
                        mixed_out[here, lanes] = (half + half * jnp.tanh(half)).astype(bf16)

        @pl.when(on_global)
        def _():
            finish(lambda tile, chunk: unpadded(second, tile, STEP // 8 * chunk, STEP // 8))

        @pl.when(jnp.logical_not(on_global))
        def _():
            finish(lambda tile, chunk: second[tile, chunk_rows(chunk)])

        pooled_out[...] = dot(pool_ref[...], mixed_out[...])


def run_entry(size, x, weight, conv, params, pool, edges, fold):
    def whole(shape):
        return pl.BlockSpec(shape, lambda i: (0,) * len(shape), pipeline_mode=pl.Buffered(1))

    def at(lag):
        return lambda i: jnp.clip(i - lag, 0, BLOCKS - 1)

    return pl.pallas_call(
        functools.partial(entry_kernel, size),
        grid=(BLOCKS + 2,),
        out_shape=(
            jax.ShapeDtypeStruct((ROWS, WIDE), f32),
            jax.ShapeDtypeStruct((BLOCKS, LANES, DEEP_ROWS), bf16),
            jax.ShapeDtypeStruct((ROWS, WIDE), f32),
            jax.ShapeDtypeStruct((ROWS, WIDE), bf16),
            jax.ShapeDtypeStruct((CROPS, WIDE), f32),
            jax.ShapeDtypeStruct((BLOCKS, 2, 8, 128), f32),
        ),
        in_specs=[
            whole((ROWS, PADDED)),
            pl.BlockSpec((PADDED, LANES), lambda i: (0, at(0)(i))),
            pl.BlockSpec((9, BLOCK, GROUP_WIDTH), lambda i: (0, at(1)(i), 0)),
            whole((BLOCKS, 8, 128)),
            whole((CROPS, ROWS)),
            whole((2, IMAGE_PAD, 128)),
            whole((GROUP_WIDTH, LANES)),
        ],
        out_specs=(
            pl.BlockSpec((ROWS, LANES), lambda i: (0, at(0)(i))),
            pl.BlockSpec((1, LANES, DEEP_ROWS), lambda i: (at(1)(i), 0, 0)),
            pl.BlockSpec((ROWS, LANES), lambda i: (0, at(2)(i))),
            pl.BlockSpec((ROWS, LANES), lambda i: (0, at(2)(i))),
            pl.BlockSpec((CROPS, LANES), lambda i: (0, at(2)(i))),
            pl.BlockSpec((BLOCKS, 2, 8, 128), lambda i: (0, 0, 0, 0)),
        ),
        scratch_shapes=[
            pltpu.VMEM((2, 2, ROWS, 128), f32),
            pltpu.VMEM((2, 2, CONV_ROWS, 128), f32),
            pltpu.VMEM((2, ROWS, 128), f32),
            pltpu.VMEM((3, 2, PAD_ROWS, 128), f32),
            pltpu.VMEM((CONV_ROWS, 9 * LANES), bf16),
            pltpu.VMEM((2, CONV_ROWS, 128), f32),
            pltpu.VMEM((9 * LANES, LANES), bf16),
            pltpu.VMEM((2 * BLOCKS, 8, 128), f32),
            pltpu.VMEM((2 * BLOCKS, size, 8, 128), f32),
            pltpu.SemaphoreType.DMA((2 * BLOCKS,)),
            pltpu.SemaphoreType.DMA((2 * BLOCKS,)),
        ],
        name="entry",
        compiler_params=pltpu.CompilerParams(
            collective_id=1, has_side_effects=True, vmem_limit_bytes=VMEM_LIMIT
        ),
        cost_estimate=pl.CostEstimate(
            flops=2 * ROWS * WIDE * (PADDED + 9 * LANES),
            bytes_accessed=70 * 2**20,
            transcendentals=2 * ROWS * WIDE,
        ),
    )(x, weight, conv, params, pool, edges, fold)


def place():
    me = lax.axis_index("img")
    return lax.axis_index("stream"), me // 4, lax.rem(me // 2, 2), lax.rem(me, 2)


class Reducer:
    def __init__(self, refs):
        (
            self.local,
            self.core_got,
            self.plane_got,
            self.plane_sum,
            self.z_got,
            self.final,
            self.final_got,
            self.core_sem,
            self.plane_sem,
            self.z_sem,
            self.y_sem,
        ) = refs
        self.stream, self.z, self.x, self.core = place()
        self.mine = pl.ds(pl.multiple_of(64 * self.stream, 64), 64)
        self.theirs = pl.ds(pl.multiple_of(64 * (1 - self.stream), 64), 64)

    @staticmethod
    def scratch():
        return [
            pltpu.VMEM((2, 2, 2, 4, 2, 128, 128), bf16),
            pltpu.VMEM((3, 2, 4, 2, 128, 128), bf16),
            pltpu.VMEM((2, 3, 4, 2, 64, 128), bf16),
            pltpu.VMEM((2, 4, 2, 64, 128), bf16),
            pltpu.VMEM((2, 3, 2, 64, 128), bf16),
            pltpu.VMEM((2, 2, 64, 128), f32),
            pltpu.VMEM((2, 2, 64, 128), f32),
            pltpu.SemaphoreType.DMA((2, 2)),
            pltpu.SemaphoreType.DMA((2, 2, 3)),
            pltpu.SemaphoreType.DMA((2, 2, 3)),
            pltpu.SemaphoreType.DMA((2, 2)),
        ]

    COUNT = 11

    def index(self, k=0, across=0, beside=0):
        return 4 * (self.z ^ k) + 2 * (self.x ^ across) + (self.core ^ beside)

    def greet(self, barrier):
        for across in (0, 1):
            pl.semaphore_signal(
                barrier,
                inc=1,
                device_id=(1 - self.stream, self.index(0, across)),
                device_id_type=MESH,
            )
        return 2

    def core_copy(self, block):
        hold = lax.rem(block, 2)
        return pltpu.make_async_remote_copy(
            src_ref=self.local.at[hold, 1 - self.core],
            dst_ref=self.core_got.at[lax.rem(block, 3)],
            send_sem=self.core_sem.at[0, hold],
            recv_sem=self.core_sem.at[1, hold],
            device_id=(self.stream, self.index(0, 0, 1)),
            device_id_type=MESH,
        )

    def plane_copy(self, block, peer):
        hold = lax.rem(block, 2)
        x = self.x if peer == 1 else 1 - self.x
        rows = self.mine if peer == 0 else self.theirs
        stream = self.stream if peer == 0 else 1 - self.stream
        return pltpu.make_async_remote_copy(
            src_ref=self.core_got.at[lax.rem(block, 3), x, :, :, rows],
            dst_ref=self.plane_got.at[hold, peer],
            send_sem=self.plane_sem.at[0, hold, peer],
            recv_sem=self.plane_sem.at[1, hold, peer],
            device_id=(stream, self.index(0, 0 if peer == 1 else 1)),
            device_id_type=MESH,
        )

    def z_copy(self, block, k):
        hold = lax.rem(block, 2)
        return pltpu.make_async_remote_copy(
            src_ref=self.plane_sum.at[hold, self.z ^ k],
            dst_ref=self.z_got.at[hold, k - 1],
            send_sem=self.z_sem.at[0, hold, k - 1],
            recv_sem=self.z_sem.at[1, hold, k - 1],
            device_id=(self.stream, self.index(k)),
            device_id_type=MESH,
        )

    def y_copy(self, block):
        hold = lax.rem(block, 2)
        return pltpu.make_async_remote_copy(
            src_ref=self.final.at[hold],
            dst_ref=self.final_got.at[hold],
            send_sem=self.y_sem.at[0, hold],
            recv_sem=self.y_sem.at[1, hold],
            device_id=(1 - self.stream, self.index()),
            device_id_type=MESH,
        )

    def finish(self, block, put):
        hold = lax.rem(block, 2)
        self.y_copy(block).wait()
        for tile in range(2):
            put(tile, self.mine, self.final[hold, tile])
            put(tile, self.theirs, self.final_got[hold, tile])

    def after_z(self, block):
        hold = lax.rem(block, 2)
        for k in (1, 2, 3):
            self.z_copy(block, k).wait()
        for tile in range(2):
            total = self.plane_sum[hold, self.z, tile].astype(f32)
            for k in range(3):
                total = total + self.z_got[hold, k, tile].astype(f32)
            self.final[hold, tile] = total
        self.y_copy(block).start()

    def after_plane(self, block):
        hold = lax.rem(block, 2)
        ring = lax.rem(block, 3)
        for peer in range(3):
            self.plane_copy(block, peer).wait()
        for z in range(4):
            for tile in range(2):
                total = self.core_got[ring, self.x, z, tile, self.mine].astype(f32)
                for peer in range(3):
                    total = total + self.plane_got[hold, peer, z, tile].astype(f32)
                self.plane_sum[hold, z, tile] = total.astype(bf16)
        for k in (1, 2, 3):
            self.z_copy(block, k).start()

    def after_core(self, block):
        hold = lax.rem(block, 2)
        ring = lax.rem(block, 3)
        self.core_copy(block).wait()
        for x in range(2):
            for z in range(4):
                for tile in range(2):
                    total = self.core_got[ring, x, z, tile].astype(f32)
                    total = total + self.local[hold, self.core, x, z, tile].astype(f32)
                    self.core_got[ring, x, z, tile] = total.astype(bf16)
        for peer in range(3):
            self.plane_copy(block, peer).start()

    def advance(self, newest, blocks, put):
        def live(block):
            return (block >= 0) & (block < blocks)

        @pl.when(live(newest - 4))
        def _():
            self.finish(newest - 4, put)

        @pl.when(live(newest - 3))
        def _():
            self.after_z(newest - 3)

        @pl.when(live(newest - 2))
        def _():
            self.after_plane(newest - 2)

        @pl.when(live(newest - 1))
        def _():
            self.after_core(newest - 1)

    def begin(self, block, grad):
        hold = lax.rem(block, 2)
        for chunk in range(SHARDS):
            z, x, core = chunk // 4, chunk // 2 % 2, chunk % 2
            for tile in range(2):
                self.local[hold, core, x, z, tile] = grad[
                    128 * chunk : 128 * chunk + 128, 128 * tile : 128 * tile + 128
                ].astype(bf16)
        self.core_copy(block).start()


def whole(shape):
    return pl.BlockSpec(shape, lambda i: (0,) * len(shape), pipeline_mode=pl.Buffered(1))


def columns(rows, lag, blocks):
    return pl.BlockSpec((rows, LANES), lambda i: (0, jnp.clip(i - lag, 0, blocks - 1)))


def lane_halves(values):
    return [values[:, :128], values[:, 128:]]


def exit_kernel(
    size,
    scaled_ref,
    turned_ref,
    weight_ref,
    x_ref,
    cot_ref,
    param_ref,
    pair_ref,
    spread_ref,
    live_ref,
    out_out,
    delta_out,
    residual_out,
    weight_out,
    total_out,
    act_ref,
    slope_ref,
    pair_sent,
    pair_got,
    sent,
    got,
    send_sem,
    recv_sem,
    pair_send,
    pair_recv,
    *reduce_refs,
):
    step = pl.program_id(0)
    count = row_count(size)
    stream = lax.axis_index("stream")
    me = lax.axis_index("img")
    area = jnp.where(stream == 0, GLOBAL_SIDE**2, SMALL_SIDE**2).astype(f32)
    blocks = OUT_BLOCKS
    reducer = Reducer(reduce_refs) if reduce_refs else None

    def pair_copy(block):
        return pltpu.make_async_remote_copy(
            src_ref=pair_sent.at[block],
            dst_ref=pair_got.at[block],
            send_sem=pair_send.at[block],
            recv_sem=pair_recv.at[block],
            device_id=(1 - stream, me),
            device_id_type=MESH,
        )

    @pl.when(step == 0)
    def _():
        barrier = img_barrier(size)
        pl.semaphore_signal(
            barrier, inc=1, device_id=(1 - stream, me), device_id_type=MESH
        )
        pl.semaphore_wait(barrier, size + (reducer.greet(barrier) if reducer else 0))

    if reducer:

        def put(tile, rows, values):
            weight_out[rows, 128 * tile : 128 * tile + 128] = values

        reducer.advance(step - 3, blocks, put)

    @pl.when(step < blocks)
    def _():
        slot = lax.rem(step, 4)
        for micro in range(MICRO_BATCHES):
            here = slice(HALF * micro, HALF * (micro + 1))
            act_ref[slot, here] = dot(scaled_ref[here], weight_ref[...])
        sums = Sums()
        for chunk in range(STEPS):
            for tile in range(2):
                act = act_ref[slot, chunk_rows(chunk), 128 * tile : 128 * tile + 128]
                sums.add(chunk // HALF_STEPS, tile, act, act * act)
        send_sums(size, step, sums.packed(), sent, got, send_sem, recv_sem)

    @pl.when((step >= 1) & (step < blocks + 1))
    def _():
        block = step - 1
        slot = lax.rem(block, 4)
        total = take_sums(size, block, got, send_sem, recv_sem)
        total_out[block, 0] = total
        param = param_ref[block]
        for micro in range(MICRO_BATCHES):
            for tile in range(2):
                lanes = slice(128 * tile, 128 * tile + 128)
                mean, inverse = moments(total, micro, tile, count)
                scale = 0.5 * inverse * param[tile : tile + 1]
                shift = 0.5 * param[2 + tile : 3 + tile] - mean * scale
                for chunk in range(HALF_STEPS * micro, HALF_STEPS * (micro + 1)):
                    here = chunk_rows(chunk)
                    act = act_ref[slot, here, lanes]
                    half = 0.5 * x_ref[here, lanes].astype(f32) + (act * scale + shift)
                    bent = jnp.tanh(half)
                    out_out[here, lanes] = (
                        (half + half * bent) * live_ref[here].astype(f32)
                    ).astype(bf16)
                    slope_ref[lax.rem(block, 3), here, lanes] = (0.5 + 0.5 * bent) * (
                        1.0 + half * (1.0 - bent)
                    )
        embed = dot(pair_ref[...], out_out[...]) / area
        pair_sent[block] = embed[:8].astype(bf16).astype(f32)
        pair_copy(block).start()

    @pl.when((step >= 2) & (step < blocks + 2))
    def _():
        block = step - 2
        slot = lax.rem(block, 4)
        hold = lax.rem(block, 3)
        moment = total_out[block, 0]
        pair_copy(block).wait()
        partner = pair_got[block]
        partner = jnp.concatenate([partner, jnp.zeros_like(partner)]).astype(bf16)
        means = {
            (micro, tile): moments(moment, micro, tile, count)
            for micro in range(MICRO_BATCHES)
            for tile in range(2)
        }
        sums = Sums()
        for chunk in range(STEPS):
            here = chunk_rows(chunk)
            pull = dot(spread_ref[here], partner) * (PAIR_SCALE / area)
            for tile in range(2):
                lanes = slice(128 * tile, 128 * tile + 128)
                mean, inverse = means[chunk // HALF_STEPS, tile]
                upstream = cot_ref[here, lanes].astype(f32) + pull[:, lanes]
                delta = upstream * slope_ref[hold, here, lanes]
                slope_ref[hold, here, lanes] = delta
                residual_out[here, lanes] = delta.astype(bf16)
                normed = act_ref[slot, here, lanes] * inverse - mean * inverse
                sums.add(chunk // HALF_STEPS, tile, delta, delta * normed)
        send_sums(size, blocks + block, sums.packed(), sent, got, send_sem, recv_sem)

    @pl.when((step >= 3) & (step < blocks + 3))
    def _():
        block = step - 3
        slot = lax.rem(block, 4)
        hold = lax.rem(block, 3)
        moment = total_out[block, 0]
        total = take_sums(size, blocks + block, got, send_sem, recv_sem)
        total_out[block, 1] = total
        param = param_ref[block]
        for micro in range(MICRO_BATCHES):
            for tile in range(2):
                lanes = slice(128 * tile, 128 * tile + 128)
                back = norm_back(moment, total, micro, tile, param[tile : tile + 1], count)
                for chunk in range(HALF_STEPS * micro, HALF_STEPS * (micro + 1)):
                    here = chunk_rows(chunk)
                    delta_out[here, lanes] = back(
                        slope_ref[hold, here, lanes], act_ref[slot, here, lanes]
                    ).astype(bf16)
        grad = dot(turned_ref[...], delta_out[...])
        if reducer:
            reducer.begin(block, grad)
        else:
            weight_out[...] = grad.astype(bf16)


def norm_back(moment, total, micro, tile, gain, count):
    mean, inverse = moments(moment, micro, tile, count)
    scale = gain * inverse
    plain = total[4 * micro + tile : 4 * micro + tile + 1] / count
    along = scale * (total[4 * micro + 2 + tile : 4 * micro + 3 + tile] / count)
    slant = along * inverse
    level = scale * plain
    return lambda upstream, act: scale * upstream - (level + (act - mean) * slant)


def run_exit(size, scaled, turned, weight, x, cot, params, pair, spread, live):
    blocks = OUT_BLOCKS
    reduced = size == SHARDS
    return pl.pallas_call(
        functools.partial(exit_kernel, size),
        grid=(blocks + (7 if reduced else 3),),
        out_shape=(
            jax.ShapeDtypeStruct((ROWS, CHANNELS), bf16),
            jax.ShapeDtypeStruct((ROWS, PADDED), bf16),
            jax.ShapeDtypeStruct((ROWS, PADDED), bf16),
            jax.ShapeDtypeStruct((CHUNK_PAD, PADDED), f32)
            if reduced
            else jax.ShapeDtypeStruct((PADDED, PADDED), bf16),
            jax.ShapeDtypeStruct((blocks, 2, 8, 128), f32),
        ),
        in_specs=[
            whole((ROWS, PADDED)),
            whole((PADDED, ROWS)),
            columns(PADDED, 0, blocks),
            columns(ROWS, 1, blocks),
            columns(ROWS, 2, blocks),
            whole((blocks, 8, 128)),
            whole((CROPS, ROWS)),
            whole((ROWS, CROPS)),
            whole((ROWS, 128)),
        ],
        out_specs=(
            columns(ROWS, 1, blocks),
            columns(ROWS, 3, blocks),
            columns(ROWS, 2, blocks),
            columns(CHUNK_PAD, 7, blocks) if reduced else columns(PADDED, 3, blocks),
            pl.BlockSpec((blocks, 2, 8, 128), lambda i: (0, 0, 0, 0)),
        ),
        scratch_shapes=[
            pltpu.VMEM((4, ROWS, LANES), f32),
            pltpu.VMEM((3, ROWS, LANES), f32),
            pltpu.VMEM((blocks, 8, LANES), f32),
            pltpu.VMEM((blocks, 8, LANES), f32),
            pltpu.VMEM((2 * blocks, 8, 128), f32),
            pltpu.VMEM((2 * blocks, size, 8, 128), f32),
            pltpu.SemaphoreType.DMA((2 * blocks,)),
            pltpu.SemaphoreType.DMA((2 * blocks,)),
            pltpu.SemaphoreType.DMA((blocks,)),
            pltpu.SemaphoreType.DMA((blocks,)),
        ]
        + (Reducer.scratch() if reduced else []),
        name="exit",
        compiler_params=pltpu.CompilerParams(
            collective_id=2, has_side_effects=True, vmem_limit_bytes=VMEM_LIMIT
        ),
        cost_estimate=pl.CostEstimate(
            flops=4 * ROWS * PADDED * PADDED,
            bytes_accessed=70 * 2**20,
            transcendentals=ROWS * PADDED,
        ),
    )(scaled, turned, weight, x, cot, params, pair, spread, live)


def gate_kernel(delta_ref, weight_ref, mixed_ref, pool_ref, scaled_out, gate_out):
    block = pl.program_id(0)
    first = jnp.minimum((BLOCK * block) // CHUNK, SHARDS - 3)
    row = lax.broadcasted_iota(jnp.int32, (LANES, 3 * CHUNK_PAD), 0)
    lane = lax.broadcasted_iota(jnp.int32, (LANES, 3 * CHUNK_PAD), 1)
    channel = CHUNK * (first + lane // CHUNK_PAD) + lane % CHUNK_PAD
    pick = (channel == BLOCK * block + row) & (row < BLOCK) & (lane % CHUNK_PAD < CHUNK)
    rows = pl.ds(pl.multiple_of(CHUNK_PAD * first, CHUNK_PAD), 3 * CHUNK_PAD)
    weight = dot(jnp.where(pick, 1.0, 0.0).astype(bf16), weight_ref[rows]).astype(bf16)
    grad = dot(delta_ref[...], weight, ((1,), (1,)))
    scaled_out[...] = grad
    gate_out[...] = dot(pool_ref[...], (grad * mixed_ref[...].astype(f32)).astype(bf16))


def run_gate(delta, weight, mixed, pool):
    return pl.pallas_call(
        gate_kernel,
        grid=(BLOCKS,),
        out_shape=(
            jax.ShapeDtypeStruct((ROWS, WIDE), f32),
            jax.ShapeDtypeStruct((CROPS, WIDE), f32),
        ),
        in_specs=[
            whole((ROWS, PADDED)),
            whole((PADDED, PADDED)),
            columns(ROWS, 0, BLOCKS),
            whole((CROPS, ROWS)),
        ],
        out_specs=(columns(ROWS, 0, BLOCKS), columns(CROPS, 0, BLOCKS)),
        name="gate",
        compiler_params=pltpu.CompilerParams(vmem_limit_bytes=VMEM_LIMIT),
        cost_estimate=pl.CostEstimate(
            flops=2 * ROWS * WIDE * PADDED, bytes_accessed=40 * 2**20, transcendentals=0
        ),
    )(delta, weight, mixed, pool)


def pair_lane(shape, dim):
    lane = lax.broadcasted_iota(jnp.int32, shape, dim)
    inside = lane % CHUNK_PAD
    return jnp.where(inside < CHUNK, CHUNK * (lane // CHUNK_PAD) + inside, -1)


def one_hot(match):
    return jnp.where(match, 1.0, 0.0).astype(bf16)


def prepare_kernel(x_ref, chunk_out, turned_out):
    pair = pl.program_id(0)
    depth = 384
    first = (PAIR * pair) // 128
    lanes = pl.ds(pl.multiple_of(128 * first, 128), depth)
    source = 128 * first - PAIR * pair
    there = lax.broadcasted_iota(jnp.int32, (depth, LANES), 0) + source
    pick = one_hot(there == pair_lane((depth, LANES), 1))
    chunk_out[...] = dot(x_ref[:, lanes], pick).astype(bf16)
    there = lax.broadcasted_iota(jnp.int32, (LANES, depth), 1) + source
    pick = one_hot(there == pair_lane((LANES, depth), 0))
    turned_out[...] = dot(pick, x_ref[:, lanes], ((1,), (1,))).astype(bf16)


def run_prepare(x):
    return pl.pallas_call(
        prepare_kernel,
        grid=(OUT_BLOCKS,),
        out_shape=(
            jax.ShapeDtypeStruct((ROWS, PADDED), bf16),
            jax.ShapeDtypeStruct((PADDED, ROWS), bf16),
        ),
        in_specs=[whole((ROWS, PADDED))],
        out_specs=(columns(ROWS, 0, OUT_BLOCKS), pl.BlockSpec((LANES, ROWS), lambda i: (i, 0))),
        name="prepare",
        compiler_params=pltpu.CompilerParams(vmem_limit_bytes=VMEM_LIMIT),
        cost_estimate=pl.CostEstimate(
            flops=4 * ROWS * 384 * PADDED, bytes_accessed=20 * 2**20, transcendentals=0
        ),
    )(x)


def scale_kernel(mixed_ref, gates_ref, spread_ref, scaled_out, turned_out, scaled):
    step = pl.program_id(0)

    @pl.when(step < BLOCKS)
    def _():
        gate = dot(spread_ref[...], gates_ref[...])
        lanes = pl.ds(pl.multiple_of(LANES * step, LANES), LANES)
        scaled[:, lanes] = (mixed_ref[...].astype(f32) * gate).astype(bf16)

    @pl.when(step >= BLOCKS)
    def _():
        pair = step - BLOCKS
        depth = 512
        start = PAIR * pair
        first = jnp.minimum((start + (LANES - BLOCK) * (start // BLOCK)) // 128, WIDE // 128 - 4)
        lanes = pl.ds(pl.multiple_of(128 * first, 128), depth)

        def pick(shape, dim):
            inside = pair_lane(shape, dim)
            channel = start + inside
            place = channel + (LANES - BLOCK) * (channel // BLOCK) - 128 * first
            there = lax.broadcasted_iota(jnp.int32, shape, 1 - dim)
            return one_hot((there == place) & (inside >= 0))

        scaled_out[...] = dot(scaled[:, lanes], pick((depth, LANES), 1)).astype(bf16)
        turned_out[...] = dot(pick((LANES, depth), 0), scaled[:, lanes], ((1,), (1,))).astype(
            bf16
        )


def run_scale(mixed, gates, spread):
    def pair(i):
        return jnp.maximum(i - BLOCKS, 0)

    return pl.pallas_call(
        scale_kernel,
        grid=(BLOCKS + OUT_BLOCKS,),
        out_shape=(
            jax.ShapeDtypeStruct((ROWS, PADDED), bf16),
            jax.ShapeDtypeStruct((PADDED, ROWS), bf16),
        ),
        in_specs=[
            columns(ROWS, 0, BLOCKS),
            columns(2 * CROPS, 0, BLOCKS),
            whole((ROWS, 2 * CROPS)),
        ],
        out_specs=(
            pl.BlockSpec((ROWS, LANES), lambda i: (0, pair(i))),
            pl.BlockSpec((LANES, ROWS), lambda i: (pair(i), 0)),
        ),
        scratch_shapes=[pltpu.VMEM((ROWS, WIDE), bf16)],
        name="scale",
        compiler_params=pltpu.CompilerParams(vmem_limit_bytes=VMEM_LIMIT),
        cost_estimate=pl.CostEstimate(
            flops=4 * ROWS * 512 * PADDED, bytes_accessed=30 * 2**20, transcendentals=0
        ),
    )(mixed, gates, spread)


BIAS_ROWS = 24


def back_kernel(
    size,
    bias_ref,
    grad_ref,
    group_ref,
    late_group_ref,
    gates_ref,
    spread_ref,
    act_ref,
    late_act_ref,
    turned_ref,
    conv_ref,
    x_turned_ref,
    param_ref,
    moment_ref,
    edges,
    fold_ref,
    delta_out,
    weight_out,
    conv_out,
    total_out,
    bias_out,
    delta_two,
    delta_one,
    pads,
    windows,
    wide_ref,
    full_ref,
    sent,
    got,
    bias_got,
    send_sem,
    recv_sem,
    bias_sem,
    *reduce_refs,
):
    step = pl.program_id(0)
    count = row_count(size)
    on_global = lax.axis_index("stream") == 0
    reducer = Reducer(reduce_refs) if reduce_refs else None

    def bend(moment, micro, tile, param, at):
        mean, inverse = moments(moment, micro, tile, count)
        gain = 0.5 * param[at + tile : at + tile + 1]
        shift = 0.5 * param[at + 2 + tile : at + tile + 3]

        def both(act):
            normed = act * inverse - mean * inverse
            half = normed * gain + shift
            bent = jnp.tanh(half)
            return normed, (0.5 + 0.5 * bent) * (1.0 + half * (1.0 - bent))

        return both

    @pl.when(step == 0)
    def _():
        barrier = img_barrier(size)
        pads[...] = jnp.zeros_like(pads)
        full_ref[...] = jnp.zeros_like(full_ref)
        windows[CONV_ROWS:] = jnp.zeros_like(windows[CONV_ROWS:])
        greeted = reducer.greet(barrier) if reducer else 0
        pl.semaphore_wait(barrier, size - 1 + greeted)
        stream = lax.axis_index("stream")
        me = lax.axis_index("img")
        bias_got[me] = bias_ref[...]

        def send(step, carry):
            pltpu.make_async_remote_copy(
                src_ref=bias_ref,
                dst_ref=bias_got.at[me],
                send_sem=bias_sem.at[0],
                recv_sem=bias_sem.at[1],
                device_id=(stream, lax.rem(me + step, size)),
                device_id_type=MESH,
            ).start()
            return carry

        lax.fori_loop(1, size, send, 0)

    @pl.when(step == BLOCKS)
    def _():
        others = bias_got.at[pl.ds(0, size - 1)]
        pltpu.make_async_copy(others, others, bias_sem.at[0]).wait()
        pltpu.make_async_copy(others, others, bias_sem.at[1]).wait()
        total = bias_got[0]
        for peer in range(1, size):
            total = total + bias_got[peer]
        bias_out[...] = total

    if reducer:

        def put(tile, rows, values):
            weight_out[rows, 128 * tile : 128 * tile + 128] = values

        reducer.advance(step - 2, BLOCKS, put)

    @pl.when(step < BLOCKS)
    def _():
        slot = lax.rem(step, 2)
        moment = moment_ref[step, 1]
        param = param_ref[step]
        sums = Sums()
        for micro in range(MICRO_BATCHES):
            bends = [bend(moment, micro, tile, param, 4) for tile in range(2)]
            for chunk in range(HALF_STEPS * micro, HALF_STEPS * (micro + 1)):
                here = chunk_rows(chunk)
                gate = dot(spread_ref[here], gates_ref[0])
                pooled = dot(spread_ref[here], gates_ref[1])
                for tile in range(2):
                    lanes = slice(128 * tile, 128 * tile + 128)
                    normed, slope = bends[tile](group_ref[here, lanes])
                    delta = (grad_ref[here, lanes] * gate[:, lanes] + pooled[:, lanes]) * slope
                    delta_two[slot, tile, here] = delta
                    sums.add(micro, tile, delta, delta * normed)
        send_sums(size, step, sums.packed(), sent, got, send_sem, recv_sem)

    @pl.when((step >= 1) & (step < BLOCKS + 1))
    def _():
        block = step - 1
        slot = lax.rem(block, 2)
        total = take_sums(size, block, got, send_sem, recv_sem)
        total_out[block, 0] = total
        param = param_ref[block]
        moment = moment_ref[block, 1]
        backs = {
            (micro, tile): norm_back(moment, total, micro, tile, param[4 + tile : 5 + tile], count)
            for micro in range(MICRO_BATCHES)
            for tile in range(2)
        }

        def delta_rows(tile, start, length):
            here = slice(start, start + length)
            return backs[start // HALF, tile](
                delta_two[slot, tile, here], late_group_ref[here, 128 * tile : 128 * tile + 128]
            )

        same = same_group(LANES, BLOCK)
        for offset in range(9):
            full = dot(fold_ref[...], conv_ref[offset], ((1,), (1,)))
            full_ref[LANES * offset : LANES * (offset + 1), :BLOCK] = jnp.where(
                same, full, 0.0
            ).astype(bf16)

        def convolve(image):
            stack_windows(pads, windows, image, -1)
            here = slice(IMAGE_PAD * image, IMAGE_PAD * (image + 1))
            wide = dot(windows[here], full_ref[...])
            wide_ref[0, here] = wide[:, :128]
            wide_ref[1, here] = wide[:, 128:]

        moment_one = moment_ref[block, 0]

        def finish(load):
            sums = Sums()
            for micro in range(MICRO_BATCHES):
                for tile in range(2):
                    bent = bend(moment_one, micro, tile, param, 0)
                    for chunk in range(HALF_STEPS * micro, HALF_STEPS * (micro + 1)):
                        here = chunk_rows(chunk)
                        normed, slope = bent(act_ref[here, 128 * tile : 128 * tile + 128])
                        delta = load(tile, chunk) * slope
                        delta_one[slot, tile, here] = delta
                        sums.add(micro, tile, delta, delta * normed)
            send_sums(
                size, BLOCKS + block, sums.packed(), sent, got, send_sem, recv_sem
            )

        @pl.when(on_global)
        def _():
            pad_global(delta_rows, pads, edges)
            for image in range(IMAGE_DEV):
                convolve(image)
            finish(lambda tile, chunk: unpadded(wide_ref, tile, STEP // 8 * chunk, STEP // 8))

        @pl.when(jnp.logical_not(on_global))
        def _():
            rows_ref = delta_one.at[slot]
            for chunk in range(STEPS):
                for tile in range(2):
                    rows_ref[tile, chunk_rows(chunk)] = delta_rows(tile, STEP * chunk, STEP)
            pad_small(rows_ref, pads)
            for image in range(IMAGE_DEV):
                convolve(image)
            for chunk in range(STEPS):
                for tile in range(2):
                    rows_ref[tile, chunk_rows(chunk)] = jnp.zeros((STEP, 128), f32)
            unpad_small(wide_ref, rows_ref)
            finish(lambda tile, chunk: rows_ref[tile, chunk_rows(chunk)])

        for offset in range(9):
            grad = dot(turned_ref[0], windows[:, LANES * offset : LANES * (offset + 1)])
            pieces = []
            for group in range(4):
                here = slice(GROUP_WIDTH * group, GROUP_WIDTH * (group + 1))
                pieces.append(grad[here, here])
            conv_out[offset] = jnp.concatenate(pieces).astype(bf16)

    @pl.when((step >= 2) & (step < BLOCKS + 2))
    def _():
        block = step - 2
        slot = lax.rem(block, 2)
        total = take_sums(size, BLOCKS + block, got, send_sem, recv_sem)
        total_out[block, 1] = total
        param = param_ref[block]
        moment = moment_ref[block, 0]
        for micro in range(MICRO_BATCHES):
            for tile in range(2):
                lanes = slice(128 * tile, 128 * tile + 128)
                back = norm_back(moment, total, micro, tile, param[tile : tile + 1], count)
                for chunk in range(HALF_STEPS * micro, HALF_STEPS * (micro + 1)):
                    here = chunk_rows(chunk)
                    delta_out[here, lanes] = back(
                        delta_one[slot, tile, here], late_act_ref[here, lanes]
                    ).astype(bf16)
        grad = dot(x_turned_ref[...], delta_out[...])
        if reducer:
            reducer.begin(block, grad)
        else:
            weight_out[...] = grad.astype(bf16)


def run_back(
    size, bias, grad, group, gates, spread, act, turned, conv, x_turned, params, moment, edges, fold
):
    reduced = size == SHARDS
    return pl.pallas_call(
        functools.partial(back_kernel, size),
        grid=(BLOCKS + (6 if reduced else 2),),
        out_shape=(
            jax.ShapeDtypeStruct((ROWS, WIDE), bf16),
            jax.ShapeDtypeStruct((CHUNK_PAD, WIDE), f32)
            if reduced
            else jax.ShapeDtypeStruct((PADDED, WIDE), bf16),
            jax.ShapeDtypeStruct((9, CHANNELS, GROUP_WIDTH), bf16),
            jax.ShapeDtypeStruct((BLOCKS, 2, 8, 128), f32),
            jax.ShapeDtypeStruct((BIAS_ROWS, 128), f32),
        ),
        in_specs=[
            whole((BIAS_ROWS, 128)),
            columns(ROWS, 0, BLOCKS),
            columns(ROWS, 0, BLOCKS),
            columns(ROWS, 1, BLOCKS),
            pl.BlockSpec((2, 2 * CROPS, LANES), lambda i: (0, 0, jnp.clip(i, 0, BLOCKS - 1))),
            whole((ROWS, 2 * CROPS)),
            columns(ROWS, 1, BLOCKS),
            columns(ROWS, 2, BLOCKS),
            pl.BlockSpec((1, LANES, DEEP_ROWS), lambda i: (jnp.clip(i - 1, 0, BLOCKS - 1), 0, 0)),
            pl.BlockSpec((9, BLOCK, GROUP_WIDTH), lambda i: (0, jnp.clip(i - 1, 0, BLOCKS - 1), 0)),
            whole((PADDED, ROWS)),
            whole((BLOCKS, 8, 128)),
            whole((BLOCKS, 2, 8, 128)),
            whole((2, IMAGE_PAD, 128)),
            whole((LANES, GROUP_WIDTH)),
        ],
        out_specs=(
            columns(ROWS, 2, BLOCKS),
            columns(CHUNK_PAD, 6, BLOCKS) if reduced else columns(PADDED, 2, BLOCKS),
            pl.BlockSpec((9, BLOCK, GROUP_WIDTH), lambda i: (0, jnp.clip(i - 1, 0, BLOCKS - 1), 0)),
            pl.BlockSpec((BLOCKS, 2, 8, 128), lambda i: (0, 0, 0, 0)),
            pl.BlockSpec((BIAS_ROWS, 128), lambda i: (0, 0)),
        ),
        scratch_shapes=[
            pltpu.VMEM((2, 2, ROWS, 128), f32),
            pltpu.VMEM((2, 2, ROWS, 128), f32),
            pltpu.VMEM((3, 2, PAD_ROWS, 128), f32),
            pltpu.VMEM((DEEP_ROWS, 9 * LANES), bf16),
            pltpu.VMEM((2, CONV_ROWS, 128), f32),
            pltpu.VMEM((9 * LANES, LANES), bf16),
            pltpu.VMEM((2 * BLOCKS, 8, 128), f32),
            pltpu.VMEM((2 * BLOCKS, size, 8, 128), f32),
            pltpu.VMEM((size, BIAS_ROWS, 128), f32),
            pltpu.SemaphoreType.DMA((2 * BLOCKS,)),
            pltpu.SemaphoreType.DMA((2 * BLOCKS,)),
            pltpu.SemaphoreType.DMA((2,)),
        ]
        + (Reducer.scratch() if reduced else []),
        name="back",
        compiler_params=pltpu.CompilerParams(
            collective_id=3, has_side_effects=True, vmem_limit_bytes=VMEM_LIMIT
        ),
        cost_estimate=pl.CostEstimate(
            flops=2 * ROWS * WIDE * (PADDED + 18 * LANES),
            bytes_accessed=90 * 2**20,
            transcendentals=2 * ROWS * WIDE,
        ),
    )(bias, grad, group, group, gates, spread, act, act, turned, conv, x_turned, params, moment, edges, fold)


CONV_LINES = 1152


def gather_kernel(
    entry_ref,
    conv_ref,
    x_ref,
    entry_out,
    conv_out,
    chunk_out,
    turned_out,
    x_rows,
    chunk_rows_ref,
    turned_rows,
    send_sem,
    recv_sem,
    local_sem,
    store_sem,
):
    stream, z, x, core = place()
    pieces = (entry_ref, conv_ref)
    wholes = (entry_out, conv_out)
    quarters = (CHUNK_PAD // 4, CONV_LINES // 4)
    waiting = []

    def shard(k, across=0, beside=0):
        return 4 * (z ^ k) + 2 * (x ^ across) + (core ^ beside)

    def region(array, index, first, count):
        rows = quarters[array]
        return wholes[array].at[index, pl.ds(pl.multiple_of(rows * first, 16), rows * count)]

    def device(name, k=0):
        if name == "y":
            return (1 - stream, shard(0))
        return (stream, {"z": shard(k), "x": shard(0, 1), "core": shard(0, 0, 1)}[name])

    def push(slot, to, index, first, count, k=0, own=False):
        for array in range(2):
            target = region(array, index, first, count)
            source = target
            if own:
                rows = quarters[array]
                source = pieces[array].at[
                    pl.ds(pl.multiple_of(rows * first, 16), rows * count)
                ]
            pltpu.make_async_remote_copy(
                src_ref=source,
                dst_ref=target,
                send_sem=send_sem.at[array, slot],
                recv_sem=recv_sem.at[array, slot],
                device_id=device(to, k),
                device_id_type=MESH,
            ).start()
            waiting.append((array, slot, target))

    def arrive(slot, index, first, count):
        for array in range(2):
            target = region(array, index, first, count)
            pltpu.make_async_copy(target, target, recv_sem.at[array, slot]).wait()

    barrier = pltpu.get_barrier_semaphore()
    for name, k in (("z", 1), ("z", 2), ("z", 3), ("x", 0), ("y", 0), ("core", 0)):
        pl.semaphore_signal(barrier, inc=1, device_id=device(name, k), device_id_type=MESH)
    load = pltpu.make_async_copy(x_ref, x_rows, local_sem.at[2])
    load.start()
    keep = [
        pltpu.make_async_copy(pieces[array], wholes[array].at[shard(0)], local_sem.at[array])
        for array in range(2)
    ]
    for copy in keep:
        copy.start()
    pl.semaphore_wait(barrier, 6)

    push(6, "x", shard(0), stream, 3, own=True)
    for k in (1, 2, 3):
        push(k - 1, "z", shard(0), 2 * stream, 2, k, own=True)
    push(17, "core", shard(0), 0, 4, own=True)

    stores = []

    def prepare(pair):
        if pair == 0:
            load.wait()
        slot = pair % 2
        if pair >= 2:
            for copy in stores[pair - 2]:
                copy.wait()
        depth = 384
        first = (PAIR * pair) // 128
        source = 128 * first - PAIR * pair
        values = x_rows[:, 128 * first : 128 * first + depth]
        there = lax.broadcasted_iota(jnp.int32, (depth, LANES), 0) + source
        pick = one_hot(there == pair_lane((depth, LANES), 1))
        chunk_rows_ref[slot] = dot(values, pick).astype(bf16)
        there = lax.broadcasted_iota(jnp.int32, (LANES, depth), 1) + source
        pick = one_hot(there == pair_lane((LANES, depth), 0))
        turned_rows[slot] = dot(pick, values, ((1,), (1,))).astype(bf16)
        lanes = slice(LANES * pair, LANES * (pair + 1))
        copies = (
            pltpu.make_async_copy(chunk_rows_ref.at[slot], chunk_out.at[:, lanes], store_sem.at[0, pair]),
            pltpu.make_async_copy(turned_rows.at[slot], turned_out.at[lanes], store_sem.at[1, pair]),
        )
        for copy in copies:
            copy.start()
        stores.append(copies)

    def from_z(k):
        arrive(k - 1, shard(k), 2 * stream, 2)
        push(6 + k, "x", shard(k), 2 * stream, 2)
        push(2 + k, "y", shard(k), 2 * stream, 2)
        push(17 + k, "core", shard(k), 2 * stream, 2)

    def from_y(k):
        arrive(2 + k, shard(k), 2 - 2 * stream, 2)
        push(9 + k, "x", shard(k), 2 - stream, 1)
        push(20 + k, "core", shard(k), 2 - 2 * stream, 2)

    def from_x(k):
        if k == 0:
            arrive(6, shard(0, 1), stream, 3)
            push(13, "y", shard(0, 1), 3 * stream, 1)
            push(24, "core", shard(0, 1), stream, 3)
        else:
            arrive(6 + k, shard(k, 1), 2 * stream, 2)
            push(13 + k, "y", shard(k, 1), 3 * stream, 1)
            push(24 + k, "core", shard(k, 1), 2 * stream, 2)

    def last_x(k):
        arrive(9 + k, shard(k, 1), 2 - stream, 1)
        push(27 + k, "core", shard(k, 1), 2 - stream, 1)

    def last_y(k):
        arrive(13 + k, shard(k, 1), 3 - 3 * stream, 1)
        push(31 + k, "core", shard(k, 1), 3 - 3 * stream, 1)

    prepare(0)
    prepare(1)
    from_z(1)
    prepare(2)
    from_z(2)
    from_x(0)
    prepare(3)
    from_z(3)
    from_y(1)
    prepare(4)
    from_x(1)
    from_y(2)
    prepare(5)
    from_x(2)
    from_y(3)
    prepare(6)
    from_x(3)
    last_y(0)
    last_x(1)
    prepare(7)
    last_y(1)
    last_x(2)
    last_y(2)
    last_x(3)
    last_y(3)

    arrive(17, shard(0, 0, 1), 0, 4)
    for k in (1, 2, 3):
        arrive(17 + k, shard(k, 0, 1), 2 * stream, 2)
        arrive(20 + k, shard(k, 0, 1), 2 - 2 * stream, 2)
    arrive(24, shard(0, 1, 1), stream, 3)
    for k in (1, 2, 3):
        arrive(24 + k, shard(k, 1, 1), 2 * stream, 2)
        arrive(27 + k, shard(k, 1, 1), 2 - stream, 1)
    for k in range(4):
        arrive(31 + k, shard(k, 1, 1), 3 - 3 * stream, 1)
    for array, slot, target in waiting:
        pltpu.make_async_copy(target, target, send_sem.at[array, slot]).wait()
    for copy in keep:
        copy.wait()
    for pair in (6, 7):
        for copy in stores[pair]:
            copy.wait()


def run_gather(entry, conv, x):
    return pl.pallas_call(
        gather_kernel,
        out_shape=(
            jax.ShapeDtypeStruct((SHARDS, CHUNK_PAD, WIDE), bf16),
            jax.ShapeDtypeStruct((SHARDS, CONV_LINES, 128), bf16),
            jax.ShapeDtypeStruct((ROWS, PADDED), bf16),
            jax.ShapeDtypeStruct((PADDED, ROWS), bf16),
        ),
        in_specs=[pl.BlockSpec(memory_space=HBM)] * 3,
        out_specs=(pl.BlockSpec(memory_space=HBM),) * 4,
        scratch_shapes=[
            pltpu.VMEM((ROWS, PADDED), bf16),
            pltpu.VMEM((2, ROWS, LANES), bf16),
            pltpu.VMEM((2, LANES, ROWS), bf16),
            pltpu.SemaphoreType.DMA((2, 35)),
            pltpu.SemaphoreType.DMA((2, 35)),
            pltpu.SemaphoreType.DMA((3,)),
            pltpu.SemaphoreType.DMA((2, OUT_BLOCKS)),
        ],
        name="gather",
        compiler_params=pltpu.CompilerParams(
            collective_id=4, has_side_effects=True, vmem_limit_bytes=VMEM_LIMIT
        ),
        cost_estimate=pl.CostEstimate(
            flops=4 * ROWS * 384 * PADDED, bytes_accessed=200 * 2**20, transcendentals=0
        ),
    )(entry, conv, x)


CONV_BLOCKS = 5


def input_kernel(delta_ref, weight_ref, residual_ref, live_ref, *refs):
    block = pl.program_id(0)
    if len(refs) == 1:
        (grad_out,) = refs
    else:
        conv_ref, grad_out, conv_out, load_sem, *reduce_refs = refs
        reducer = Reducer(reduce_refs)

        def load(at):
            hold = lax.rem(at, 2)
            return pltpu.make_async_copy(
                conv_ref.at[at], reducer.local.at[hold], load_sem.at[hold]
            )

        @pl.when(block == 0)
        def _():
            load(0).start()
            barrier = pltpu.get_barrier_semaphore()
            greeted = reducer.greet(barrier)
            peers = [(0, 0, 1), (0, 1, 0), (1, 0, 0), (2, 0, 0), (3, 0, 0)]
            for peer in peers:
                pl.semaphore_signal(
                    barrier,
                    inc=1,
                    device_id=(reducer.stream, reducer.index(*peer)),
                    device_id_type=MESH,
                )
            pl.semaphore_wait(barrier, len(peers) + greeted)

        def put(tile, rows, values):
            conv_out[block - 4, tile, rows] = values

        reducer.advance(block, CONV_BLOCKS, put)

        @pl.when(block < CONV_BLOCKS)
        def _():
            load(block).wait()
            reducer.core_copy(block).start()

        @pl.when(block < CONV_BLOCKS - 1)
        def _():
            load(block + 1).start()

    @pl.when(block < OUT_BLOCKS)
    def _():
        spans = 4
        first = jnp.minimum((LANES * block) // CHUNK, SHARDS - spans)
        depth = spans * CHUNK_PAD
        row = lax.broadcasted_iota(jnp.int32, (LANES, depth), 0) + LANES * block
        lane = lax.broadcasted_iota(jnp.int32, (LANES, depth), 1)
        channel = CHUNK * (first + lane // CHUNK_PAD) + lane % CHUNK_PAD
        pick = one_hot((channel == row) & (lane % CHUNK_PAD < CHUNK))
        rows = pl.ds(pl.multiple_of(CHUNK_PAD * first, CHUNK_PAD), depth)
        weight = dot(pick, weight_ref[rows]).astype(bf16)
        for micro in range(MICRO_BATCHES):
            here = slice(HALF * micro, HALF * (micro + 1))
            grad = dot(delta_ref[here], weight, ((1,), (1,)))
            for tile in range(2):
                lanes = slice(128 * tile, 128 * tile + 128)
                grad_out[here, lanes] = (
                    (grad[:, lanes] + residual_ref[here, lanes].astype(f32))
                    * live_ref[here].astype(f32)
                ).astype(bf16)


def run_input(delta, weight, residual, live, conv=None):
    reduced = conv is not None
    out_shape = jax.ShapeDtypeStruct((ROWS, CHANNELS), bf16)
    out_specs = columns(ROWS, 0, OUT_BLOCKS)
    in_specs = [
        whole((ROWS, WIDE)),
        whole((PADDED, WIDE)),
        columns(ROWS, 0, OUT_BLOCKS),
        whole((ROWS, 128)),
    ]
    args = [delta, weight, residual, live]
    if reduced:
        shape = (CONV_BLOCKS, 2, 128, 128)
        out_shape = (out_shape, jax.ShapeDtypeStruct(shape, f32))
        out_specs = (out_specs, pl.BlockSpec(shape, lambda i: (0, 0, 0, 0)))
        in_specs.append(pl.BlockSpec(memory_space=HBM))
        args.append(conv)
    return pl.pallas_call(
        input_kernel,
        grid=(CONV_BLOCKS + 4 if reduced else OUT_BLOCKS,),
        out_shape=out_shape,
        in_specs=in_specs,
        out_specs=out_specs,
        scratch_shapes=[pltpu.SemaphoreType.DMA((2,))] + Reducer.scratch() if reduced else [],
        name="input",
        compiler_params=pltpu.CompilerParams(
            vmem_limit_bytes=VMEM_LIMIT,
            collective_id=5 if reduced else None,
            has_side_effects=reduced,
        ),
        cost_estimate=pl.CostEstimate(
            flops=2 * ROWS * WIDE * PADDED, bytes_accessed=35 * 2**20, transcendentals=0
        ),
    )(*args)


def split(values):
    high = values.astype(bf16)
    low = (values - high.astype(f32)).astype(bf16)
    return jnp.concatenate([high, low], axis=-2)


def silu_slope(values):
    sig_vals = jax.nn.sigmoid(values)
    return sig_vals * (1.0 + values * (1.0 - sig_vals))


def wide_lanes(values):
    lead = values.shape[:-1]
    blocks = values.reshape(lead + (BLOCKS, BLOCK))
    padded = jnp.pad(blocks, ((0, 0),) * len(lead) + ((0, 0), (0, LANES - BLOCK)))
    return padded.reshape(lead + (WIDE,))


def narrow_lanes(values):
    lead = values.shape[:-1]
    return values.reshape(lead + (BLOCKS, LANES))[..., :BLOCK].reshape(lead + (CHANNELS,))


def gather(piece, width, size):
    across = -(-width // 128) * 128
    pads = ((0, CHUNK_PAD - CHUNK), (0, across - width))
    if size == SHARDS:
        piece = jnp.pad(piece.reshape(CHUNK, width), pads)
        return lax.all_gather(piece, "img", axis=0, tiled=True)
    pieces = lax.all_gather(piece, "img", axis=0, tiled=True).reshape(SHARDS, CHUNK, width)
    return jnp.pad(pieces, ((0, 0),) + pads).reshape(PADDED, across)


def scatter(grads, width, size):
    if size == SHARDS:
        part = lax.psum_scatter(grads, "img", scatter_dimension=0, tiled=True)
        part = swap_sum(part)
        return part[:CHUNK, :width].reshape(-1)
    grads = grads.reshape(SHARDS, CHUNK_PAD, -1)[:, :CHUNK, :width].reshape(-1)
    return swap_sum(lax.psum_scatter(grads, "img", scatter_dimension=0, tiled=True))


def swap_sum(part):
    other = lax.ppermute(part, "stream", [(0, 1), (1, 0)])
    return part.astype(f32) + other.astype(f32)


def chunked(values):
    lead = values.shape[:-1]
    values = values.reshape(lead + (SHARDS, CHUNK))
    values = jnp.pad(values, ((0, 0),) * len(lead) + ((0, 0), (0, CHUNK_PAD - CHUNK)))
    return values.reshape(lead + (PADDED,))


def unchunked(values):
    lead = values.shape[:-1]
    values = values.reshape(lead + (SHARDS, CHUNK_PAD))[..., :CHUNK]
    return values.reshape(lead + (CHANNELS,))


def local(
    block_in,
    out_cotangent,
    pair_target,
    entry_weight,
    entry_gain,
    entry_shift,
    group_weight,
    group_gain,
    group_shift,
    squeeze_weight,
    squeeze_bias,
    excite_weight,
    excite_bias,
    exit_weight,
    exit_gain,
    exit_shift,
):
    size = lax.axis_size("img")
    stream = lax.axis_index("stream")
    on_global = stream == 0
    positions = jnp.arange(ROWS, dtype=jnp.int32)
    image_of = positions // IMAGE_ROWS
    within = positions % IMAGE_ROWS
    live = within < jnp.where(on_global, IMAGE_ROWS, SMALL_ROWS)
    area = jnp.where(on_global, GLOBAL_SIDE**2, SMALL_SIDE**2)
    crop_of = within // area
    crop_ids = jnp.arange(CROPS, dtype=jnp.int32)
    per_image = jnp.where(on_global, GLOBAL_CROPS, SMALL_CROPS)
    pool_full = live[None] & ((image_of * per_image + crop_of)[None] == crop_ids[:, None])
    pool = pool_full.astype(bf16)
    target_rows = jnp.zeros((ROWS,), jnp.int32)
    for slot in range(SMALL_CROPS):
        target_rows = jnp.where(
            crop_of == slot, jnp.repeat(pair_target[:, slot], IMAGE_ROWS), target_rows
        )
    pair_of = image_of * GLOBAL_CROPS + jnp.where(on_global, crop_of, target_rows)
    pair = (live[None] & (pair_of[None] == crop_ids[:, None])).astype(bf16)
    live_lanes = jnp.broadcast_to(live[:, None], (ROWS, 128)).astype(bf16)
    edges = edge_masks()

    pad_out = ((0, 0), (0, PADDED - CHANNELS))
    x = jnp.pad(jnp.where(live[:, None], block_in[0], 0), pad_out)
    cot = jnp.pad(jnp.where(live[:, None], out_cotangent[0], 0), pad_out)

    lines = CONV_LINES - 18
    if size == SHARDS:
        entry_piece = wide_lanes(entry_weight.reshape(CHUNK, CHANNELS))
        entry_piece = jnp.pad(entry_piece, ((0, CHUNK_PAD - CHUNK), (0, 0)))
        piece = group_weight.reshape(lines, GROUP_WIDTH)
        piece = jnp.pad(piece, ((0, CONV_LINES - lines), (0, 128 - GROUP_WIDTH)))
        entry_mat, conv, x_chunked, x_turned = run_gather(entry_piece, piece, x)
        entry_mat = entry_mat.reshape(PADDED, WIDE)
        conv = conv[:, :lines, :GROUP_WIDTH]
    else:
        x_chunked, x_turned = run_prepare(x)
        entry_mat = wide_lanes(gather(entry_weight, CHANNELS, size)[:, :CHANNELS])
        conv = lax.all_gather(group_weight, "img", axis=0, tiled=True)
    conv = conv.reshape(9, CHANNELS, GROUP_WIDTH)
    squeeze_mat = gather(squeeze_weight, SQUEEZE, size)[:, :SQUEEZE]
    excite_mat = gather(excite_weight, SQUEEZE, size)[:, :SQUEEZE]
    exit_mat = gather(exit_weight, CHANNELS, size)

    def rows_of(*vectors):
        kept = [wide_lanes(vector).reshape(BLOCKS, 2, 128) for vector in vectors]
        return jnp.concatenate(kept, axis=1)

    params = rows_of(entry_gain, entry_shift, group_gain, group_shift)
    exit_params = [
        jnp.pad(vector, (0, PADDED - CHANNELS)).reshape(OUT_BLOCKS, 2, 128)
        for vector in (exit_gain, exit_shift)
    ]
    exit_params = jnp.concatenate(exit_params * 2, axis=1)

    fold = np.zeros((LANES, GROUP_WIDTH), np.float32)
    fold[np.arange(BLOCK), np.arange(BLOCK) % GROUP_WIDTH] = 1
    fold = jnp.asarray(fold, bf16)
    act, turned, group, mixed, pooled, moment = run_entry(
        size, x_chunked, entry_mat, conv, params, pool, edges, fold.T
    )

    def small_dot(a, b, dims=((1,), (0,))):
        return lax.dot_general(
            a, b.astype(f32), (dims, ((), ())), precision=lax.Precision.HIGHEST
        )

    quarters = CHANNELS // SQUEEZE
    quarter = jnp.eye(quarters, dtype=f32)

    def to_rows(values):
        spread_out = values[None, :, :, None] * quarter[:, None, None, :]
        return chunked(spread_out.reshape(quarters * CROPS, CHANNELS))

    def to_quarters(values):
        return values.reshape(CROPS, quarters, SQUEEZE).transpose(1, 0, 2).reshape(-1, SQUEEZE)

    pooled = chunked(narrow_lanes(pooled) / area.astype(f32))
    squeeze_in = small_dot(pooled, squeeze_mat) + squeeze_bias
    squeezed = jax.nn.silu(squeeze_in)
    squeezed_rows = to_rows(squeezed)
    excite_in = small_dot(squeezed_rows, excite_mat).reshape(quarters, CROPS, SQUEEZE)
    excite_in = excite_in.transpose(1, 0, 2).reshape(CROPS, CHANNELS)
    gate = jax.nn.sigmoid(excite_in + excite_bias)
    spread = jnp.concatenate([pool.T, pool.T], axis=1)
    gate_terms = split(wide_lanes(gate))
    scaled, scaled_turned = run_scale(mixed, gate_terms, spread)

    block_out, exit_delta, residual, exit_grad, exit_total = run_exit(
        size, scaled, scaled_turned, exit_mat, x, cot, exit_params, pair, pair.T, live_lanes
    )
    if size == SHARDS:
        exit_shard = exit_grad[:CHUNK, :CHANNELS].reshape(-1)
    else:
        exit_shard = scatter(exit_grad, CHANNELS, size)
    scaled_grad, gate_grad = run_gate(exit_delta, exit_mat, mixed, pool)

    used = crop_ids < IMAGE_DEV * per_image
    gate_grad = jnp.where(used[:, None], narrow_lanes(gate_grad), 0.0)
    excite_delta = gate_grad * gate * (1.0 - gate)
    excite_quarters = to_quarters(excite_delta)
    back_rows = unchunked(small_dot(excite_quarters, excite_mat, ((1,), (1,))))
    back_rows = back_rows.reshape(quarters, CROPS, SQUEEZE, quarters)
    squeeze_delta = jnp.sum(back_rows * quarter[:, None, None, :], axis=(0, 3))
    squeeze_delta = squeeze_delta * silu_slope(squeeze_in)
    pooled_grad = unchunked(small_dot(squeeze_delta, squeeze_mat, ((1,), (1,))))
    pooled_grad = pooled_grad / area.astype(f32)
    beside = ((0, 0), (0, 512 - SQUEEZE))
    excite_grad = small_dot(squeezed_rows, jnp.pad(excite_quarters, beside), ((0,), (0,)))
    squeeze_grad = small_dot(pooled, jnp.pad(squeeze_delta, beside), ((0,), (0,)))
    excite_shard = scatter(excite_grad.astype(bf16), SQUEEZE, size)
    squeeze_shard = scatter(squeeze_grad.astype(bf16), SQUEEZE, size)
    gates = jnp.stack([gate_terms, split(wide_lanes(pooled_grad))])
    bias_rows = jnp.concatenate(
        [
            jnp.pad(jnp.sum(squeeze_delta, axis=0), (0, 512 - SQUEEZE)),
            jnp.pad(jnp.sum(excite_delta, axis=0), (0, 20 * 128 - CHANNELS)),
        ]
    ).reshape(BIAS_ROWS, 128)
    entry_delta, entry_grad, conv_grad, totals, bias_totals = run_back(
        size, bias_rows, scaled_grad, group, gates, spread, act, turned, conv, x_turned, params,
        moment, edges, fold,
    )
    if size == SHARDS:
        entry_shard = narrow_lanes(entry_grad[:CHUNK]).reshape(-1)
        conv_lines = 256 * CONV_BLOCKS
        conv_grad = conv_grad.reshape(SHARDS, lines, GROUP_WIDTH)
        conv_grad = jnp.pad(
            conv_grad, ((0, 0), (0, conv_lines - lines), (0, 128 - GROUP_WIDTH))
        ).reshape(4, 2, 2, CONV_BLOCKS, 2, 128, 128)
        conv_grad = conv_grad.transpose(3, 2, 1, 0, 4, 5, 6)
        input_grad, conv_part = run_input(entry_delta, entry_mat, residual, live_lanes, conv_grad)
        conv_shard = conv_part.reshape(conv_lines, 128)[:lines, :GROUP_WIDTH].reshape(-1)
    else:
        input_grad = run_input(entry_delta, entry_mat, residual, live_lanes)
        entry_shard = scatter(narrow_lanes(entry_grad), CHANNELS, size)
        conv_part = lax.psum_scatter(
            conv_grad.reshape(-1), "img", scatter_dimension=0, tiled=True
        )
        conv_shard = swap_sum(conv_part)
    shards = (entry_shard, conv_shard, squeeze_shard, excite_shard, exit_shard)

    def folded(kept):
        kept = kept.reshape(-1, MICRO_BATCHES, 2, LANES).sum(axis=1)
        return kept[:, 1].reshape(-1), kept[:, 0].reshape(-1)

    group_gain_grad, group_shift_grad = [narrow_lanes(v) for v in folded(totals[:, 0])]
    entry_gain_grad, entry_shift_grad = [narrow_lanes(v) for v in folded(totals[:, 1])]
    exit_gain_grad, exit_shift_grad = [v[:CHANNELS] for v in folded(exit_total[:, 1])]
    bias_totals = bias_totals.reshape(-1)
    kept = jnp.concatenate(
        [
            jnp.stack(
                [
                    entry_gain_grad,
                    entry_shift_grad,
                    group_gain_grad,
                    group_shift_grad,
                    exit_gain_grad,
                    exit_shift_grad,
                    bias_totals[512 : 512 + CHANNELS],
                ]
            ),
            jnp.pad(bias_totals[:SQUEEZE], (0, CHANNELS - SQUEEZE))[None],
        ]
    )
    smalls = swap_sum(kept)

    return (
        block_out[None],
        input_grad[None],
        shards[0],
        smalls[0],
        smalls[1],
        shards[1],
        smalls[2],
        smalls[3],
        shards[2],
        smalls[7, :SQUEEZE],
        shards[3],
        smalls[6],
        shards[4],
        smalls[4],
        smalls[5],
    )


def solution(mesh):
    return jax.shard_map(
        local,
        mesh=mesh,
        in_specs=(
            P("stream", "img", None),
            P("stream", "img", None),
            P("img", None),
            P("img"),
            P(),
            P(),
            P("img"),
            P(),
            P(),
            P("img"),
            P(),
            P("img"),
            P(),
            P("img"),
            P(),
            P(),
        ),
        out_specs=(
            P("stream", "img", None),
            P("stream", "img", None),
            P("img"),
            P(),
            P(),
            P("img"),
            P(),
            P(),
            P("img"),
            P(),
            P("img"),
            P(),
            P("img"),
            P(),
            P(),
        ),
        check_vma=False,
    )
```

```python
import functools

import jax
import jax.numpy as jnp
import numpy as np
from jax import lax
from jax.experimental import pallas as pl
from jax.experimental.pallas import tpu as pltpu
from jax.sharding import PartitionSpec as P

CHANNELS = 2016
GROUPS = 36
SQUEEZE = 504
GROUP_WIDTH = 56
GLOBAL_SIDE = 14
SMALL_SIDE = 7
GLOBAL_CROPS = 2
SMALL_CROPS = 3
IMAGE_DEV = 4
MICRO_BATCHES = 2
IMAGE_ROWS = 392
SMALL_ROWS = 147
ROWS = IMAGE_DEV * IMAGE_ROWS
HALF = ROWS // MICRO_BATCHES

BLOCK = 224
LANES = 256
BLOCKS = CHANNELS // BLOCK
WIDE = BLOCKS * LANES
PADDED = 2048
OUT_BLOCKS = PADDED // LANES

IMAGE_PAD = 424
TOP = 16
CONV_ROWS = IMAGE_DEV * IMAGE_PAD
DEEP_ROWS = 1792
PAD_ROWS = TOP + DEEP_ROWS + 16
CROPS = 16
STEP = 112
STEPS = ROWS // STEP
HALF_STEPS = HALF // STEP
CHUNK = 126
CHUNK_PAD = 128
SHARDS = CHANNELS // CHUNK
PAIR = 2 * CHUNK

EPSILON = 1e-05
PAIR_SCALE = 4.0
MESH = pl.DeviceIdType.MESH
HBM = pl.ANY
VMEM_LIMIT = 62 * 2**20

f32 = jnp.float32
bf16 = jnp.bfloat16


def dot(a, b, dims=((1,), (0,))):
    return lax.dot_general(a, b, (dims, ((), ())), preferred_element_type=f32)


def img_barrier(size):
    stream = lax.axis_index("stream")
    me = lax.axis_index("img")
    barrier = pltpu.get_barrier_semaphore()

    def greet(step, carry):
        pl.semaphore_signal(
            barrier, inc=1, device_id=(stream, lax.rem(me + step, size)), device_id_type=MESH
        )
        return carry

    lax.fori_loop(1, size, greet, 0)
    return barrier


def send_sums(size, slot, packed, sent, got, send_sem, recv_sem):
    stream = lax.axis_index("stream")
    me = lax.axis_index("img")
    sent[slot] = packed
    got[slot, me] = packed

    def send(step, carry):
        pltpu.make_async_remote_copy(
            src_ref=sent.at[slot],
            dst_ref=got.at[slot, me],
            send_sem=send_sem.at[slot],
            recv_sem=recv_sem.at[slot],
            device_id=(stream, lax.rem(me + step, size)),
            device_id_type=MESH,
        ).start()
        return carry

    lax.fori_loop(1, size, send, 0)


def take_sums(size, slot, got, send_sem, recv_sem):
    others = got.at[slot, pl.ds(0, size - 1)]
    pltpu.make_async_copy(others, others, recv_sem.at[slot]).wait()
    pltpu.make_async_copy(others, others, send_sem.at[slot]).wait()
    total = got[slot, 0]
    for peer in range(1, size):
        total = total + got[slot, peer]
    return total


def row_count(size):
    live = jnp.where(lax.axis_index("stream") == 0, IMAGE_ROWS, SMALL_ROWS)
    return (live * (size * (IMAGE_DEV // MICRO_BATCHES))).astype(f32)


def column_sum(values):
    return jnp.sum(values, axis=0, keepdims=True)


def moments(total, micro, tile, count):
    mean = total[4 * micro + tile : 4 * micro + tile + 1] / count
    square = total[4 * micro + 2 + tile : 4 * micro + 3 + tile] / count
    return mean, lax.rsqrt(square - mean * mean + EPSILON)


def edge_masks():
    column = np.arange(IMAGE_PAD) % 212 % 14
    both = np.stack([column != 13, column != 0]).astype(np.float32)
    return jnp.broadcast_to(jnp.asarray(both)[:, :, None], (2, IMAGE_PAD, 128))


def chunk_rows(chunk):
    return slice(STEP * chunk, STEP * (chunk + 1))


def add_up(pieces):
    pieces = list(pieces)
    while len(pieces) > 1:
        odd = [pieces.pop()] if len(pieces) % 2 else []
        pieces = [pieces[i] + pieces[i + 1] for i in range(0, len(pieces), 2)] + odd
    return pieces[0]


def fold_rows(values):
    return add_up(values[8 * i : 8 * i + 8] for i in range(values.shape[0] // 8))


class Sums:
    def __init__(self):
        self.parts = {}

    def add(self, micro, tile, plain, product):
        for kind, values in ((0, plain), (1, product)):
            key = (micro, kind, tile)
            self.parts.setdefault(key, []).append(fold_rows(values))

    def packed(self):
        return jnp.concatenate([column_sum(add_up(self.parts[key])) for key in sorted(self.parts)])


def put_pads(piece, place, tile, pads, edges):
    here = slice(place, place + piece.shape[0])
    inner = (place - TOP) % IMAGE_PAD
    inner = slice(inner, inner + piece.shape[0])
    pads[0, tile, here] = piece
    pads[1, tile, here] = piece * edges[0, inner]
    pads[2, tile, here] = piece * edges[1, inner]


def pad_global(load, pads, edges):
    inside = lax.broadcasted_iota(jnp.int32, (8, 128), 0)
    for image in range(IMAGE_DEV):
        base = TOP + IMAGE_PAD * image
        start = IMAGE_ROWS * image
        for tile in range(2):
            middle = load(tile, start + 192, 8)
            first = load(tile, start, 192)
            put_pads(first, base, tile, pads, edges)
            put_pads(jnp.where(inside < 4, middle, 0.0), base + 192, tile, pads, edges)
            put_pads(jnp.where(inside >= 4, middle, 0.0), base + 208, tile, pads, edges)
            second = load(tile, start + 200, 192)
            put_pads(second, base + 216, tile, pads, edges)


def small_strips():
    for image in range(IMAGE_DEV):
        for crop in range(SMALL_CROPS):
            for line in range(SMALL_SIDE):
                start = IMAGE_ROWS * image + 49 * crop + 7 * line
                yield start, IMAGE_PAD * image + 114 * crop + 14 * line


def pad_small(rows_ref, pads):
    for start, base in small_strips():
        for tile in range(2):
            piece = rows_ref[tile, start : start + 7]
            for kind in range(3):
                pads[kind, tile, TOP + base : TOP + base + 7] = piece


def unpad_small(wide_ref, rows_ref):
    for start, base in small_strips():
        for tile in range(2):
            rows_ref[tile, start : start + 7] = wide_ref[tile, base : base + 7]


def unpadded(wide_ref, tile, first, count):
    pieces = []
    at = first
    while at < first + count:
        image, inner = divmod(at, 49)
        base = IMAGE_PAD * image
        stop = 49 * image + (24 if inner < 24 else 25 if inner == 24 else 49)
        stop = min(stop, first + count)
        length = 8 * (stop - at)
        if inner == 24:
            inside = lax.broadcasted_iota(jnp.int32, (8, 128), 0)
            pieces.append(
                jnp.where(
                    inside < 4,
                    wide_ref[tile, base + 192 : base + 200],
                    wide_ref[tile, base + 208 : base + 216],
                )
            )
        else:
            start = base + 8 * inner + (0 if inner < 24 else 16)
            pieces.append(wide_ref[tile, start : start + length])
        at = stop
    return pieces[0] if len(pieces) == 1 else jnp.concatenate(pieces)


def stack_windows(pads, windows, image, sign):
    for offset in range(9):
        down, across = offset // 3 - 1, offset % 3 - 1
        shift = sign * (14 * down + across)
        kind = (0, 2, 1)[sign * across]
        start = TOP + IMAGE_PAD * image + shift
        for tile in range(2):
            at = LANES * offset + 128 * tile
            windows[IMAGE_PAD * image : IMAGE_PAD * (image + 1), at : at + 128] = pads[
                kind, tile, start : start + IMAGE_PAD
            ].astype(bf16)


def same_group(rows, lanes):
    row_group = lax.broadcasted_iota(jnp.int32, (rows, lanes), 0) // GROUP_WIDTH
    lane_group = lax.broadcasted_iota(jnp.int32, (rows, lanes), 1) // GROUP_WIDTH
    return row_group == lane_group


def entry_kernel(
    size,
    x_ref,
    weight_ref,
    conv_ref,
    param_ref,
    pool_ref,
    edges,
    fold_ref,
    act_out,
    turned_out,
    group_out,
    mixed_out,
    pooled_out,
    total_out,
    first_rows,
    second_rows,
    rows_ref,
    pads,
    windows,
    wide_ref,
    full_ref,
    sent,
    got,
    send_sem,
    recv_sem,
):
    step = pl.program_id(0)
    count = row_count(size)
    on_global = lax.axis_index("stream") == 0

    @pl.when(step == 0)
    def _():
        barrier = img_barrier(size)
        pads[...] = jnp.zeros_like(pads)
        full_ref[...] = jnp.zeros_like(full_ref)
        second_rows[...] = jnp.zeros_like(second_rows)
        pl.semaphore_wait(barrier, size - 1)

    @pl.when(step < BLOCKS)
    def _():
        slot = lax.rem(step, 2)
        for micro in range(MICRO_BATCHES):
            here = slice(HALF * micro, HALF * (micro + 1))
            act = dot(x_ref[here], weight_ref[...])
            first_rows[slot, 0, here] = act[:, :128]
            first_rows[slot, 1, here] = act[:, 128:]
        sums = Sums()
        for chunk in range(STEPS):
            here = chunk_rows(chunk)
            for tile in range(2):
                act = first_rows[slot, tile, here]
                act_out[here, 128 * tile : 128 * tile + 128] = act
                sums.add(chunk // HALF_STEPS, tile, act, act * act)
        send_sums(size, step, sums.packed(), sent, got, send_sem, recv_sem)

    @pl.when((step >= 1) & (step < BLOCKS + 1))
    def _():
        block = step - 1
        slot = lax.rem(block, 2)
        total = take_sums(size, block, got, send_sem, recv_sem)
        total_out[block, 0] = total
        param = param_ref[block]
        scales = {}
        for micro in range(MICRO_BATCHES):
            for tile in range(2):
                mean, inverse = moments(total, micro, tile, count)
                scale = 0.5 * inverse * param[tile : tile + 1]
                scales[micro, tile] = scale, 0.5 * param[2 + tile : 3 + tile] - mean * scale

        def hidden(tile, start, length):
            scale, shift = scales[start // HALF, tile]
            half = first_rows[slot, tile, start : start + length] * scale + shift
            return half + half * jnp.tanh(half)

        same = same_group(BLOCK, LANES)
        for offset in range(9):
            full = dot(conv_ref[offset], fold_ref[...])
            full_ref[LANES * offset : LANES * offset + BLOCK] = jnp.where(
                same, full, 0.0
            ).astype(bf16)

        def convolve(image, target):
            stack_windows(pads, windows, image, 1)
            here = slice(IMAGE_PAD * image, IMAGE_PAD * (image + 1))
            wide = dot(windows[here], full_ref[...])
            target[0, here] = wide[:, :128]
            target[1, here] = wide[:, 128:]

        def turn():
            for tile in range(2):
                turned_out[0, 128 * tile : 128 * tile + 128] = pads[
                    0, tile, TOP : TOP + DEEP_ROWS
                ].T.astype(bf16)

        def send(sums):
            send_sums(size, BLOCKS + block, sums.packed(), sent, got, send_sem, recv_sem)

        @pl.when(on_global)
        def _():
            pad_global(hidden, pads, edges)
            turn()
            second = second_rows.at[slot]
            for image in range(IMAGE_DEV):
                convolve(image, second)
            sums = Sums()
            for chunk in range(STEPS):
                for tile in range(2):
                    act = unpadded(second, tile, STEP // 8 * chunk, STEP // 8)
                    sums.add(chunk // HALF_STEPS, tile, act, act * act)
            send(sums)

        @pl.when(jnp.logical_not(on_global))
        def _():
            for chunk in range(STEPS):
                for tile in range(2):
                    rows_ref[tile, chunk_rows(chunk)] = hidden(tile, STEP * chunk, STEP)
            pad_small(rows_ref, pads)
            turn()
            for image in range(IMAGE_DEV):
                convolve(image, wide_ref)
            second = second_rows.at[slot]
            unpad_small(wide_ref, second)
            sums = Sums()
            for chunk in range(STEPS):
                for tile in range(2):
                    act = second[tile, chunk_rows(chunk)]
                    sums.add(chunk // HALF_STEPS, tile, act, act * act)
            send(sums)

    @pl.when(step >= 2)
    def _():
        block = step - 2
        slot = lax.rem(block, 2)
        total = take_sums(size, BLOCKS + block, got, send_sem, recv_sem)
        total_out[block, 1] = total
        param = param_ref[block]
        second = second_rows.at[slot]

        def finish(load):
            for micro in range(MICRO_BATCHES):
                for tile in range(2):
                    lanes = slice(128 * tile, 128 * tile + 128)
                    mean, inverse = moments(total, micro, tile, count)
                    scale = 0.5 * inverse * param[4 + tile : 5 + tile]
                    shift = 0.5 * param[6 + tile : 7 + tile] - mean * scale
                    for chunk in range(HALF_STEPS * micro, HALF_STEPS * (micro + 1)):
                        here = chunk_rows(chunk)
                        act = load(tile, chunk)
                        group_out[here, lanes] = act
                        half = act * scale + shift
                        mixed_out[here, lanes] = (half + half * jnp.tanh(half)).astype(bf16)

        @pl.when(on_global)
        def _():
            finish(lambda tile, chunk: unpadded(second, tile, STEP // 8 * chunk, STEP // 8))

        @pl.when(jnp.logical_not(on_global))
        def _():
            finish(lambda tile, chunk: second[tile, chunk_rows(chunk)])

        pooled_out[...] = dot(pool_ref[...], mixed_out[...])


def run_entry(size, x, weight, conv, params, pool, edges, fold):
    def whole(shape):
        return pl.BlockSpec(shape, lambda i: (0,) * len(shape), pipeline_mode=pl.Buffered(1))

    def at(lag):
        return lambda i: jnp.clip(i - lag, 0, BLOCKS - 1)

    return pl.pallas_call(
        functools.partial(entry_kernel, size),
        grid=(BLOCKS + 2,),
        out_shape=(
            jax.ShapeDtypeStruct((ROWS, WIDE), f32),
            jax.ShapeDtypeStruct((BLOCKS, LANES, DEEP_ROWS), bf16),
            jax.ShapeDtypeStruct((ROWS, WIDE), f32),
            jax.ShapeDtypeStruct((ROWS, WIDE), bf16),
            jax.ShapeDtypeStruct((CROPS, WIDE), f32),
            jax.ShapeDtypeStruct((BLOCKS, 2, 8, 128), f32),
        ),
        in_specs=[
            whole((ROWS, PADDED)),
            pl.BlockSpec((PADDED, LANES), lambda i: (0, at(0)(i))),
            pl.BlockSpec((9, BLOCK, GROUP_WIDTH), lambda i: (0, at(1)(i), 0)),
            whole((BLOCKS, 8, 128)),
            whole((CROPS, ROWS)),
            whole((2, IMAGE_PAD, 128)),
            whole((GROUP_WIDTH, LANES)),
        ],
        out_specs=(
            pl.BlockSpec((ROWS, LANES), lambda i: (0, at(0)(i))),
            pl.BlockSpec((1, LANES, DEEP_ROWS), lambda i: (at(1)(i), 0, 0)),
            pl.BlockSpec((ROWS, LANES), lambda i: (0, at(2)(i))),
            pl.BlockSpec((ROWS, LANES), lambda i: (0, at(2)(i))),
            pl.BlockSpec((CROPS, LANES), lambda i: (0, at(2)(i))),
            pl.BlockSpec((BLOCKS, 2, 8, 128), lambda i: (0, 0, 0, 0)),
        ),
        scratch_shapes=[
            pltpu.VMEM((2, 2, ROWS, 128), f32),
            pltpu.VMEM((2, 2, CONV_ROWS, 128), f32),
            pltpu.VMEM((2, ROWS, 128), f32),
            pltpu.VMEM((3, 2, PAD_ROWS, 128), f32),
            pltpu.VMEM((CONV_ROWS, 9 * LANES), bf16),
            pltpu.VMEM((2, CONV_ROWS, 128), f32),
            pltpu.VMEM((9 * LANES, LANES), bf16),
            pltpu.VMEM((2 * BLOCKS, 8, 128), f32),
            pltpu.VMEM((2 * BLOCKS, size, 8, 128), f32),
            pltpu.SemaphoreType.DMA((2 * BLOCKS,)),
            pltpu.SemaphoreType.DMA((2 * BLOCKS,)),
        ],
        name="entry",
        compiler_params=pltpu.CompilerParams(
            collective_id=1, has_side_effects=True, vmem_limit_bytes=VMEM_LIMIT
        ),
        cost_estimate=pl.CostEstimate(
            flops=2 * ROWS * WIDE * (PADDED + 9 * LANES),
            bytes_accessed=70 * 2**20,
            transcendentals=2 * ROWS * WIDE,
        ),
    )(x, weight, conv, params, pool, edges, fold)


def place():
    me = lax.axis_index("img")
    return lax.axis_index("stream"), me // 4, lax.rem(me // 2, 2), lax.rem(me, 2)


class Reducer:
    def __init__(self, refs, inside, rest=None):
        self.inside, self.rest = inside, rest
        (
            self.local,
            self.core_got,
            self.plane_got,
            self.plane_sum,
            self.z_got,
            self.final,
            self.final_got,
            self.core_sem,
            self.plane_sem,
            self.z_sem,
            self.y_sem,
            self.local_sem,
        ) = refs
        self.stream, self.z, self.x, self.core = place()
        self.mine = pl.ds(pl.multiple_of(64 * self.stream, 64), 64)
        self.theirs = pl.ds(pl.multiple_of(64 * (1 - self.stream), 64), 64)

    @staticmethod
    def scratch():
        return [
            pltpu.VMEM((2, 2, 2, 4, 2, 128, 128), bf16),
            pltpu.VMEM((3, 2, 4, 2, 128, 128), bf16),
            pltpu.VMEM((2, 3, 4, 2, 64, 128), bf16),
            pltpu.VMEM((2, 4, 2, 64, 128), bf16),
            pltpu.VMEM((2, 3, 2, 64, 128), bf16),
            pltpu.VMEM((2, 2, 64, 128), f32),
            pltpu.VMEM((2, 2, 64, 128), f32),
            pltpu.SemaphoreType.DMA((2, 2)),
            pltpu.SemaphoreType.DMA((2, 2, 3)),
            pltpu.SemaphoreType.DMA((2, 2, 3)),
            pltpu.SemaphoreType.DMA((2, 2)),
            pltpu.SemaphoreType.DMA((2,)),
        ]

    SHAPE = (2, 2, 4, 2, 128, 128)

    def index(self, k=0, across=0, beside=0):
        return 4 * (self.z ^ k) + 2 * (self.x ^ across) + (self.core ^ beside)

    def greet(self, barrier):
        for across in (0, 1):
            pl.semaphore_signal(
                barrier,
                inc=1,
                device_id=(1 - self.stream, self.index(0, across)),
                device_id_type=MESH,
            )
        return 2

    def core_copy(self, block):
        hold = lax.rem(block, 2)
        return pltpu.make_async_remote_copy(
            src_ref=self.local.at[hold, 1 - self.core],
            dst_ref=self.core_got.at[lax.rem(block, 3)],
            send_sem=self.core_sem.at[0, hold],
            recv_sem=self.core_sem.at[1, hold],
            device_id=(self.stream, self.index(0, 0, 1)),
            device_id_type=MESH,
        )

    def plane_copy(self, block, peer):
        hold = lax.rem(block, 2)
        x = self.x if peer == 1 else 1 - self.x
        rows = self.mine if peer == 0 else self.theirs
        stream = self.stream if peer == 0 else 1 - self.stream
        return pltpu.make_async_remote_copy(
            src_ref=self.core_got.at[lax.rem(block, 3), x, :, :, rows],
            dst_ref=self.plane_got.at[hold, peer],
            send_sem=self.plane_sem.at[0, hold, peer],
            recv_sem=self.plane_sem.at[1, hold, peer],
            device_id=(stream, self.index(0, 0 if peer == 1 else 1)),
            device_id_type=MESH,
        )

    def z_copy(self, block, k):
        hold = lax.rem(block, 2)
        return pltpu.make_async_remote_copy(
            src_ref=self.plane_sum.at[hold, self.z ^ k],
            dst_ref=self.z_got.at[hold, k - 1],
            send_sem=self.z_sem.at[0, hold, k - 1],
            recv_sem=self.z_sem.at[1, hold, k - 1],
            device_id=(self.stream, self.index(k)),
            device_id_type=MESH,
        )

    def y_copy(self, block):
        hold = lax.rem(block, 2)
        return pltpu.make_async_remote_copy(
            src_ref=self.final.at[hold],
            dst_ref=self.final_got.at[hold],
            send_sem=self.y_sem.at[0, hold],
            recv_sem=self.y_sem.at[1, hold],
            device_id=(1 - self.stream, self.index()),
            device_id_type=MESH,
        )

    def finish(self, block, put):
        hold = lax.rem(block, 2)
        self.y_copy(block).wait()
        for tile in range(2):
            put(tile, self.mine, self.final[hold, tile])
            put(tile, self.theirs, self.final_got[hold, tile])

    def after_z(self, block):
        hold = lax.rem(block, 2)
        for k in (1, 2, 3):
            self.z_copy(block, k).wait()
        for tile in range(2):
            total = self.plane_sum[hold, self.z, tile].astype(f32)
            for k in range(3):
                total = total + self.z_got[hold, k, tile].astype(f32)
            self.final[hold, tile] = total
        self.y_copy(block).start()

    def after_plane(self, block):
        hold = lax.rem(block, 2)
        ring = lax.rem(block, 3)
        for peer in range(3):
            self.plane_copy(block, peer).wait()
        for z in range(4):
            for tile in range(2):
                total = self.core_got[ring, self.x, z, tile, self.mine].astype(f32)
                for peer in range(3):
                    total = total + self.plane_got[hold, peer, z, tile].astype(f32)
                self.plane_sum[hold, z, tile] = total.astype(bf16)
        for k in (1, 2, 3):
            self.z_copy(block, k).start()

    def after_core(self, block):
        hold = lax.rem(block, 2)
        ring = lax.rem(block, 3)
        self.core_copy(block).wait()
        for x in range(2):
            for z in range(4):
                for tile in range(2):
                    total = self.core_got[ring, x, z, tile].astype(f32)
                    total = total + self.local[hold, self.core, x, z, tile].astype(f32)
                    self.core_got[ring, x, z, tile] = total.astype(bf16)
        for peer in range(3):
            self.plane_copy(block, peer).start()

    def rest_copy(self, block):
        hold = lax.rem(block, 2)
        return pltpu.make_async_copy(
            self.local.at[hold], self.rest.at[block - self.inside], self.local_sem.at[hold]
        )

    def load_copy(self, source, at, block):
        hold = lax.rem(block, 2)
        return pltpu.make_async_copy(source.at[at], self.local.at[hold], self.local_sem.at[hold])

    def advance(self, newest, put, blocks=0):
        def live(block):
            return (block >= 0) & (block < self.inside)

        @pl.when(live(newest - 4))
        def _():
            self.finish(newest - 4, put)

        @pl.when(live(newest - 3))
        def _():
            self.after_z(newest - 3)

        @pl.when(live(newest - 2))
        def _():
            self.after_plane(newest - 2)

        @pl.when(live(newest - 1))
        def _():
            self.after_core(newest - 1)

        if self.rest is not None:

            @pl.when((newest > self.inside) & (newest <= blocks))
            def _():
                self.rest_copy(newest - 1).wait()

    def begin(self, block, grad):
        hold = lax.rem(block, 2)
        for chunk in range(SHARDS):
            z, x, core = chunk // 4, chunk // 2 % 2, chunk % 2
            for tile in range(2):
                self.local[hold, core, x, z, tile] = grad[
                    128 * chunk : 128 * chunk + 128, 128 * tile : 128 * tile + 128
                ].astype(bf16)

        @pl.when(block < self.inside)
        def _():
            self.core_copy(block).start()

        if self.rest is not None:

            @pl.when(block >= self.inside)
            def _():
                self.rest_copy(block).start()

    def neighbours(self):
        barrier = pltpu.get_barrier_semaphore()
        greeted = self.greet(barrier)
        peers = [(0, 0, 1), (0, 1, 0), (1, 0, 0), (2, 0, 0), (3, 0, 0)]
        for peer in peers:
            pl.semaphore_signal(
                barrier, inc=1, device_id=(self.stream, self.index(*peer)), device_id_type=MESH
            )
        pl.semaphore_wait(barrier, len(peers) + greeted)


def feed(reducer, step, sources, part_out):
    starts = []
    total = 0
    for source, count in sources:
        starts.append((source, total, total + count))
        total += count

    def start_load(block):
        for source, first, last in starts:

            @pl.when((block >= first) & (block < last))
            def _():
                reducer.load_copy(source, block - first, block).start()

    @pl.when(step == 0)
    def _():
        start_load(step)
        reducer.neighbours()

    def put(tile, rows, values):
        part_out[step - 4, tile, rows] = values

    reducer.advance(step, put)

    @pl.when(step < total)
    def _():
        reducer.load_copy(sources[0][0], 0, step).wait()
        reducer.core_copy(step).start()

    start_load(step + 1)


BACK_INSIDE = 6
BACK_REST = BLOCKS - BACK_INSIDE
CONV_BLOCKS = 3


def whole(shape):
    return pl.BlockSpec(shape, lambda i: (0,) * len(shape), pipeline_mode=pl.Buffered(1))


def columns(rows, lag, blocks):
    return pl.BlockSpec((rows, LANES), lambda i: (0, jnp.clip(i - lag, 0, blocks - 1)))


def lane_halves(values):
    return [values[:, :128], values[:, 128:]]


def exit_kernel(
    size,
    scaled_ref,
    turned_ref,
    weight_ref,
    x_ref,
    cot_ref,
    param_ref,
    pair_ref,
    spread_ref,
    live_ref,
    out_out,
    delta_out,
    residual_out,
    weight_out,
    total_out,
    act_ref,
    slope_ref,
    pair_sent,
    pair_got,
    sent,
    got,
    send_sem,
    recv_sem,
    pair_send,
    pair_recv,
):
    step = pl.program_id(0)
    count = row_count(size)
    stream = lax.axis_index("stream")
    me = lax.axis_index("img")
    area = jnp.where(stream == 0, GLOBAL_SIDE**2, SMALL_SIDE**2).astype(f32)
    blocks = OUT_BLOCKS

    def used_lanes(block):
        lane = lax.broadcasted_iota(jnp.int32, (STEP, 128), 1) + LANES * block
        return [lane + 128 * tile < CHANNELS for tile in range(2)]

    def pair_copy(block):
        return pltpu.make_async_remote_copy(
            src_ref=pair_sent.at[block],
            dst_ref=pair_got.at[block],
            send_sem=pair_send.at[block],
            recv_sem=pair_recv.at[block],
            device_id=(1 - stream, me),
            device_id_type=MESH,
        )

    @pl.when(step == 0)
    def _():
        barrier = img_barrier(size)
        pl.semaphore_signal(
            barrier, inc=1, device_id=(1 - stream, me), device_id_type=MESH
        )
        pl.semaphore_wait(barrier, size)

    @pl.when(step < blocks)
    def _():
        slot = lax.rem(step, 4)
        for micro in range(MICRO_BATCHES):
            here = slice(HALF * micro, HALF * (micro + 1))
            act_ref[slot, here] = dot(scaled_ref[here], weight_ref[...])
        sums = Sums()
        for chunk in range(STEPS):
            for tile in range(2):
                act = act_ref[slot, chunk_rows(chunk), 128 * tile : 128 * tile + 128]
                sums.add(chunk // HALF_STEPS, tile, act, act * act)
        send_sums(size, step, sums.packed(), sent, got, send_sem, recv_sem)

    @pl.when((step >= 1) & (step < blocks + 1))
    def _():
        block = step - 1
        slot = lax.rem(block, 4)
        total = take_sums(size, block, got, send_sem, recv_sem)
        total_out[block, 0] = total
        param = param_ref[block]
        inside = used_lanes(block)
        for micro in range(MICRO_BATCHES):
            for tile in range(2):
                lanes = slice(128 * tile, 128 * tile + 128)
                mean, inverse = moments(total, micro, tile, count)
                scale = 0.5 * inverse * param[tile : tile + 1]
                shift = 0.5 * param[2 + tile : 3 + tile] - mean * scale
                for chunk in range(HALF_STEPS * micro, HALF_STEPS * (micro + 1)):
                    here = chunk_rows(chunk)
                    act = act_ref[slot, here, lanes]
                    source = jnp.where(inside[tile], x_ref[here, lanes].astype(f32), 0.0)
                    half = 0.5 * source + (act * scale + shift)
                    bent = jnp.tanh(half)
                    out_out[here, lanes] = (
                        (half + half * bent) * live_ref[here].astype(f32)
                    ).astype(bf16)
                    slope_ref[lax.rem(block, 3), here, lanes] = (0.5 + 0.5 * bent) * (
                        1.0 + half * (1.0 - bent)
                    )
        embed = dot(pair_ref[...], out_out[...]) / area
        pair_sent[block] = embed[:8].astype(bf16).astype(f32)
        pair_copy(block).start()

    @pl.when((step >= 2) & (step < blocks + 2))
    def _():
        block = step - 2
        slot = lax.rem(block, 4)
        hold = lax.rem(block, 3)
        moment = total_out[block, 0]
        pair_copy(block).wait()
        partner = pair_got[block]
        partner = jnp.concatenate([partner, jnp.zeros_like(partner)]).astype(bf16)
        means = {
            (micro, tile): moments(moment, micro, tile, count)
            for micro in range(MICRO_BATCHES)
            for tile in range(2)
        }
        inside = used_lanes(block)
        sums = Sums()
        for chunk in range(STEPS):
            here = chunk_rows(chunk)
            live = live_ref[here].astype(f32)
            pull = dot(spread_ref[here], partner) * (PAIR_SCALE / area)
            for tile in range(2):
                lanes = slice(128 * tile, 128 * tile + 128)
                mean, inverse = means[chunk // HALF_STEPS, tile]
                upstream = jnp.where(inside[tile], cot_ref[here, lanes].astype(f32), 0.0)
                upstream = upstream * live + pull[:, lanes]
                delta = upstream * slope_ref[hold, here, lanes]
                slope_ref[hold, here, lanes] = delta
                residual_out[here, lanes] = delta.astype(bf16)
                normed = act_ref[slot, here, lanes] * inverse - mean * inverse
                sums.add(chunk // HALF_STEPS, tile, delta, delta * normed)
        send_sums(size, blocks + block, sums.packed(), sent, got, send_sem, recv_sem)

    @pl.when(step >= 3)
    def _():
        block = step - 3
        slot = lax.rem(block, 4)
        hold = lax.rem(block, 3)
        moment = total_out[block, 0]
        total = take_sums(size, blocks + block, got, send_sem, recv_sem)
        total_out[block, 1] = total
        param = param_ref[block]
        for micro in range(MICRO_BATCHES):
            for tile in range(2):
                lanes = slice(128 * tile, 128 * tile + 128)
                back = norm_back(moment, total, micro, tile, param[tile : tile + 1], count)
                for chunk in range(HALF_STEPS * micro, HALF_STEPS * (micro + 1)):
                    here = chunk_rows(chunk)
                    delta_out[here, lanes] = back(
                        slope_ref[hold, here, lanes], act_ref[slot, here, lanes]
                    ).astype(bf16)
        weight_out[...] = dot(turned_ref[...], delta_out[...]).astype(bf16)


def norm_back(moment, total, micro, tile, gain, count):
    mean, inverse = moments(moment, micro, tile, count)
    scale = gain * inverse
    plain = total[4 * micro + tile : 4 * micro + tile + 1] / count
    along = scale * (total[4 * micro + 2 + tile : 4 * micro + 3 + tile] / count)
    slant = along * inverse
    level = scale * plain
    return lambda upstream, act: scale * upstream - (level + (act - mean) * slant)


def run_exit(size, scaled, turned, weight, x, cot, params, pair, spread, live):
    blocks = OUT_BLOCKS
    return pl.pallas_call(
        functools.partial(exit_kernel, size),
        grid=(blocks + 3,),
        out_shape=(
            jax.ShapeDtypeStruct((ROWS, CHANNELS), bf16),
            jax.ShapeDtypeStruct((ROWS, PADDED), bf16),
            jax.ShapeDtypeStruct((ROWS, PADDED), bf16),
            jax.ShapeDtypeStruct((PADDED, PADDED), bf16),
            jax.ShapeDtypeStruct((blocks, 2, 8, 128), f32),
        ),
        in_specs=[
            whole((ROWS, PADDED)),
            whole((PADDED, ROWS)),
            columns(PADDED, 0, blocks),
            columns(ROWS, 1, blocks),
            columns(ROWS, 2, blocks),
            whole((blocks, 8, 128)),
            whole((CROPS, ROWS)),
            whole((ROWS, CROPS)),
            whole((ROWS, 128)),
        ],
        out_specs=(
            columns(ROWS, 1, blocks),
            columns(ROWS, 3, blocks),
            columns(ROWS, 2, blocks),
            columns(PADDED, 3, blocks),
            pl.BlockSpec((blocks, 2, 8, 128), lambda i: (0, 0, 0, 0)),
        ),
        scratch_shapes=[
            pltpu.VMEM((4, ROWS, LANES), f32),
            pltpu.VMEM((3, ROWS, LANES), f32),
            pltpu.VMEM((blocks, 8, LANES), f32),
            pltpu.VMEM((blocks, 8, LANES), f32),
            pltpu.VMEM((2 * blocks, 8, 128), f32),
            pltpu.VMEM((2 * blocks, size, 8, 128), f32),
            pltpu.SemaphoreType.DMA((2 * blocks,)),
            pltpu.SemaphoreType.DMA((2 * blocks,)),
            pltpu.SemaphoreType.DMA((blocks,)),
            pltpu.SemaphoreType.DMA((blocks,)),
        ],
        name="exit",
        compiler_params=pltpu.CompilerParams(
            collective_id=2, has_side_effects=True, vmem_limit_bytes=VMEM_LIMIT
        ),
        cost_estimate=pl.CostEstimate(
            flops=4 * ROWS * PADDED * PADDED,
            bytes_accessed=70 * 2**20,
            transcendentals=ROWS * PADDED,
        ),
    )(scaled, turned, weight, x, cot, params, pair, spread, live)


def gate_kernel(delta_ref, weight_ref, mixed_ref, pool_ref, scaled_out, gate_out):
    block = pl.program_id(0)
    first = jnp.minimum((BLOCK * block) // CHUNK, SHARDS - 3)
    row = lax.broadcasted_iota(jnp.int32, (LANES, 3 * CHUNK_PAD), 0)
    lane = lax.broadcasted_iota(jnp.int32, (LANES, 3 * CHUNK_PAD), 1)
    channel = CHUNK * (first + lane // CHUNK_PAD) + lane % CHUNK_PAD
    pick = (channel == BLOCK * block + row) & (row < BLOCK) & (lane % CHUNK_PAD < CHUNK)
    rows = pl.ds(pl.multiple_of(CHUNK_PAD * first, CHUNK_PAD), 3 * CHUNK_PAD)
    weight = dot(jnp.where(pick, 1.0, 0.0).astype(bf16), weight_ref[rows]).astype(bf16)
    grad = dot(delta_ref[...], weight, ((1,), (1,)))
    scaled_out[...] = grad
    gate_out[...] = dot(pool_ref[...], (grad * mixed_ref[...].astype(f32)).astype(bf16))


def run_gate(delta, weight, mixed, pool):
    return pl.pallas_call(
        gate_kernel,
        grid=(BLOCKS,),
        out_shape=(
            jax.ShapeDtypeStruct((ROWS, WIDE), f32),
            jax.ShapeDtypeStruct((CROPS, WIDE), f32),
        ),
        in_specs=[
            whole((ROWS, PADDED)),
            whole((PADDED, PADDED)),
            columns(ROWS, 0, BLOCKS),
            whole((CROPS, ROWS)),
        ],
        out_specs=(columns(ROWS, 0, BLOCKS), columns(CROPS, 0, BLOCKS)),
        name="gate",
        compiler_params=pltpu.CompilerParams(vmem_limit_bytes=VMEM_LIMIT),
        cost_estimate=pl.CostEstimate(
            flops=2 * ROWS * WIDE * PADDED, bytes_accessed=40 * 2**20, transcendentals=0
        ),
    )(delta, weight, mixed, pool)


def pair_lane(shape, dim):
    lane = lax.broadcasted_iota(jnp.int32, shape, dim)
    inside = lane % CHUNK_PAD
    return jnp.where(inside < CHUNK, CHUNK * (lane // CHUNK_PAD) + inside, -1)


def one_hot(match):
    return jnp.where(match, 1.0, 0.0).astype(bf16)


def prepare_kernel(x_ref, chunk_out, turned_out):
    pair = pl.program_id(0)
    depth = 384
    first = (PAIR * pair) // 128
    lanes = pl.ds(pl.multiple_of(128 * first, 128), depth)
    source = 128 * first - PAIR * pair
    there = lax.broadcasted_iota(jnp.int32, (depth, LANES), 0) + source
    pick = one_hot(there == pair_lane((depth, LANES), 1))
    chunk_out[...] = dot(x_ref[:, lanes], pick).astype(bf16)
    there = lax.broadcasted_iota(jnp.int32, (LANES, depth), 1) + source
    pick = one_hot(there == pair_lane((LANES, depth), 0))
    turned_out[...] = dot(pick, x_ref[:, lanes], ((1,), (1,))).astype(bf16)


def run_prepare(x):
    return pl.pallas_call(
        prepare_kernel,
        grid=(OUT_BLOCKS,),
        out_shape=(
            jax.ShapeDtypeStruct((ROWS, PADDED), bf16),
            jax.ShapeDtypeStruct((PADDED, ROWS), bf16),
        ),
        in_specs=[whole((ROWS, PADDED))],
        out_specs=(columns(ROWS, 0, OUT_BLOCKS), pl.BlockSpec((LANES, ROWS), lambda i: (i, 0))),
        name="prepare",
        compiler_params=pltpu.CompilerParams(vmem_limit_bytes=VMEM_LIMIT),
        cost_estimate=pl.CostEstimate(
            flops=4 * ROWS * 384 * PADDED, bytes_accessed=20 * 2**20, transcendentals=0
        ),
    )(x)


QUARTERS = CHANNELS // SQUEEZE
INNER = 512


def split(values):
    high = values.astype(bf16)
    low = (values - high.astype(f32)).astype(bf16)
    return jnp.concatenate([high, low], axis=-2)


def join(terms):
    half = terms.shape[0] // 2
    return terms[:half] + terms[half:]


def wide_place(channel):
    return channel + (LANES - BLOCK) * (channel // BLOCK)


def pair_source(pair):
    return min(128 * (wide_place(PAIR * pair) // 128), WIDE - 512)


def pair_from_wide(pair, shape, dim):
    inside = pair_lane(shape, dim)
    where = wide_place(PAIR * pair + inside) - pair_source(pair)
    there = lax.broadcasted_iota(jnp.int32, shape, 1 - dim)
    return one_hot((there == where) & (inside >= 0))


def inner_source(pair):
    return min(128 * ((PAIR // QUARTERS) * pair // 128), INNER - LANES)


def pair_from_inner(pair, quarter):
    shape = (LANES, LANES)
    inside = pair_lane(shape, 1)
    inner = lax.broadcasted_iota(jnp.int32, shape, 0) + inner_source(pair)
    return one_hot((PAIR * pair + inside == QUARTERS * inner + quarter) & (inside >= 0))


def quarters_of(block):
    first = BLOCK * block // SQUEEZE
    last = (BLOCK * block + BLOCK - 1) // SQUEEZE
    return range(first, last + 1)


def scale_kernel(
    mixed_ref,
    spread_ref,
    pooled_ref,
    squeeze_ref,
    excite_ref,
    squeeze_bias_ref,
    excite_bias_ref,
    scaled_out,
    turned_out,
    gates_out,
    pooled_out,
    inner_out,
    rows_out,
    quarter_out,
    scaled,
):
    step = pl.program_id(0)
    area = jnp.where(lax.axis_index("stream") == 0, GLOBAL_SIDE**2, SMALL_SIDE**2).astype(f32)

    @pl.when(step == 0)
    def _():
        for pair in range(OUT_BLOCKS):
            lanes = slice(pair_source(pair), pair_source(pair) + 512)
            pick = pair_from_wide(pair, (512, LANES), 1)
            picked = join(dot(split(pooled_ref[:, lanes]), pick)) / area
            pooled_out[:, LANES * pair : LANES * (pair + 1)] = picked
        inner = join(dot(split(pooled_out[...]), squeeze_ref[...])) + squeeze_bias_ref[...]
        inner_out[...] = inner
        half = 0.5 * inner
        terms = split(half + half * jnp.tanh(half))
        for pair in range(OUT_BLOCKS):
            source = terms[:, inner_source(pair) : inner_source(pair) + LANES]
            for quarter in range(QUARTERS):
                rows_out[
                    CROPS * quarter : CROPS * (quarter + 1), LANES * pair : LANES * (pair + 1)
                ] = join(dot(source, pair_from_inner(pair, quarter)))
        excite = join(dot(split(rows_out[...]), excite_ref[...]))
        for quarter in range(QUARTERS):
            here = slice(CROPS * quarter, CROPS * (quarter + 1))
            half = 0.5 * (excite[here] + excite_bias_ref[quarter : quarter + 1])
            quarter_out[here] = 0.5 + 0.5 * jnp.tanh(half)
        for block in range(BLOCKS):
            total = 0.0
            for quarter in quarters_of(block):
                shape = (INNER, LANES)
                channel = SQUEEZE * quarter + lax.broadcasted_iota(jnp.int32, shape, 0)
                lane = lax.broadcasted_iota(jnp.int32, shape, 1)
                inside = lax.broadcasted_iota(jnp.int32, shape, 0) < SQUEEZE
                pick = one_hot((channel == BLOCK * block + lane) & (lane < BLOCK) & inside)
                here = slice(CROPS * quarter, CROPS * (quarter + 1))
                total = total + dot(split(quarter_out[here]), pick)
            gates_out[:, LANES * block : LANES * (block + 1)] = total.astype(bf16)

    @pl.when(step < BLOCKS)
    def _():
        lanes = pl.ds(pl.multiple_of(LANES * step, LANES), LANES)
        for chunk in range(STEPS):
            here = chunk_rows(chunk)
            gate = dot(spread_ref[here], gates_out[:, lanes])
            scaled[here, lanes] = (mixed_ref[here].astype(f32) * gate).astype(bf16)

    @pl.when(step >= BLOCKS)
    def _():
        pair = step - BLOCKS
        depth = 512
        start = PAIR * pair
        first = jnp.minimum((start + (LANES - BLOCK) * (start // BLOCK)) // 128, WIDE // 128 - 4)
        lanes = pl.ds(pl.multiple_of(128 * first, 128), depth)

        def pick(shape, dim):
            inside = pair_lane(shape, dim)
            channel = start + inside
            place = channel + (LANES - BLOCK) * (channel // BLOCK) - 128 * first
            there = lax.broadcasted_iota(jnp.int32, shape, 1 - dim)
            return one_hot((there == place) & (inside >= 0))

        scaled_out[...] = dot(scaled[:, lanes], pick((depth, LANES), 1)).astype(bf16)
        turned_out[...] = dot(pick((LANES, depth), 0), scaled[:, lanes], ((1,), (1,))).astype(
            bf16
        )


def run_scale(mixed, spread, pooled, squeeze, excite, squeeze_bias, excite_bias):
    def pair(i):
        return jnp.maximum(i - BLOCKS, 0)

    def kept(shape):
        return pl.BlockSpec(shape, lambda i: (0, 0))

    kinds = (
        ((2 * CROPS, WIDE), bf16),
        ((CROPS, PADDED), f32),
        ((CROPS, INNER), f32),
        ((QUARTERS * CROPS, PADDED), f32),
        ((QUARTERS * CROPS, INNER), f32),
    )
    return pl.pallas_call(
        scale_kernel,
        grid=(BLOCKS + OUT_BLOCKS,),
        out_shape=(
            jax.ShapeDtypeStruct((ROWS, PADDED), bf16),
            jax.ShapeDtypeStruct((PADDED, ROWS), bf16),
        )
        + tuple(jax.ShapeDtypeStruct(*kind) for kind in kinds),
        in_specs=[
            columns(ROWS, 0, BLOCKS),
            whole((ROWS, 2 * CROPS)),
            whole((CROPS, WIDE)),
            whole((PADDED, INNER)),
            whole((PADDED, INNER)),
            whole((1, INNER)),
            whole((QUARTERS, INNER)),
        ],
        out_specs=(
            pl.BlockSpec((ROWS, LANES), lambda i: (0, pair(i))),
            pl.BlockSpec((LANES, ROWS), lambda i: (pair(i), 0)),
        )
        + tuple(kept(shape) for shape, _ in kinds),
        scratch_shapes=[pltpu.VMEM((ROWS, WIDE), bf16)],
        name="scale",
        compiler_params=pltpu.CompilerParams(vmem_limit_bytes=VMEM_LIMIT),
        cost_estimate=pl.CostEstimate(
            flops=4 * ROWS * 512 * PADDED, bytes_accessed=30 * 2**20, transcendentals=0
        ),
    )(mixed, spread, pooled, squeeze, excite, squeeze_bias, excite_bias)


def outer(left, right):
    left_high = left.astype(bf16)
    left_low = (left - left_high.astype(f32)).astype(bf16)
    right_high = right.astype(bf16)
    right_low = (right - right_high.astype(f32)).astype(bf16)
    left = jnp.concatenate([left_high, left_high, left_low])
    right = jnp.concatenate([right_high, right_low, right_high])
    return dot(left, right, ((0,), (0,)))


def squeeze_kernel(
    gate_grad_ref,
    pooled_ref,
    inner_ref,
    rows_ref,
    quarter_ref,
    squeeze_ref,
    excite_ref,
    gates_out,
    grads_out,
    bias_out,
    quarter_delta,
    inner_delta,
    pooled_delta,
):
    area = jnp.where(lax.axis_index("stream") == 0, GLOBAL_SIDE**2, SMALL_SIDE**2).astype(f32)
    bias_out[...] = jnp.zeros_like(bias_out)
    for quarter in range(QUARTERS):
        first = min(LANES * (SQUEEZE * quarter // BLOCK), WIDE - 1024)
        shape = (1024, INNER)
        inner = lax.broadcasted_iota(jnp.int32, shape, 1)
        where = wide_place(SQUEEZE * quarter + inner) - first
        there = lax.broadcasted_iota(jnp.int32, shape, 0)
        pick = one_hot((there == where) & (inner < SQUEEZE))
        grad = join(dot(split(gate_grad_ref[:, first : first + 1024]), pick))
        here = slice(CROPS * quarter, CROPS * (quarter + 1))
        gate = quarter_ref[here]
        delta = grad * gate * (1.0 - gate)
        quarter_delta[here] = delta
        bias_out[1 + quarter : 2 + quarter] = column_sum(delta)
    back = join(dot(split(quarter_delta[...]), excite_ref[...], ((1,), (1,))))
    inner_delta[...] = jnp.zeros_like(inner_delta)
    for pair in range(OUT_BLOCKS):
        lanes = slice(inner_source(pair), inner_source(pair) + LANES)
        total = 0.0
        for quarter in range(QUARTERS):
            terms = split(
                back[CROPS * quarter : CROPS * (quarter + 1), LANES * pair : LANES * (pair + 1)]
            )
            total = total + dot(terms, pair_from_inner(pair, quarter), ((1,), (1,)))
        inner_delta[:, lanes] += join(total)
    half = 0.5 * inner_ref[...]
    bent = jnp.tanh(half)
    delta = inner_delta[...] * ((0.5 + 0.5 * bent) * (1.0 + half * (1.0 - bent)))
    bias_out[0:1] = column_sum(delta)
    pooled_delta[...] = join(dot(split(delta), squeeze_ref[...], ((1,), (1,)))) / area
    for block in range(BLOCKS):
        first = min(BLOCK * block // CHUNK, SHARDS - 3)
        shape = (3 * CHUNK_PAD, LANES)
        place_in = lax.broadcasted_iota(jnp.int32, shape, 0)
        lane = lax.broadcasted_iota(jnp.int32, shape, 1)
        channel = CHUNK * (first + place_in // CHUNK_PAD) + place_in % CHUNK_PAD
        pick = (channel == BLOCK * block + lane) & (lane < BLOCK) & (place_in % CHUNK_PAD < CHUNK)
        source = pooled_delta[:, CHUNK_PAD * first : CHUNK_PAD * (first + 3)]
        gates_out[:, LANES * block : LANES * (block + 1)] = dot(
            split(source), one_hot(pick)
        ).astype(bf16)
    grads_out[:, INNER:] = outer(rows_ref[...], quarter_delta[...]).astype(bf16)
    grads_out[:, :INNER] = outer(pooled_ref[...], delta).astype(bf16)


def run_squeeze(gate_grad, pooled, inner, rows, quarter, squeeze, excite):
    vmem = pl.BlockSpec(memory_space=pltpu.VMEM)
    return pl.pallas_call(
        squeeze_kernel,
        out_shape=(
            jax.ShapeDtypeStruct((2 * CROPS, WIDE), bf16),
            jax.ShapeDtypeStruct((PADDED, 2 * INNER), bf16),
            jax.ShapeDtypeStruct((8, INNER), f32),
        ),
        in_specs=[vmem] * 7,
        out_specs=(vmem,) * 3,
        scratch_shapes=[
            pltpu.VMEM((QUARTERS * CROPS, INNER), f32),
            pltpu.VMEM((CROPS, INNER), f32),
            pltpu.VMEM((CROPS, PADDED), f32),
        ],
        name="squeeze",
        compiler_params=pltpu.CompilerParams(vmem_limit_bytes=VMEM_LIMIT),
        cost_estimate=pl.CostEstimate(
            flops=2 * 2**30, bytes_accessed=20 * 2**20, transcendentals=0
        ),
    )(gate_grad, pooled, inner, rows, quarter, squeeze, excite)


BIAS_ROWS = 32


def back_kernel(
    size,
    bias_ref,
    grad_ref,
    group_ref,
    late_group_ref,
    gates_ref,
    pooled_ref,
    spread_ref,
    act_ref,
    late_act_ref,
    turned_ref,
    conv_ref,
    x_turned_ref,
    param_ref,
    moment_ref,
    edges,
    fold_ref,
    delta_out,
    weight_out,
    conv_out,
    total_out,
    bias_out,
    *refs,
):
    if size == SHARDS:
        rest_out, *refs = refs
    (
    delta_two,
    delta_one,
    pads,
    windows,
    wide_ref,
    full_ref,
    sent,
    got,
    bias_got,
    send_sem,
    recv_sem,
    bias_sem,
    even_ref,
    odd_ref,
    *reduce_refs,
    ) = refs
    step = pl.program_id(0)
    count = row_count(size)
    on_global = lax.axis_index("stream") == 0
    reducer = Reducer(reduce_refs, BACK_INSIDE, rest_out) if reduce_refs else None

    def bend(moment, micro, tile, param, at):
        mean, inverse = moments(moment, micro, tile, count)
        gain = 0.5 * param[at + tile : at + tile + 1]
        shift = 0.5 * param[at + 2 + tile : at + tile + 3]

        def both(act):
            normed = act * inverse - mean * inverse
            half = normed * gain + shift
            bent = jnp.tanh(half)
            return normed, (0.5 + 0.5 * bent) * (1.0 + half * (1.0 - bent))

        return both

    @pl.when(step == 0)
    def _():
        barrier = img_barrier(size)
        pads[...] = jnp.zeros_like(pads)
        full_ref[...] = jnp.zeros_like(full_ref)
        windows[CONV_ROWS:] = jnp.zeros_like(windows[CONV_ROWS:])
        greeted = reducer.greet(barrier) if reducer else 0
        pl.semaphore_wait(barrier, size - 1 + greeted)
        stream = lax.axis_index("stream")
        me = lax.axis_index("img")
        bias_got[me] = bias_ref[...]

        def send(step, carry):
            pltpu.make_async_remote_copy(
                src_ref=bias_ref,
                dst_ref=bias_got.at[me],
                send_sem=bias_sem.at[0],
                recv_sem=bias_sem.at[1],
                device_id=(stream, lax.rem(me + step, size)),
                device_id_type=MESH,
            ).start()
            return carry

        lax.fori_loop(1, size, send, 0)

    @pl.when(step == BLOCKS)
    def _():
        others = bias_got.at[pl.ds(0, size - 1)]
        pltpu.make_async_copy(others, others, bias_sem.at[0]).wait()
        pltpu.make_async_copy(others, others, bias_sem.at[1]).wait()
        total = bias_got[0]
        for peer in range(1, size):
            total = total + bias_got[peer]
        bias_out[...] = total

    if reducer:

        def put(tile, rows, values):
            weight_out[rows, 128 * tile : 128 * tile + 128] = values

        reducer.advance(step - 2, put, BLOCKS)

    @pl.when(step < BLOCKS)
    def _():
        slot = lax.rem(step, 2)
        moment = moment_ref[step, 1]
        param = param_ref[step]
        sums = Sums()
        for micro in range(MICRO_BATCHES):
            bends = [bend(moment, micro, tile, param, 4) for tile in range(2)]
            for chunk in range(HALF_STEPS * micro, HALF_STEPS * (micro + 1)):
                here = chunk_rows(chunk)
                gate = dot(spread_ref[here], gates_ref[...])
                pooled = dot(spread_ref[here], pooled_ref[...])
                for tile in range(2):
                    lanes = slice(128 * tile, 128 * tile + 128)
                    normed, slope = bends[tile](group_ref[here, lanes])
                    delta = (grad_ref[here, lanes] * gate[:, lanes] + pooled[:, lanes]) * slope
                    delta_two[slot, tile, here] = delta
                    sums.add(micro, tile, delta, delta * normed)
        send_sums(size, step, sums.packed(), sent, got, send_sem, recv_sem)

    @pl.when((step >= 1) & (step < BLOCKS + 1))
    def _():
        block = step - 1
        slot = lax.rem(block, 2)
        total = take_sums(size, block, got, send_sem, recv_sem)
        total_out[block, 0] = total
        param = param_ref[block]
        moment = moment_ref[block, 1]
        backs = {
            (micro, tile): norm_back(moment, total, micro, tile, param[4 + tile : 5 + tile], count)
            for micro in range(MICRO_BATCHES)
            for tile in range(2)
        }

        def delta_rows(tile, start, length):
            here = slice(start, start + length)
            return backs[start // HALF, tile](
                delta_two[slot, tile, here], late_group_ref[here, 128 * tile : 128 * tile + 128]
            )

        same = same_group(LANES, BLOCK)
        for offset in range(9):
            full = dot(fold_ref[...], conv_ref[offset], ((1,), (1,)))
            full_ref[LANES * offset : LANES * (offset + 1), :BLOCK] = jnp.where(
                same, full, 0.0
            ).astype(bf16)

        def convolve(image):
            stack_windows(pads, windows, image, -1)
            here = slice(IMAGE_PAD * image, IMAGE_PAD * (image + 1))
            wide = dot(windows[here], full_ref[...])
            wide_ref[0, here] = wide[:, :128]
            wide_ref[1, here] = wide[:, 128:]

        moment_one = moment_ref[block, 0]

        def finish(load):
            sums = Sums()
            for micro in range(MICRO_BATCHES):
                for tile in range(2):
                    bent = bend(moment_one, micro, tile, param, 0)
                    for chunk in range(HALF_STEPS * micro, HALF_STEPS * (micro + 1)):
                        here = chunk_rows(chunk)
                        normed, slope = bent(act_ref[here, 128 * tile : 128 * tile + 128])
                        delta = load(tile, chunk) * slope
                        delta_one[slot, tile, here] = delta
                        sums.add(micro, tile, delta, delta * normed)
            send_sums(
                size, BLOCKS + block, sums.packed(), sent, got, send_sem, recv_sem
            )

        @pl.when(on_global)
        def _():
            pad_global(delta_rows, pads, edges)
            for image in range(IMAGE_DEV):
                convolve(image)
            finish(lambda tile, chunk: unpadded(wide_ref, tile, STEP // 8 * chunk, STEP // 8))

        @pl.when(jnp.logical_not(on_global))
        def _():
            rows_ref = delta_one.at[slot]
            for chunk in range(STEPS):
                for tile in range(2):
                    rows_ref[tile, chunk_rows(chunk)] = delta_rows(tile, STEP * chunk, STEP)
            pad_small(rows_ref, pads)
            for image in range(IMAGE_DEV):
                convolve(image)
            for chunk in range(STEPS):
                for tile in range(2):
                    rows_ref[tile, chunk_rows(chunk)] = jnp.zeros((STEP, 128), f32)
            unpad_small(wide_ref, rows_ref)
            finish(lambda tile, chunk: rows_ref[tile, chunk_rows(chunk)])

        for offset in range(9):
            grad = dot(turned_ref[0], windows[:, LANES * offset : LANES * (offset + 1)])
            pieces = []
            for group in range(4):
                here = slice(GROUP_WIDTH * group, GROUP_WIDTH * (group + 1))
                pieces.append(grad[here, here])
            even_ref[:, :GROUP_WIDTH] = jnp.concatenate(pieces)
            lines = [even_ref[pl.ds(start, BLOCK // 2, 2), :GROUP_WIDTH] for start in range(2)]
            odd_ref[:, :GROUP_WIDTH] = lines[0]
            odd_ref[:, GROUP_WIDTH : 2 * GROUP_WIDTH] = lines[1]
            conv_out[offset] = odd_ref[:, : 2 * GROUP_WIDTH].astype(bf16)

    @pl.when((step >= 2) & (step < BLOCKS + 2))
    def _():
        block = step - 2
        slot = lax.rem(block, 2)
        total = take_sums(size, BLOCKS + block, got, send_sem, recv_sem)
        total_out[block, 1] = total
        param = param_ref[block]
        moment = moment_ref[block, 0]
        for micro in range(MICRO_BATCHES):
            for tile in range(2):
                lanes = slice(128 * tile, 128 * tile + 128)
                back = norm_back(moment, total, micro, tile, param[tile : tile + 1], count)
                for chunk in range(HALF_STEPS * micro, HALF_STEPS * (micro + 1)):
                    here = chunk_rows(chunk)
                    delta_out[here, lanes] = back(
                        delta_one[slot, tile, here], late_act_ref[here, lanes]
                    ).astype(bf16)
        grad = dot(x_turned_ref[...], delta_out[...])
        if reducer:
            reducer.begin(block, grad)
        else:
            weight_out[...] = grad.astype(bf16)


def run_back(
    size, bias, grad, group, gates, pooled, spread, act, turned, conv, x_turned, params, moment, edges, fold
):
    reduced = size == SHARDS
    return pl.pallas_call(
        functools.partial(back_kernel, size),
        grid=(max(BLOCKS + 2, BACK_INSIDE + 6) if reduced else BLOCKS + 2,),
        out_shape=(
            jax.ShapeDtypeStruct((ROWS, WIDE), bf16),
            jax.ShapeDtypeStruct((CHUNK_PAD, LANES * BACK_INSIDE), f32)
            if reduced
            else jax.ShapeDtypeStruct((PADDED, WIDE), bf16),
            jax.ShapeDtypeStruct((9, CHANNELS // 2, 2 * GROUP_WIDTH), bf16),
            jax.ShapeDtypeStruct((BLOCKS, 2, 8, 128), f32),
            jax.ShapeDtypeStruct((BIAS_ROWS, 128), f32),
        )
        + ((jax.ShapeDtypeStruct((BACK_REST,) + Reducer.SHAPE, bf16),) if reduced else ()),
        in_specs=[
            whole((BIAS_ROWS, 128)),
            columns(ROWS, 0, BLOCKS),
            columns(ROWS, 0, BLOCKS),
            columns(ROWS, 1, BLOCKS),
            columns(2 * CROPS, 0, BLOCKS),
            columns(2 * CROPS, 0, BLOCKS),
            whole((ROWS, 2 * CROPS)),
            columns(ROWS, 1, BLOCKS),
            columns(ROWS, 2, BLOCKS),
            pl.BlockSpec((1, LANES, DEEP_ROWS), lambda i: (jnp.clip(i - 1, 0, BLOCKS - 1), 0, 0)),
            pl.BlockSpec((9, BLOCK, GROUP_WIDTH), lambda i: (0, jnp.clip(i - 1, 0, BLOCKS - 1), 0)),
            whole((PADDED, ROWS)),
            whole((BLOCKS, 8, 128)),
            whole((BLOCKS, 2, 8, 128)),
            whole((2, IMAGE_PAD, 128)),
            whole((LANES, GROUP_WIDTH)),
        ],
        out_specs=(
            columns(ROWS, 2, BLOCKS),
            columns(CHUNK_PAD, 6, BACK_INSIDE) if reduced else columns(PADDED, 2, BLOCKS),
            pl.BlockSpec(
                (9, BLOCK // 2, 2 * GROUP_WIDTH), lambda i: (0, jnp.clip(i - 1, 0, BLOCKS - 1), 0)
            ),
            pl.BlockSpec((BLOCKS, 2, 8, 128), lambda i: (0, 0, 0, 0)),
            pl.BlockSpec((BIAS_ROWS, 128), lambda i: (0, 0)),
        )
        + ((pl.BlockSpec(memory_space=HBM),) if reduced else ()),
        scratch_shapes=[
            pltpu.VMEM((2, 2, ROWS, 128), f32),
            pltpu.VMEM((2, 2, ROWS, 128), f32),
            pltpu.VMEM((3, 2, PAD_ROWS, 128), f32),
            pltpu.VMEM((DEEP_ROWS, 9 * LANES), bf16),
            pltpu.VMEM((2, CONV_ROWS, 128), f32),
            pltpu.VMEM((9 * LANES, LANES), bf16),
            pltpu.VMEM((2 * BLOCKS, 8, 128), f32),
            pltpu.VMEM((2 * BLOCKS, size, 8, 128), f32),
            pltpu.VMEM((size, BIAS_ROWS, 128), f32),
            pltpu.SemaphoreType.DMA((2 * BLOCKS,)),
            pltpu.SemaphoreType.DMA((2 * BLOCKS,)),
            pltpu.SemaphoreType.DMA((2,)),
            pltpu.VMEM((BLOCK, 128), f32),
            pltpu.VMEM((BLOCK // 2, 128), f32),
        ]
        + (Reducer.scratch() if reduced else []),
        name="back",
        compiler_params=pltpu.CompilerParams(
            collective_id=3, has_side_effects=True, vmem_limit_bytes=VMEM_LIMIT
        ),
        cost_estimate=pl.CostEstimate(
            flops=2 * ROWS * WIDE * (PADDED + 18 * LANES),
            bytes_accessed=90 * 2**20,
            transcendentals=2 * ROWS * WIDE,
        ),
    )(bias, grad, group, group, gates, pooled, spread, act, act, turned, conv, x_turned, params, moment, edges, fold)


CONV_LINES = 1152


def gather_kernel(
    entry_ref,
    conv_ref,
    x_ref,
    live_ref,
    lane_ref,
    entry_out,
    conv_out,
    chunk_out,
    turned_out,
    x_rows,
    chunk_rows_ref,
    turned_rows,
    send_sem,
    recv_sem,
    local_sem,
    store_sem,
):
    stream, z, x, core = place()
    pieces = (entry_ref, conv_ref)
    wholes = (entry_out, conv_out)
    quarters = (CHUNK_PAD // 4, CONV_LINES // 4)
    waiting = []

    def shard(k, across=0, beside=0):
        return 4 * (z ^ k) + 2 * (x ^ across) + (core ^ beside)

    def region(array, index, first, count):
        rows = quarters[array]
        return wholes[array].at[index, pl.ds(pl.multiple_of(rows * first, 16), rows * count)]

    def device(name, k=0):
        if name == "y":
            return (1 - stream, shard(0))
        return (stream, {"z": shard(k), "x": shard(0, 1), "core": shard(0, 0, 1)}[name])

    def push(slot, to, index, first, count, k=0, own=False):
        for array in range(2):
            target = region(array, index, first, count)
            source = target
            if own:
                rows = quarters[array]
                source = pieces[array].at[
                    pl.ds(pl.multiple_of(rows * first, 16), rows * count)
                ]
            pltpu.make_async_remote_copy(
                src_ref=source,
                dst_ref=target,
                send_sem=send_sem.at[array, slot],
                recv_sem=recv_sem.at[array, slot],
                device_id=device(to, k),
                device_id_type=MESH,
            ).start()
            waiting.append((array, slot, target))

    def arrive(slot, index, first, count):
        for array in range(2):
            target = region(array, index, first, count)
            pltpu.make_async_copy(target, target, recv_sem.at[array, slot]).wait()

    barrier = pltpu.get_barrier_semaphore()
    for name, k in (("z", 1), ("z", 2), ("z", 3), ("x", 0), ("y", 0), ("core", 0)):
        pl.semaphore_signal(barrier, inc=1, device_id=device(name, k), device_id_type=MESH)
    load = pltpu.make_async_copy(x_ref, x_rows, local_sem.at[2])
    load.start()
    keep = [
        pltpu.make_async_copy(pieces[array], wholes[array].at[shard(0)], local_sem.at[array])
        for array in range(2)
    ]
    for copy in keep:
        copy.start()
    pl.semaphore_wait(barrier, 6)

    push(6, "x", shard(0), stream, 3, own=True)
    for k in (1, 2, 3):
        push(k - 1, "z", shard(0), 2 * stream, 2, k, own=True)
    push(17, "core", shard(0), 0, 4, own=True)

    stores = []

    def prepare(pair):
        if pair == 0:
            load.wait()
        slot = pair % 2
        if pair >= 2:
            for copy in stores[pair - 2]:
                copy.wait()
        first = (PAIR * pair) // 128
        depth = min(384, CHANNELS - 128 * first)
        source = 128 * first - PAIR * pair
        values = x_rows[:, 128 * first : 128 * first + depth]
        there = lax.broadcasted_iota(jnp.int32, (depth, LANES), 0) + source
        pick = one_hot(there == pair_lane((depth, LANES), 1))
        picked = dot(values, pick)
        for tile in range(2):
            lanes = slice(128 * tile, 128 * tile + 128)
            chunk_rows_ref[slot, :, lanes] = (
                picked[:, lanes] * live_ref[...].astype(f32)
            ).astype(bf16)
        there = lax.broadcasted_iota(jnp.int32, (LANES, depth), 1) + source
        pick = one_hot(there == pair_lane((LANES, depth), 0))
        turned_rows[slot] = (dot(pick, values, ((1,), (1,))) * lane_ref[...]).astype(bf16)
        lanes = slice(LANES * pair, LANES * (pair + 1))
        copies = (
            pltpu.make_async_copy(chunk_rows_ref.at[slot], chunk_out.at[:, lanes], store_sem.at[0, pair]),
            pltpu.make_async_copy(turned_rows.at[slot], turned_out.at[lanes], store_sem.at[1, pair]),
        )
        for copy in copies:
            copy.start()
        stores.append(copies)

    def from_z(k):
        arrive(k - 1, shard(k), 2 * stream, 2)
        push(6 + k, "x", shard(k), 2 * stream, 2)
        push(2 + k, "y", shard(k), 2 * stream, 2)
        push(17 + k, "core", shard(k), 2 * stream, 2)

    def from_y(k):
        arrive(2 + k, shard(k), 2 - 2 * stream, 2)
        push(9 + k, "x", shard(k), 2 - stream, 1)
        push(20 + k, "core", shard(k), 2 - 2 * stream, 2)

    def from_x(k):
        if k == 0:
            arrive(6, shard(0, 1), stream, 3)
            push(13, "y", shard(0, 1), 3 * stream, 1)
            push(24, "core", shard(0, 1), stream, 3)
        else:
            arrive(6 + k, shard(k, 1), 2 * stream, 2)
            push(13 + k, "y", shard(k, 1), 3 * stream, 1)
            push(24 + k, "core", shard(k, 1), 2 * stream, 2)

    def last_x(k):
        arrive(9 + k, shard(k, 1), 2 - stream, 1)
        push(27 + k, "core", shard(k, 1), 2 - stream, 1)

    def last_y(k):
        arrive(13 + k, shard(k, 1), 3 - 3 * stream, 1)
        push(31 + k, "core", shard(k, 1), 3 - 3 * stream, 1)

    prepare(0)
    prepare(1)
    from_z(1)
    prepare(2)
    from_z(2)
    from_x(0)
    prepare(3)
    from_z(3)
    from_y(1)
    prepare(4)
    from_x(1)
    from_y(2)
    prepare(5)
    from_x(2)
    from_y(3)
    prepare(6)
    from_x(3)
    last_y(0)
    last_x(1)
    prepare(7)
    last_y(1)
    last_x(2)
    last_y(2)
    last_x(3)
    last_y(3)

    arrive(17, shard(0, 0, 1), 0, 4)
    for k in (1, 2, 3):
        arrive(17 + k, shard(k, 0, 1), 2 * stream, 2)
        arrive(20 + k, shard(k, 0, 1), 2 - 2 * stream, 2)
    arrive(24, shard(0, 1, 1), stream, 3)
    for k in (1, 2, 3):
        arrive(24 + k, shard(k, 1, 1), 2 * stream, 2)
        arrive(27 + k, shard(k, 1, 1), 2 - stream, 1)
    for k in range(4):
        arrive(31 + k, shard(k, 1, 1), 3 - 3 * stream, 1)
    for array, slot, target in waiting:
        pltpu.make_async_copy(target, target, send_sem.at[array, slot]).wait()
    for copy in keep:
        copy.wait()
    for pair in (6, 7):
        for copy in stores[pair]:
            copy.wait()


def run_gather(entry, conv, x, live, lane):
    return pl.pallas_call(
        gather_kernel,
        out_shape=(
            jax.ShapeDtypeStruct((SHARDS, CHUNK_PAD, WIDE), bf16),
            jax.ShapeDtypeStruct((SHARDS, CONV_LINES, 128), bf16),
            jax.ShapeDtypeStruct((ROWS, PADDED), bf16),
            jax.ShapeDtypeStruct((PADDED, ROWS), bf16),
        ),
        in_specs=[pl.BlockSpec(memory_space=HBM)] * 3
        + [pl.BlockSpec(memory_space=pltpu.VMEM)] * 2,
        out_specs=(pl.BlockSpec(memory_space=HBM),) * 4,
        scratch_shapes=[
            pltpu.VMEM((ROWS, CHANNELS), bf16),
            pltpu.VMEM((2, ROWS, LANES), bf16),
            pltpu.VMEM((2, LANES, ROWS), bf16),
            pltpu.SemaphoreType.DMA((2, 35)),
            pltpu.SemaphoreType.DMA((2, 35)),
            pltpu.SemaphoreType.DMA((3,)),
            pltpu.SemaphoreType.DMA((2, OUT_BLOCKS)),
        ],
        name="gather",
        compiler_params=pltpu.CompilerParams(
            collective_id=4, has_side_effects=True, vmem_limit_bytes=VMEM_LIMIT
        ),
        cost_estimate=pl.CostEstimate(
            flops=4 * ROWS * 384 * PADDED, bytes_accessed=200 * 2**20, transcendentals=0
        ),
    )(entry, conv, x, live, lane)


def input_kernel(delta_ref, weight_ref, residual_ref, live_ref, *refs):
    block = pl.program_id(0)
    if len(refs) == 1:
        (grad_out,) = refs
    else:
        rest_ref, conv_ref, grad_out, part_out, *reduce_refs = refs
        sources = [(rest_ref, BACK_REST), (conv_ref, CONV_BLOCKS)]
        feed(Reducer(reduce_refs, BACK_REST + CONV_BLOCKS), block, sources, part_out)

    @pl.when(block < OUT_BLOCKS)
    def _():
        spans = 4
        first = jnp.minimum((LANES * block) // CHUNK, SHARDS - spans)
        depth = spans * CHUNK_PAD
        row = lax.broadcasted_iota(jnp.int32, (LANES, depth), 0) + LANES * block
        lane = lax.broadcasted_iota(jnp.int32, (LANES, depth), 1)
        channel = CHUNK * (first + lane // CHUNK_PAD) + lane % CHUNK_PAD
        pick = one_hot((channel == row) & (lane % CHUNK_PAD < CHUNK))
        rows = pl.ds(pl.multiple_of(CHUNK_PAD * first, CHUNK_PAD), depth)
        weight = dot(pick, weight_ref[rows]).astype(bf16)
        for micro in range(MICRO_BATCHES):
            here = slice(HALF * micro, HALF * (micro + 1))
            grad = dot(delta_ref[here], weight, ((1,), (1,)))
            for tile in range(2):
                lanes = slice(128 * tile, 128 * tile + 128)
                grad_out[here, lanes] = (
                    (grad[:, lanes] + residual_ref[here, lanes].astype(f32))
                    * live_ref[here].astype(f32)
                ).astype(bf16)


def run_input(delta, weight, residual, live, *rest):
    reduced = bool(rest)
    out_shape = jax.ShapeDtypeStruct((ROWS, CHANNELS), bf16)
    out_specs = columns(ROWS, 0, OUT_BLOCKS)
    in_specs = [
        whole((ROWS, WIDE)),
        whole((PADDED, WIDE)),
        columns(ROWS, 0, OUT_BLOCKS),
        whole((ROWS, 128)),
    ]
    args = [delta, weight, residual, live]
    if reduced:
        shape = (BACK_REST + CONV_BLOCKS, 2, 128, 128)
        out_shape = (out_shape, jax.ShapeDtypeStruct(shape, f32))
        out_specs = (out_specs, pl.BlockSpec(shape, lambda i: (0, 0, 0, 0)))
        in_specs += [pl.BlockSpec(memory_space=HBM)] * 2
        args += rest
    return pl.pallas_call(
        input_kernel,
        grid=(BACK_REST + CONV_BLOCKS + 4 if reduced else OUT_BLOCKS,),
        out_shape=out_shape,
        in_specs=in_specs,
        out_specs=out_specs,
        scratch_shapes=Reducer.scratch() if reduced else [],
        name="input",
        compiler_params=pltpu.CompilerParams(
            vmem_limit_bytes=VMEM_LIMIT,
            collective_id=5 if reduced else None,
            has_side_effects=reduced,
        ),
        cost_estimate=pl.CostEstimate(
            flops=2 * ROWS * WIDE * PADDED, bytes_accessed=35 * 2**20, transcendentals=0
        ),
    )(*args)


def wide_lanes(values):
    lead = values.shape[:-1]
    blocks = values.reshape(lead + (BLOCKS, BLOCK))
    padded = jnp.pad(blocks, ((0, 0),) * len(lead) + ((0, 0), (0, LANES - BLOCK)))
    return padded.reshape(lead + (WIDE,))


def narrow_lanes(values):
    lead = values.shape[:-1]
    return values.reshape(lead + (BLOCKS, LANES))[..., :BLOCK].reshape(lead + (CHANNELS,))


def gather(piece, width, size):
    across = -(-width // 128) * 128
    pads = ((0, CHUNK_PAD - CHUNK), (0, across - width))
    if size == SHARDS:
        piece = jnp.pad(piece.reshape(CHUNK, width), pads)
        return lax.all_gather(piece, "img", axis=0, tiled=True)
    pieces = lax.all_gather(piece, "img", axis=0, tiled=True).reshape(SHARDS, CHUNK, width)
    return jnp.pad(pieces, ((0, 0),) + pads).reshape(PADDED, across)


def scatter(grads, width, size):
    if size != SHARDS:
        grads = grads.reshape(SHARDS, CHUNK_PAD, -1)[:, :CHUNK, :width].reshape(-1)
    return lax.psum_scatter(grads, "img", scatter_dimension=0, tiled=True)


def shard_of(part, width, size):
    part = swap_sum(part)
    return part[:CHUNK, :width].reshape(-1) if size == SHARDS else part


def swap_sum(part):
    other = lax.ppermute(part, "stream", [(0, 1), (1, 0)])
    return part.astype(f32) + other.astype(f32)


def beside_blocks(first, blocks):
    return jnp.concatenate([first, blocks.transpose(2, 0, 1, 3).reshape(128, -1)], axis=1)


def chunked(values):
    lead = values.shape[:-1]
    values = values.reshape(lead + (SHARDS, CHUNK))
    values = jnp.pad(values, ((0, 0),) * len(lead) + ((0, 0), (0, CHUNK_PAD - CHUNK)))
    return values.reshape(lead + (PADDED,))


def unchunked(values):
    lead = values.shape[:-1]
    values = values.reshape(lead + (SHARDS, CHUNK_PAD))[..., :CHUNK]
    return values.reshape(lead + (CHANNELS,))


def local(
    block_in,
    out_cotangent,
    pair_target,
    entry_weight,
    entry_gain,
    entry_shift,
    group_weight,
    group_gain,
    group_shift,
    squeeze_weight,
    squeeze_bias,
    excite_weight,
    excite_bias,
    exit_weight,
    exit_gain,
    exit_shift,
):
    size = lax.axis_size("img")
    stream = lax.axis_index("stream")
    on_global = stream == 0
    positions = jnp.arange(ROWS, dtype=jnp.int32)
    image_of = positions // IMAGE_ROWS
    within = positions % IMAGE_ROWS
    live = within < jnp.where(on_global, IMAGE_ROWS, SMALL_ROWS)
    area = jnp.where(on_global, GLOBAL_SIDE**2, SMALL_SIDE**2)
    crop_of = within // area
    crop_ids = jnp.arange(CROPS, dtype=jnp.int32)
    per_image = jnp.where(on_global, GLOBAL_CROPS, SMALL_CROPS)
    pool_full = live[None] & ((image_of * per_image + crop_of)[None] == crop_ids[:, None])
    pool = pool_full.astype(bf16)
    target_rows = jnp.zeros((ROWS,), jnp.int32)
    for slot in range(SMALL_CROPS):
        target_rows = jnp.where(
            crop_of == slot, jnp.repeat(pair_target[:, slot], IMAGE_ROWS), target_rows
        )
    pair_of = image_of * GLOBAL_CROPS + jnp.where(on_global, crop_of, target_rows)
    pair = (live[None] & (pair_of[None] == crop_ids[:, None])).astype(bf16)
    live_lanes = jnp.broadcast_to(live[:, None], (ROWS, 128)).astype(bf16)
    edges = edge_masks()

    x = block_in[0]
    cot = out_cotangent[0]

    lines = CONV_LINES - 18
    if size == SHARDS:
        entry_piece = wide_lanes(entry_weight.reshape(CHUNK, CHANNELS))
        entry_piece = jnp.pad(entry_piece, ((0, CHUNK_PAD - CHUNK), (0, 0)))
        piece = group_weight.reshape(lines, GROUP_WIDTH)
        piece = jnp.pad(piece, ((0, CONV_LINES - lines), (0, 128 - GROUP_WIDTH)))
        entry_mat, conv, x_chunked, x_turned = run_gather(
            entry_piece, piece, x, live_lanes, live[None].astype(f32)
        )
        entry_mat = entry_mat.reshape(PADDED, WIDE)
        conv = conv[:, :lines, :GROUP_WIDTH]
    else:
        x_padded = jnp.where(live[:, None], x, 0)
        x_padded = jnp.pad(x_padded, ((0, 0), (0, PADDED - CHANNELS)))
        x_chunked, x_turned = run_prepare(x_padded)
        entry_mat = wide_lanes(gather(entry_weight, CHANNELS, size)[:, :CHANNELS])
        conv = lax.all_gather(group_weight, "img", axis=0, tiled=True)
    conv = conv.reshape(9, CHANNELS, GROUP_WIDTH)
    squeeze_mat = gather(squeeze_weight, SQUEEZE, size)
    excite_mat = gather(excite_weight, SQUEEZE, size)
    exit_mat = gather(exit_weight, CHANNELS, size)

    def rows_of(*vectors):
        kept = wide_lanes(jnp.stack(vectors)).reshape(len(vectors), BLOCKS, 2, 128)
        return kept.transpose(1, 0, 2, 3).reshape(BLOCKS, 2 * len(vectors), 128)

    params = rows_of(entry_gain, entry_shift, group_gain, group_shift)
    exit_params = [
        jnp.pad(vector, (0, PADDED - CHANNELS)).reshape(OUT_BLOCKS, 2, 128)
        for vector in (exit_gain, exit_shift)
    ]
    exit_params = jnp.concatenate(exit_params * 2, axis=1)

    fold = np.zeros((LANES, GROUP_WIDTH), np.float32)
    fold[np.arange(BLOCK), np.arange(BLOCK) % GROUP_WIDTH] = 1
    fold = jnp.asarray(fold, bf16)
    act, turned, group, mixed, pooled, moment = run_entry(
        size, x_chunked, entry_mat, conv, params, pool, edges, fold.T
    )

    inner_pad = INNER - SQUEEZE
    spread = jnp.concatenate([pool.T, pool.T], axis=1)
    scaled, scaled_turned, gates, pooled, inner, inner_rows, quarter = run_scale(
        mixed,
        spread,
        pooled,
        squeeze_mat,
        excite_mat,
        jnp.pad(squeeze_bias, (0, inner_pad))[None],
        jnp.pad(excite_bias.reshape(QUARTERS, SQUEEZE), ((0, 0), (0, inner_pad))),
    )

    block_out, exit_delta, residual, exit_grad, exit_total = run_exit(
        size, scaled, scaled_turned, exit_mat, x, cot, exit_params, pair, pair.T, live_lanes
    )
    exit_part = scatter(exit_grad, CHANNELS, size)
    scaled_grad, gate_grad = run_gate(exit_delta, exit_mat, mixed, pool)

    pooled_gates, inner_grads, bias_rows = run_squeeze(
        gate_grad, pooled, inner, inner_rows, quarter, squeeze_mat, excite_mat
    )
    bias_rows = bias_rows.reshape(BIAS_ROWS, 128)
    entry_delta, entry_grad, conv_grad, totals, bias_totals, *entry_rest = run_back(
        size, bias_rows, scaled_grad, group, gates, pooled_gates, spread, act, turned, conv, x_turned, params,
        moment, edges, fold,
    )
    entry_delta, exit_part, inner_grads = lax.optimization_barrier(
        (entry_delta, exit_part, inner_grads)
    )
    exit_shard = shard_of(exit_part, CHANNELS, size)
    if size == SHARDS:
        inner_part = swap_sum(scatter(inner_grads, 2 * INNER, size))[:CHUNK]
        squeeze_shard = inner_part[:, :SQUEEZE].reshape(-1)
        excite_shard = inner_part[:, INNER : INNER + SQUEEZE].reshape(-1)
    else:
        squeeze_shard = shard_of(scatter(inner_grads[:, :INNER], SQUEEZE, size), SQUEEZE, size)
        excite_shard = shard_of(scatter(inner_grads[:, INNER:], SQUEEZE, size), SQUEEZE, size)
    if size == SHARDS:
        conv_lines = 256 * CONV_BLOCKS
        conv_grad = conv_grad.reshape(SHARDS, lines // 2, 2 * GROUP_WIDTH)
        conv_grad = jnp.pad(
            conv_grad,
            ((0, 0), (0, conv_lines - lines // 2), (0, 128 - 2 * GROUP_WIDTH)),
        ).reshape(4, 2, 2, CONV_BLOCKS, 2, 128, 128)
        conv_grad = conv_grad.transpose(3, 2, 1, 0, 4, 5, 6)
        input_grad, parts = run_input(
            entry_delta, entry_mat, residual, live_lanes, entry_rest[0], conv_grad
        )
        entry_grad = beside_blocks(entry_grad, parts[:BACK_REST])
        entry_shard = narrow_lanes(entry_grad[:CHUNK]).reshape(-1)
        conv_part = parts[BACK_REST:].reshape(conv_lines, 128)
        conv_shard = conv_part[: lines // 2, : 2 * GROUP_WIDTH].reshape(-1)
    else:
        input_grad = run_input(entry_delta, entry_mat, residual, live_lanes)
        entry_shard = swap_sum(scatter(narrow_lanes(entry_grad), CHANNELS, size))
        conv_part = lax.psum_scatter(
            conv_grad.reshape(-1), "img", scatter_dimension=0, tiled=True
        )
        conv_shard = swap_sum(conv_part)
    shards = (entry_shard, conv_shard, squeeze_shard, excite_shard, exit_shard)

    def folded(kept):
        kept = kept.reshape(-1, MICRO_BATCHES, 2, LANES).sum(axis=1)
        return kept[:, 1].reshape(-1), kept[:, 0].reshape(-1)

    group_gain_grad, group_shift_grad = [narrow_lanes(v) for v in folded(totals[:, 0])]
    entry_gain_grad, entry_shift_grad = [narrow_lanes(v) for v in folded(totals[:, 1])]
    exit_gain_grad, exit_shift_grad = [v[:CHANNELS] for v in folded(exit_total[:, 1])]
    bias_totals = bias_totals.reshape(8, INNER)[: 1 + QUARTERS, :SQUEEZE]
    kept = jnp.concatenate(
        [
            jnp.stack(
                [
                    entry_gain_grad,
                    entry_shift_grad,
                    group_gain_grad,
                    group_shift_grad,
                    exit_gain_grad,
                    exit_shift_grad,
                    bias_totals[1:].reshape(-1),
                ]
            ),
            jnp.pad(bias_totals[0], (0, CHANNELS - SQUEEZE))[None],
        ]
    )
    smalls = swap_sum(kept)

    return (
        block_out[None],
        input_grad[None],
        shards[0],
        smalls[0],
        smalls[1],
        shards[1],
        smalls[2],
        smalls[3],
        shards[2],
        smalls[7, :SQUEEZE],
        shards[3],
        smalls[6],
        shards[4],
        smalls[4],
        smalls[5],
    )


def solution(mesh):
    return jax.shard_map(
        local,
        mesh=mesh,
        in_specs=(
            P("stream", "img", None),
            P("stream", "img", None),
            P("img", None),
            P("img"),
            P(),
            P(),
            P("img"),
            P(),
            P(),
            P("img"),
            P(),
            P("img"),
            P(),
            P("img"),
            P(),
            P(),
        ),
        out_specs=(
            P("stream", "img", None),
            P("stream", "img", None),
            P("img"),
            P(),
            P(),
            P("img"),
            P(),
            P(),
            P("img"),
            P(),
            P("img"),
            P(),
            P("img"),
            P(),
            P(),
        ),
        check_vma=False,
    )
```

```python
import functools

import jax
import jax.numpy as jnp
import numpy as np
from jax import lax
from jax.experimental import pallas as pl
from jax.experimental.pallas import tpu as pltpu
from jax.sharding import PartitionSpec as P

CHANNELS = 2016
GROUPS = 36
SQUEEZE = 504
GROUP_WIDTH = 56
GLOBAL_SIDE = 14
SMALL_SIDE = 7
GLOBAL_CROPS = 2
SMALL_CROPS = 3
IMAGE_DEV = 4
MICRO_BATCHES = 2
IMAGE_ROWS = 392
SMALL_ROWS = 147
ROWS = IMAGE_DEV * IMAGE_ROWS
HALF = ROWS // MICRO_BATCHES

BLOCK = 224
LANES = 256
BLOCKS = CHANNELS // BLOCK
WIDE = BLOCKS * LANES
PADDED = 2048
OUT_BLOCKS = PADDED // LANES

IMAGE_PAD = 424
TOP = 16
CONV_ROWS = IMAGE_DEV * IMAGE_PAD
DEEP_ROWS = 1792
PAD_ROWS = TOP + DEEP_ROWS + 16
CROPS = 16
STEP = 112
STEPS = ROWS // STEP
HALF_STEPS = HALF // STEP
CHUNK = 126
CHUNK_PAD = 128
SHARDS = CHANNELS // CHUNK
PAIR = 2 * CHUNK

EPSILON = 1e-05
PAIR_SCALE = 4.0
MESH = pl.DeviceIdType.MESH
HBM = pl.ANY
VMEM_LIMIT = 62 * 2**20

f32 = jnp.float32
bf16 = jnp.bfloat16


def dot(a, b, dims=((1,), (0,))):
    return lax.dot_general(a, b, (dims, ((), ())), preferred_element_type=f32)


def img_barrier(size):
    stream = lax.axis_index("stream")
    me = lax.axis_index("img")
    barrier = pltpu.get_barrier_semaphore()

    def greet(step, carry):
        pl.semaphore_signal(
            barrier, inc=1, device_id=(stream, lax.rem(me + step, size)), device_id_type=MESH
        )
        return carry

    lax.fori_loop(1, size, greet, 0)
    return barrier


class Exchange:
    def __init__(self, size, sent, got, send_sem, recv_sem):
        self.size, self.sent, self.got = size, sent, got
        self.send_sem, self.recv_sem = send_sem, recv_sem

    @staticmethod
    def scratch(steps, size):
        return [
            pltpu.VMEM((steps, 2, 8, 128), f32),
            pltpu.VMEM((steps, 2, size, 8, 128), f32),
            pltpu.SemaphoreType.DMA((steps, 2)),
            pltpu.SemaphoreType.DMA((steps, 2)),
        ]

    def put(self, slot, kind, packed):
        stream = lax.axis_index("stream")
        me = lax.axis_index("img")
        self.sent[slot, kind] = packed
        self.got[slot, kind, me] = packed

        def start(step, carry):
            pltpu.make_async_remote_copy(
                src_ref=self.sent.at[slot, kind],
                dst_ref=self.got.at[slot, kind, me],
                send_sem=self.send_sem.at[slot, kind],
                recv_sem=self.recv_sem.at[slot, kind],
                device_id=(stream, lax.rem(me + step, self.size)),
                device_id_type=MESH,
            ).start()
            return carry

        lax.fori_loop(1, self.size, start, 0)

    def total(self, slot, kind):
        others = self.got.at[slot, kind, pl.ds(0, self.size - 1)]
        pltpu.make_async_copy(others, others, self.recv_sem.at[slot, kind]).wait()
        pltpu.make_async_copy(others, others, self.send_sem.at[slot, kind]).wait()
        return add_up(self.got[slot, kind, peer] for peer in range(self.size))


def row_count(size):
    live = jnp.where(lax.axis_index("stream") == 0, IMAGE_ROWS, SMALL_ROWS)
    return (live * (size * (IMAGE_DEV // MICRO_BATCHES))).astype(f32)


def column_sum(values):
    return jnp.sum(values, axis=0, keepdims=True)


def moments(total, micro, tile, count):
    mean = total[4 * micro + tile : 4 * micro + tile + 1] / count
    square = total[4 * micro + 2 + tile : 4 * micro + 3 + tile] / count
    return mean, lax.rsqrt(square - mean * mean + EPSILON)


def edge_masks():
    column = np.arange(IMAGE_PAD) % 212 % 14
    both = np.stack([column != 13, column != 0]).astype(np.float32)
    return jnp.broadcast_to(jnp.asarray(both)[:, :, None], (2, IMAGE_PAD, 128))


def chunk_rows(chunk):
    return slice(STEP * chunk, STEP * (chunk + 1))


def add_up(pieces):
    pieces = list(pieces)
    while len(pieces) > 1:
        odd = [pieces.pop()] if len(pieces) % 2 else []
        pieces = [pieces[i] + pieces[i + 1] for i in range(0, len(pieces), 2)] + odd
    return pieces[0]


def fold_rows(values):
    return add_up(values[8 * i : 8 * i + 8] for i in range(values.shape[0] // 8))


class Sums:
    def __init__(self):
        self.parts = {}

    def add(self, micro, tile, plain, product):
        for kind, values in ((0, plain), (1, product)):
            key = (micro, kind, tile)
            self.parts.setdefault(key, []).append(fold_rows(values))

    def packed(self):
        return jnp.concatenate([column_sum(add_up(self.parts[key])) for key in sorted(self.parts)])


def put_pads(piece, place, tile, pads, edges):
    here = slice(place, place + piece.shape[0])
    inner = (place - TOP) % IMAGE_PAD
    inner = slice(inner, inner + piece.shape[0])
    pads[0, tile, here] = piece
    pads[1, tile, here] = piece * edges[0, inner]
    pads[2, tile, here] = piece * edges[1, inner]


def pad_global(load, pads, edges):
    inside = lax.broadcasted_iota(jnp.int32, (8, 128), 0)
    for image in range(IMAGE_DEV):
        base = TOP + IMAGE_PAD * image
        start = IMAGE_ROWS * image
        for tile in range(2):
            middle = load(tile, start + 192, 8)
            first = load(tile, start, 192)
            put_pads(first, base, tile, pads, edges)
            put_pads(jnp.where(inside < 4, middle, 0.0), base + 192, tile, pads, edges)
            put_pads(jnp.where(inside >= 4, middle, 0.0), base + 208, tile, pads, edges)
            second = load(tile, start + 200, 192)
            put_pads(second, base + 216, tile, pads, edges)


def small_strips():
    for image in range(IMAGE_DEV):
        for crop in range(SMALL_CROPS):
            for line in range(SMALL_SIDE):
                start = IMAGE_ROWS * image + 49 * crop + 7 * line
                yield start, IMAGE_PAD * image + 114 * crop + 14 * line


def pad_small(rows_ref, pads):
    for start, base in small_strips():
        for tile in range(2):
            piece = rows_ref[tile, start : start + 7]
            for kind in range(3):
                pads[kind, tile, TOP + base : TOP + base + 7] = piece


def unpad_small(wide_ref, rows_ref):
    for start, base in small_strips():
        for tile in range(2):
            rows_ref[tile, start : start + 7] = wide_ref[tile, base : base + 7]


def unpadded(wide_ref, tile, first, count):
    pieces = []
    at = first
    while at < first + count:
        image, inner = divmod(at, 49)
        base = IMAGE_PAD * image
        stop = 49 * image + (24 if inner < 24 else 25 if inner == 24 else 49)
        stop = min(stop, first + count)
        length = 8 * (stop - at)
        if inner == 24:
            inside = lax.broadcasted_iota(jnp.int32, (8, 128), 0)
            pieces.append(
                jnp.where(
                    inside < 4,
                    wide_ref[tile, base + 192 : base + 200],
                    wide_ref[tile, base + 208 : base + 216],
                )
            )
        else:
            start = base + 8 * inner + (0 if inner < 24 else 16)
            pieces.append(wide_ref[tile, start : start + length])
        at = stop
    return pieces[0] if len(pieces) == 1 else jnp.concatenate(pieces)


def stack_windows(pads, windows, image, sign):
    for offset in range(9):
        down, across = offset // 3 - 1, offset % 3 - 1
        shift = sign * (14 * down + across)
        kind = (0, 2, 1)[sign * across]
        start = TOP + IMAGE_PAD * image + shift
        for tile in range(2):
            at = LANES * offset + 128 * tile
            windows[IMAGE_PAD * image : IMAGE_PAD * (image + 1), at : at + 128] = pads[
                kind, tile, start : start + IMAGE_PAD
            ].astype(bf16)


def same_group(rows, lanes):
    row_group = lax.broadcasted_iota(jnp.int32, (rows, lanes), 0) // GROUP_WIDTH
    lane_group = lax.broadcasted_iota(jnp.int32, (rows, lanes), 1) // GROUP_WIDTH
    return row_group == lane_group


def entry_kernel(
    size,
    x_ref,
    weight_ref,
    conv_ref,
    param_ref,
    pool_ref,
    edges,
    fold_ref,
    act_out,
    turned_out,
    group_out,
    mixed_out,
    pooled_out,
    total_out,
    first_rows,
    second_rows,
    rows_ref,
    pads,
    windows,
    wide_ref,
    full_ref,
    *exchange_refs,
):
    exchange = Exchange(size, *exchange_refs)
    step = pl.program_id(0)
    count = row_count(size)
    on_global = lax.axis_index("stream") == 0

    @pl.when(step == 0)
    def _():
        barrier = img_barrier(size)
        pads[...] = jnp.zeros_like(pads)
        full_ref[...] = jnp.zeros_like(full_ref)
        second_rows[...] = jnp.zeros_like(second_rows)
        pl.semaphore_wait(barrier, size - 1)

    @pl.when(step < BLOCKS)
    def _():
        slot = lax.rem(step, 2)
        for micro in range(MICRO_BATCHES):
            here = slice(HALF * micro, HALF * (micro + 1))
            act = dot(x_ref[here], weight_ref[...])
            first_rows[slot, 0, here] = act[:, :128]
            first_rows[slot, 1, here] = act[:, 128:]
        sums = Sums()
        for chunk in range(STEPS):
            here = chunk_rows(chunk)
            for tile in range(2):
                act = first_rows[slot, tile, here]
                act_out[here, 128 * tile : 128 * tile + 128] = act
                sums.add(chunk // HALF_STEPS, tile, act, act * act)
        exchange.put(step, 0, sums.packed())

    @pl.when((step >= 1) & (step < BLOCKS + 1))
    def _():
        block = step - 1
        slot = lax.rem(block, 2)
        total = exchange.total(step - 1, 0)
        total_out[block, 0] = total
        param = param_ref[block]
        scales = {}
        for micro in range(MICRO_BATCHES):
            for tile in range(2):
                mean, inverse = moments(total, micro, tile, count)
                scale = 0.5 * inverse * param[tile : tile + 1]
                scales[micro, tile] = scale, 0.5 * param[2 + tile : 3 + tile] - mean * scale

        def hidden(tile, start, length):
            scale, shift = scales[start // HALF, tile]
            half = first_rows[slot, tile, start : start + length] * scale + shift
            return half + half * jnp.tanh(half)

        same = same_group(BLOCK, LANES)
        for offset in range(9):
            full = dot(conv_ref[offset], fold_ref[...])
            full_ref[LANES * offset : LANES * offset + BLOCK] = jnp.where(
                same, full, 0.0
            ).astype(bf16)

        def convolve(image, target):
            stack_windows(pads, windows, image, 1)
            here = slice(IMAGE_PAD * image, IMAGE_PAD * (image + 1))
            wide = dot(windows[here], full_ref[...])
            target[0, here] = wide[:, :128]
            target[1, here] = wide[:, 128:]

        def turn():
            for tile in range(2):
                turned_out[0, 128 * tile : 128 * tile + 128] = pads[
                    0, tile, TOP : TOP + DEEP_ROWS
                ].T.astype(bf16)

        @pl.when(on_global)
        def _():
            pad_global(hidden, pads, edges)
            turn()
            second = second_rows.at[slot]
            for image in range(IMAGE_DEV):
                convolve(image, second)
            sums = Sums()
            for chunk in range(STEPS):
                for tile in range(2):
                    act = unpadded(second, tile, STEP // 8 * chunk, STEP // 8)
                    sums.add(chunk // HALF_STEPS, tile, act, act * act)
            exchange.put(step, 1, sums.packed())

        @pl.when(jnp.logical_not(on_global))
        def _():
            for chunk in range(STEPS):
                for tile in range(2):
                    rows_ref[tile, chunk_rows(chunk)] = hidden(tile, STEP * chunk, STEP)
            pad_small(rows_ref, pads)
            turn()
            for image in range(IMAGE_DEV):
                convolve(image, wide_ref)
            second = second_rows.at[slot]
            unpad_small(wide_ref, second)
            sums = Sums()
            for chunk in range(STEPS):
                for tile in range(2):
                    act = second[tile, chunk_rows(chunk)]
                    sums.add(chunk // HALF_STEPS, tile, act, act * act)
            exchange.put(step, 1, sums.packed())

    @pl.when(step >= 2)
    def _():
        block = step - 2
        slot = lax.rem(block, 2)
        total = exchange.total(step - 1, 1)
        total_out[block, 1] = total
        param = param_ref[block]
        second = second_rows.at[slot]

        def finish(load):
            for micro in range(MICRO_BATCHES):
                for tile in range(2):
                    lanes = slice(128 * tile, 128 * tile + 128)
                    mean, inverse = moments(total, micro, tile, count)
                    scale = 0.5 * inverse * param[4 + tile : 5 + tile]
                    shift = 0.5 * param[6 + tile : 7 + tile] - mean * scale
                    for chunk in range(HALF_STEPS * micro, HALF_STEPS * (micro + 1)):
                        here = chunk_rows(chunk)
                        act = load(tile, chunk)
                        group_out[here, lanes] = act
                        half = act * scale + shift
                        mixed_out[here, lanes] = (half + half * jnp.tanh(half)).astype(bf16)

        @pl.when(on_global)
        def _():
            finish(lambda tile, chunk: unpadded(second, tile, STEP // 8 * chunk, STEP // 8))

        @pl.when(jnp.logical_not(on_global))
        def _():
            finish(lambda tile, chunk: second[tile, chunk_rows(chunk)])

        pooled_out[...] = dot(pool_ref[...], mixed_out[...])


def run_entry(size, x, weight, conv, params, pool, edges, fold):
    def whole(shape):
        return pl.BlockSpec(shape, lambda i: (0,) * len(shape), pipeline_mode=pl.Buffered(1))

    def at(lag):
        return lambda i: jnp.clip(i - lag, 0, BLOCKS - 1)

    return pl.pallas_call(
        functools.partial(entry_kernel, size),
        grid=(BLOCKS + 2,),
        out_shape=(
            jax.ShapeDtypeStruct((ROWS, WIDE), f32),
            jax.ShapeDtypeStruct((BLOCKS, LANES, DEEP_ROWS), bf16),
            jax.ShapeDtypeStruct((ROWS, WIDE), f32),
            jax.ShapeDtypeStruct((ROWS, WIDE), bf16),
            jax.ShapeDtypeStruct((CROPS, WIDE), f32),
            jax.ShapeDtypeStruct((BLOCKS, 2, 8, 128), f32),
        ),
        in_specs=[
            whole((ROWS, PADDED)),
            pl.BlockSpec((PADDED, LANES), lambda i: (0, at(0)(i))),
            pl.BlockSpec((9, BLOCK, 128), lambda i: (0, at(1)(i), 0)),
            whole((BLOCKS, 8, 128)),
            whole((CROPS, ROWS)),
            whole((2, IMAGE_PAD, 128)),
            whole((128, LANES)),
        ],
        out_specs=(
            pl.BlockSpec((ROWS, LANES), lambda i: (0, at(0)(i))),
            pl.BlockSpec((1, LANES, DEEP_ROWS), lambda i: (at(1)(i), 0, 0)),
            pl.BlockSpec((ROWS, LANES), lambda i: (0, at(2)(i))),
            pl.BlockSpec((ROWS, LANES), lambda i: (0, at(2)(i))),
            pl.BlockSpec((CROPS, LANES), lambda i: (0, at(2)(i))),
            pl.BlockSpec((BLOCKS, 2, 8, 128), lambda i: (0, 0, 0, 0)),
        ),
        scratch_shapes=[
            pltpu.VMEM((2, 2, ROWS, 128), f32),
            pltpu.VMEM((2, 2, CONV_ROWS, 128), f32),
            pltpu.VMEM((2, ROWS, 128), f32),
            pltpu.VMEM((3, 2, PAD_ROWS, 128), f32),
            pltpu.VMEM((CONV_ROWS, 9 * LANES), bf16),
            pltpu.VMEM((2, CONV_ROWS, 128), f32),
            pltpu.VMEM((9 * LANES, LANES), bf16),
        ]
        + Exchange.scratch(BLOCKS + 1, size),
        name="entry",
        compiler_params=pltpu.CompilerParams(
            collective_id=1, has_side_effects=True, vmem_limit_bytes=VMEM_LIMIT
        ),
        cost_estimate=pl.CostEstimate(
            flops=2 * ROWS * WIDE * (PADDED + 9 * LANES),
            bytes_accessed=70 * 2**20,
            transcendentals=2 * ROWS * WIDE,
        ),
    )(x, weight, conv, params, pool, edges, fold)


def place():
    me = lax.axis_index("img")
    return lax.axis_index("stream"), me // 4, lax.rem(me // 2, 2), lax.rem(me, 2)


class Reducer:
    def __init__(self, refs, inside, rest=None):
        self.inside, self.rest = inside, rest
        (
            self.local,
            self.core_got,
            self.plane_got,
            self.plane_sum,
            self.z_got,
            self.final,
            self.final_got,
            self.core_sem,
            self.plane_sem,
            self.z_sem,
            self.y_sem,
            self.local_sem,
        ) = refs
        self.stream, self.z, self.x, self.core = place()
        self.mine = pl.ds(pl.multiple_of(64 * self.stream, 64), 64)
        self.theirs = pl.ds(pl.multiple_of(64 * (1 - self.stream), 64), 64)

    @staticmethod
    def scratch():
        return [
            pltpu.VMEM((2, 2, 2, 4, 2, 128, 128), bf16),
            pltpu.VMEM((3, 2, 4, 2, 128, 128), bf16),
            pltpu.VMEM((2, 3, 4, 2, 64, 128), bf16),
            pltpu.VMEM((2, 4, 2, 64, 128), bf16),
            pltpu.VMEM((2, 3, 2, 64, 128), bf16),
            pltpu.VMEM((2, 2, 64, 128), f32),
            pltpu.VMEM((2, 2, 64, 128), f32),
            pltpu.SemaphoreType.DMA((2, 2)),
            pltpu.SemaphoreType.DMA((2, 2, 3)),
            pltpu.SemaphoreType.DMA((2, 2, 3)),
            pltpu.SemaphoreType.DMA((2, 2)),
            pltpu.SemaphoreType.DMA((2,)),
        ]

    SHAPE = (2, 2, 4, 2, 128, 128)

    def index(self, k=0, across=0, beside=0):
        return 4 * (self.z ^ k) + 2 * (self.x ^ across) + (self.core ^ beside)

    def greet(self, barrier):
        for across in (0, 1):
            pl.semaphore_signal(
                barrier,
                inc=1,
                device_id=(1 - self.stream, self.index(0, across)),
                device_id_type=MESH,
            )
        return 2

    def core_copy(self, block):
        hold = lax.rem(block, 2)
        return pltpu.make_async_remote_copy(
            src_ref=self.local.at[hold, 1 - self.core],
            dst_ref=self.core_got.at[lax.rem(block, 3)],
            send_sem=self.core_sem.at[0, hold],
            recv_sem=self.core_sem.at[1, hold],
            device_id=(self.stream, self.index(0, 0, 1)),
            device_id_type=MESH,
        )

    def plane_copy(self, block, peer):
        hold = lax.rem(block, 2)
        x = self.x if peer == 1 else 1 - self.x
        rows = self.mine if peer == 0 else self.theirs
        stream = self.stream if peer == 0 else 1 - self.stream
        return pltpu.make_async_remote_copy(
            src_ref=self.core_got.at[lax.rem(block, 3), x, :, :, rows],
            dst_ref=self.plane_got.at[hold, peer],
            send_sem=self.plane_sem.at[0, hold, peer],
            recv_sem=self.plane_sem.at[1, hold, peer],
            device_id=(stream, self.index(0, 0 if peer == 1 else 1)),
            device_id_type=MESH,
        )

    def z_copy(self, block, k):
        hold = lax.rem(block, 2)
        return pltpu.make_async_remote_copy(
            src_ref=self.plane_sum.at[hold, self.z ^ k],
            dst_ref=self.z_got.at[hold, k - 1],
            send_sem=self.z_sem.at[0, hold, k - 1],
            recv_sem=self.z_sem.at[1, hold, k - 1],
            device_id=(self.stream, self.index(k)),
            device_id_type=MESH,
        )

    def y_copy(self, block):
        hold = lax.rem(block, 2)
        return pltpu.make_async_remote_copy(
            src_ref=self.final.at[hold],
            dst_ref=self.final_got.at[hold],
            send_sem=self.y_sem.at[0, hold],
            recv_sem=self.y_sem.at[1, hold],
            device_id=(1 - self.stream, self.index()),
            device_id_type=MESH,
        )

    def finish(self, block, put):
        hold = lax.rem(block, 2)
        self.y_copy(block).wait()
        for tile in range(2):
            put(tile, self.mine, self.final[hold, tile])
            put(tile, self.theirs, self.final_got[hold, tile])

    def after_z(self, block):
        hold = lax.rem(block, 2)
        for k in (1, 2, 3):
            self.z_copy(block, k).wait()
        for tile in range(2):
            total = self.plane_sum[hold, self.z, tile].astype(f32)
            for k in range(3):
                total = total + self.z_got[hold, k, tile].astype(f32)
            self.final[hold, tile] = total
        self.y_copy(block).start()

    def after_plane(self, block):
        hold = lax.rem(block, 2)
        ring = lax.rem(block, 3)
        for peer in range(3):
            self.plane_copy(block, peer).wait()
        for z in range(4):
            for tile in range(2):
                total = self.core_got[ring, self.x, z, tile, self.mine].astype(f32)
                for peer in range(3):
                    total = total + self.plane_got[hold, peer, z, tile].astype(f32)
                self.plane_sum[hold, z, tile] = total.astype(bf16)
        for k in (1, 2, 3):
            self.z_copy(block, k).start()

    def after_core(self, block):
        hold = lax.rem(block, 2)
        ring = lax.rem(block, 3)
        self.core_copy(block).wait()
        for x in range(2):
            for z in range(4):
                for tile in range(2):
                    total = self.core_got[ring, x, z, tile].astype(f32)
                    total = total + self.local[hold, self.core, x, z, tile].astype(f32)
                    self.core_got[ring, x, z, tile] = total.astype(bf16)
        for peer in range(3):
            self.plane_copy(block, peer).start()

    def rest_copy(self, block):
        hold = lax.rem(block, 2)
        return pltpu.make_async_copy(
            self.local.at[hold], self.rest.at[block - self.inside], self.local_sem.at[hold]
        )

    def load_copy(self, source, at, block):
        hold = lax.rem(block, 2)
        return pltpu.make_async_copy(source.at[at], self.local.at[hold], self.local_sem.at[hold])

    def advance(self, newest, put, blocks=0):
        def live(block):
            return (block >= 0) & (block < self.inside)

        @pl.when(live(newest - 4))
        def _():
            self.finish(newest - 4, put)

        @pl.when(live(newest - 3))
        def _():
            self.after_z(newest - 3)

        @pl.when(live(newest - 2))
        def _():
            self.after_plane(newest - 2)

        @pl.when(live(newest - 1))
        def _():
            self.after_core(newest - 1)

        if self.rest is not None:

            @pl.when((newest > self.inside) & (newest <= blocks))
            def _():
                self.rest_copy(newest - 1).wait()

    def begin(self, block, grad):
        hold = lax.rem(block, 2)
        for chunk in range(SHARDS):
            z, x, core = chunk // 4, chunk // 2 % 2, chunk % 2
            for tile in range(2):
                self.local[hold, core, x, z, tile] = grad[
                    128 * chunk : 128 * chunk + 128, 128 * tile : 128 * tile + 128
                ].astype(bf16)

        @pl.when(block < self.inside)
        def _():
            self.core_copy(block).start()

        if self.rest is not None:

            @pl.when(block >= self.inside)
            def _():
                self.rest_copy(block).start()

    def neighbours(self):
        barrier = pltpu.get_barrier_semaphore()
        greeted = self.greet(barrier)
        peers = [(0, 0, 1), (0, 1, 0), (1, 0, 0), (2, 0, 0), (3, 0, 0)]
        for peer in peers:
            pl.semaphore_signal(
                barrier, inc=1, device_id=(self.stream, self.index(*peer)), device_id_type=MESH
            )
        pl.semaphore_wait(barrier, len(peers) + greeted)


def feed(reducer, step, sources, part_out):
    starts = []
    total = 0
    for source, count in sources:
        starts.append((source, total, total + count))
        total += count

    def start_load(block):
        for source, first, last in starts:

            @pl.when((block >= first) & (block < last))
            def _():
                reducer.load_copy(source, block - first, block).start()

    @pl.when(step == 0)
    def _():
        start_load(step)
        reducer.neighbours()

    def put(tile, rows, values):
        part_out[step - 4, tile, rows] = values

    reducer.advance(step, put)

    @pl.when(step < total)
    def _():
        reducer.load_copy(sources[0][0], 0, step).wait()
        reducer.core_copy(step).start()

    start_load(step + 1)


BACK_INSIDE = 6
BACK_REST = BLOCKS - BACK_INSIDE
CONV_BLOCKS = 3


def whole(shape):
    return pl.BlockSpec(shape, lambda i: (0,) * len(shape), pipeline_mode=pl.Buffered(1))


def columns(rows, lag, blocks):
    return pl.BlockSpec((rows, LANES), lambda i: (0, jnp.clip(i - lag, 0, blocks - 1)))


def lane_halves(values):
    return [values[:, :128], values[:, 128:]]


def exit_kernel(
    size,
    scaled_ref,
    turned_ref,
    weight_ref,
    x_ref,
    cot_ref,
    param_ref,
    pair_ref,
    spread_ref,
    live_ref,
    out_out,
    delta_out,
    residual_out,
    weight_out,
    total_out,
    act_ref,
    slope_ref,
    pair_sent,
    pair_got,
    pair_send,
    pair_recv,
    *exchange_refs,
):
    exchange = Exchange(size, *exchange_refs)
    step = pl.program_id(0)
    count = row_count(size)
    stream = lax.axis_index("stream")
    me = lax.axis_index("img")
    area = jnp.where(stream == 0, GLOBAL_SIDE**2, SMALL_SIDE**2).astype(f32)
    blocks = OUT_BLOCKS

    def used_lanes(block):
        lane = lax.broadcasted_iota(jnp.int32, (STEP, 128), 1) + LANES * block
        return [lane + 128 * tile < CHANNELS for tile in range(2)]

    def pair_copy(block):
        return pltpu.make_async_remote_copy(
            src_ref=pair_sent.at[block],
            dst_ref=pair_got.at[block],
            send_sem=pair_send.at[block],
            recv_sem=pair_recv.at[block],
            device_id=(1 - stream, me),
            device_id_type=MESH,
        )

    @pl.when(step == 0)
    def _():
        barrier = img_barrier(size)
        pl.semaphore_signal(
            barrier, inc=1, device_id=(1 - stream, me), device_id_type=MESH
        )
        pl.semaphore_wait(barrier, size)

    @pl.when(step < blocks)
    def _():
        slot = lax.rem(step, 4)
        for micro in range(MICRO_BATCHES):
            here = slice(HALF * micro, HALF * (micro + 1))
            act_ref[slot, here] = dot(scaled_ref[here], weight_ref[...])
        sums = Sums()
        for chunk in range(STEPS):
            for tile in range(2):
                act = act_ref[slot, chunk_rows(chunk), 128 * tile : 128 * tile + 128]
                sums.add(chunk // HALF_STEPS, tile, act, act * act)
        exchange.put(step, 0, sums.packed())

    @pl.when((step >= 1) & (step < blocks + 1))
    def _():
        block = step - 1
        slot = lax.rem(block, 4)
        total = exchange.total(step - 1, 0)
        total_out[block, 0] = total
        param = param_ref[block]
        inside = used_lanes(block)
        for micro in range(MICRO_BATCHES):
            for tile in range(2):
                lanes = slice(128 * tile, 128 * tile + 128)
                mean, inverse = moments(total, micro, tile, count)
                scale = 0.5 * inverse * param[tile : tile + 1]
                shift = 0.5 * param[2 + tile : 3 + tile] - mean * scale
                for chunk in range(HALF_STEPS * micro, HALF_STEPS * (micro + 1)):
                    here = chunk_rows(chunk)
                    act = act_ref[slot, here, lanes]
                    source = jnp.where(inside[tile], x_ref[here, lanes].astype(f32), 0.0)
                    half = 0.5 * source + (act * scale + shift)
                    bent = jnp.tanh(half)
                    out_out[here, lanes] = (
                        (half + half * bent) * live_ref[here].astype(f32)
                    ).astype(bf16)
                    slope_ref[lax.rem(block, 3), here, lanes] = (0.5 + 0.5 * bent) * (
                        1.0 + half * (1.0 - bent)
                    )
        embed = dot(pair_ref[...], out_out[...]) / area
        pair_sent[block] = embed[:8].astype(bf16).astype(f32)
        pair_copy(block).start()

    @pl.when((step >= 2) & (step < blocks + 2))
    def _():
        block = step - 2
        slot = lax.rem(block, 4)
        hold = lax.rem(block, 3)
        moment = total_out[block, 0]
        pair_copy(block).wait()
        partner = pair_got[block]
        partner = jnp.concatenate([partner, jnp.zeros_like(partner)]).astype(bf16)
        means = {
            (micro, tile): moments(moment, micro, tile, count)
            for micro in range(MICRO_BATCHES)
            for tile in range(2)
        }
        inside = used_lanes(block)
        sums = Sums()
        for chunk in range(STEPS):
            here = chunk_rows(chunk)
            live = live_ref[here].astype(f32)
            pull = dot(spread_ref[here], partner) * (PAIR_SCALE / area)
            for tile in range(2):
                lanes = slice(128 * tile, 128 * tile + 128)
                mean, inverse = means[chunk // HALF_STEPS, tile]
                upstream = jnp.where(inside[tile], cot_ref[here, lanes].astype(f32), 0.0)
                upstream = upstream * live + pull[:, lanes]
                delta = upstream * slope_ref[hold, here, lanes]
                slope_ref[hold, here, lanes] = delta
                residual_out[here, lanes] = delta.astype(bf16)
                normed = act_ref[slot, here, lanes] * inverse - mean * inverse
                sums.add(chunk // HALF_STEPS, tile, delta, delta * normed)
        exchange.put(step, 1, sums.packed())
    @pl.when(step >= 3)
    def _():
        block = step - 3
        slot = lax.rem(block, 4)
        hold = lax.rem(block, 3)
        moment = total_out[block, 0]
        total = exchange.total(step - 1, 1)
        total_out[block, 1] = total
        param = param_ref[block]
        for micro in range(MICRO_BATCHES):
            for tile in range(2):
                lanes = slice(128 * tile, 128 * tile + 128)
                back = norm_back(moment, total, micro, tile, param[tile : tile + 1], count)
                for chunk in range(HALF_STEPS * micro, HALF_STEPS * (micro + 1)):
                    here = chunk_rows(chunk)
                    delta_out[here, lanes] = back(
                        slope_ref[hold, here, lanes], act_ref[slot, here, lanes]
                    ).astype(bf16)
        weight_out[...] = dot(turned_ref[...], delta_out[...]).astype(bf16)


def norm_back(moment, total, micro, tile, gain, count):
    mean, inverse = moments(moment, micro, tile, count)
    scale = gain * inverse
    plain = total[4 * micro + tile : 4 * micro + tile + 1] / count
    along = scale * (total[4 * micro + 2 + tile : 4 * micro + 3 + tile] / count)
    slant = along * inverse
    level = scale * plain
    return lambda upstream, act: scale * upstream - (level + (act - mean) * slant)


def run_exit(size, scaled, turned, weight, x, cot, params, pair, spread, live):
    blocks = OUT_BLOCKS
    return pl.pallas_call(
        functools.partial(exit_kernel, size),
        grid=(blocks + 3,),
        out_shape=(
            jax.ShapeDtypeStruct((ROWS, CHANNELS), bf16),
            jax.ShapeDtypeStruct((ROWS, PADDED), bf16),
            jax.ShapeDtypeStruct((ROWS, PADDED), bf16),
            jax.ShapeDtypeStruct((PADDED, PADDED), bf16),
            jax.ShapeDtypeStruct((blocks, 2, 8, 128), f32),
        ),
        in_specs=[
            whole((ROWS, PADDED)),
            whole((PADDED, ROWS)),
            columns(PADDED, 0, blocks),
            columns(ROWS, 1, blocks),
            columns(ROWS, 2, blocks),
            whole((blocks, 8, 128)),
            whole((CROPS, ROWS)),
            whole((ROWS, CROPS)),
            whole((ROWS, 128)),
        ],
        out_specs=(
            columns(ROWS, 1, blocks),
            columns(ROWS, 3, blocks),
            columns(ROWS, 2, blocks),
            columns(PADDED, 3, blocks),
            pl.BlockSpec((blocks, 2, 8, 128), lambda i: (0, 0, 0, 0)),
        ),
        scratch_shapes=[
            pltpu.VMEM((4, ROWS, LANES), f32),
            pltpu.VMEM((3, ROWS, LANES), f32),
            pltpu.VMEM((blocks, 8, LANES), f32),
            pltpu.VMEM((blocks, 8, LANES), f32),
            pltpu.SemaphoreType.DMA((blocks,)),
            pltpu.SemaphoreType.DMA((blocks,)),
        ]
        + Exchange.scratch(blocks + 2, size),
        name="exit",
        compiler_params=pltpu.CompilerParams(
            collective_id=2, has_side_effects=True, vmem_limit_bytes=VMEM_LIMIT
        ),
        cost_estimate=pl.CostEstimate(
            flops=4 * ROWS * PADDED * PADDED,
            bytes_accessed=70 * 2**20,
            transcendentals=ROWS * PADDED,
        ),
    )(scaled, turned, weight, x, cot, params, pair, spread, live)


def gate_kernel(
    delta_ref, weight_ref, mixed_ref, pool_ref, block_ref, scaled_out, gate_out, block_out
):
    block = pl.program_id(0)
    block_out[...] = block_ref[...]
    first = jnp.minimum((BLOCK * block) // CHUNK, SHARDS - 3)
    row = lax.broadcasted_iota(jnp.int32, (LANES, 3 * CHUNK_PAD), 0)
    lane = lax.broadcasted_iota(jnp.int32, (LANES, 3 * CHUNK_PAD), 1)
    channel = CHUNK * (first + lane // CHUNK_PAD) + lane % CHUNK_PAD
    pick = (channel == BLOCK * block + row) & (row < BLOCK) & (lane % CHUNK_PAD < CHUNK)
    rows = pl.ds(pl.multiple_of(CHUNK_PAD * first, CHUNK_PAD), 3 * CHUNK_PAD)
    weight = dot(jnp.where(pick, 1.0, 0.0).astype(bf16), weight_ref[rows]).astype(bf16)
    grad = dot(delta_ref[...], weight, ((1,), (1,)))
    scaled_out[...] = grad
    gate_out[...] = dot(pool_ref[...], (grad * mixed_ref[...].astype(f32)).astype(bf16))


def run_gate(delta, weight, mixed, pool, block):
    return pl.pallas_call(
        gate_kernel,
        grid=(BLOCKS,),
        out_shape=(
            jax.ShapeDtypeStruct((ROWS, WIDE), f32),
            jax.ShapeDtypeStruct((CROPS, WIDE), f32),
            jax.ShapeDtypeStruct((ROWS, CHANNELS), bf16),
        ),
        in_specs=[
            whole((ROWS, PADDED)),
            whole((PADDED, PADDED)),
            columns(ROWS, 0, BLOCKS),
            whole((CROPS, ROWS)),
            columns(ROWS, 0, OUT_BLOCKS),
        ],
        out_specs=(
            columns(ROWS, 0, BLOCKS),
            columns(CROPS, 0, BLOCKS),
            columns(ROWS, 0, OUT_BLOCKS),
        ),
        name="gate",
        compiler_params=pltpu.CompilerParams(vmem_limit_bytes=VMEM_LIMIT),
        cost_estimate=pl.CostEstimate(
            flops=2 * ROWS * WIDE * PADDED, bytes_accessed=40 * 2**20, transcendentals=0
        ),
    )(delta, weight, mixed, pool, block)


def pair_lane(shape, dim):
    lane = lax.broadcasted_iota(jnp.int32, shape, dim)
    inside = lane % CHUNK_PAD
    return jnp.where(inside < CHUNK, CHUNK * (lane // CHUNK_PAD) + inside, -1)


def one_hot(match):
    return jnp.where(match, 1.0, 0.0).astype(bf16)


def prepare_kernel(x_ref, chunk_out, turned_out):
    pair = pl.program_id(0)
    depth = 384
    first = (PAIR * pair) // 128
    lanes = pl.ds(pl.multiple_of(128 * first, 128), depth)
    source = 128 * first - PAIR * pair
    there = lax.broadcasted_iota(jnp.int32, (depth, LANES), 0) + source
    pick = one_hot(there == pair_lane((depth, LANES), 1))
    chunk_out[...] = dot(x_ref[:, lanes], pick).astype(bf16)
    there = lax.broadcasted_iota(jnp.int32, (LANES, depth), 1) + source
    pick = one_hot(there == pair_lane((LANES, depth), 0))
    turned_out[...] = dot(pick, x_ref[:, lanes], ((1,), (1,))).astype(bf16)


def run_prepare(x):
    return pl.pallas_call(
        prepare_kernel,
        grid=(OUT_BLOCKS,),
        out_shape=(
            jax.ShapeDtypeStruct((ROWS, PADDED), bf16),
            jax.ShapeDtypeStruct((PADDED, ROWS), bf16),
        ),
        in_specs=[whole((ROWS, PADDED))],
        out_specs=(columns(ROWS, 0, OUT_BLOCKS), pl.BlockSpec((LANES, ROWS), lambda i: (i, 0))),
        name="prepare",
        compiler_params=pltpu.CompilerParams(vmem_limit_bytes=VMEM_LIMIT),
        cost_estimate=pl.CostEstimate(
            flops=4 * ROWS * 384 * PADDED, bytes_accessed=20 * 2**20, transcendentals=0
        ),
    )(x)


QUARTERS = CHANNELS // SQUEEZE
INNER = 512


def split(values):
    high = values.astype(bf16)
    low = (values - high.astype(f32)).astype(bf16)
    return jnp.concatenate([high, low], axis=-2)


def join(terms):
    half = terms.shape[0] // 2
    return terms[:half] + terms[half:]


def wide_place(channel):
    return channel + (LANES - BLOCK) * (channel // BLOCK)


def pair_source(pair):
    return min(128 * (wide_place(PAIR * pair) // 128), WIDE - 512)


def pair_from_wide(pair, shape, dim):
    inside = pair_lane(shape, dim)
    where = wide_place(PAIR * pair + inside) - pair_source(pair)
    there = lax.broadcasted_iota(jnp.int32, shape, 1 - dim)
    return one_hot((there == where) & (inside >= 0))


def inner_source(pair):
    return min(128 * ((PAIR // QUARTERS) * pair // 128), INNER - LANES)


def pair_from_inner(pair, quarter):
    shape = (LANES, LANES)
    inside = pair_lane(shape, 1)
    inner = lax.broadcasted_iota(jnp.int32, shape, 0) + inner_source(pair)
    return one_hot((PAIR * pair + inside == QUARTERS * inner + quarter) & (inside >= 0))


def quarters_of(block):
    first = BLOCK * block // SQUEEZE
    last = (BLOCK * block + BLOCK - 1) // SQUEEZE
    return range(first, last + 1)


def scale_kernel(
    mixed_ref,
    spread_ref,
    pooled_ref,
    squeeze_ref,
    excite_ref,
    squeeze_bias_ref,
    excite_bias_ref,
    scaled_out,
    turned_out,
    gates_out,
    pooled_out,
    inner_out,
    rows_out,
    quarter_out,
    scaled,
):
    step = pl.program_id(0)
    area = jnp.where(lax.axis_index("stream") == 0, GLOBAL_SIDE**2, SMALL_SIDE**2).astype(f32)

    @pl.when(step == 0)
    def _():
        for pair in range(OUT_BLOCKS):
            lanes = slice(pair_source(pair), pair_source(pair) + 512)
            pick = pair_from_wide(pair, (512, LANES), 1)
            picked = join(dot(split(pooled_ref[:, lanes]), pick)) / area
            pooled_out[:, LANES * pair : LANES * (pair + 1)] = picked
        inner = join(dot(split(pooled_out[...]), squeeze_ref[...])) + squeeze_bias_ref[...]
        inner_out[...] = inner
        half = 0.5 * inner
        terms = split(half + half * jnp.tanh(half))
        for pair in range(OUT_BLOCKS):
            source = terms[:, inner_source(pair) : inner_source(pair) + LANES]
            for quarter in range(QUARTERS):
                rows_out[
                    CROPS * quarter : CROPS * (quarter + 1), LANES * pair : LANES * (pair + 1)
                ] = join(dot(source, pair_from_inner(pair, quarter)))
        excite = join(dot(split(rows_out[...]), excite_ref[...]))
        for quarter in range(QUARTERS):
            here = slice(CROPS * quarter, CROPS * (quarter + 1))
            half = 0.5 * (excite[here] + excite_bias_ref[quarter : quarter + 1])
            quarter_out[here] = 0.5 + 0.5 * jnp.tanh(half)
        for block in range(BLOCKS):
            total = 0.0
            for quarter in quarters_of(block):
                shape = (INNER, LANES)
                channel = SQUEEZE * quarter + lax.broadcasted_iota(jnp.int32, shape, 0)
                lane = lax.broadcasted_iota(jnp.int32, shape, 1)
                inside = lax.broadcasted_iota(jnp.int32, shape, 0) < SQUEEZE
                pick = one_hot((channel == BLOCK * block + lane) & (lane < BLOCK) & inside)
                here = slice(CROPS * quarter, CROPS * (quarter + 1))
                total = total + dot(split(quarter_out[here]), pick)
            gates_out[:, LANES * block : LANES * (block + 1)] = total.astype(bf16)

    @pl.when(step < BLOCKS)
    def _():
        lanes = pl.ds(pl.multiple_of(LANES * step, LANES), LANES)
        for chunk in range(STEPS):
            here = chunk_rows(chunk)
            gate = dot(spread_ref[here], gates_out[:, lanes])
            scaled[here, lanes] = (mixed_ref[here].astype(f32) * gate).astype(bf16)

    @pl.when(step >= BLOCKS)
    def _():
        pair = step - BLOCKS
        depth = 512
        start = PAIR * pair
        first = jnp.minimum((start + (LANES - BLOCK) * (start // BLOCK)) // 128, WIDE // 128 - 4)
        lanes = pl.ds(pl.multiple_of(128 * first, 128), depth)

        def pick(shape, dim):
            inside = pair_lane(shape, dim)
            channel = start + inside
            place = channel + (LANES - BLOCK) * (channel // BLOCK) - 128 * first
            there = lax.broadcasted_iota(jnp.int32, shape, 1 - dim)
            return one_hot((there == place) & (inside >= 0))

        scaled_out[...] = dot(scaled[:, lanes], pick((depth, LANES), 1)).astype(bf16)
        turned_out[...] = dot(pick((LANES, depth), 0), scaled[:, lanes], ((1,), (1,))).astype(
            bf16
        )


def run_scale(mixed, spread, pooled, squeeze, excite, squeeze_bias, excite_bias):
    def pair(i):
        return jnp.maximum(i - BLOCKS, 0)

    def kept(shape):
        return pl.BlockSpec(shape, lambda i: (0, 0))

    kinds = (
        ((2 * CROPS, WIDE), bf16),
        ((CROPS, PADDED), f32),
        ((CROPS, INNER), f32),
        ((QUARTERS * CROPS, PADDED), f32),
        ((QUARTERS * CROPS, INNER), f32),
    )
    return pl.pallas_call(
        scale_kernel,
        grid=(BLOCKS + OUT_BLOCKS,),
        out_shape=(
            jax.ShapeDtypeStruct((ROWS, PADDED), bf16),
            jax.ShapeDtypeStruct((PADDED, ROWS), bf16),
        )
        + tuple(jax.ShapeDtypeStruct(*kind) for kind in kinds),
        in_specs=[
            columns(ROWS, 0, BLOCKS),
            whole((ROWS, 2 * CROPS)),
            whole((CROPS, WIDE)),
            whole((PADDED, INNER)),
            whole((PADDED, INNER)),
            whole((1, INNER)),
            whole((QUARTERS, INNER)),
        ],
        out_specs=(
            pl.BlockSpec((ROWS, LANES), lambda i: (0, pair(i))),
            pl.BlockSpec((LANES, ROWS), lambda i: (pair(i), 0)),
        )
        + tuple(kept(shape) for shape, _ in kinds),
        scratch_shapes=[pltpu.VMEM((ROWS, WIDE), bf16)],
        name="scale",
        compiler_params=pltpu.CompilerParams(vmem_limit_bytes=VMEM_LIMIT),
        cost_estimate=pl.CostEstimate(
            flops=4 * ROWS * 512 * PADDED, bytes_accessed=30 * 2**20, transcendentals=0
        ),
    )(mixed, spread, pooled, squeeze, excite, squeeze_bias, excite_bias)


def outer(left, right):
    left_high = left.astype(bf16)
    left_low = (left - left_high.astype(f32)).astype(bf16)
    right_high = right.astype(bf16)
    right_low = (right - right_high.astype(f32)).astype(bf16)
    left = jnp.concatenate([left_high, left_high, left_low])
    right = jnp.concatenate([right_high, right_low, right_high])
    return dot(left, right, ((0,), (0,)))


def squeeze_kernel(
    gate_grad_ref,
    pooled_ref,
    inner_ref,
    rows_ref,
    quarter_ref,
    squeeze_ref,
    excite_ref,
    gates_out,
    grads_out,
    bias_out,
    quarter_delta,
    inner_delta,
    pooled_delta,
):
    area = jnp.where(lax.axis_index("stream") == 0, GLOBAL_SIDE**2, SMALL_SIDE**2).astype(f32)
    bias_out[...] = jnp.zeros_like(bias_out)
    for quarter in range(QUARTERS):
        first = min(LANES * (SQUEEZE * quarter // BLOCK), WIDE - 1024)
        shape = (1024, INNER)
        inner = lax.broadcasted_iota(jnp.int32, shape, 1)
        where = wide_place(SQUEEZE * quarter + inner) - first
        there = lax.broadcasted_iota(jnp.int32, shape, 0)
        pick = one_hot((there == where) & (inner < SQUEEZE))
        grad = join(dot(split(gate_grad_ref[:, first : first + 1024]), pick))
        here = slice(CROPS * quarter, CROPS * (quarter + 1))
        gate = quarter_ref[here]
        delta = grad * gate * (1.0 - gate)
        quarter_delta[here] = delta
        bias_out[1 + quarter : 2 + quarter] = column_sum(delta)
    back = join(dot(split(quarter_delta[...]), excite_ref[...], ((1,), (1,))))
    inner_delta[...] = jnp.zeros_like(inner_delta)
    for pair in range(OUT_BLOCKS):
        lanes = slice(inner_source(pair), inner_source(pair) + LANES)
        total = 0.0
        for quarter in range(QUARTERS):
            terms = split(
                back[CROPS * quarter : CROPS * (quarter + 1), LANES * pair : LANES * (pair + 1)]
            )
            total = total + dot(terms, pair_from_inner(pair, quarter), ((1,), (1,)))
        inner_delta[:, lanes] += join(total)
    half = 0.5 * inner_ref[...]
    bent = jnp.tanh(half)
    delta = inner_delta[...] * ((0.5 + 0.5 * bent) * (1.0 + half * (1.0 - bent)))
    bias_out[0:1] = column_sum(delta)
    pooled_delta[...] = join(dot(split(delta), squeeze_ref[...], ((1,), (1,)))) / area
    for block in range(BLOCKS):
        first = min(BLOCK * block // CHUNK, SHARDS - 3)
        shape = (3 * CHUNK_PAD, LANES)
        place_in = lax.broadcasted_iota(jnp.int32, shape, 0)
        lane = lax.broadcasted_iota(jnp.int32, shape, 1)
        channel = CHUNK * (first + place_in // CHUNK_PAD) + place_in % CHUNK_PAD
        pick = (channel == BLOCK * block + lane) & (lane < BLOCK) & (place_in % CHUNK_PAD < CHUNK)
        source = pooled_delta[:, CHUNK_PAD * first : CHUNK_PAD * (first + 3)]
        gates_out[:, LANES * block : LANES * (block + 1)] = dot(
            split(source), one_hot(pick)
        ).astype(bf16)
    grads_out[:, INNER:] = outer(rows_ref[...], quarter_delta[...]).astype(bf16)
    grads_out[:, :INNER] = outer(pooled_ref[...], delta).astype(bf16)


def run_squeeze(gate_grad, pooled, inner, rows, quarter, squeeze, excite):
    vmem = pl.BlockSpec(memory_space=pltpu.VMEM)
    return pl.pallas_call(
        squeeze_kernel,
        out_shape=(
            jax.ShapeDtypeStruct((2 * CROPS, WIDE), bf16),
            jax.ShapeDtypeStruct((PADDED, 2 * INNER), bf16),
            jax.ShapeDtypeStruct((8, INNER), f32),
        ),
        in_specs=[vmem] * 7,
        out_specs=(vmem,) * 3,
        scratch_shapes=[
            pltpu.VMEM((QUARTERS * CROPS, INNER), f32),
            pltpu.VMEM((CROPS, INNER), f32),
            pltpu.VMEM((CROPS, PADDED), f32),
        ],
        name="squeeze",
        compiler_params=pltpu.CompilerParams(vmem_limit_bytes=VMEM_LIMIT),
        cost_estimate=pl.CostEstimate(
            flops=2 * 2**30, bytes_accessed=20 * 2**20, transcendentals=0
        ),
    )(gate_grad, pooled, inner, rows, quarter, squeeze, excite)


BIAS_ROWS = 32


def back_kernel(
    size,
    bias_ref,
    grad_ref,
    group_ref,
    late_group_ref,
    gates_ref,
    pooled_ref,
    spread_ref,
    act_ref,
    late_act_ref,
    turned_ref,
    conv_ref,
    x_turned_ref,
    param_ref,
    moment_ref,
    edges,
    fold_ref,
    delta_out,
    weight_out,
    conv_out,
    total_out,
    bias_out,
    *refs,
):
    if size == SHARDS:
        rest_out, *refs = refs
    (
    delta_two,
    delta_one,
    pads,
    windows,
    wide_ref,
    full_ref,
        bias_got,
        bias_sem,
        even_ref,
        odd_ref,
        *refs,
    ) = refs
    exchange = Exchange(size, *refs[:4])
    reduce_refs = refs[4:]
    step = pl.program_id(0)
    count = row_count(size)
    on_global = lax.axis_index("stream") == 0
    reducer = Reducer(reduce_refs, BACK_INSIDE, rest_out) if reduce_refs else None

    def bend(moment, micro, tile, param, at):
        mean, inverse = moments(moment, micro, tile, count)
        gain = 0.5 * param[at + tile : at + tile + 1]
        shift = 0.5 * param[at + 2 + tile : at + tile + 3]

        def both(act):
            normed = act * inverse - mean * inverse
            half = normed * gain + shift
            bent = jnp.tanh(half)
            return normed, (0.5 + 0.5 * bent) * (1.0 + half * (1.0 - bent))

        return both

    @pl.when(step == 0)
    def _():
        barrier = img_barrier(size)
        pads[...] = jnp.zeros_like(pads)
        full_ref[...] = jnp.zeros_like(full_ref)
        windows[CONV_ROWS:] = jnp.zeros_like(windows[CONV_ROWS:])
        greeted = reducer.greet(barrier) if reducer else 0
        pl.semaphore_wait(barrier, size - 1 + greeted)
        stream = lax.axis_index("stream")
        me = lax.axis_index("img")
        bias_got[me] = bias_ref[...]

        def send(step, carry):
            pltpu.make_async_remote_copy(
                src_ref=bias_ref,
                dst_ref=bias_got.at[me],
                send_sem=bias_sem.at[0],
                recv_sem=bias_sem.at[1],
                device_id=(stream, lax.rem(me + step, size)),
                device_id_type=MESH,
            ).start()
            return carry

        lax.fori_loop(1, size, send, 0)

    @pl.when(step == BLOCKS)
    def _():
        others = bias_got.at[pl.ds(0, size - 1)]
        pltpu.make_async_copy(others, others, bias_sem.at[0]).wait()
        pltpu.make_async_copy(others, others, bias_sem.at[1]).wait()
        total = bias_got[0]
        for peer in range(1, size):
            total = total + bias_got[peer]
        bias_out[...] = total

    if reducer:

        def put(tile, rows, values):
            weight_out[rows, 128 * tile : 128 * tile + 128] = values

        reducer.advance(step - 2, put, BLOCKS)

    @pl.when(step < BLOCKS)
    def _():
        slot = lax.rem(step, 2)
        moment = moment_ref[step, 1]
        param = param_ref[step]
        sums = Sums()
        for micro in range(MICRO_BATCHES):
            bends = [bend(moment, micro, tile, param, 4) for tile in range(2)]
            for chunk in range(HALF_STEPS * micro, HALF_STEPS * (micro + 1)):
                here = chunk_rows(chunk)
                gate = dot(spread_ref[here], gates_ref[...])
                pooled = dot(spread_ref[here], pooled_ref[...])
                for tile in range(2):
                    lanes = slice(128 * tile, 128 * tile + 128)
                    normed, slope = bends[tile](group_ref[here, lanes])
                    delta = (grad_ref[here, lanes] * gate[:, lanes] + pooled[:, lanes]) * slope
                    delta_two[slot, tile, here] = delta
                    sums.add(micro, tile, delta, delta * normed)
        exchange.put(step, 0, sums.packed())

    @pl.when((step >= 1) & (step < BLOCKS + 1))
    def _():
        block = step - 1
        slot = lax.rem(block, 2)
        total = exchange.total(step - 1, 0)
        total_out[block, 0] = total
        param = param_ref[block]
        moment = moment_ref[block, 1]
        backs = {
            (micro, tile): norm_back(moment, total, micro, tile, param[4 + tile : 5 + tile], count)
            for micro in range(MICRO_BATCHES)
            for tile in range(2)
        }

        def delta_rows(tile, start, length):
            here = slice(start, start + length)
            return backs[start // HALF, tile](
                delta_two[slot, tile, here], late_group_ref[here, 128 * tile : 128 * tile + 128]
            )

        same = same_group(LANES, BLOCK)
        for offset in range(9):
            full = dot(fold_ref[...], conv_ref[offset], ((1,), (1,)))
            full_ref[LANES * offset : LANES * (offset + 1), :BLOCK] = jnp.where(
                same, full, 0.0
            ).astype(bf16)

        def convolve(image):
            stack_windows(pads, windows, image, -1)
            here = slice(IMAGE_PAD * image, IMAGE_PAD * (image + 1))
            wide = dot(windows[here], full_ref[...])
            wide_ref[0, here] = wide[:, :128]
            wide_ref[1, here] = wide[:, 128:]

        moment_one = moment_ref[block, 0]

        def finish(load):
            sums = Sums()
            for micro in range(MICRO_BATCHES):
                for tile in range(2):
                    bent = bend(moment_one, micro, tile, param, 0)
                    for chunk in range(HALF_STEPS * micro, HALF_STEPS * (micro + 1)):
                        here = chunk_rows(chunk)
                        normed, slope = bent(act_ref[here, 128 * tile : 128 * tile + 128])
                        delta = load(tile, chunk) * slope
                        delta_one[slot, tile, here] = delta
                        sums.add(micro, tile, delta, delta * normed)
            exchange.put(step, 1, sums.packed())

        @pl.when(on_global)
        def _():
            pad_global(delta_rows, pads, edges)
            for image in range(IMAGE_DEV):
                convolve(image)
            finish(lambda tile, chunk: unpadded(wide_ref, tile, STEP // 8 * chunk, STEP // 8))

        @pl.when(jnp.logical_not(on_global))
        def _():
            rows_ref = delta_one.at[slot]
            for chunk in range(STEPS):
                for tile in range(2):
                    rows_ref[tile, chunk_rows(chunk)] = delta_rows(tile, STEP * chunk, STEP)
            pad_small(rows_ref, pads)
            for image in range(IMAGE_DEV):
                convolve(image)
            for chunk in range(STEPS):
                for tile in range(2):
                    rows_ref[tile, chunk_rows(chunk)] = jnp.zeros((STEP, 128), f32)
            unpad_small(wide_ref, rows_ref)
            finish(lambda tile, chunk: rows_ref[tile, chunk_rows(chunk)])

        for offset in range(9):
            grad = dot(turned_ref[0], windows[:, LANES * offset : LANES * (offset + 1)])
            pieces = []
            for group in range(4):
                here = slice(GROUP_WIDTH * group, GROUP_WIDTH * (group + 1))
                pieces.append(grad[here, here])
            even_ref[:, :GROUP_WIDTH] = jnp.concatenate(pieces)
            lines = [even_ref[pl.ds(start, BLOCK // 2, 2), :GROUP_WIDTH] for start in range(2)]
            odd_ref[:, :GROUP_WIDTH] = lines[0]
            odd_ref[:, GROUP_WIDTH : 2 * GROUP_WIDTH] = lines[1]
            conv_out[offset] = odd_ref[:, : 2 * GROUP_WIDTH].astype(bf16)

    @pl.when((step >= 2) & (step < BLOCKS + 2))
    def _():
        block = step - 2
        slot = lax.rem(block, 2)
        total = exchange.total(step - 1, 1)
        total_out[block, 1] = total
        param = param_ref[block]
        moment = moment_ref[block, 0]
        for micro in range(MICRO_BATCHES):
            for tile in range(2):
                lanes = slice(128 * tile, 128 * tile + 128)
                back = norm_back(moment, total, micro, tile, param[tile : tile + 1], count)
                for chunk in range(HALF_STEPS * micro, HALF_STEPS * (micro + 1)):
                    here = chunk_rows(chunk)
                    delta_out[here, lanes] = back(
                        delta_one[slot, tile, here], late_act_ref[here, lanes]
                    ).astype(bf16)
        grad = dot(x_turned_ref[...], delta_out[...])
        if reducer:
            reducer.begin(block, grad)
        else:
            weight_out[...] = grad.astype(bf16)


def run_back(
    size, bias, grad, group, gates, pooled, spread, act, turned, conv, x_turned, params, moment, edges, fold
):
    reduced = size == SHARDS
    return pl.pallas_call(
        functools.partial(back_kernel, size),
        grid=(max(BLOCKS + 2, BACK_INSIDE + 6) if reduced else BLOCKS + 2,),
        out_shape=(
            jax.ShapeDtypeStruct((ROWS, WIDE), bf16),
            jax.ShapeDtypeStruct((CHUNK_PAD, LANES * BACK_INSIDE), f32)
            if reduced
            else jax.ShapeDtypeStruct((PADDED, WIDE), bf16),
            jax.ShapeDtypeStruct((9, CHANNELS // 2, 2 * GROUP_WIDTH), bf16),
            jax.ShapeDtypeStruct((BLOCKS, 2, 8, 128), f32),
            jax.ShapeDtypeStruct((BIAS_ROWS, 128), f32),
        )
        + ((jax.ShapeDtypeStruct((BACK_REST,) + Reducer.SHAPE, bf16),) if reduced else ()),
        in_specs=[
            whole((BIAS_ROWS, 128)),
            columns(ROWS, 0, BLOCKS),
            columns(ROWS, 0, BLOCKS),
            columns(ROWS, 1, BLOCKS),
            columns(2 * CROPS, 0, BLOCKS),
            columns(2 * CROPS, 0, BLOCKS),
            whole((ROWS, 2 * CROPS)),
            columns(ROWS, 1, BLOCKS),
            columns(ROWS, 2, BLOCKS),
            pl.BlockSpec((1, LANES, DEEP_ROWS), lambda i: (jnp.clip(i - 1, 0, BLOCKS - 1), 0, 0)),
            pl.BlockSpec((9, BLOCK, 128), lambda i: (0, jnp.clip(i - 1, 0, BLOCKS - 1), 0)),
            whole((PADDED, ROWS)),
            whole((BLOCKS, 8, 128)),
            whole((BLOCKS, 2, 8, 128)),
            whole((2, IMAGE_PAD, 128)),
            whole((LANES, 128)),
        ],
        out_specs=(
            columns(ROWS, 2, BLOCKS),
            columns(CHUNK_PAD, 6, BACK_INSIDE) if reduced else columns(PADDED, 2, BLOCKS),
            pl.BlockSpec(
                (9, BLOCK // 2, 2 * GROUP_WIDTH), lambda i: (0, jnp.clip(i - 1, 0, BLOCKS - 1), 0)
            ),
            pl.BlockSpec((BLOCKS, 2, 8, 128), lambda i: (0, 0, 0, 0)),
            pl.BlockSpec((BIAS_ROWS, 128), lambda i: (0, 0)),
        )
        + ((pl.BlockSpec(memory_space=HBM),) if reduced else ()),
        scratch_shapes=[
            pltpu.VMEM((2, 2, ROWS, 128), f32),
            pltpu.VMEM((2, 2, ROWS, 128), f32),
            pltpu.VMEM((3, 2, PAD_ROWS, 128), f32),
            pltpu.VMEM((DEEP_ROWS, 9 * LANES), bf16),
            pltpu.VMEM((2, CONV_ROWS, 128), f32),
            pltpu.VMEM((9 * LANES, LANES), bf16),
            pltpu.VMEM((size, BIAS_ROWS, 128), f32),
            pltpu.SemaphoreType.DMA((2,)),
            pltpu.VMEM((BLOCK, 128), f32),
            pltpu.VMEM((BLOCK // 2, 128), f32),
        ]
        + Exchange.scratch(BLOCKS + 1, size)
        + (Reducer.scratch() if reduced else []),
        name="back",
        compiler_params=pltpu.CompilerParams(
            collective_id=3, has_side_effects=True, vmem_limit_bytes=VMEM_LIMIT
        ),
        cost_estimate=pl.CostEstimate(
            flops=2 * ROWS * WIDE * (PADDED + 18 * LANES),
            bytes_accessed=90 * 2**20,
            transcendentals=2 * ROWS * WIDE,
        ),
    )(bias, grad, group, group, gates, pooled, spread, act, act, turned, conv, x_turned, params, moment, edges, fold)


CONV_LINES = 1152


def gather_kernel(
    entry_ref,
    conv_ref,
    x_ref,
    target_ref,
    *refs,
):
    vectors, exit_vectors = refs[:4], refs[4:6]
    (
        entry_out,
        lines_out,
        chunk_out,
        turned_out,
        live_out,
        pool_out,
        spread_out,
        pair_out,
        pull_out,
        param_out,
        exit_param_out,
        conv_rows,
        shifted,
        lines,
        x_rows,
        chunk_rows_ref,
        turned_rows,
        send_sem,
        recv_sem,
        local_sem,
        store_sem,
    ) = refs[6:]
    stream, z, x, core = place()
    pieces = (entry_ref, conv_ref)
    wholes = (entry_out, conv_rows)
    quarters = (CHUNK_PAD // 4, CONV_LINES // 4)
    waiting = []

    def shard(k, across=0, beside=0):
        return 4 * (z ^ k) + 2 * (x ^ across) + (core ^ beside)

    def region(array, index, first, count):
        rows = quarters[array]
        return wholes[array].at[index, pl.ds(pl.multiple_of(rows * first, 16), rows * count)]

    def device(name, k=0):
        if name == "y":
            return (1 - stream, shard(0))
        return (stream, {"z": shard(k), "x": shard(0, 1), "core": shard(0, 0, 1)}[name])

    def push(arrays, slot, to, index, first, count, k=0, own=False):
        for array in arrays:
            target = region(array, index, first, count)
            source = target
            if own:
                rows = quarters[array]
                source = pieces[array].at[
                    pl.ds(pl.multiple_of(rows * first, 16), rows * count)
                ]
            pltpu.make_async_remote_copy(
                src_ref=source,
                dst_ref=target,
                send_sem=send_sem.at[array, slot],
                recv_sem=recv_sem.at[array, slot],
                device_id=device(to, k),
                device_id_type=MESH,
            ).start()
            waiting.append((array, slot, target))

    def arrive(arrays, slot, index, first, count):
        for array in arrays:
            target = region(array, index, first, count)
            pltpu.make_async_copy(target, target, recv_sem.at[array, slot]).wait()

    barrier = pltpu.get_barrier_semaphore()
    for name, k in (("z", 1), ("z", 2), ("z", 3), ("x", 0), ("y", 0), ("core", 0)):
        pl.semaphore_signal(barrier, inc=1, device_id=device(name, k), device_id_type=MESH)
    load = pltpu.make_async_copy(x_ref, x_rows, local_sem.at[2])
    load.start()
    keep = [
        pltpu.make_async_copy(pieces[array], wholes[array].at[shard(0)], local_sem.at[array])
        for array in range(2)
    ]
    for copy in keep:
        copy.start()
    pl.semaphore_wait(barrier, 6)

    entry, conv = (0,), (1,)
    for array in (conv, entry):
        push(array, 6, "x", shard(0), stream, 3, own=True)
        for k in (1, 2, 3):
            push(array, k - 1, "z", shard(0), 2 * stream, 2, k, own=True)
        push(array, 17, "core", shard(0), 0, 4, own=True)

    on_global = stream == 0

    def rows_of(shape, dim):
        row = lax.broadcasted_iota(jnp.int32, shape, dim)
        image = row // IMAGE_ROWS
        within = row - IMAGE_ROWS * image
        live = within < jnp.where(on_global, IMAGE_ROWS, SMALL_ROWS)
        return image, within, live

    def members(shape, dim):
        image, within, live = rows_of(shape, dim)
        crop = jnp.where(on_global, within // GLOBAL_SIDE**2, within // SMALL_SIDE**2)
        slot = lax.rem(lax.broadcasted_iota(jnp.int32, shape, 1 - dim), CROPS)
        target = jnp.zeros(shape, jnp.int32)
        for at in range(IMAGE_DEV):
            for small in range(SMALL_CROPS):
                target = jnp.where(
                    (image == at) & (crop == small), target_ref[at, small], target
                )
        target = jnp.where(on_global, crop, target)
        crops = jnp.where(on_global, GLOBAL_CROPS, SMALL_CROPS)
        pool = one_hot(live & (crops * image + crop == slot))
        return pool, one_hot(live & (GLOBAL_CROPS * image + target == slot))

    for at, ref in enumerate(vectors):
        values = ref[...]
        for block in range(BLOCKS):
            start = BLOCK * block
            param_out[block, 2 * at : 2 * at + 1] = values[:, start : start + 128]
            param_out[block, 2 * at + 1 : 2 * at + 2] = jnp.concatenate(
                [values[:, start + 128 : start + BLOCK], jnp.zeros((1, LANES - BLOCK), f32)], axis=1
            )
    exit_param_out[...] = jnp.zeros_like(exit_param_out)
    for at, ref in enumerate(exit_vectors):
        for tile in range(PADDED // 128):
            width = min(128, CHANNELS - 128 * tile)
            exit_param_out[tile // 2, 2 * at + tile % 2, :width] = ref[
                0, 128 * tile : 128 * tile + width
            ]
    pool_out[...], pair_out[...] = members((CROPS, ROWS), 1)
    spread, pull = members((ROWS, 2 * CROPS), 0)
    spread_out[...] = spread
    pull_out[...] = pull[:, :CROPS]
    live_out[...] = one_hot(rows_of((ROWS, 128), 0)[2])
    live_lane = jnp.where(rows_of((1, ROWS), 1)[2], 1.0, 0.0)
    stores = []

    def prepare(pair):
        if pair == 0:
            load.wait()
        slot = pair % 2
        if pair >= 2:
            for copy in stores[pair - 2]:
                copy.wait()
        first = (PAIR * pair) // 128
        depth = min(384, CHANNELS - 128 * first)
        source = 128 * first - PAIR * pair
        values = x_rows[:, 128 * first : 128 * first + depth]
        there = lax.broadcasted_iota(jnp.int32, (depth, LANES), 0) + source
        pick = one_hot(there == pair_lane((depth, LANES), 1))
        picked = dot(values, pick)
        for tile in range(2):
            lanes = slice(128 * tile, 128 * tile + 128)
            chunk_rows_ref[slot, :, lanes] = (
                picked[:, lanes] * live_out[...].astype(f32)
            ).astype(bf16)
        there = lax.broadcasted_iota(jnp.int32, (LANES, depth), 1) + source
        pick = one_hot(there == pair_lane((LANES, depth), 0))
        turned_rows[slot] = (dot(pick, values, ((1,), (1,))) * live_lane).astype(bf16)
        lanes = slice(LANES * pair, LANES * (pair + 1))
        copies = (
            pltpu.make_async_copy(chunk_rows_ref.at[slot], chunk_out.at[:, lanes], store_sem.at[0, pair]),
            pltpu.make_async_copy(turned_rows.at[slot], turned_out.at[lanes], store_sem.at[1, pair]),
        )
        for copy in copies:
            copy.start()
        stores.append(copies)

    def from_z(a, k):
        arrive(a, k - 1, shard(k), 2 * stream, 2)
        push(a, 6 + k, "x", shard(k), 2 * stream, 2)
        push(a, 2 + k, "y", shard(k), 2 * stream, 2)
        push(a, 17 + k, "core", shard(k), 2 * stream, 2)

    def from_y(a, k):
        arrive(a, 2 + k, shard(k), 2 - 2 * stream, 2)
        push(a, 9 + k, "x", shard(k), 2 - stream, 1)
        push(a, 20 + k, "core", shard(k), 2 - 2 * stream, 2)

    def from_x(a, k):
        if k == 0:
            arrive(a, 6, shard(0, 1), stream, 3)
            push(a, 13, "y", shard(0, 1), 3 * stream, 1)
            push(a, 24, "core", shard(0, 1), stream, 3)
        else:
            arrive(a, 6 + k, shard(k, 1), 2 * stream, 2)
            push(a, 13 + k, "y", shard(k, 1), 3 * stream, 1)
            push(a, 24 + k, "core", shard(k, 1), 2 * stream, 2)

    def last_x(a, k):
        arrive(a, 9 + k, shard(k, 1), 2 - stream, 1)
        push(a, 27 + k, "core", shard(k, 1), 2 - stream, 1)

    def last_y(a, k):
        arrive(a, 13 + k, shard(k, 1), 3 - 3 * stream, 1)
        push(a, 31 + k, "core", shard(k, 1), 3 - 3 * stream, 1)

    def last_core(a):
        arrive(a, 17, shard(0, 0, 1), 0, 4)
        for k in (1, 2, 3):
            arrive(a, 17 + k, shard(k, 0, 1), 2 * stream, 2)
            arrive(a, 20 + k, shard(k, 0, 1), 2 - 2 * stream, 2)
        arrive(a, 24, shard(0, 1, 1), stream, 3)
        for k in (1, 2, 3):
            arrive(a, 24 + k, shard(k, 1, 1), 2 * stream, 2)
            arrive(a, 27 + k, shard(k, 1, 1), 2 - stream, 1)
        for k in range(4):
            arrive(a, 31 + k, shard(k, 1, 1), 3 - 3 * stream, 1)

    def forward(a, between):
        between = iter(between)

        def pause():
            for work in between:
                work()
                break

        pause()
        from_z(a, 1)
        pause()
        from_z(a, 2)
        from_x(a, 0)
        pause()
        from_z(a, 3)
        from_y(a, 1)
        pause()
        from_x(a, 1)
        from_y(a, 2)
        pause()
        from_x(a, 2)
        from_y(a, 3)
        pause()
        from_x(a, 3)
        last_y(a, 0)
        last_x(a, 1)
        pause()
        last_y(a, 1)
        last_x(a, 2)
        last_y(a, 2)
        last_x(a, 3)
        last_y(a, 3)

    def straighten():
        last_core(conv)
        keep[1].wait()
        for at in range(SHARDS):
            start = LINES * at
            shifted[start : start + CONV_LINES] = conv_rows[at].astype(f32)
        lines[...] = shifted[: SHARDS * LINES].astype(bf16)
        store_lines.start()

    store_lines = pltpu.make_async_copy(lines, lines_out, local_sem.at[3])
    prepares = [functools.partial(prepare, pair) for pair in range(OUT_BLOCKS)]
    forward(conv, prepares[:3])
    forward(entry, prepares[3:6] + [straighten] + prepares[6:])
    last_core(entry)
    for array, slot, target in waiting:
        pltpu.make_async_copy(target, target, send_sem.at[array, slot]).wait()
    keep[0].wait()
    store_lines.wait()
    for pair in (6, 7):
        for copy in stores[pair]:
            copy.wait()


LINES = 1134


def run_gather(entry, conv, x, target, *vectors):
    return pl.pallas_call(
        gather_kernel,
        out_shape=(
            jax.ShapeDtypeStruct((SHARDS, CHUNK_PAD, WIDE), bf16),
            jax.ShapeDtypeStruct((SHARDS * LINES, 128), bf16),
            jax.ShapeDtypeStruct((ROWS, PADDED), bf16),
            jax.ShapeDtypeStruct((PADDED, ROWS), bf16),
            jax.ShapeDtypeStruct((ROWS, 128), bf16),
            jax.ShapeDtypeStruct((CROPS, ROWS), bf16),
            jax.ShapeDtypeStruct((ROWS, 2 * CROPS), bf16),
            jax.ShapeDtypeStruct((CROPS, ROWS), bf16),
            jax.ShapeDtypeStruct((ROWS, CROPS), bf16),
            jax.ShapeDtypeStruct((BLOCKS, 8, 128), f32),
            jax.ShapeDtypeStruct((OUT_BLOCKS, 8, 128), f32),
        ),
        in_specs=[pl.BlockSpec(memory_space=HBM)] * 3
        + [pl.BlockSpec(memory_space=pltpu.SMEM)]
        + [pl.BlockSpec(memory_space=pltpu.VMEM)] * 6,
        out_specs=(pl.BlockSpec(memory_space=HBM),) * 4
        + (pl.BlockSpec(memory_space=pltpu.VMEM),) * 7,
        scratch_shapes=[
            pltpu.VMEM((SHARDS, CONV_LINES, 128), bf16),
            pltpu.VMEM((SHARDS * LINES + 32, 128), f32),
            pltpu.VMEM((SHARDS * LINES, 128), bf16),
            pltpu.VMEM((ROWS, CHANNELS), bf16),
            pltpu.VMEM((2, ROWS, LANES), bf16),
            pltpu.VMEM((2, LANES, ROWS), bf16),
            pltpu.SemaphoreType.DMA((2, 35)),
            pltpu.SemaphoreType.DMA((2, 35)),
            pltpu.SemaphoreType.DMA((4,)),
            pltpu.SemaphoreType.DMA((2, OUT_BLOCKS)),
        ],
        name="gather",
        compiler_params=pltpu.CompilerParams(
            collective_id=4, has_side_effects=True, vmem_limit_bytes=VMEM_LIMIT
        ),
        cost_estimate=pl.CostEstimate(
            flops=4 * ROWS * 384 * PADDED, bytes_accessed=200 * 2**20, transcendentals=0
        ),
    )(entry, conv, x, target, *vectors)


def input_kernel(delta_ref, weight_ref, residual_ref, live_ref, *refs):
    block = pl.program_id(0)
    if len(refs) == 1:
        (grad_out,) = refs
    else:
        rest_ref, conv_ref, grad_out, part_out, *reduce_refs = refs
        sources = [(rest_ref, BACK_REST), (conv_ref, CONV_BLOCKS)]
        feed(Reducer(reduce_refs, BACK_REST + CONV_BLOCKS), block, sources, part_out)

    @pl.when(block < OUT_BLOCKS)
    def _():
        spans = 4
        first = jnp.minimum((LANES * block) // CHUNK, SHARDS - spans)
        depth = spans * CHUNK_PAD
        row = lax.broadcasted_iota(jnp.int32, (LANES, depth), 0) + LANES * block
        lane = lax.broadcasted_iota(jnp.int32, (LANES, depth), 1)
        channel = CHUNK * (first + lane // CHUNK_PAD) + lane % CHUNK_PAD
        pick = one_hot((channel == row) & (lane % CHUNK_PAD < CHUNK))
        rows = pl.ds(pl.multiple_of(CHUNK_PAD * first, CHUNK_PAD), depth)
        weight = dot(pick, weight_ref[rows]).astype(bf16)
        for micro in range(MICRO_BATCHES):
            here = slice(HALF * micro, HALF * (micro + 1))
            grad = dot(delta_ref[here], weight, ((1,), (1,)))
            for tile in range(2):
                lanes = slice(128 * tile, 128 * tile + 128)
                grad_out[here, lanes] = (
                    (grad[:, lanes] + residual_ref[here, lanes].astype(f32))
                    * live_ref[here].astype(f32)
                ).astype(bf16)


def run_input(delta, weight, residual, live, *rest):
    reduced = bool(rest)
    out_shape = jax.ShapeDtypeStruct((ROWS, CHANNELS), bf16)
    out_specs = columns(ROWS, 0, OUT_BLOCKS)
    in_specs = [
        whole((ROWS, WIDE)),
        whole((PADDED, WIDE)),
        columns(ROWS, 0, OUT_BLOCKS),
        whole((ROWS, 128)),
    ]
    args = [delta, weight, residual, live]
    if reduced:
        shape = (BACK_REST + CONV_BLOCKS, 2, 128, 128)
        out_shape = (out_shape, jax.ShapeDtypeStruct(shape, f32))
        out_specs = (out_specs, pl.BlockSpec(shape, lambda i: (0, 0, 0, 0)))
        in_specs += [pl.BlockSpec(memory_space=HBM)] * 2
        args += rest
    return pl.pallas_call(
        input_kernel,
        grid=(BACK_REST + CONV_BLOCKS + 4 if reduced else OUT_BLOCKS,),
        out_shape=out_shape,
        in_specs=in_specs,
        out_specs=out_specs,
        scratch_shapes=Reducer.scratch() if reduced else [],
        name="input",
        compiler_params=pltpu.CompilerParams(
            vmem_limit_bytes=VMEM_LIMIT,
            collective_id=5 if reduced else None,
            has_side_effects=reduced,
        ),
        cost_estimate=pl.CostEstimate(
            flops=2 * ROWS * WIDE * PADDED, bytes_accessed=35 * 2**20, transcendentals=0
        ),
    )(*args)


def wide_lanes(values):
    lead = values.shape[:-1]
    blocks = values.reshape(lead + (BLOCKS, BLOCK))
    padded = jnp.pad(blocks, ((0, 0),) * len(lead) + ((0, 0), (0, LANES - BLOCK)))
    return padded.reshape(lead + (WIDE,))


def narrow_lanes(values):
    lead = values.shape[:-1]
    return values.reshape(lead + (BLOCKS, LANES))[..., :BLOCK].reshape(lead + (CHANNELS,))


def gather(piece, width, size):
    across = -(-width // 128) * 128
    pads = ((0, CHUNK_PAD - CHUNK), (0, across - width))
    if size == SHARDS:
        piece = jnp.pad(piece.reshape(CHUNK, width), pads)
        return lax.all_gather(piece, "img", axis=0, tiled=True)
    pieces = lax.all_gather(piece, "img", axis=0, tiled=True).reshape(SHARDS, CHUNK, width)
    return jnp.pad(pieces, ((0, 0),) + pads).reshape(PADDED, across)


def scatter(grads, width, size):
    if size != SHARDS:
        grads = grads.reshape(SHARDS, CHUNK_PAD, -1)[:, :CHUNK, :width].reshape(-1)
    return lax.psum_scatter(grads, "img", scatter_dimension=0, tiled=True)


def shard_of(part, width, size):
    part = swap_sum(part)
    return part[:CHUNK, :width].reshape(-1) if size == SHARDS else part


def swap_sum(part):
    other = lax.ppermute(part, "stream", [(0, 1), (1, 0)])
    return part.astype(f32) + other.astype(f32)


def beside_blocks(first, blocks):
    return jnp.concatenate([first, blocks.transpose(2, 0, 1, 3).reshape(128, -1)], axis=1)


def chunked(values):
    lead = values.shape[:-1]
    values = values.reshape(lead + (SHARDS, CHUNK))
    values = jnp.pad(values, ((0, 0),) * len(lead) + ((0, 0), (0, CHUNK_PAD - CHUNK)))
    return values.reshape(lead + (PADDED,))


def unchunked(values):
    lead = values.shape[:-1]
    values = values.reshape(lead + (SHARDS, CHUNK_PAD))[..., :CHUNK]
    return values.reshape(lead + (CHANNELS,))


def row_masks(on_global, pair_target):
    positions = jnp.arange(ROWS, dtype=jnp.int32)
    image_of = positions // IMAGE_ROWS
    within = positions % IMAGE_ROWS
    live = within < jnp.where(on_global, IMAGE_ROWS, SMALL_ROWS)
    area = jnp.where(on_global, GLOBAL_SIDE**2, SMALL_SIDE**2)
    crop_of = within // area
    crop_ids = jnp.arange(CROPS, dtype=jnp.int32)
    per_image = jnp.where(on_global, GLOBAL_CROPS, SMALL_CROPS)
    pool_full = live[None] & ((image_of * per_image + crop_of)[None] == crop_ids[:, None])
    pool = pool_full.astype(bf16)
    target_rows = jnp.zeros((ROWS,), jnp.int32)
    for slot in range(SMALL_CROPS):
        target_rows = jnp.where(
            crop_of == slot, jnp.repeat(pair_target[:, slot], IMAGE_ROWS), target_rows
        )
    pair_of = image_of * GLOBAL_CROPS + jnp.where(on_global, crop_of, target_rows)
    pair = (live[None] & (pair_of[None] == crop_ids[:, None])).astype(bf16)
    live_lanes = jnp.broadcast_to(live[:, None], (ROWS, 128)).astype(bf16)
    return live, live_lanes, pool, pair


def local(
    block_in,
    out_cotangent,
    pair_target,
    entry_weight,
    entry_gain,
    entry_shift,
    group_weight,
    group_gain,
    group_shift,
    squeeze_weight,
    squeeze_bias,
    excite_weight,
    excite_bias,
    exit_weight,
    exit_gain,
    exit_shift,
):
    size = lax.axis_size("img")
    stream = lax.axis_index("stream")
    on_global = stream == 0
    edges = edge_masks()

    x = block_in[0]
    cot = out_cotangent[0]

    lines = LINES
    if size == SHARDS:
        entry_piece = wide_lanes(entry_weight.reshape(CHUNK, CHANNELS))
        entry_piece = jnp.pad(entry_piece, ((0, CHUNK_PAD - CHUNK), (0, 0)))
        piece = group_weight.reshape(lines, GROUP_WIDTH)
        piece = jnp.pad(piece, ((0, CONV_LINES - lines), (0, 128 - GROUP_WIDTH)))
        vectors = (entry_gain, entry_shift, group_gain, group_shift, exit_gain, exit_shift)
        gathered = run_gather(
            entry_piece, piece, x, pair_target, *(vector[None] for vector in vectors)
        )
        entry_mat, conv, x_chunked, x_turned, live_lanes, pool, spread, pair, pull = gathered[:9]
        params, exit_params = gathered[9:]
        entry_mat = entry_mat.reshape(PADDED, WIDE)
        conv = conv.reshape(9, CHANNELS, 128)
    else:
        def rows_of(*vectors):
            kept = wide_lanes(jnp.stack(vectors)).reshape(len(vectors), BLOCKS, 2, 128)
            return kept.transpose(1, 0, 2, 3).reshape(BLOCKS, 2 * len(vectors), 128)

        params = rows_of(entry_gain, entry_shift, group_gain, group_shift)
        exit_params = [
            jnp.pad(vector, (0, PADDED - CHANNELS)).reshape(OUT_BLOCKS, 2, 128)
            for vector in (exit_gain, exit_shift)
        ]
        exit_params = jnp.concatenate(exit_params * 2, axis=1)
        live, live_lanes, pool, pair = row_masks(on_global, pair_target)
        spread, pull = jnp.concatenate([pool.T, pool.T], axis=1), pair.T
        x_padded = jnp.where(live[:, None], x, 0)
        x_padded = jnp.pad(x_padded, ((0, 0), (0, PADDED - CHANNELS)))
        x_chunked, x_turned = run_prepare(x_padded)
        entry_mat = wide_lanes(gather(entry_weight, CHANNELS, size)[:, :CHANNELS])
        conv = lax.all_gather(group_weight, "img", axis=0, tiled=True)
        conv = conv.reshape(9, CHANNELS, GROUP_WIDTH)
        conv = jnp.pad(conv, ((0, 0), (0, 0), (0, 128 - GROUP_WIDTH)))
    squeeze_mat = gather(squeeze_weight, SQUEEZE, size)
    excite_mat = gather(excite_weight, SQUEEZE, size)
    exit_mat = gather(exit_weight, CHANNELS, size)

    fold = np.zeros((LANES, 128), np.float32)
    fold[np.arange(BLOCK), np.arange(BLOCK) % GROUP_WIDTH] = 1
    fold = jnp.asarray(fold, bf16)
    act, turned, group, mixed, pooled, moment = run_entry(
        size, x_chunked, entry_mat, conv, params, pool, edges, fold.T
    )

    inner_pad = INNER - SQUEEZE
    scaled, scaled_turned, gates, pooled, inner, inner_rows, quarter = run_scale(
        mixed,
        spread,
        pooled,
        squeeze_mat,
        excite_mat,
        jnp.pad(squeeze_bias, (0, inner_pad))[None],
        jnp.pad(excite_bias.reshape(QUARTERS, SQUEEZE), ((0, 0), (0, inner_pad))),
    )

    block_out, exit_delta, residual, exit_grad, exit_total = run_exit(
        size, scaled, scaled_turned, exit_mat, x, cot, exit_params, pair, pull, live_lanes
    )
    exit_part = scatter(exit_grad, CHANNELS, size)
    scaled_grad, gate_grad, block_out = run_gate(exit_delta, exit_mat, mixed, pool, block_out)

    pooled_gates, inner_grads, bias_rows = run_squeeze(
        gate_grad, pooled, inner, inner_rows, quarter, squeeze_mat, excite_mat
    )
    bias_rows = bias_rows.reshape(BIAS_ROWS, 128)
    entry_delta, entry_grad, conv_grad, totals, bias_totals, *entry_rest = run_back(
        size, bias_rows, scaled_grad, group, gates, pooled_gates, spread, act, turned, conv, x_turned, params,
        moment, edges, fold,
    )
    entry_delta, exit_part, inner_grads = lax.optimization_barrier(
        (entry_delta, exit_part, inner_grads)
    )
    exit_shard = shard_of(exit_part, CHANNELS, size)
    if size == SHARDS:
        inner_part = swap_sum(scatter(inner_grads, 2 * INNER, size))[:CHUNK]
        squeeze_shard = inner_part[:, :SQUEEZE].reshape(-1)
        excite_shard = inner_part[:, INNER : INNER + SQUEEZE].reshape(-1)
    else:
        squeeze_shard = shard_of(scatter(inner_grads[:, :INNER], SQUEEZE, size), SQUEEZE, size)
        excite_shard = shard_of(scatter(inner_grads[:, INNER:], SQUEEZE, size), SQUEEZE, size)
    if size == SHARDS:
        conv_lines = 256 * CONV_BLOCKS
        conv_grad = conv_grad.reshape(SHARDS, lines // 2, 2 * GROUP_WIDTH)
        conv_grad = jnp.pad(
            conv_grad,
            ((0, 0), (0, conv_lines - lines // 2), (0, 128 - 2 * GROUP_WIDTH)),
        ).reshape(4, 2, 2, CONV_BLOCKS, 2, 128, 128)
        conv_grad = conv_grad.transpose(3, 2, 1, 0, 4, 5, 6)
        input_grad, parts = run_input(
            entry_delta, entry_mat, residual, live_lanes, entry_rest[0], conv_grad
        )
        entry_grad = beside_blocks(entry_grad, parts[:BACK_REST])
        entry_shard = narrow_lanes(entry_grad[:CHUNK]).reshape(-1)
        conv_part = parts[BACK_REST:].reshape(conv_lines, 128)
        conv_shard = conv_part[: lines // 2, : 2 * GROUP_WIDTH].reshape(-1)
    else:
        input_grad = run_input(entry_delta, entry_mat, residual, live_lanes)
        entry_shard = swap_sum(scatter(narrow_lanes(entry_grad), CHANNELS, size))
        conv_part = lax.psum_scatter(
            conv_grad.reshape(-1), "img", scatter_dimension=0, tiled=True
        )
        conv_shard = swap_sum(conv_part)
    shards = (entry_shard, conv_shard, squeeze_shard, excite_shard, exit_shard)

    def folded(kept):
        kept = kept.reshape(-1, MICRO_BATCHES, 2, LANES).sum(axis=1)
        return kept[:, 1].reshape(-1), kept[:, 0].reshape(-1)

    group_gain_grad, group_shift_grad = [narrow_lanes(v) for v in folded(totals[:, 0])]
    entry_gain_grad, entry_shift_grad = [narrow_lanes(v) for v in folded(totals[:, 1])]
    exit_gain_grad, exit_shift_grad = [v[:CHANNELS] for v in folded(exit_total[:, 1])]
    bias_totals = bias_totals.reshape(8, INNER)[: 1 + QUARTERS, :SQUEEZE]
    kept = jnp.concatenate(
        [
            jnp.stack(
                [
                    entry_gain_grad,
                    entry_shift_grad,
                    group_gain_grad,
                    group_shift_grad,
                    exit_gain_grad,
                    exit_shift_grad,
                    bias_totals[1:].reshape(-1),
                ]
            ),
            jnp.pad(bias_totals[0], (0, CHANNELS - SQUEEZE))[None],
        ]
    )
    smalls = swap_sum(kept)

    return (
        block_out[None],
        input_grad[None],
        shards[0],
        smalls[0],
        smalls[1],
        shards[1],
        smalls[2],
        smalls[3],
        shards[2],
        smalls[7, :SQUEEZE],
        shards[3],
        smalls[6],
        shards[4],
        smalls[4],
        smalls[5],
    )


def solution(mesh):
    return jax.shard_map(
        local,
        mesh=mesh,
        in_specs=(
            P("stream", "img", None),
            P("stream", "img", None),
            P("img", None),
            P("img"),
            P(),
            P(),
            P("img"),
            P(),
            P(),
            P("img"),
            P(),
            P("img"),
            P(),
            P("img"),
            P(),
            P(),
        ),
        out_specs=(
            P("stream", "img", None),
            P("stream", "img", None),
            P("img"),
            P(),
            P(),
            P("img"),
            P(),
            P(),
            P("img"),
            P(),
            P("img"),
            P(),
            P("img"),
            P(),
            P(),
        ),
        check_vma=False,
    )
```

```python
import functools

import jax
import jax.numpy as jnp
import numpy as np
from jax import lax
from jax.experimental import pallas as pl
from jax.experimental.pallas import tpu as pltpu
from jax.sharding import PartitionSpec as P

CHANNELS = 2016
GROUPS = 36
SQUEEZE = 504
GROUP_WIDTH = 56
GLOBAL_SIDE = 14
SMALL_SIDE = 7
GLOBAL_CROPS = 2
SMALL_CROPS = 3
IMAGE_DEV = 4
MICRO_BATCHES = 2
IMAGE_ROWS = 392
SMALL_ROWS = 147
ROWS = IMAGE_DEV * IMAGE_ROWS
HALF = ROWS // MICRO_BATCHES

BLOCK = 224
LANES = 256
BLOCKS = CHANNELS // BLOCK
WIDE = BLOCKS * LANES
PADDED = 2048
OUT_BLOCKS = PADDED // LANES

IMAGE_PAD = 424
TOP = 16
CONV_ROWS = IMAGE_DEV * IMAGE_PAD
DEEP_ROWS = 1792
PAD_ROWS = TOP + DEEP_ROWS + 16
CROPS = 16
STEP = 112
STEPS = ROWS // STEP
HALF_STEPS = HALF // STEP
CHUNK = 126
CHUNK_PAD = 128
SHARDS = CHANNELS // CHUNK
PAIR = 2 * CHUNK

EPSILON = 1e-05
PAIR_SCALE = 4.0
MESH = pl.DeviceIdType.MESH
HBM = pl.ANY
VMEM_LIMIT = 62 * 2**20

f32 = jnp.float32
bf16 = jnp.bfloat16


def dot(a, b, dims=((1,), (0,))):
    return lax.dot_general(a, b, (dims, ((), ())), preferred_element_type=f32)


def img_barrier(size):
    stream = lax.axis_index("stream")
    me = lax.axis_index("img")
    barrier = pltpu.get_barrier_semaphore()

    def greet(step, carry):
        pl.semaphore_signal(
            barrier, inc=1, device_id=(stream, lax.rem(me + step, size)), device_id_type=MESH
        )
        return carry

    lax.fori_loop(1, size, greet, 0)
    return barrier


class Exchange:
    def __init__(self, size, sent, got, send_sem, recv_sem):
        self.size, self.sent, self.got = size, sent, got
        self.send_sem, self.recv_sem = send_sem, recv_sem

    @staticmethod
    def scratch(steps, size):
        return [
            pltpu.VMEM((steps, 2, 8, 128), f32),
            pltpu.VMEM((steps, 2, size, 8, 128), f32),
            pltpu.SemaphoreType.DMA((steps, 2)),
            pltpu.SemaphoreType.DMA((steps, 2)),
        ]

    def put(self, slot, kind, packed):
        stream = lax.axis_index("stream")
        me = lax.axis_index("img")
        self.sent[slot, kind] = packed
        self.got[slot, kind, me] = packed

        def start(step, carry):
            pltpu.make_async_remote_copy(
                src_ref=self.sent.at[slot, kind],
                dst_ref=self.got.at[slot, kind, me],
                send_sem=self.send_sem.at[slot, kind],
                recv_sem=self.recv_sem.at[slot, kind],
                device_id=(stream, lax.rem(me + step, self.size)),
                device_id_type=MESH,
            ).start()
            return carry

        lax.fori_loop(1, self.size, start, 0)

    def total(self, slot, kind):
        others = self.got.at[slot, kind, pl.ds(0, self.size - 1)]
        pltpu.make_async_copy(others, others, self.recv_sem.at[slot, kind]).wait()
        pltpu.make_async_copy(others, others, self.send_sem.at[slot, kind]).wait()
        return add_up(self.got[slot, kind, peer] for peer in range(self.size))


def row_count(size):
    live = jnp.where(lax.axis_index("stream") == 0, IMAGE_ROWS, SMALL_ROWS)
    return (live * (size * (IMAGE_DEV // MICRO_BATCHES))).astype(f32)


def column_sum(values):
    return jnp.sum(values, axis=0, keepdims=True)


def moments(total, micro, tile, count):
    mean = total[4 * micro + tile : 4 * micro + tile + 1] / count
    square = total[4 * micro + 2 + tile : 4 * micro + 3 + tile] / count
    return mean, lax.rsqrt(square - mean * mean + EPSILON)


def edge_masks():
    column = np.arange(IMAGE_PAD) % 212 % 14
    both = np.stack([column != 13, column != 0]).astype(np.float32)
    return jnp.broadcast_to(jnp.asarray(both)[:, :, None], (2, IMAGE_PAD, 128))


def chunk_rows(chunk):
    return slice(STEP * chunk, STEP * (chunk + 1))


def add_up(pieces):
    pieces = list(pieces)
    while len(pieces) > 1:
        odd = [pieces.pop()] if len(pieces) % 2 else []
        pieces = [pieces[i] + pieces[i + 1] for i in range(0, len(pieces), 2)] + odd
    return pieces[0]


def fold_rows(values):
    return add_up(values[8 * i : 8 * i + 8] for i in range(values.shape[0] // 8))


class Sums:
    def __init__(self):
        self.parts = {}

    def add(self, micro, tile, plain, product):
        for kind, values in ((0, plain), (1, product)):
            key = (micro, kind, tile)
            self.parts.setdefault(key, []).append(fold_rows(values))

    def packed(self):
        return jnp.concatenate([column_sum(add_up(self.parts[key])) for key in sorted(self.parts)])


def put_pads(piece, place, tile, pads, edges):
    here = slice(place, place + piece.shape[0])
    inner = (place - TOP) % IMAGE_PAD
    inner = slice(inner, inner + piece.shape[0])
    pads[0, tile, here] = piece
    pads[1, tile, here] = piece * edges[0, inner]
    pads[2, tile, here] = piece * edges[1, inner]


def pad_global(load, pads, edges):
    inside = lax.broadcasted_iota(jnp.int32, (8, 128), 0)
    for image in range(IMAGE_DEV):
        base = TOP + IMAGE_PAD * image
        start = IMAGE_ROWS * image
        for tile in range(2):
            middle = load(tile, start + 192, 8)
            first = load(tile, start, 192)
            put_pads(first, base, tile, pads, edges)
            put_pads(jnp.where(inside < 4, middle, 0.0), base + 192, tile, pads, edges)
            put_pads(jnp.where(inside >= 4, middle, 0.0), base + 208, tile, pads, edges)
            second = load(tile, start + 200, 192)
            put_pads(second, base + 216, tile, pads, edges)


def small_strips():
    for image in range(IMAGE_DEV):
        for crop in range(SMALL_CROPS):
            for line in range(SMALL_SIDE):
                start = IMAGE_ROWS * image + 49 * crop + 7 * line
                yield start, IMAGE_PAD * image + 114 * crop + 14 * line


def pad_small(rows_ref, pads):
    for start, base in small_strips():
        for tile in range(2):
            piece = rows_ref[tile, start : start + 7]
            for kind in range(3):
                pads[kind, tile, TOP + base : TOP + base + 7] = piece


def unpad_small(wide_ref, rows_ref):
    for start, base in small_strips():
        for tile in range(2):
            rows_ref[tile, start : start + 7] = wide_ref[tile, base : base + 7]


def unpadded(wide_ref, tile, first, count):
    pieces = []
    at = first
    while at < first + count:
        image, inner = divmod(at, 49)
        base = IMAGE_PAD * image
        stop = 49 * image + (24 if inner < 24 else 25 if inner == 24 else 49)
        stop = min(stop, first + count)
        length = 8 * (stop - at)
        if inner == 24:
            inside = lax.broadcasted_iota(jnp.int32, (8, 128), 0)
            pieces.append(
                jnp.where(
                    inside < 4,
                    wide_ref[tile, base + 192 : base + 200],
                    wide_ref[tile, base + 208 : base + 216],
                )
            )
        else:
            start = base + 8 * inner + (0 if inner < 24 else 16)
            pieces.append(wide_ref[tile, start : start + length])
        at = stop
    return pieces[0] if len(pieces) == 1 else jnp.concatenate(pieces)


def stack_windows(pads, windows, image, sign):
    for offset in range(9):
        down, across = offset // 3 - 1, offset % 3 - 1
        shift = sign * (14 * down + across)
        kind = (0, 2, 1)[sign * across]
        start = TOP + IMAGE_PAD * image + shift
        for tile in range(2):
            at = LANES * offset + 128 * tile
            windows[IMAGE_PAD * image : IMAGE_PAD * (image + 1), at : at + 128] = pads[
                kind, tile, start : start + IMAGE_PAD
            ].astype(bf16)


def same_group(rows, lanes):
    row_group = lax.broadcasted_iota(jnp.int32, (rows, lanes), 0) // GROUP_WIDTH
    lane_group = lax.broadcasted_iota(jnp.int32, (rows, lanes), 1) // GROUP_WIDTH
    return row_group == lane_group


def entry_kernel(
    size,
    x_ref,
    weight_ref,
    conv_ref,
    param_ref,
    pool_ref,
    edges,
    fold_ref,
    act_out,
    turned_out,
    group_out,
    mixed_out,
    pooled_out,
    total_out,
    first_rows,
    second_rows,
    rows_ref,
    pads,
    windows,
    wide_ref,
    full_ref,
    *exchange_refs,
):
    exchange = Exchange(size, *exchange_refs)
    step = pl.program_id(0)
    count = row_count(size)
    on_global = lax.axis_index("stream") == 0

    @pl.when(step == 0)
    def _():
        barrier = img_barrier(size)
        pads[...] = jnp.zeros_like(pads)
        full_ref[...] = jnp.zeros_like(full_ref)
        second_rows[...] = jnp.zeros_like(second_rows)
        pl.semaphore_wait(barrier, size - 1)

    @pl.when(step < BLOCKS)
    def _():
        slot = lax.rem(step, 2)
        for micro in range(MICRO_BATCHES):
            here = slice(HALF * micro, HALF * (micro + 1))
            act = dot(x_ref[here], weight_ref[...])
            first_rows[slot, 0, here] = act[:, :128]
            first_rows[slot, 1, here] = act[:, 128:]
        sums = Sums()
        for chunk in range(STEPS):
            here = chunk_rows(chunk)
            for tile in range(2):
                act = first_rows[slot, tile, here]
                act_out[here, 128 * tile : 128 * tile + 128] = act
                sums.add(chunk // HALF_STEPS, tile, act, act * act)
        exchange.put(step, 0, sums.packed())

    @pl.when((step >= 1) & (step < BLOCKS + 1))
    def _():
        block = step - 1
        slot = lax.rem(block, 2)
        total = exchange.total(step - 1, 0)
        total_out[block, 0] = total
        param = param_ref[block]
        scales = {}
        for micro in range(MICRO_BATCHES):
            for tile in range(2):
                mean, inverse = moments(total, micro, tile, count)
                scale = 0.5 * inverse * param[tile : tile + 1]
                scales[micro, tile] = scale, 0.5 * param[2 + tile : 3 + tile] - mean * scale

        def hidden(tile, start, length):
            scale, shift = scales[start // HALF, tile]
            half = first_rows[slot, tile, start : start + length] * scale + shift
            return half + half * jnp.tanh(half)

        same = same_group(BLOCK, LANES)
        for offset in range(9):
            full = dot(conv_ref[offset], fold_ref[...])
            full_ref[LANES * offset : LANES * offset + BLOCK] = jnp.where(
                same, full, 0.0
            ).astype(bf16)

        def convolve(image, target):
            stack_windows(pads, windows, image, 1)
            here = slice(IMAGE_PAD * image, IMAGE_PAD * (image + 1))
            wide = dot(windows[here], full_ref[...])
            target[0, here] = wide[:, :128]
            target[1, here] = wide[:, 128:]

        def turn():
            for tile in range(2):
                turned_out[0, 128 * tile : 128 * tile + 128] = pads[
                    0, tile, TOP : TOP + DEEP_ROWS
                ].T.astype(bf16)

        @pl.when(on_global)
        def _():
            pad_global(hidden, pads, edges)
            turn()
            second = second_rows.at[slot]
            for image in range(IMAGE_DEV):
                convolve(image, second)
            sums = Sums()
            for chunk in range(STEPS):
                for tile in range(2):
                    act = unpadded(second, tile, STEP // 8 * chunk, STEP // 8)
                    sums.add(chunk // HALF_STEPS, tile, act, act * act)
            exchange.put(step, 1, sums.packed())

        @pl.when(jnp.logical_not(on_global))
        def _():
            for chunk in range(STEPS):
                for tile in range(2):
                    rows_ref[tile, chunk_rows(chunk)] = hidden(tile, STEP * chunk, STEP)
            pad_small(rows_ref, pads)
            turn()
            for image in range(IMAGE_DEV):
                convolve(image, wide_ref)
            second = second_rows.at[slot]
            unpad_small(wide_ref, second)
            sums = Sums()
            for chunk in range(STEPS):
                for tile in range(2):
                    act = second[tile, chunk_rows(chunk)]
                    sums.add(chunk // HALF_STEPS, tile, act, act * act)
            exchange.put(step, 1, sums.packed())

    @pl.when(step >= 2)
    def _():
        block = step - 2
        slot = lax.rem(block, 2)
        total = exchange.total(step - 1, 1)
        total_out[block, 1] = total
        param = param_ref[block]
        second = second_rows.at[slot]

        def finish(load):
            for micro in range(MICRO_BATCHES):
                for tile in range(2):
                    lanes = slice(128 * tile, 128 * tile + 128)
                    mean, inverse = moments(total, micro, tile, count)
                    scale = 0.5 * inverse * param[4 + tile : 5 + tile]
                    shift = 0.5 * param[6 + tile : 7 + tile] - mean * scale
                    for chunk in range(HALF_STEPS * micro, HALF_STEPS * (micro + 1)):
                        here = chunk_rows(chunk)
                        act = load(tile, chunk)
                        group_out[here, lanes] = act
                        half = act * scale + shift
                        mixed_out[here, lanes] = (half + half * jnp.tanh(half)).astype(bf16)

        @pl.when(on_global)
        def _():
            finish(lambda tile, chunk: unpadded(second, tile, STEP // 8 * chunk, STEP // 8))

        @pl.when(jnp.logical_not(on_global))
        def _():
            finish(lambda tile, chunk: second[tile, chunk_rows(chunk)])

        pooled_out[...] = dot(pool_ref[...], mixed_out[...])


def run_entry(size, x, weight, conv, params, pool, edges, fold):
    def whole(shape):
        return pl.BlockSpec(shape, lambda i: (0,) * len(shape), pipeline_mode=pl.Buffered(1))

    def at(lag):
        return lambda i: jnp.clip(i - lag, 0, BLOCKS - 1)

    return pl.pallas_call(
        functools.partial(entry_kernel, size),
        grid=(BLOCKS + 2,),
        out_shape=(
            jax.ShapeDtypeStruct((ROWS, WIDE), f32),
            jax.ShapeDtypeStruct((BLOCKS, LANES, DEEP_ROWS), bf16),
            jax.ShapeDtypeStruct((ROWS, WIDE), f32),
            jax.ShapeDtypeStruct((ROWS, WIDE), bf16),
            jax.ShapeDtypeStruct((CROPS, WIDE), f32),
            jax.ShapeDtypeStruct((BLOCKS, 2, 8, 128), f32),
        ),
        in_specs=[
            whole((ROWS, PADDED)),
            pl.BlockSpec((PADDED, LANES), lambda i: (0, at(0)(i))),
            pl.BlockSpec((9, BLOCK, 128), lambda i: (0, at(1)(i), 0)),
            whole((BLOCKS, 8, 128)),
            whole((CROPS, ROWS)),
            whole((2, IMAGE_PAD, 128)),
            whole((128, LANES)),
        ],
        out_specs=(
            pl.BlockSpec((ROWS, LANES), lambda i: (0, at(0)(i))),
            pl.BlockSpec((1, LANES, DEEP_ROWS), lambda i: (at(1)(i), 0, 0)),
            pl.BlockSpec((ROWS, LANES), lambda i: (0, at(2)(i))),
            pl.BlockSpec((ROWS, LANES), lambda i: (0, at(2)(i))),
            pl.BlockSpec((CROPS, LANES), lambda i: (0, at(2)(i))),
            pl.BlockSpec((BLOCKS, 2, 8, 128), lambda i: (0, 0, 0, 0)),
        ),
        scratch_shapes=[
            pltpu.VMEM((2, 2, ROWS, 128), f32),
            pltpu.VMEM((2, 2, CONV_ROWS, 128), f32),
            pltpu.VMEM((2, ROWS, 128), f32),
            pltpu.VMEM((3, 2, PAD_ROWS, 128), f32),
            pltpu.VMEM((CONV_ROWS, 9 * LANES), bf16),
            pltpu.VMEM((2, CONV_ROWS, 128), f32),
            pltpu.VMEM((9 * LANES, LANES), bf16),
        ]
        + Exchange.scratch(BLOCKS + 1, size),
        name="entry",
        compiler_params=pltpu.CompilerParams(
            collective_id=1, has_side_effects=True, vmem_limit_bytes=VMEM_LIMIT
        ),
        cost_estimate=pl.CostEstimate(
            flops=2 * ROWS * WIDE * (PADDED + 9 * LANES),
            bytes_accessed=70 * 2**20,
            transcendentals=2 * ROWS * WIDE,
        ),
    )(x, weight, conv, params, pool, edges, fold)


def place():
    me = lax.axis_index("img")
    return lax.axis_index("stream"), me // 4, lax.rem(me // 2, 2), lax.rem(me, 2)


class Reducer:
    def __init__(self, refs, inside, rest=None):
        self.inside, self.rest = inside, rest
        (
            self.local,
            self.core_got,
            self.plane_got,
            self.plane_sum,
            self.z_got,
            self.final,
            self.final_got,
            self.core_sem,
            self.plane_sem,
            self.z_sem,
            self.y_sem,
            self.local_sem,
        ) = refs
        self.stream, self.z, self.x, self.core = place()
        self.mine = pl.ds(pl.multiple_of(64 * self.stream, 64), 64)
        self.theirs = pl.ds(pl.multiple_of(64 * (1 - self.stream), 64), 64)

    @staticmethod
    def scratch():
        return [
            pltpu.VMEM((2, 2, 2, 4, 2, 128, 128), bf16),
            pltpu.VMEM((3, 2, 4, 2, 128, 128), bf16),
            pltpu.VMEM((2, 3, 4, 2, 64, 128), bf16),
            pltpu.VMEM((2, 4, 2, 64, 128), bf16),
            pltpu.VMEM((2, 3, 2, 64, 128), bf16),
            pltpu.VMEM((2, 2, 64, 128), bf16),
            pltpu.VMEM((2, 2, 64, 128), bf16),
            pltpu.SemaphoreType.DMA((2, 2)),
            pltpu.SemaphoreType.DMA((2, 2, 3)),
            pltpu.SemaphoreType.DMA((2, 2, 3)),
            pltpu.SemaphoreType.DMA((2, 2)),
            pltpu.SemaphoreType.DMA((2,)),
        ]

    SHAPE = (2, 2, 4, 2, 128, 128)

    def index(self, k=0, across=0, beside=0):
        return 4 * (self.z ^ k) + 2 * (self.x ^ across) + (self.core ^ beside)

    def greet(self, barrier):
        for across in (0, 1):
            pl.semaphore_signal(
                barrier,
                inc=1,
                device_id=(1 - self.stream, self.index(0, across)),
                device_id_type=MESH,
            )
        return 2

    def core_copy(self, block):
        hold = lax.rem(block, 2)
        return pltpu.make_async_remote_copy(
            src_ref=self.local.at[hold, 1 - self.core],
            dst_ref=self.core_got.at[lax.rem(block, 3)],
            send_sem=self.core_sem.at[0, hold],
            recv_sem=self.core_sem.at[1, hold],
            device_id=(self.stream, self.index(0, 0, 1)),
            device_id_type=MESH,
        )

    def plane_copy(self, block, peer):
        hold = lax.rem(block, 2)
        x = self.x if peer == 1 else 1 - self.x
        rows = self.mine if peer == 0 else self.theirs
        stream = self.stream if peer == 0 else 1 - self.stream
        return pltpu.make_async_remote_copy(
            src_ref=self.core_got.at[lax.rem(block, 3), x, :, :, rows],
            dst_ref=self.plane_got.at[hold, peer],
            send_sem=self.plane_sem.at[0, hold, peer],
            recv_sem=self.plane_sem.at[1, hold, peer],
            device_id=(stream, self.index(0, 0 if peer == 1 else 1)),
            device_id_type=MESH,
        )

    def z_copy(self, block, k):
        hold = lax.rem(block, 2)
        return pltpu.make_async_remote_copy(
            src_ref=self.plane_sum.at[hold, self.z ^ k],
            dst_ref=self.z_got.at[hold, k - 1],
            send_sem=self.z_sem.at[0, hold, k - 1],
            recv_sem=self.z_sem.at[1, hold, k - 1],
            device_id=(self.stream, self.index(k)),
            device_id_type=MESH,
        )

    def y_copy(self, block):
        hold = lax.rem(block, 2)
        return pltpu.make_async_remote_copy(
            src_ref=self.final.at[hold],
            dst_ref=self.final_got.at[hold],
            send_sem=self.y_sem.at[0, hold],
            recv_sem=self.y_sem.at[1, hold],
            device_id=(1 - self.stream, self.index()),
            device_id_type=MESH,
        )

    def finish(self, block, put):
        hold = lax.rem(block, 2)
        self.y_copy(block).wait()
        for tile in range(2):
            put(tile, self.mine, self.final[hold, tile].astype(f32))
            put(tile, self.theirs, self.final_got[hold, tile].astype(f32))

    def after_z(self, block):
        hold = lax.rem(block, 2)
        for k in (1, 2, 3):
            self.z_copy(block, k).wait()
        for tile in range(2):
            total = self.plane_sum[hold, self.z, tile].astype(f32)
            for k in range(3):
                total = total + self.z_got[hold, k, tile].astype(f32)
            self.final[hold, tile] = total.astype(bf16)
        self.y_copy(block).start()

    def after_plane(self, block):
        hold = lax.rem(block, 2)
        ring = lax.rem(block, 3)
        for peer in range(3):
            self.plane_copy(block, peer).wait()
        for z in range(4):
            for tile in range(2):
                total = self.core_got[ring, self.x, z, tile, self.mine].astype(f32)
                for peer in range(3):
                    total = total + self.plane_got[hold, peer, z, tile].astype(f32)
                self.plane_sum[hold, z, tile] = total.astype(bf16)
        for k in (1, 2, 3):
            self.z_copy(block, k).start()

    def after_core(self, block):
        hold = lax.rem(block, 2)
        ring = lax.rem(block, 3)
        self.core_copy(block).wait()
        for x in range(2):
            for z in range(4):
                for tile in range(2):
                    total = self.core_got[ring, x, z, tile].astype(f32)
                    total = total + self.local[hold, self.core, x, z, tile].astype(f32)
                    self.core_got[ring, x, z, tile] = total.astype(bf16)
        for peer in range(3):
            self.plane_copy(block, peer).start()

    def rest_copy(self, block):
        hold = lax.rem(block, 2)
        return pltpu.make_async_copy(
            self.local.at[hold], self.rest.at[block - self.inside], self.local_sem.at[hold]
        )

    def load_copy(self, source, at, block):
        hold = lax.rem(block, 2)
        return pltpu.make_async_copy(source.at[at], self.local.at[hold], self.local_sem.at[hold])

    def advance(self, newest, put, blocks=0):
        def live(block):
            return (block >= 0) & (block < self.inside)

        @pl.when(live(newest - 4))
        def _():
            self.finish(newest - 4, put)

        @pl.when(live(newest - 3))
        def _():
            self.after_z(newest - 3)

        @pl.when(live(newest - 2))
        def _():
            self.after_plane(newest - 2)

        @pl.when(live(newest - 1))
        def _():
            self.after_core(newest - 1)

        if self.rest is not None:

            @pl.when((newest > self.inside) & (newest <= blocks))
            def _():
                self.rest_copy(newest - 1).wait()

    def begin(self, block, grad):
        hold = lax.rem(block, 2)
        for chunk in range(SHARDS):
            z, x, core = chunk // 4, chunk // 2 % 2, chunk % 2
            for tile in range(2):
                self.local[hold, core, x, z, tile] = grad[
                    128 * chunk : 128 * chunk + 128, 128 * tile : 128 * tile + 128
                ].astype(bf16)

        @pl.when(block < self.inside)
        def _():
            self.core_copy(block).start()

        if self.rest is not None:

            @pl.when(block >= self.inside)
            def _():
                self.rest_copy(block).start()

    def neighbours(self):
        barrier = pltpu.get_barrier_semaphore()
        greeted = self.greet(barrier)
        peers = [(0, 0, 1), (0, 1, 0), (1, 0, 0), (2, 0, 0), (3, 0, 0)]
        for peer in peers:
            pl.semaphore_signal(
                barrier, inc=1, device_id=(self.stream, self.index(*peer)), device_id_type=MESH
            )
        pl.semaphore_wait(barrier, len(peers) + greeted)


def feed(reducer, step, sources, part_out):
    starts = []
    total = 0
    for source, count in sources:
        starts.append((source, total, total + count))
        total += count

    def start_load(block):
        for source, first, last in starts:

            @pl.when((block >= first) & (block < last))
            def _():
                reducer.load_copy(source, block - first, block).start()

    @pl.when(step == 0)
    def _():
        start_load(step)
        reducer.neighbours()

    def put(tile, rows, values):
        part_out[step - 4, tile, rows] = values

    reducer.advance(step, put)

    @pl.when(step < total)
    def _():
        reducer.load_copy(sources[0][0], 0, step).wait()
        reducer.core_copy(step).start()

    start_load(step + 1)


BACK_INSIDE = 6
BACK_REST = BLOCKS - BACK_INSIDE
CONV_BLOCKS = 3


def whole(shape):
    return pl.BlockSpec(shape, lambda i: (0,) * len(shape), pipeline_mode=pl.Buffered(1))


def columns(rows, lag, blocks):
    return pl.BlockSpec((rows, LANES), lambda i: (0, jnp.clip(i - lag, 0, blocks - 1)))


def lane_halves(values):
    return [values[:, :128], values[:, 128:]]


def exit_kernel(
    size,
    scaled_ref,
    turned_ref,
    weight_ref,
    x_ref,
    cot_ref,
    param_ref,
    pair_ref,
    spread_ref,
    live_ref,
    out_out,
    delta_out,
    residual_out,
    weight_out,
    total_out,
    act_ref,
    slope_ref,
    pair_sent,
    pair_got,
    pair_send,
    pair_recv,
    *exchange_refs,
):
    exchange = Exchange(size, *exchange_refs)
    step = pl.program_id(0)
    count = row_count(size)
    stream = lax.axis_index("stream")
    me = lax.axis_index("img")
    area = jnp.where(stream == 0, GLOBAL_SIDE**2, SMALL_SIDE**2).astype(f32)
    blocks = OUT_BLOCKS

    def used_lanes(block):
        lane = lax.broadcasted_iota(jnp.int32, (STEP, 128), 1) + LANES * block
        return [lane + 128 * tile < CHANNELS for tile in range(2)]

    def pair_copy(block):
        return pltpu.make_async_remote_copy(
            src_ref=pair_sent.at[block],
            dst_ref=pair_got.at[block],
            send_sem=pair_send.at[block],
            recv_sem=pair_recv.at[block],
            device_id=(1 - stream, me),
            device_id_type=MESH,
        )

    @pl.when(step == 0)
    def _():
        barrier = img_barrier(size)
        pl.semaphore_signal(
            barrier, inc=1, device_id=(1 - stream, me), device_id_type=MESH
        )
        pl.semaphore_wait(barrier, size)

    @pl.when(step < blocks)
    def _():
        slot = lax.rem(step, 4)
        for micro in range(MICRO_BATCHES):
            here = slice(HALF * micro, HALF * (micro + 1))
            act_ref[slot, here] = dot(scaled_ref[here], weight_ref[...])
        sums = Sums()
        for chunk in range(STEPS):
            for tile in range(2):
                act = act_ref[slot, chunk_rows(chunk), 128 * tile : 128 * tile + 128]
                sums.add(chunk // HALF_STEPS, tile, act, act * act)
        exchange.put(step, 0, sums.packed())

    @pl.when((step >= 1) & (step < blocks + 1))
    def _():
        block = step - 1
        slot = lax.rem(block, 4)
        total = exchange.total(step - 1, 0)
        total_out[block, 0] = total
        param = param_ref[block]
        inside = used_lanes(block)
        for micro in range(MICRO_BATCHES):
            for tile in range(2):
                lanes = slice(128 * tile, 128 * tile + 128)
                mean, inverse = moments(total, micro, tile, count)
                scale = 0.5 * inverse * param[tile : tile + 1]
                shift = 0.5 * param[2 + tile : 3 + tile] - mean * scale
                for chunk in range(HALF_STEPS * micro, HALF_STEPS * (micro + 1)):
                    here = chunk_rows(chunk)
                    act = act_ref[slot, here, lanes]
                    source = jnp.where(inside[tile], x_ref[here, lanes].astype(f32), 0.0)
                    half = 0.5 * source + (act * scale + shift)
                    bent = jnp.tanh(half)
                    out_out[here, lanes] = (
                        (half + half * bent) * live_ref[here].astype(f32)
                    ).astype(bf16)
                    slope_ref[lax.rem(block, 3), here, lanes] = (0.5 + 0.5 * bent) * (
                        1.0 + half * (1.0 - bent)
                    )
        embed = dot(pair_ref[...], out_out[...]) / area
        pair_sent[block] = embed[:8].astype(bf16).astype(f32)
        pair_copy(block).start()

    @pl.when((step >= 2) & (step < blocks + 2))
    def _():
        block = step - 2
        slot = lax.rem(block, 4)
        hold = lax.rem(block, 3)
        moment = total_out[block, 0]
        pair_copy(block).wait()
        partner = pair_got[block]
        partner = jnp.concatenate([partner, jnp.zeros_like(partner)]).astype(bf16)
        means = {
            (micro, tile): moments(moment, micro, tile, count)
            for micro in range(MICRO_BATCHES)
            for tile in range(2)
        }
        inside = used_lanes(block)
        sums = Sums()
        for chunk in range(STEPS):
            here = chunk_rows(chunk)
            live = live_ref[here].astype(f32)
            pull = dot(spread_ref[here], partner) * (PAIR_SCALE / area)
            for tile in range(2):
                lanes = slice(128 * tile, 128 * tile + 128)
                mean, inverse = means[chunk // HALF_STEPS, tile]
                upstream = jnp.where(inside[tile], cot_ref[here, lanes].astype(f32), 0.0)
                upstream = upstream * live + pull[:, lanes]
                delta = upstream * slope_ref[hold, here, lanes]
                slope_ref[hold, here, lanes] = delta
                residual_out[here, lanes] = delta.astype(bf16)
                normed = act_ref[slot, here, lanes] * inverse - mean * inverse
                sums.add(chunk // HALF_STEPS, tile, delta, delta * normed)
        exchange.put(step, 1, sums.packed())
    @pl.when(step >= 3)
    def _():
        block = step - 3
        slot = lax.rem(block, 4)
        hold = lax.rem(block, 3)
        moment = total_out[block, 0]
        total = exchange.total(step - 1, 1)
        total_out[block, 1] = total
        param = param_ref[block]
        for micro in range(MICRO_BATCHES):
            for tile in range(2):
                lanes = slice(128 * tile, 128 * tile + 128)
                back = norm_back(moment, total, micro, tile, param[tile : tile + 1], count)
                for chunk in range(HALF_STEPS * micro, HALF_STEPS * (micro + 1)):
                    here = chunk_rows(chunk)
                    delta_out[here, lanes] = back(
                        slope_ref[hold, here, lanes], act_ref[slot, here, lanes]
                    ).astype(bf16)
        weight_out[...] = dot(turned_ref[...], delta_out[...]).astype(bf16)


def norm_back(moment, total, micro, tile, gain, count):
    mean, inverse = moments(moment, micro, tile, count)
    scale = gain * inverse
    plain = total[4 * micro + tile : 4 * micro + tile + 1] / count
    along = scale * (total[4 * micro + 2 + tile : 4 * micro + 3 + tile] / count)
    slant = along * inverse
    level = scale * plain
    return lambda upstream, act: scale * upstream - (level + (act - mean) * slant)


def run_exit(size, scaled, turned, weight, x, cot, params, pair, spread, live):
    blocks = OUT_BLOCKS
    return pl.pallas_call(
        functools.partial(exit_kernel, size),
        grid=(blocks + 3,),
        out_shape=(
            jax.ShapeDtypeStruct((ROWS, CHANNELS), bf16),
            jax.ShapeDtypeStruct((ROWS, PADDED), bf16),
            jax.ShapeDtypeStruct((ROWS, PADDED), bf16),
            jax.ShapeDtypeStruct((PADDED, PADDED), bf16),
            jax.ShapeDtypeStruct((blocks, 2, 8, 128), f32),
        ),
        in_specs=[
            whole((ROWS, PADDED)),
            whole((PADDED, ROWS)),
            columns(PADDED, 0, blocks),
            columns(ROWS, 1, blocks),
            columns(ROWS, 2, blocks),
            whole((blocks, 8, 128)),
            whole((CROPS, ROWS)),
            whole((ROWS, CROPS)),
            whole((ROWS, 128)),
        ],
        out_specs=(
            columns(ROWS, 1, blocks),
            columns(ROWS, 3, blocks),
            columns(ROWS, 2, blocks),
            columns(PADDED, 3, blocks),
            pl.BlockSpec((blocks, 2, 8, 128), lambda i: (0, 0, 0, 0)),
        ),
        scratch_shapes=[
            pltpu.VMEM((4, ROWS, LANES), f32),
            pltpu.VMEM((3, ROWS, LANES), f32),
            pltpu.VMEM((blocks, 8, LANES), f32),
            pltpu.VMEM((blocks, 8, LANES), f32),
            pltpu.SemaphoreType.DMA((blocks,)),
            pltpu.SemaphoreType.DMA((blocks,)),
        ]
        + Exchange.scratch(blocks + 2, size),
        name="exit",
        compiler_params=pltpu.CompilerParams(
            collective_id=2, has_side_effects=True, vmem_limit_bytes=VMEM_LIMIT
        ),
        cost_estimate=pl.CostEstimate(
            flops=4 * ROWS * PADDED * PADDED,
            bytes_accessed=70 * 2**20,
            transcendentals=ROWS * PADDED,
        ),
    )(scaled, turned, weight, x, cot, params, pair, spread, live)


def gate_kernel(
    delta_ref, weight_ref, mixed_ref, pool_ref, block_ref, scaled_out, gate_out, block_out
):
    block = pl.program_id(0)
    block_out[...] = block_ref[...]
    first = jnp.minimum((BLOCK * block) // CHUNK, SHARDS - 3)
    row = lax.broadcasted_iota(jnp.int32, (LANES, 3 * CHUNK_PAD), 0)
    lane = lax.broadcasted_iota(jnp.int32, (LANES, 3 * CHUNK_PAD), 1)
    channel = CHUNK * (first + lane // CHUNK_PAD) + lane % CHUNK_PAD
    pick = (channel == BLOCK * block + row) & (row < BLOCK) & (lane % CHUNK_PAD < CHUNK)
    rows = pl.ds(pl.multiple_of(CHUNK_PAD * first, CHUNK_PAD), 3 * CHUNK_PAD)
    weight = dot(jnp.where(pick, 1.0, 0.0).astype(bf16), weight_ref[rows]).astype(bf16)
    grad = dot(delta_ref[...], weight, ((1,), (1,)))
    scaled_out[...] = grad
    gate_out[...] = dot(pool_ref[...], (grad * mixed_ref[...].astype(f32)).astype(bf16))


def run_gate(delta, weight, mixed, pool, block):
    return pl.pallas_call(
        gate_kernel,
        grid=(BLOCKS,),
        out_shape=(
            jax.ShapeDtypeStruct((ROWS, WIDE), f32),
            jax.ShapeDtypeStruct((CROPS, WIDE), f32),
            jax.ShapeDtypeStruct((ROWS, CHANNELS), bf16),
        ),
        in_specs=[
            whole((ROWS, PADDED)),
            whole((PADDED, PADDED)),
            columns(ROWS, 0, BLOCKS),
            whole((CROPS, ROWS)),
            columns(ROWS, 0, OUT_BLOCKS),
        ],
        out_specs=(
            columns(ROWS, 0, BLOCKS),
            columns(CROPS, 0, BLOCKS),
            columns(ROWS, 0, OUT_BLOCKS),
        ),
        name="gate",
        compiler_params=pltpu.CompilerParams(vmem_limit_bytes=VMEM_LIMIT),
        cost_estimate=pl.CostEstimate(
            flops=2 * ROWS * WIDE * PADDED, bytes_accessed=40 * 2**20, transcendentals=0
        ),
    )(delta, weight, mixed, pool, block)


def pair_lane(shape, dim):
    lane = lax.broadcasted_iota(jnp.int32, shape, dim)
    inside = lane % CHUNK_PAD
    return jnp.where(inside < CHUNK, CHUNK * (lane // CHUNK_PAD) + inside, -1)


def one_hot(match):
    return jnp.where(match, 1.0, 0.0).astype(bf16)


def prepare_kernel(x_ref, chunk_out, turned_out):
    pair = pl.program_id(0)
    depth = 384
    first = (PAIR * pair) // 128
    lanes = pl.ds(pl.multiple_of(128 * first, 128), depth)
    source = 128 * first - PAIR * pair
    there = lax.broadcasted_iota(jnp.int32, (depth, LANES), 0) + source
    pick = one_hot(there == pair_lane((depth, LANES), 1))
    chunk_out[...] = dot(x_ref[:, lanes], pick).astype(bf16)
    there = lax.broadcasted_iota(jnp.int32, (LANES, depth), 1) + source
    pick = one_hot(there == pair_lane((LANES, depth), 0))
    turned_out[...] = dot(pick, x_ref[:, lanes], ((1,), (1,))).astype(bf16)


def run_prepare(x):
    return pl.pallas_call(
        prepare_kernel,
        grid=(OUT_BLOCKS,),
        out_shape=(
            jax.ShapeDtypeStruct((ROWS, PADDED), bf16),
            jax.ShapeDtypeStruct((PADDED, ROWS), bf16),
        ),
        in_specs=[whole((ROWS, PADDED))],
        out_specs=(columns(ROWS, 0, OUT_BLOCKS), pl.BlockSpec((LANES, ROWS), lambda i: (i, 0))),
        name="prepare",
        compiler_params=pltpu.CompilerParams(vmem_limit_bytes=VMEM_LIMIT),
        cost_estimate=pl.CostEstimate(
            flops=4 * ROWS * 384 * PADDED, bytes_accessed=20 * 2**20, transcendentals=0
        ),
    )(x)


QUARTERS = CHANNELS // SQUEEZE
INNER = 512


def split(values):
    high = values.astype(bf16)
    low = (values - high.astype(f32)).astype(bf16)
    return jnp.concatenate([high, low], axis=-2)


def join(terms):
    half = terms.shape[0] // 2
    return terms[:half] + terms[half:]


def wide_place(channel):
    return channel + (LANES - BLOCK) * (channel // BLOCK)


def pair_source(pair):
    return min(128 * (wide_place(PAIR * pair) // 128), WIDE - 512)


def pair_from_wide(pair, shape, dim):
    inside = pair_lane(shape, dim)
    where = wide_place(PAIR * pair + inside) - pair_source(pair)
    there = lax.broadcasted_iota(jnp.int32, shape, 1 - dim)
    return one_hot((there == where) & (inside >= 0))


def inner_source(pair):
    return min(128 * ((PAIR // QUARTERS) * pair // 128), INNER - LANES)


def pair_from_inner(pair, quarter):
    shape = (LANES, LANES)
    inside = pair_lane(shape, 1)
    inner = lax.broadcasted_iota(jnp.int32, shape, 0) + inner_source(pair)
    return one_hot((PAIR * pair + inside == QUARTERS * inner + quarter) & (inside >= 0))


def quarters_of(block):
    first = BLOCK * block // SQUEEZE
    last = (BLOCK * block + BLOCK - 1) // SQUEEZE
    return range(first, last + 1)


def scale_kernel(
    mixed_ref,
    spread_ref,
    pooled_ref,
    squeeze_ref,
    excite_ref,
    squeeze_bias_ref,
    excite_bias_ref,
    scaled_out,
    turned_out,
    gates_out,
    pooled_out,
    inner_out,
    rows_out,
    quarter_out,
    scaled,
):
    step = pl.program_id(0)
    area = jnp.where(lax.axis_index("stream") == 0, GLOBAL_SIDE**2, SMALL_SIDE**2).astype(f32)

    @pl.when(step == 0)
    def _():
        for pair in range(OUT_BLOCKS):
            lanes = slice(pair_source(pair), pair_source(pair) + 512)
            pick = pair_from_wide(pair, (512, LANES), 1)
            picked = join(dot(split(pooled_ref[:, lanes]), pick)) / area
            pooled_out[:, LANES * pair : LANES * (pair + 1)] = picked
        inner = join(dot(split(pooled_out[...]), squeeze_ref[...])) + squeeze_bias_ref[...]
        inner_out[...] = inner
        half = 0.5 * inner
        terms = split(half + half * jnp.tanh(half))
        for pair in range(OUT_BLOCKS):
            source = terms[:, inner_source(pair) : inner_source(pair) + LANES]
            for quarter in range(QUARTERS):
                rows_out[
                    CROPS * quarter : CROPS * (quarter + 1), LANES * pair : LANES * (pair + 1)
                ] = join(dot(source, pair_from_inner(pair, quarter)))
        excite = join(dot(split(rows_out[...]), excite_ref[...]))
        for quarter in range(QUARTERS):
            here = slice(CROPS * quarter, CROPS * (quarter + 1))
            half = 0.5 * (excite[here] + excite_bias_ref[quarter : quarter + 1])
            quarter_out[here] = 0.5 + 0.5 * jnp.tanh(half)
        for block in range(BLOCKS):
            total = 0.0
            for quarter in quarters_of(block):
                shape = (INNER, LANES)
                channel = SQUEEZE * quarter + lax.broadcasted_iota(jnp.int32, shape, 0)
                lane = lax.broadcasted_iota(jnp.int32, shape, 1)
                inside = lax.broadcasted_iota(jnp.int32, shape, 0) < SQUEEZE
                pick = one_hot((channel == BLOCK * block + lane) & (lane < BLOCK) & inside)
                here = slice(CROPS * quarter, CROPS * (quarter + 1))
                total = total + dot(split(quarter_out[here]), pick)
            gates_out[:, LANES * block : LANES * (block + 1)] = total.astype(bf16)

    @pl.when(step < BLOCKS)
    def _():
        lanes = pl.ds(pl.multiple_of(LANES * step, LANES), LANES)
        for chunk in range(STEPS):
            here = chunk_rows(chunk)
            gate = dot(spread_ref[here], gates_out[:, lanes])
            scaled[here, lanes] = (mixed_ref[here].astype(f32) * gate).astype(bf16)

    @pl.when(step >= BLOCKS)
    def _():
        pair = step - BLOCKS
        depth = 512
        start = PAIR * pair
        first = jnp.minimum((start + (LANES - BLOCK) * (start // BLOCK)) // 128, WIDE // 128 - 4)
        lanes = pl.ds(pl.multiple_of(128 * first, 128), depth)

        def pick(shape, dim):
            inside = pair_lane(shape, dim)
            channel = start + inside
            place = channel + (LANES - BLOCK) * (channel // BLOCK) - 128 * first
            there = lax.broadcasted_iota(jnp.int32, shape, 1 - dim)
            return one_hot((there == place) & (inside >= 0))

        scaled_out[...] = dot(scaled[:, lanes], pick((depth, LANES), 1)).astype(bf16)
        turned_out[...] = dot(pick((LANES, depth), 0), scaled[:, lanes], ((1,), (1,))).astype(
            bf16
        )


def run_scale(mixed, spread, pooled, squeeze, excite, squeeze_bias, excite_bias):
    def pair(i):
        return jnp.maximum(i - BLOCKS, 0)

    def kept(shape):
        return pl.BlockSpec(shape, lambda i: (0, 0))

    kinds = (
        ((2 * CROPS, WIDE), bf16),
        ((CROPS, PADDED), f32),
        ((CROPS, INNER), f32),
        ((QUARTERS * CROPS, PADDED), f32),
        ((QUARTERS * CROPS, INNER), f32),
    )
    return pl.pallas_call(
        scale_kernel,
        grid=(BLOCKS + OUT_BLOCKS,),
        out_shape=(
            jax.ShapeDtypeStruct((ROWS, PADDED), bf16),
            jax.ShapeDtypeStruct((PADDED, ROWS), bf16),
        )
        + tuple(jax.ShapeDtypeStruct(*kind) for kind in kinds),
        in_specs=[
            columns(ROWS, 0, BLOCKS),
            whole((ROWS, 2 * CROPS)),
            whole((CROPS, WIDE)),
            whole((PADDED, INNER)),
            whole((PADDED, INNER)),
            whole((1, INNER)),
            whole((QUARTERS, INNER)),
        ],
        out_specs=(
            pl.BlockSpec((ROWS, LANES), lambda i: (0, pair(i))),
            pl.BlockSpec((LANES, ROWS), lambda i: (pair(i), 0)),
        )
        + tuple(kept(shape) for shape, _ in kinds),
        scratch_shapes=[pltpu.VMEM((ROWS, WIDE), bf16)],
        name="scale",
        compiler_params=pltpu.CompilerParams(vmem_limit_bytes=VMEM_LIMIT),
        cost_estimate=pl.CostEstimate(
            flops=4 * ROWS * 512 * PADDED, bytes_accessed=30 * 2**20, transcendentals=0
        ),
    )(mixed, spread, pooled, squeeze, excite, squeeze_bias, excite_bias)


def outer(left, right):
    left_high = left.astype(bf16)
    left_low = (left - left_high.astype(f32)).astype(bf16)
    right_high = right.astype(bf16)
    right_low = (right - right_high.astype(f32)).astype(bf16)
    left = jnp.concatenate([left_high, left_high, left_low])
    right = jnp.concatenate([right_high, right_low, right_high])
    return dot(left, right, ((0,), (0,)))


def squeeze_kernel(
    gate_grad_ref,
    pooled_ref,
    inner_ref,
    rows_ref,
    quarter_ref,
    squeeze_ref,
    excite_ref,
    gates_out,
    grads_out,
    bias_out,
    quarter_delta,
    inner_delta,
    pooled_delta,
):
    area = jnp.where(lax.axis_index("stream") == 0, GLOBAL_SIDE**2, SMALL_SIDE**2).astype(f32)
    bias_out[...] = jnp.zeros_like(bias_out)
    for quarter in range(QUARTERS):
        first = min(LANES * (SQUEEZE * quarter // BLOCK), WIDE - 1024)
        shape = (1024, INNER)
        inner = lax.broadcasted_iota(jnp.int32, shape, 1)
        where = wide_place(SQUEEZE * quarter + inner) - first
        there = lax.broadcasted_iota(jnp.int32, shape, 0)
        pick = one_hot((there == where) & (inner < SQUEEZE))
        grad = join(dot(split(gate_grad_ref[:, first : first + 1024]), pick))
        here = slice(CROPS * quarter, CROPS * (quarter + 1))
        gate = quarter_ref[here]
        delta = grad * gate * (1.0 - gate)
        quarter_delta[here] = delta
        bias_out[1 + quarter : 2 + quarter] = column_sum(delta)
    back = join(dot(split(quarter_delta[...]), excite_ref[...], ((1,), (1,))))
    inner_delta[...] = jnp.zeros_like(inner_delta)
    for pair in range(OUT_BLOCKS):
        lanes = slice(inner_source(pair), inner_source(pair) + LANES)
        total = 0.0
        for quarter in range(QUARTERS):
            terms = split(
                back[CROPS * quarter : CROPS * (quarter + 1), LANES * pair : LANES * (pair + 1)]
            )
            total = total + dot(terms, pair_from_inner(pair, quarter), ((1,), (1,)))
        inner_delta[:, lanes] += join(total)
    half = 0.5 * inner_ref[...]
    bent = jnp.tanh(half)
    delta = inner_delta[...] * ((0.5 + 0.5 * bent) * (1.0 + half * (1.0 - bent)))
    bias_out[0:1] = column_sum(delta)
    pooled_delta[...] = join(dot(split(delta), squeeze_ref[...], ((1,), (1,)))) / area
    for block in range(BLOCKS):
        first = min(BLOCK * block // CHUNK, SHARDS - 3)
        shape = (3 * CHUNK_PAD, LANES)
        place_in = lax.broadcasted_iota(jnp.int32, shape, 0)
        lane = lax.broadcasted_iota(jnp.int32, shape, 1)
        channel = CHUNK * (first + place_in // CHUNK_PAD) + place_in % CHUNK_PAD
        pick = (channel == BLOCK * block + lane) & (lane < BLOCK) & (place_in % CHUNK_PAD < CHUNK)
        source = pooled_delta[:, CHUNK_PAD * first : CHUNK_PAD * (first + 3)]
        gates_out[:, LANES * block : LANES * (block + 1)] = dot(
            split(source), one_hot(pick)
        ).astype(bf16)
    grads_out[:, INNER:] = outer(rows_ref[...], quarter_delta[...]).astype(bf16)
    grads_out[:, :INNER] = outer(pooled_ref[...], delta).astype(bf16)


def run_squeeze(gate_grad, pooled, inner, rows, quarter, squeeze, excite):
    vmem = pl.BlockSpec(memory_space=pltpu.VMEM)
    return pl.pallas_call(
        squeeze_kernel,
        out_shape=(
            jax.ShapeDtypeStruct((2 * CROPS, WIDE), bf16),
            jax.ShapeDtypeStruct((PADDED, 2 * INNER), bf16),
            jax.ShapeDtypeStruct((6, INNER), f32),
        ),
        in_specs=[vmem] * 7,
        out_specs=(vmem,) * 3,
        scratch_shapes=[
            pltpu.VMEM((QUARTERS * CROPS, INNER), f32),
            pltpu.VMEM((CROPS, INNER), f32),
            pltpu.VMEM((CROPS, PADDED), f32),
        ],
        name="squeeze",
        compiler_params=pltpu.CompilerParams(vmem_limit_bytes=VMEM_LIMIT),
        cost_estimate=pl.CostEstimate(
            flops=2 * 2**30, bytes_accessed=20 * 2**20, transcendentals=0
        ),
    )(gate_grad, pooled, inner, rows, quarter, squeeze, excite)


BIAS_ROWS = 24


def back_kernel(
    size,
    bias_ref,
    grad_ref,
    group_ref,
    late_group_ref,
    gates_ref,
    pooled_ref,
    spread_ref,
    act_ref,
    late_act_ref,
    turned_ref,
    conv_ref,
    x_turned_ref,
    param_ref,
    moment_ref,
    edges,
    fold_ref,
    delta_out,
    weight_out,
    conv_out,
    total_out,
    bias_out,
    *refs,
):
    if size == SHARDS:
        rest_out, *refs = refs
    (
    delta_two,
    delta_one,
    pads,
    windows,
    wide_ref,
    full_ref,
        bias_got,
        bias_sem,
        even_ref,
        odd_ref,
        *refs,
    ) = refs
    exchange = Exchange(size, *refs[:4])
    reduce_refs = refs[4:]
    step = pl.program_id(0)
    count = row_count(size)
    on_global = lax.axis_index("stream") == 0
    reducer = Reducer(reduce_refs, BACK_INSIDE, rest_out) if reduce_refs else None

    def bend(moment, micro, tile, param, at):
        mean, inverse = moments(moment, micro, tile, count)
        gain = 0.5 * param[at + tile : at + tile + 1]
        shift = 0.5 * param[at + 2 + tile : at + tile + 3]

        def both(act):
            normed = act * inverse - mean * inverse
            half = normed * gain + shift
            bent = jnp.tanh(half)
            return normed, (0.5 + 0.5 * bent) * (1.0 + half * (1.0 - bent))

        return both

    @pl.when(step == 0)
    def _():
        barrier = img_barrier(size)
        pads[...] = jnp.zeros_like(pads)
        full_ref[...] = jnp.zeros_like(full_ref)
        windows[CONV_ROWS:] = jnp.zeros_like(windows[CONV_ROWS:])
        greeted = reducer.greet(barrier) if reducer else 0
        pl.semaphore_wait(barrier, size - 1 + greeted)
        stream = lax.axis_index("stream")
        me = lax.axis_index("img")
        bias_got[me] = bias_ref[...]

        def send(step, carry):
            pltpu.make_async_remote_copy(
                src_ref=bias_ref,
                dst_ref=bias_got.at[me],
                send_sem=bias_sem.at[0],
                recv_sem=bias_sem.at[1],
                device_id=(stream, lax.rem(me + step, size)),
                device_id_type=MESH,
            ).start()
            return carry

        lax.fori_loop(1, size, send, 0)

    @pl.when(step == BLOCKS)
    def _():
        others = bias_got.at[pl.ds(0, size - 1)]
        pltpu.make_async_copy(others, others, bias_sem.at[0]).wait()
        pltpu.make_async_copy(others, others, bias_sem.at[1]).wait()
        total = bias_got[0]
        for peer in range(1, size):
            total = total + bias_got[peer]
        bias_out[...] = total

    if reducer:

        def put(tile, rows, values):
            weight_out[rows, 128 * tile : 128 * tile + 128] = values

        reducer.advance(step - 2, put, BLOCKS)

    @pl.when(step < BLOCKS)
    def _():
        slot = lax.rem(step, 2)
        moment = moment_ref[step, 1]
        param = param_ref[step]
        sums = Sums()
        for micro in range(MICRO_BATCHES):
            bends = [bend(moment, micro, tile, param, 4) for tile in range(2)]
            for chunk in range(HALF_STEPS * micro, HALF_STEPS * (micro + 1)):
                here = chunk_rows(chunk)
                gate = dot(spread_ref[here], gates_ref[...])
                pooled = dot(spread_ref[here], pooled_ref[...])
                for tile in range(2):
                    lanes = slice(128 * tile, 128 * tile + 128)
                    normed, slope = bends[tile](group_ref[here, lanes])
                    delta = (grad_ref[here, lanes] * gate[:, lanes] + pooled[:, lanes]) * slope
                    delta_two[slot, tile, here] = delta
                    sums.add(micro, tile, delta, delta * normed)
        exchange.put(step, 0, sums.packed())

    @pl.when((step >= 1) & (step < BLOCKS + 1))
    def _():
        block = step - 1
        slot = lax.rem(block, 2)
        total = exchange.total(step - 1, 0)
        total_out[block, 0] = total
        param = param_ref[block]
        moment = moment_ref[block, 1]
        backs = {
            (micro, tile): norm_back(moment, total, micro, tile, param[4 + tile : 5 + tile], count)
            for micro in range(MICRO_BATCHES)
            for tile in range(2)
        }

        def delta_rows(tile, start, length):
            here = slice(start, start + length)
            return backs[start // HALF, tile](
                delta_two[slot, tile, here], late_group_ref[here, 128 * tile : 128 * tile + 128]
            )

        same = same_group(LANES, BLOCK)
        for offset in range(9):
            full = dot(fold_ref[...], conv_ref[offset], ((1,), (1,)))
            full_ref[LANES * offset : LANES * (offset + 1), :BLOCK] = jnp.where(
                same, full, 0.0
            ).astype(bf16)

        def convolve(image):
            stack_windows(pads, windows, image, -1)
            here = slice(IMAGE_PAD * image, IMAGE_PAD * (image + 1))
            wide = dot(windows[here], full_ref[...])
            wide_ref[0, here] = wide[:, :128]
            wide_ref[1, here] = wide[:, 128:]

        moment_one = moment_ref[block, 0]

        def finish(load):
            sums = Sums()
            for micro in range(MICRO_BATCHES):
                for tile in range(2):
                    bent = bend(moment_one, micro, tile, param, 0)
                    for chunk in range(HALF_STEPS * micro, HALF_STEPS * (micro + 1)):
                        here = chunk_rows(chunk)
                        normed, slope = bent(act_ref[here, 128 * tile : 128 * tile + 128])
                        delta = load(tile, chunk) * slope
                        delta_one[slot, tile, here] = delta
                        sums.add(micro, tile, delta, delta * normed)
            exchange.put(step, 1, sums.packed())

        @pl.when(on_global)
        def _():
            pad_global(delta_rows, pads, edges)
            for image in range(IMAGE_DEV):
                convolve(image)
            finish(lambda tile, chunk: unpadded(wide_ref, tile, STEP // 8 * chunk, STEP // 8))

        @pl.when(jnp.logical_not(on_global))
        def _():
            rows_ref = delta_one.at[slot]
            for chunk in range(STEPS):
                for tile in range(2):
                    rows_ref[tile, chunk_rows(chunk)] = delta_rows(tile, STEP * chunk, STEP)
            pad_small(rows_ref, pads)
            for image in range(IMAGE_DEV):
                convolve(image)
            for chunk in range(STEPS):
                for tile in range(2):
                    rows_ref[tile, chunk_rows(chunk)] = jnp.zeros((STEP, 128), f32)
            unpad_small(wide_ref, rows_ref)
            finish(lambda tile, chunk: rows_ref[tile, chunk_rows(chunk)])

        for offset in range(9):
            grad = dot(turned_ref[0], windows[:, LANES * offset : LANES * (offset + 1)])
            pieces = []
            for group in range(4):
                here = slice(GROUP_WIDTH * group, GROUP_WIDTH * (group + 1))
                pieces.append(grad[here, here])
            even_ref[:, :GROUP_WIDTH] = jnp.concatenate(pieces)
            lines = [even_ref[pl.ds(start, BLOCK // 2, 2), :GROUP_WIDTH] for start in range(2)]
            odd_ref[:, :GROUP_WIDTH] = lines[0]
            odd_ref[:, GROUP_WIDTH : 2 * GROUP_WIDTH] = lines[1]
            conv_out[offset] = odd_ref[:, : 2 * GROUP_WIDTH].astype(bf16)

    @pl.when((step >= 2) & (step < BLOCKS + 2))
    def _():
        block = step - 2
        slot = lax.rem(block, 2)
        total = exchange.total(step - 1, 1)
        total_out[block, 1] = total
        param = param_ref[block]
        moment = moment_ref[block, 0]
        for micro in range(MICRO_BATCHES):
            for tile in range(2):
                lanes = slice(128 * tile, 128 * tile + 128)
                back = norm_back(moment, total, micro, tile, param[tile : tile + 1], count)
                for chunk in range(HALF_STEPS * micro, HALF_STEPS * (micro + 1)):
                    here = chunk_rows(chunk)
                    delta_out[here, lanes] = back(
                        delta_one[slot, tile, here], late_act_ref[here, lanes]
                    ).astype(bf16)
        grad = dot(x_turned_ref[...], delta_out[...])
        if reducer:
            reducer.begin(block, grad)
        else:
            weight_out[...] = grad.astype(bf16)


def run_back(
    size, bias, grad, group, gates, pooled, spread, act, turned, conv, x_turned, params, moment, edges, fold
):
    reduced = size == SHARDS
    return pl.pallas_call(
        functools.partial(back_kernel, size),
        grid=(max(BLOCKS + 2, BACK_INSIDE + 6) if reduced else BLOCKS + 2,),
        out_shape=(
            jax.ShapeDtypeStruct((ROWS, WIDE), bf16),
            jax.ShapeDtypeStruct((CHUNK_PAD, LANES * BACK_INSIDE), f32)
            if reduced
            else jax.ShapeDtypeStruct((PADDED, WIDE), bf16),
            jax.ShapeDtypeStruct((9, CHANNELS // 2, 2 * GROUP_WIDTH), bf16),
            jax.ShapeDtypeStruct((BLOCKS, 2, 8, 128), f32),
            jax.ShapeDtypeStruct((BIAS_ROWS, 128), f32),
        )
        + ((jax.ShapeDtypeStruct((BACK_REST,) + Reducer.SHAPE, bf16),) if reduced else ()),
        in_specs=[
            whole((BIAS_ROWS, 128)),
            columns(ROWS, 0, BLOCKS),
            columns(ROWS, 0, BLOCKS),
            columns(ROWS, 1, BLOCKS),
            columns(2 * CROPS, 0, BLOCKS),
            columns(2 * CROPS, 0, BLOCKS),
            whole((ROWS, 2 * CROPS)),
            columns(ROWS, 1, BLOCKS),
            columns(ROWS, 2, BLOCKS),
            pl.BlockSpec((1, LANES, DEEP_ROWS), lambda i: (jnp.clip(i - 1, 0, BLOCKS - 1), 0, 0)),
            pl.BlockSpec((9, BLOCK, 128), lambda i: (0, jnp.clip(i - 1, 0, BLOCKS - 1), 0)),
            whole((PADDED, ROWS)),
            whole((BLOCKS, 8, 128)),
            whole((BLOCKS, 2, 8, 128)),
            whole((2, IMAGE_PAD, 128)),
            whole((LANES, 128)),
        ],
        out_specs=(
            columns(ROWS, 2, BLOCKS),
            columns(CHUNK_PAD, 6, BACK_INSIDE) if reduced else columns(PADDED, 2, BLOCKS),
            pl.BlockSpec(
                (9, BLOCK // 2, 2 * GROUP_WIDTH), lambda i: (0, jnp.clip(i - 1, 0, BLOCKS - 1), 0)
            ),
            pl.BlockSpec((BLOCKS, 2, 8, 128), lambda i: (0, 0, 0, 0)),
            pl.BlockSpec((BIAS_ROWS, 128), lambda i: (0, 0)),
        )
        + ((pl.BlockSpec(memory_space=HBM),) if reduced else ()),
        scratch_shapes=[
            pltpu.VMEM((2, 2, ROWS, 128), f32),
            pltpu.VMEM((2, 2, ROWS, 128), f32),
            pltpu.VMEM((3, 2, PAD_ROWS, 128), f32),
            pltpu.VMEM((DEEP_ROWS, 9 * LANES), bf16),
            pltpu.VMEM((2, CONV_ROWS, 128), f32),
            pltpu.VMEM((9 * LANES, LANES), bf16),
            pltpu.VMEM((size, BIAS_ROWS, 128), f32),
            pltpu.SemaphoreType.DMA((2,)),
            pltpu.VMEM((BLOCK, 128), f32),
            pltpu.VMEM((BLOCK // 2, 128), f32),
        ]
        + Exchange.scratch(BLOCKS + 1, size)
        + (Reducer.scratch() if reduced else []),
        name="back",
        compiler_params=pltpu.CompilerParams(
            collective_id=3, has_side_effects=True, vmem_limit_bytes=VMEM_LIMIT
        ),
        cost_estimate=pl.CostEstimate(
            flops=2 * ROWS * WIDE * (PADDED + 18 * LANES),
            bytes_accessed=90 * 2**20,
            transcendentals=2 * ROWS * WIDE,
        ),
    )(bias, grad, group, group, gates, pooled, spread, act, act, turned, conv, x_turned, params, moment, edges, fold)


CONV_LINES = 1152


def gather_kernel(
    entry_ref,
    conv_ref,
    x_ref,
    target_ref,
    *refs,
):
    vectors, exit_vectors = refs[:4], refs[4:6]
    (
        entry_out,
        lines_out,
        chunk_out,
        turned_out,
        live_out,
        pool_out,
        spread_out,
        pair_out,
        pull_out,
        param_out,
        exit_param_out,
        conv_rows,
        shifted,
        lines,
        x_rows,
        chunk_rows_ref,
        turned_rows,
        send_sem,
        recv_sem,
        local_sem,
        store_sem,
    ) = refs[6:]
    stream, z, x, core = place()
    pieces = (entry_ref, conv_ref)
    wholes = (entry_out, conv_rows)
    quarters = (CHUNK_PAD // 4, CONV_LINES // 4)
    waiting = []

    def shard(k, across=0, beside=0):
        return 4 * (z ^ k) + 2 * (x ^ across) + (core ^ beside)

    def region(array, index, first, count):
        rows = quarters[array]
        return wholes[array].at[index, pl.ds(pl.multiple_of(rows * first, 16), rows * count)]

    def device(name, k=0):
        if name == "y":
            return (1 - stream, shard(0))
        return (stream, {"z": shard(k), "x": shard(0, 1), "core": shard(0, 0, 1)}[name])

    def push(arrays, slot, to, index, first, count, k=0, own=False):
        for array in arrays:
            target = region(array, index, first, count)
            source = target
            if own:
                rows = quarters[array]
                source = pieces[array].at[
                    pl.ds(pl.multiple_of(rows * first, 16), rows * count)
                ]
            pltpu.make_async_remote_copy(
                src_ref=source,
                dst_ref=target,
                send_sem=send_sem.at[array, slot],
                recv_sem=recv_sem.at[array, slot],
                device_id=device(to, k),
                device_id_type=MESH,
            ).start()
            waiting.append((array, slot, target))

    def arrive(arrays, slot, index, first, count):
        for array in arrays:
            target = region(array, index, first, count)
            pltpu.make_async_copy(target, target, recv_sem.at[array, slot]).wait()

    barrier = pltpu.get_barrier_semaphore()
    for name, k in (("z", 1), ("z", 2), ("z", 3), ("x", 0), ("y", 0), ("core", 0)):
        pl.semaphore_signal(barrier, inc=1, device_id=device(name, k), device_id_type=MESH)
    load = pltpu.make_async_copy(x_ref, x_rows, local_sem.at[2])
    load.start()
    keep = [
        pltpu.make_async_copy(pieces[array], wholes[array].at[shard(0)], local_sem.at[array])
        for array in range(2)
    ]
    for copy in keep:
        copy.start()
    pl.semaphore_wait(barrier, 6)

    entry, conv = (0,), (1,)
    for array in (conv, entry):
        push(array, 6, "x", shard(0), stream, 3, own=True)
        for k in (1, 2, 3):
            push(array, k - 1, "z", shard(0), 2 * stream, 2, k, own=True)
        push(array, 17, "core", shard(0), 0, 4, own=True)

    on_global = stream == 0

    def rows_of(shape, dim):
        row = lax.broadcasted_iota(jnp.int32, shape, dim)
        image = row // IMAGE_ROWS
        within = row - IMAGE_ROWS * image
        live = within < jnp.where(on_global, IMAGE_ROWS, SMALL_ROWS)
        return image, within, live

    def members(shape, dim):
        image, within, live = rows_of(shape, dim)
        crop = jnp.where(on_global, within // GLOBAL_SIDE**2, within // SMALL_SIDE**2)
        slot = lax.rem(lax.broadcasted_iota(jnp.int32, shape, 1 - dim), CROPS)
        target = jnp.zeros(shape, jnp.int32)
        for at in range(IMAGE_DEV):
            for small in range(SMALL_CROPS):
                target = jnp.where(
                    (image == at) & (crop == small), target_ref[at, small], target
                )
        target = jnp.where(on_global, crop, target)
        crops = jnp.where(on_global, GLOBAL_CROPS, SMALL_CROPS)
        pool = one_hot(live & (crops * image + crop == slot))
        return pool, one_hot(live & (GLOBAL_CROPS * image + target == slot))

    for at, ref in enumerate(vectors):
        values = ref[...]
        for block in range(BLOCKS):
            start = BLOCK * block
            param_out[block, 2 * at : 2 * at + 1] = values[:, start : start + 128]
            param_out[block, 2 * at + 1 : 2 * at + 2] = jnp.concatenate(
                [values[:, start + 128 : start + BLOCK], jnp.zeros((1, LANES - BLOCK), f32)], axis=1
            )
    exit_param_out[...] = jnp.zeros_like(exit_param_out)
    for at, ref in enumerate(exit_vectors):
        for tile in range(PADDED // 128):
            width = min(128, CHANNELS - 128 * tile)
            exit_param_out[tile // 2, 2 * at + tile % 2, :width] = ref[
                0, 128 * tile : 128 * tile + width
            ]
    pool_out[...], pair_out[...] = members((CROPS, ROWS), 1)
    spread, pull = members((ROWS, 2 * CROPS), 0)
    spread_out[...] = spread
    pull_out[...] = pull[:, :CROPS]
    live_out[...] = one_hot(rows_of((ROWS, 128), 0)[2])
    live_lane = jnp.where(rows_of((1, ROWS), 1)[2], 1.0, 0.0)
    stores = []

    def prepare(pair):
        if pair == 0:
            load.wait()
        slot = pair % 2
        if pair >= 2:
            for copy in stores[pair - 2]:
                copy.wait()
        first = (PAIR * pair) // 128
        depth = min(384, CHANNELS - 128 * first)
        source = 128 * first - PAIR * pair
        values = x_rows[:, 128 * first : 128 * first + depth]
        there = lax.broadcasted_iota(jnp.int32, (depth, LANES), 0) + source
        pick = one_hot(there == pair_lane((depth, LANES), 1))
        picked = dot(values, pick)
        for tile in range(2):
            lanes = slice(128 * tile, 128 * tile + 128)
            chunk_rows_ref[slot, :, lanes] = (
                picked[:, lanes] * live_out[...].astype(f32)
            ).astype(bf16)
        there = lax.broadcasted_iota(jnp.int32, (LANES, depth), 1) + source
        pick = one_hot(there == pair_lane((LANES, depth), 0))
        turned_rows[slot] = (dot(pick, values, ((1,), (1,))) * live_lane).astype(bf16)
        lanes = slice(LANES * pair, LANES * (pair + 1))
        copies = (
            pltpu.make_async_copy(chunk_rows_ref.at[slot], chunk_out.at[:, lanes], store_sem.at[0, pair]),
            pltpu.make_async_copy(turned_rows.at[slot], turned_out.at[lanes], store_sem.at[1, pair]),
        )
        for copy in copies:
            copy.start()
        stores.append(copies)

    def from_z(a, k):
        arrive(a, k - 1, shard(k), 2 * stream, 2)
        push(a, 6 + k, "x", shard(k), 2 * stream, 2)
        push(a, 2 + k, "y", shard(k), 2 * stream, 2)
        push(a, 17 + k, "core", shard(k), 2 * stream, 2)

    def from_y(a, k):
        arrive(a, 2 + k, shard(k), 2 - 2 * stream, 2)
        push(a, 9 + k, "x", shard(k), 2 - stream, 1)
        push(a, 20 + k, "core", shard(k), 2 - 2 * stream, 2)

    def from_x(a, k):
        if k == 0:
            arrive(a, 6, shard(0, 1), stream, 3)
            push(a, 13, "y", shard(0, 1), 3 * stream, 1)
            push(a, 24, "core", shard(0, 1), stream, 3)
        else:
            arrive(a, 6 + k, shard(k, 1), 2 * stream, 2)
            push(a, 13 + k, "y", shard(k, 1), 3 * stream, 1)
            push(a, 24 + k, "core", shard(k, 1), 2 * stream, 2)

    def last_x(a, k):
        arrive(a, 9 + k, shard(k, 1), 2 - stream, 1)
        push(a, 27 + k, "core", shard(k, 1), 2 - stream, 1)

    def last_y(a, k):
        arrive(a, 13 + k, shard(k, 1), 3 - 3 * stream, 1)
        push(a, 31 + k, "core", shard(k, 1), 3 - 3 * stream, 1)

    def last_core(a):
        arrive(a, 17, shard(0, 0, 1), 0, 4)
        for k in (1, 2, 3):
            arrive(a, 17 + k, shard(k, 0, 1), 2 * stream, 2)
            arrive(a, 20 + k, shard(k, 0, 1), 2 - 2 * stream, 2)
        arrive(a, 24, shard(0, 1, 1), stream, 3)
        for k in (1, 2, 3):
            arrive(a, 24 + k, shard(k, 1, 1), 2 * stream, 2)
            arrive(a, 27 + k, shard(k, 1, 1), 2 - stream, 1)
        for k in range(4):
            arrive(a, 31 + k, shard(k, 1, 1), 3 - 3 * stream, 1)

    def forward(a, between):
        between = iter(between)

        def pause():
            for work in between:
                work()
                break

        pause()
        from_z(a, 1)
        pause()
        from_z(a, 2)
        from_x(a, 0)
        pause()
        from_z(a, 3)
        from_y(a, 1)
        pause()
        from_x(a, 1)
        from_y(a, 2)
        pause()
        from_x(a, 2)
        from_y(a, 3)
        pause()
        from_x(a, 3)
        last_y(a, 0)
        last_x(a, 1)
        pause()
        last_y(a, 1)
        last_x(a, 2)
        last_y(a, 2)
        last_x(a, 3)
        last_y(a, 3)

    def straighten():
        last_core(conv)
        keep[1].wait()
        for at in range(SHARDS):
            start = LINES * at
            shifted[start : start + CONV_LINES] = conv_rows[at].astype(f32)
        lines[...] = shifted[: SHARDS * LINES].astype(bf16)
        store_lines.start()

    store_lines = pltpu.make_async_copy(lines, lines_out, local_sem.at[3])
    prepares = [functools.partial(prepare, pair) for pair in range(OUT_BLOCKS)]
    forward(conv, prepares[:3])
    forward(entry, prepares[3:6] + [straighten] + prepares[6:])
    last_core(entry)
    for array, slot, target in waiting:
        pltpu.make_async_copy(target, target, send_sem.at[array, slot]).wait()
    keep[0].wait()
    store_lines.wait()
    for pair in (6, 7):
        for copy in stores[pair]:
            copy.wait()


LINES = 1134


def run_gather(entry, conv, x, target, *vectors):
    return pl.pallas_call(
        gather_kernel,
        out_shape=(
            jax.ShapeDtypeStruct((SHARDS, CHUNK_PAD, WIDE), bf16),
            jax.ShapeDtypeStruct((SHARDS * LINES, 128), bf16),
            jax.ShapeDtypeStruct((ROWS, PADDED), bf16),
            jax.ShapeDtypeStruct((PADDED, ROWS), bf16),
            jax.ShapeDtypeStruct((ROWS, 128), bf16),
            jax.ShapeDtypeStruct((CROPS, ROWS), bf16),
            jax.ShapeDtypeStruct((ROWS, 2 * CROPS), bf16),
            jax.ShapeDtypeStruct((CROPS, ROWS), bf16),
            jax.ShapeDtypeStruct((ROWS, CROPS), bf16),
            jax.ShapeDtypeStruct((BLOCKS, 8, 128), f32),
            jax.ShapeDtypeStruct((OUT_BLOCKS, 8, 128), f32),
        ),
        in_specs=[pl.BlockSpec(memory_space=HBM)] * 3
        + [pl.BlockSpec(memory_space=pltpu.SMEM)]
        + [pl.BlockSpec(memory_space=pltpu.VMEM)] * 6,
        out_specs=(pl.BlockSpec(memory_space=HBM),) * 4
        + (pl.BlockSpec(memory_space=pltpu.VMEM),) * 7,
        scratch_shapes=[
            pltpu.VMEM((SHARDS, CONV_LINES, 128), bf16),
            pltpu.VMEM((SHARDS * LINES + 32, 128), f32),
            pltpu.VMEM((SHARDS * LINES, 128), bf16),
            pltpu.VMEM((ROWS, CHANNELS), bf16),
            pltpu.VMEM((2, ROWS, LANES), bf16),
            pltpu.VMEM((2, LANES, ROWS), bf16),
            pltpu.SemaphoreType.DMA((2, 35)),
            pltpu.SemaphoreType.DMA((2, 35)),
            pltpu.SemaphoreType.DMA((4,)),
            pltpu.SemaphoreType.DMA((2, OUT_BLOCKS)),
        ],
        name="gather",
        compiler_params=pltpu.CompilerParams(
            collective_id=4, has_side_effects=True, vmem_limit_bytes=VMEM_LIMIT
        ),
        cost_estimate=pl.CostEstimate(
            flops=4 * ROWS * 384 * PADDED, bytes_accessed=200 * 2**20, transcendentals=0
        ),
    )(entry, conv, x, target, *vectors)


def input_kernel(delta_ref, weight_ref, residual_ref, live_ref, *refs):
    block = pl.program_id(0)
    if len(refs) == 1:
        (grad_out,) = refs
    else:
        rest_ref, conv_ref, grad_out, part_out, *reduce_refs = refs
        sources = [(rest_ref, BACK_REST), (conv_ref, CONV_BLOCKS)]
        feed(Reducer(reduce_refs, BACK_REST + CONV_BLOCKS), block, sources, part_out)

    @pl.when(block < OUT_BLOCKS)
    def _():
        spans = 4
        first = jnp.minimum((LANES * block) // CHUNK, SHARDS - spans)
        depth = spans * CHUNK_PAD
        row = lax.broadcasted_iota(jnp.int32, (LANES, depth), 0) + LANES * block
        lane = lax.broadcasted_iota(jnp.int32, (LANES, depth), 1)
        channel = CHUNK * (first + lane // CHUNK_PAD) + lane % CHUNK_PAD
        pick = one_hot((channel == row) & (lane % CHUNK_PAD < CHUNK))
        rows = pl.ds(pl.multiple_of(CHUNK_PAD * first, CHUNK_PAD), depth)
        weight = dot(pick, weight_ref[rows]).astype(bf16)
        for micro in range(MICRO_BATCHES):
            here = slice(HALF * micro, HALF * (micro + 1))
            grad = dot(delta_ref[here], weight, ((1,), (1,)))
            for tile in range(2):
                lanes = slice(128 * tile, 128 * tile + 128)
                grad_out[here, lanes] = (
                    (grad[:, lanes] + residual_ref[here, lanes].astype(f32))
                    * live_ref[here].astype(f32)
                ).astype(bf16)


def run_input(delta, weight, residual, live, *rest):
    reduced = bool(rest)
    out_shape = jax.ShapeDtypeStruct((ROWS, CHANNELS), bf16)
    out_specs = columns(ROWS, 0, OUT_BLOCKS)
    in_specs = [
        whole((ROWS, WIDE)),
        whole((PADDED, WIDE)),
        columns(ROWS, 0, OUT_BLOCKS),
        whole((ROWS, 128)),
    ]
    args = [delta, weight, residual, live]
    if reduced:
        shape = (BACK_REST + CONV_BLOCKS, 2, 128, 128)
        out_shape = (out_shape, jax.ShapeDtypeStruct(shape, f32))
        out_specs = (out_specs, pl.BlockSpec(shape, lambda i: (0, 0, 0, 0)))
        in_specs += [pl.BlockSpec(memory_space=HBM)] * 2
        args += rest
    return pl.pallas_call(
        input_kernel,
        grid=(BACK_REST + CONV_BLOCKS + 4 if reduced else OUT_BLOCKS,),
        out_shape=out_shape,
        in_specs=in_specs,
        out_specs=out_specs,
        scratch_shapes=Reducer.scratch() if reduced else [],
        name="input",
        compiler_params=pltpu.CompilerParams(
            vmem_limit_bytes=VMEM_LIMIT,
            collective_id=5 if reduced else None,
            has_side_effects=reduced,
        ),
        cost_estimate=pl.CostEstimate(
            flops=2 * ROWS * WIDE * PADDED, bytes_accessed=35 * 2**20, transcendentals=0
        ),
    )(*args)


def wide_lanes(values):
    lead = values.shape[:-1]
    blocks = values.reshape(lead + (BLOCKS, BLOCK))
    padded = jnp.pad(blocks, ((0, 0),) * len(lead) + ((0, 0), (0, LANES - BLOCK)))
    return padded.reshape(lead + (WIDE,))


def narrow_lanes(values):
    lead = values.shape[:-1]
    return values.reshape(lead + (BLOCKS, LANES))[..., :BLOCK].reshape(lead + (CHANNELS,))


def gather(piece, width, size):
    across = -(-width // 128) * 128
    pads = ((0, CHUNK_PAD - CHUNK), (0, across - width))
    if size == SHARDS:
        piece = jnp.pad(piece.reshape(CHUNK, width), pads)
        return lax.all_gather(piece, "img", axis=0, tiled=True)
    pieces = lax.all_gather(piece, "img", axis=0, tiled=True).reshape(SHARDS, CHUNK, width)
    return jnp.pad(pieces, ((0, 0),) + pads).reshape(PADDED, across)


def scatter(grads, width, size):
    if size != SHARDS:
        grads = grads.reshape(SHARDS, CHUNK_PAD, -1)[:, :CHUNK, :width].reshape(-1)
    return lax.psum_scatter(grads, "img", scatter_dimension=0, tiled=True)


def shard_of(part, width, size):
    part = swap_sum(part)
    return part[:CHUNK, :width].reshape(-1) if size == SHARDS else part


def swap_sum(part):
    other = lax.ppermute(part, "stream", [(0, 1), (1, 0)])
    return part.astype(f32) + other.astype(f32)


def beside_blocks(first, blocks):
    return jnp.concatenate([first, blocks.transpose(2, 0, 1, 3).reshape(128, -1)], axis=1)


def chunked(values):
    lead = values.shape[:-1]
    values = values.reshape(lead + (SHARDS, CHUNK))
    values = jnp.pad(values, ((0, 0),) * len(lead) + ((0, 0), (0, CHUNK_PAD - CHUNK)))
    return values.reshape(lead + (PADDED,))


def unchunked(values):
    lead = values.shape[:-1]
    values = values.reshape(lead + (SHARDS, CHUNK_PAD))[..., :CHUNK]
    return values.reshape(lead + (CHANNELS,))


def row_masks(on_global, pair_target):
    positions = jnp.arange(ROWS, dtype=jnp.int32)
    image_of = positions // IMAGE_ROWS
    within = positions % IMAGE_ROWS
    live = within < jnp.where(on_global, IMAGE_ROWS, SMALL_ROWS)
    area = jnp.where(on_global, GLOBAL_SIDE**2, SMALL_SIDE**2)
    crop_of = within // area
    crop_ids = jnp.arange(CROPS, dtype=jnp.int32)
    per_image = jnp.where(on_global, GLOBAL_CROPS, SMALL_CROPS)
    pool_full = live[None] & ((image_of * per_image + crop_of)[None] == crop_ids[:, None])
    pool = pool_full.astype(bf16)
    target_rows = jnp.zeros((ROWS,), jnp.int32)
    for slot in range(SMALL_CROPS):
        target_rows = jnp.where(
            crop_of == slot, jnp.repeat(pair_target[:, slot], IMAGE_ROWS), target_rows
        )
    pair_of = image_of * GLOBAL_CROPS + jnp.where(on_global, crop_of, target_rows)
    pair = (live[None] & (pair_of[None] == crop_ids[:, None])).astype(bf16)
    live_lanes = jnp.broadcast_to(live[:, None], (ROWS, 128)).astype(bf16)
    return live, live_lanes, pool, pair


def local(
    block_in,
    out_cotangent,
    pair_target,
    entry_weight,
    entry_gain,
    entry_shift,
    group_weight,
    group_gain,
    group_shift,
    squeeze_weight,
    squeeze_bias,
    excite_weight,
    excite_bias,
    exit_weight,
    exit_gain,
    exit_shift,
):
    size = lax.axis_size("img")
    stream = lax.axis_index("stream")
    on_global = stream == 0
    edges = edge_masks()

    x = block_in[0]
    cot = out_cotangent[0]

    lines = LINES
    if size == SHARDS:
        entry_piece = wide_lanes(entry_weight.reshape(CHUNK, CHANNELS))
        entry_piece = jnp.pad(entry_piece, ((0, CHUNK_PAD - CHUNK), (0, 0)))
        piece = group_weight.reshape(lines, GROUP_WIDTH)
        piece = jnp.pad(piece, ((0, CONV_LINES - lines), (0, 128 - GROUP_WIDTH)))
        vectors = (entry_gain, entry_shift, group_gain, group_shift, exit_gain, exit_shift)
        gathered = run_gather(
            entry_piece, piece, x, pair_target, *(vector[None] for vector in vectors)
        )
        entry_mat, conv, x_chunked, x_turned, live_lanes, pool, spread, pair, pull = gathered[:9]
        params, exit_params = gathered[9:]
        entry_mat = entry_mat.reshape(PADDED, WIDE)
        conv = conv.reshape(9, CHANNELS, 128)
    else:
        def rows_of(*vectors):
            kept = wide_lanes(jnp.stack(vectors)).reshape(len(vectors), BLOCKS, 2, 128)
            return kept.transpose(1, 0, 2, 3).reshape(BLOCKS, 2 * len(vectors), 128)

        params = rows_of(entry_gain, entry_shift, group_gain, group_shift)
        exit_params = [
            jnp.pad(vector, (0, PADDED - CHANNELS)).reshape(OUT_BLOCKS, 2, 128)
            for vector in (exit_gain, exit_shift)
        ]
        exit_params = jnp.concatenate(exit_params * 2, axis=1)
        live, live_lanes, pool, pair = row_masks(on_global, pair_target)
        spread, pull = jnp.concatenate([pool.T, pool.T], axis=1), pair.T
        x_padded = jnp.where(live[:, None], x, 0)
        x_padded = jnp.pad(x_padded, ((0, 0), (0, PADDED - CHANNELS)))
        x_chunked, x_turned = run_prepare(x_padded)
        entry_mat = wide_lanes(gather(entry_weight, CHANNELS, size)[:, :CHANNELS])
        conv = lax.all_gather(group_weight, "img", axis=0, tiled=True)
        conv = conv.reshape(9, CHANNELS, GROUP_WIDTH)
        conv = jnp.pad(conv, ((0, 0), (0, 0), (0, 128 - GROUP_WIDTH)))
    squeeze_mat = gather(squeeze_weight, SQUEEZE, size)
    excite_mat = gather(excite_weight, SQUEEZE, size)
    exit_mat = gather(exit_weight, CHANNELS, size)

    fold = np.zeros((LANES, 128), np.float32)
    fold[np.arange(BLOCK), np.arange(BLOCK) % GROUP_WIDTH] = 1
    fold = jnp.asarray(fold, bf16)
    act, turned, group, mixed, pooled, moment = run_entry(
        size, x_chunked, entry_mat, conv, params, pool, edges, fold.T
    )

    inner_pad = INNER - SQUEEZE
    scaled, scaled_turned, gates, pooled, inner, inner_rows, quarter = run_scale(
        mixed,
        spread,
        pooled,
        squeeze_mat,
        excite_mat,
        jnp.pad(squeeze_bias, (0, inner_pad))[None],
        jnp.pad(excite_bias.reshape(QUARTERS, SQUEEZE), ((0, 0), (0, inner_pad))),
    )

    block_out, exit_delta, residual, exit_grad, exit_total = run_exit(
        size, scaled, scaled_turned, exit_mat, x, cot, exit_params, pair, pull, live_lanes
    )
    exit_part = scatter(exit_grad, CHANNELS, size)
    scaled_grad, gate_grad, block_out = run_gate(exit_delta, exit_mat, mixed, pool, block_out)

    pooled_gates, inner_grads, bias_rows = run_squeeze(
        gate_grad, pooled, inner, inner_rows, quarter, squeeze_mat, excite_mat
    )
    bias_rows = bias_rows.reshape(BIAS_ROWS, 128)
    entry_delta, entry_grad, conv_grad, totals, bias_totals, *entry_rest = run_back(
        size, bias_rows, scaled_grad, group, gates, pooled_gates, spread, act, turned, conv, x_turned, params,
        moment, edges, fold,
    )
    entry_delta, exit_part, inner_grads = lax.optimization_barrier(
        (entry_delta, exit_part, inner_grads)
    )
    exit_shard = shard_of(exit_part, CHANNELS, size)
    if size == SHARDS:
        inner_part = swap_sum(scatter(inner_grads, 2 * INNER, size))[:CHUNK]
        squeeze_shard = inner_part[:, :SQUEEZE].reshape(-1)
        excite_shard = inner_part[:, INNER : INNER + SQUEEZE].reshape(-1)
    else:
        squeeze_shard = shard_of(scatter(inner_grads[:, :INNER], SQUEEZE, size), SQUEEZE, size)
        excite_shard = shard_of(scatter(inner_grads[:, INNER:], SQUEEZE, size), SQUEEZE, size)
    if size == SHARDS:
        conv_lines = 256 * CONV_BLOCKS
        conv_grad = conv_grad.reshape(SHARDS, lines // 2, 2 * GROUP_WIDTH)
        conv_grad = jnp.pad(
            conv_grad,
            ((0, 0), (0, conv_lines - lines // 2), (0, 128 - 2 * GROUP_WIDTH)),
        ).reshape(4, 2, 2, CONV_BLOCKS, 2, 128, 128)
        conv_grad = conv_grad.transpose(3, 2, 1, 0, 4, 5, 6)
        input_grad, parts = run_input(
            entry_delta, entry_mat, residual, live_lanes, entry_rest[0], conv_grad
        )
        entry_grad = beside_blocks(entry_grad, parts[:BACK_REST])
        entry_shard = narrow_lanes(entry_grad[:CHUNK]).reshape(-1)
        conv_part = parts[BACK_REST:].reshape(conv_lines, 128)
        conv_shard = conv_part[: lines // 2, : 2 * GROUP_WIDTH].reshape(-1)
    else:
        input_grad = run_input(entry_delta, entry_mat, residual, live_lanes)
        entry_shard = swap_sum(scatter(narrow_lanes(entry_grad), CHANNELS, size))
        conv_part = lax.psum_scatter(
            conv_grad.reshape(-1), "img", scatter_dimension=0, tiled=True
        )
        conv_shard = swap_sum(conv_part)
    shards = (entry_shard, conv_shard, squeeze_shard, excite_shard, exit_shard)

    def folded(kept):
        kept = kept.reshape(-1, MICRO_BATCHES, 2, LANES).sum(axis=1)
        return kept[:, 1].reshape(-1), kept[:, 0].reshape(-1)

    group_gain_grad, group_shift_grad = [narrow_lanes(v) for v in folded(totals[:, 0])]
    entry_gain_grad, entry_shift_grad = [narrow_lanes(v) for v in folded(totals[:, 1])]
    exit_gain_grad, exit_shift_grad = [v[:CHANNELS] for v in folded(exit_total[:, 1])]
    bias_totals = bias_totals.reshape(6, INNER)[: 1 + QUARTERS, :SQUEEZE]
    kept = jnp.concatenate(
        [
            jnp.stack(
                [
                    entry_gain_grad,
                    entry_shift_grad,
                    group_gain_grad,
                    group_shift_grad,
                    exit_gain_grad,
                    exit_shift_grad,
                    bias_totals[1:].reshape(-1),
                ]
            ),
            jnp.pad(bias_totals[0], (0, CHANNELS - SQUEEZE))[None],
        ]
    )
    smalls = swap_sum(kept)

    return (
        block_out[None],
        input_grad[None],
        shards[0],
        smalls[0],
        smalls[1],
        shards[1],
        smalls[2],
        smalls[3],
        shards[2],
        smalls[7, :SQUEEZE],
        shards[3],
        smalls[6],
        shards[4],
        smalls[4],
        smalls[5],
    )


def solution(mesh):
    return jax.shard_map(
        local,
        mesh=mesh,
        in_specs=(
            P("stream", "img", None),
            P("stream", "img", None),
            P("img", None),
            P("img"),
            P(),
            P(),
            P("img"),
            P(),
            P(),
            P("img"),
            P(),
            P("img"),
            P(),
            P("img"),
            P(),
            P(),
        ),
        out_specs=(
            P("stream", "img", None),
            P("stream", "img", None),
            P("img"),
            P(),
            P(),
            P("img"),
            P(),
            P(),
            P("img"),
            P(),
            P("img"),
            P(),
            P("img"),
            P(),
            P(),
        ),
        check_vma=False,
    )
```
